32 devices in a mesh: seq: 2 (over x), head: 4 (over z), exp: 4 (over y, core).
Axes of the slice: x: 2, y: 2, z: 4, core: 2. Of those that a mesh axis runs over, the one named last changes fastest.
Arguments:
- x_in: bfloat16 [1024, 4096], P(('seq', 'exp'), 'head'), may hold values from -6 to 6
- z_in: bfloat16 [1024, 4096], P(('seq', 'exp'), 'head'), may hold values from -6 to 6
- b_in: bfloat16 [1024, 1024], P(('seq', 'exp'), 'head'), may hold values from -1.796875 to 1.796875
- c_in: bfloat16 [1024, 1024], P(('seq', 'exp'), 'head'), may hold values from -1.796875 to 1.796875
- dt_in: float32 [1024, 64], P(('seq', 'exp'), 'head'), may hold values from -5.4 to -1.7
- a_log: float32 [64], P('head'), may hold values from -12 to 2
- d_skip: float32 [64], P('head'), may hold values from 0.5 to 2
- norm_w: float32 [4096], P('head'), may hold values from 0.5 to 1.5
- w_out: bfloat16 [4096, 1344], P('head'), may hold values from -0.09375 to 0.09375
- resid: bfloat16 [8, 128, 1344], P(('seq', 'exp'), 'head'), may hold values from -30 to 30
- routes: int32 [8, 128, 6], P(('seq', 'exp'), 'head'), may hold values from 0 to 15, all different within a row; in each aligned block of 32 rows (0 to 31, 32 to 63, ..., all dimensions but the last counted through in order) at most 24 rows name the same one
- gates: float32 [8, 128, 6], P(('seq', 'exp'), 'head'), may hold values from 0.1 to 0.7
- moe_gain: float32 [1344], replicated, may hold values from 0.5 to 1.5
- w_up: bfloat16 [16, 1344, 928], P(('head', 'exp')), may hold values from -0.15625 to 0.15625
- w_down: bfloat16 [16, 928, 1344], P(('head', 'exp')), may hold values from -0.1875 to 0.1875
Outputs:
- output: bfloat16 [8, 128, 1344], P(('seq', 'exp'), 'head')
The draws below stay inside these ranges and needn't reach their ends.
Inputs may be any that keep to these rules, and one draw needn't show every extreme that they name: `routes`: within the 32 aligned rows of one device no expert is named more than 24 times, and in every draw some expert is named exactly 24 times within some device's rows.
All inputs are finite; a program needn't handle non-finite values.
Results may differ from the reference program's by a relative error of at most 0.018.
Values may be sent and summed in bfloat16 or wider, within the bound.
No kernel may reach another device: no remote copies, remote signals or barrier semaphores. Data moves between devices by JAX's collectives and lax.ppermute only.
A program may use at most 64 MiB of HBM per device.

```python
import math
import jax
import jax.numpy as jnp
import numpy as np
from jax import lax

D = 1344
HEADS = 64
HEAD_DIM = 64
STATE = 128
GROUPS = 8
STRETCH = 128
FFW = 928
TOPK = 6
TOK_DEV = 128
SHARDS = 8
TOKENS = 1024
INNER = 4096
ROWS_MOE = 32
EXPERTS = 16
CAP = 24


def draw_dt_in(key, part):
    subkeys = jax.random.split(jax.random.fold_in(key, 11), 4)
    blocks = TOKENS // TOK_DEV
    base_values = jax.random.uniform(subkeys[0], (blocks, TOK_DEV, HEADS), jnp.float32, -3.6, -2.6)
    coin = jax.random.uniform(subkeys[1], (blocks, 1, HEADS), jnp.float32)
    high_offset = jax.random.uniform(subkeys[2], (blocks, 1, HEADS), jnp.float32, 0.4, 0.9)
    low_offset = jax.random.uniform(subkeys[3], (blocks, 1, HEADS), jnp.float32, -1.8, -1.2)
    offset = jnp.where(coin < 0.5, high_offset, low_offset)
    return (base_values + offset).reshape(TOKENS, HEADS)


def draw_a_log(key, part):
    subkeys = jax.random.split(jax.random.fold_in(key, 23), 4)
    choose = jax.random.uniform(subkeys[0], (HEADS,), jnp.float32)
    quick = jnp.log(jax.random.uniform(subkeys[1], (HEADS,), jnp.float32, 0.45, 0.75))
    lasting = jnp.log(jax.random.uniform(subkeys[2], (HEADS,), jnp.float32, 0.7, 2.3) / (0.045 * TOKENS))
    between = lasting + jax.random.uniform(subkeys[3], (HEADS,), jnp.float32) * (quick - lasting)
    return jnp.where(choose < 0.4, quick, jnp.where(choose < 0.8, lasting, between))


def draw_resid(key, part):
    subkeys = jax.random.split(jax.random.fold_in(key, 37), 3)
    full_shape = (SHARDS, TOK_DEV, D)
    row_scale = jnp.exp(jax.random.uniform(subkeys[1], (SHARDS, TOK_DEV, 1), jnp.float32, jnp.log(0.2), jnp.log(2.0)))
    col_scale = jnp.exp(jax.random.uniform(subkeys[2], (1, 1, D), jnp.float32, jnp.log(0.3), jnp.log(3.0)))
    values = jnp.clip(jax.random.normal(subkeys[0], full_shape, jnp.float32), -3.0, 3.0)
    return (values * row_scale * col_scale).astype(jnp.bfloat16)


def block_levels(key, shape, cuts, least, top_value):
    level = 1.0
    for axis_at, blocks in cuts:
        draws = jax.random.uniform(jax.random.fold_in(jax.random.fold_in(key, 6), axis_at), (blocks,), jnp.float32, least / len(cuts), top_value / len(cuts))
        level = level * jnp.repeat(jnp.exp(draws), shape[axis_at] // blocks).reshape((-1,) + (1,) * (len(shape) - 1 - axis_at))
    return level


def deal_out(key, own, number, rows, amount, top, bound, slope):
    ranking = jax.random.permutation(key, amount)
    packed, ordinary = portions_of(amount, rows * top, bound, slope, True), portions_of(amount, rows * top, bound, slope, False)
    places = jnp.arange(amount)

    def named(sizes, offset_by):
        used = int((sizes > 0).sum())
        fixed = max(1, used // 4)
        shifted = fixed + (places - fixed + offset_by * (used - fixed)) % max(1, amount - fixed)
        return jnp.zeros((amount,), jnp.int32).at[ranking[jnp.where(places < fixed, places, shifted)]].set(jnp.asarray(sizes, jnp.int32))

    sizes = jnp.where(number % 4 == 0, named(packed, number // 4), named(ordinary, number - number // 4 - 1))
    mixed = jax.random.permutation(jax.random.fold_in(own, 3), amount)
    source_of, receiver = mixed[0:amount // 2 * 2:2], mixed[1:amount // 2 * 2:2]
    room = jnp.minimum(sizes[source_of] - 1, bound - sizes[receiver]) // 2
    room = jnp.where((source_of == ranking[0]) | (receiver == ranking[0]) | (sizes[receiver] == 0), 0, jnp.maximum(room, 0))
    shifted = jax.random.randint(jax.random.fold_in(own, 4), (amount // 2,), 0, 1 << 20) % (room + 1)
    sizes = sizes.at[source_of].add(-shifted).at[receiver].add(shifted)
    items = jnp.searchsorted(jnp.cumsum(sizes), jnp.arange(rows * top), side="right").astype(jnp.int32)
    table = items.reshape(top, rows).T
    table = table[jax.random.permutation(jax.random.fold_in(own, 1), rows)]
    offset_by = jax.random.randint(jax.random.fold_in(own, 2), (rows, 1), 0, top)
    return jnp.take_along_axis(table, (jnp.arange(top)[None, :] + offset_by) % top, axis=1)


def portions_of(count, total, bound, lean, full):
    loads = [(1 << 20) // math.isqrt(rank ** lean) + 1 for rank in range(1, count + 1)]
    largest = bound if full else min(bound, max(-(-total // count), total * loads[0] // sum(loads)))
    least = 1 if total - largest >= count - 1 else 0
    counts, rest = [largest] + [least] * (count - 1), total - largest - least * (count - 1)
    while rest > 0:
        movable = [i for i in range(1, count) if counts[i] < largest] or [i for i in range(1, count) if counts[i] < bound]
        whole, remaining = sum([loads[i] for i in movable]), rest
        for i in movable:
            addition = min(bound - counts[i], max(1, remaining * loads[i] // whole), rest)
            counts[i] = counts[i] + addition
            rest = rest - addition
    return np.array(counts)


def noise(key, extent, spread, reach, cuts=(), held_as=jnp.bfloat16):
    drawn = jax.random.normal(key, extent, jnp.float32) * spread
    if len(cuts) > 0:
        drawn = block_levels(key, extent, cuts, -0.22, 0.18) * drawn
    return jnp.clip(drawn, min=-reach, max=reach).astype(held_as)


def setup_inputs(seed: int = 0) -> dict:
    arg_keys = jax.random.split(jax.random.key(seed), 16)
    x_in = noise(arg_keys[0], (TOKENS, INNER), 1.0, 6.0, ((0, 8), (1, 4)))
    z_in = noise(arg_keys[1], (TOKENS, INNER), 1.0, 6.0, ((0, 8), (1, 4)))
    b_in = noise(arg_keys[2], (TOKENS, GROUPS * STATE), 0.3, 1.796875, ((0, 8), (1, 4)))
    c_in = noise(arg_keys[3], (TOKENS, GROUPS * STATE), 0.3, 1.796875, ((0, 8), (1, 4)))
    dt_in = draw_dt_in(jax.random.fold_in(arg_keys[15], 71), 0)
    a_log = draw_a_log(jax.random.fold_in(arg_keys[15], 71), 0)
    d_skip = jnp.clip(0.5 + 1.5 * jax.random.uniform(arg_keys[6], (HEADS,), jnp.float32) ** block_levels(arg_keys[6], (HEADS,), ((0, 4),), -0.2, 0.2), 0.5, 2.0)
    norm_w = jnp.clip(1.0 + 0.1 * jax.random.normal(arg_keys[7], (INNER,), jnp.float32), 0.5, 1.5)
    w_out = noise(arg_keys[8], (INNER, D), INNER ** -0.5, 0.09375, ((0, 4),))
    resid = draw_resid(jax.random.fold_in(arg_keys[15], 71), 0)
    routes_keys = jax.random.split(jax.random.fold_in(arg_keys[10], 1), SHARDS * TOK_DEV // ROWS_MOE)
    routes_turns = jax.random.permutation(jax.random.fold_in(arg_keys[10], 3), SHARDS * TOK_DEV // ROWS_MOE)
    routes = jax.vmap(lambda own, number: deal_out(jax.random.fold_in(arg_keys[10], 2), own, number, ROWS_MOE, EXPERTS, TOPK, CAP, 2))(routes_keys, routes_turns).reshape((SHARDS, TOK_DEV, TOPK))
    gates = jnp.clip(0.1 + 0.59999999 * jax.random.uniform(arg_keys[11], (SHARDS, TOK_DEV, TOPK), jnp.float32) ** block_levels(arg_keys[11], (SHARDS, TOK_DEV, TOPK), ((0, 8), (1, 4)), -0.2, 0.2), 0.1, 0.7)
    moe_gain = jnp.clip(1.0 + 0.1 * jax.random.normal(arg_keys[12], (D,), jnp.float32), 0.5, 1.5)
    w_up = noise(arg_keys[13], (EXPERTS, D, FFW), D ** -0.5, 0.15625, ((0, 16),))
    w_down = noise(arg_keys[14], (EXPERTS, FFW, D), FFW ** -0.5, 0.1875, ((0, 16),))
    return dict(x_in=x_in, z_in=z_in, b_in=b_in, c_in=c_in, dt_in=dt_in, a_log=a_log, d_skip=d_skip, norm_w=norm_w, w_out=w_out, resid=resid, routes=routes, gates=gates, moe_gain=moe_gain, w_up=w_up, w_down=w_down)


precise = lax.Precision.HIGHEST

def to_low(values):
    return lax.optimization_barrier(values.astype(jnp.bfloat16)).astype(jnp.float32)

def stretch_pass(carry_state, pieces):
    x_part, b_part, c_part, rate_part, step_part = pieces
    per_group = x_part.shape[1] // b_part.shape[1]
    b_heads = jnp.repeat(b_part, per_group, axis=1).astype(jnp.float32)
    c_heads = jnp.repeat(c_part, per_group, axis=1).astype(jnp.float32)
    x_float = x_part.astype(jnp.float32)
    cumulative = jnp.cumsum(rate_part, axis=0)
    cum_heads = cumulative.T
    distance = cum_heads[:, :, None] - cum_heads[:, None, :]
    length = cumulative.shape[0]
    causal = (jnp.arange(length)[:, None] >= jnp.arange(length)[None, :])[None]
    decay_mat = jnp.where(causal, jnp.exp(jnp.where(causal, distance, 0.0)), 0.0)
    weighting = decay_mat * step_part.T[:, None, :]
    scores = jnp.einsum('thn,shn->hts', c_heads, b_heads, precision=precise)
    mixing = to_low(scores * weighting)
    inside = jnp.einsum('hts,shp->thp', mixing, x_float, precision=precise)
    state_low = to_low(carry_state)
    carried = jnp.exp(cumulative)[:, :, None] * jnp.einsum('thn,hpn->thp', c_heads, state_low, precision=precise)
    tail_weight = jnp.exp(cumulative[-1][None, :] - cumulative) * step_part
    weighted_x = to_low(tail_weight[:, :, None] * x_float)
    update = jnp.einsum('shp,shn->hpn', weighted_x, b_heads, precision=precise)
    new_state = jnp.exp(cumulative[-1])[:, None, None] * carry_state + update
    return (new_state, inside + carried)

def by_stretch(values):
    return values.reshape((values.shape[0] // STRETCH, STRETCH) + values.shape[1:])

def mixer(x_in, z_in, b_in, c_in, dt_in, a_log, d_skip, norm_w):
    length, head_count = dt_in.shape
    groups = b_in.shape[1] // STATE
    low_values = x_in.reshape(length, head_count, HEAD_DIM)
    values = low_values.astype(jnp.float32)
    b_groups = b_in.reshape(length, groups, STATE)
    c_groups = c_in.reshape(length, groups, STATE)
    step_size = jax.nn.softplus(dt_in)
    log_rate = -step_size * jnp.exp(a_log)[None, :]
    zero_state = jnp.zeros((head_count, HEAD_DIM, STATE), jnp.float32)
    last_state, local_out = lax.scan(stretch_pass, zero_state, (by_stretch(low_values), by_stretch(b_groups), by_stretch(c_groups), by_stretch(log_rate), by_stretch(step_size)))
    ssm_out = local_out.reshape(length, head_count, HEAD_DIM) + d_skip[None, :, None] * values
    gated_out = ssm_out * jax.nn.silu(z_in.astype(jnp.float32).reshape(length, head_count, HEAD_DIM))
    grouped = gated_out.reshape(length, groups, -1)
    inverse = lax.rsqrt(lax.optimization_barrier(jnp.mean(grouped * grouped, axis=2, keepdims=True)) + 1e-05)
    return ((grouped * inverse).reshape(length, head_count * HEAD_DIM) * norm_w[None, :]).astype(jnp.bfloat16)

def experts(moe_in, routes, gates, w_up, w_down):
    flat_routes = routes.reshape(-1, TOPK)
    flat_gates = gates.reshape(-1, TOPK)
    length = moe_in.shape[0]
    limit = length // ROWS_MOE * CAP

    def one_expert(summed, expert):
        routed = flat_routes == expert
        weighting = lax.optimization_barrier(jnp.sum(jnp.where(routed, flat_gates, 0.0), axis=1))
        picked = jnp.any(routed, axis=1)
        row_index = jnp.nonzero(picked, size=limit, fill_value=0)[0].astype(jnp.int32)
        row_block = moe_in[row_index].astype(jnp.float32)
        up_proj = jnp.dot(row_block, w_up[expert].astype(jnp.float32), precision=precise, preferred_element_type=jnp.float32)
        activated = jnp.square(jnp.maximum(up_proj, 0.0)).astype(jnp.bfloat16)
        expert_out = jnp.dot(activated.astype(jnp.float32), w_down[expert].astype(jnp.float32), precision=precise, preferred_element_type=jnp.float32).astype(jnp.bfloat16)
        filled = jnp.arange(limit) < jnp.sum(picked.astype(jnp.int32))
        factor = jnp.where(filled, weighting[row_index], 0.0)
        return (summed.at[row_index].add(expert_out.astype(jnp.float32) * factor[:, None]), None)
    start_sum = jnp.zeros((length, moe_in.shape[1]), jnp.float32)
    moe_sum, unused = lax.scan(one_expert, start_sum, jnp.arange(EXPERTS, dtype=jnp.int32))
    return moe_sum

def reference(x_in, z_in, b_in, c_in, dt_in, a_log, d_skip, norm_w, w_out, resid, routes, gates, moe_gain, w_up, w_down):
    normed = mixer(x_in, z_in, b_in, c_in, dt_in, a_log, d_skip, norm_w)
    mixed = jnp.dot(normed, w_out, preferred_element_type=jnp.float32)
    hidden = (resid.reshape(-1, D).astype(jnp.float32) + mixed).astype(jnp.bfloat16)
    hidden_f32 = hidden.astype(jnp.float32)
    inverse = lax.rsqrt(lax.optimization_barrier(jnp.mean(hidden_f32 * hidden_f32, axis=1, keepdims=True)) + 1e-05)
    moe_in = (hidden_f32 * inverse * moe_gain[None, :]).astype(jnp.bfloat16)
    moe_sum = experts(moe_in, routes, gates, w_up, w_down)
    return (hidden_f32 + moe_sum).astype(jnp.bfloat16).reshape(resid.shape)
```

```python
import functools

import jax
import jax.numpy as jnp
from jax import lax
from jax.experimental import pallas as pl
from jax.experimental.pallas import tpu as pltpu
from jax.sharding import PartitionSpec as P

HEAD_DIM = 64
STATE = 128
LANES = 128
TILE = 16
FAR = -1e30
F32 = jnp.float32
BF16 = jnp.bfloat16


def call(kernel, outs, name, megabytes=16):
    return pl.pallas_call(
        kernel,
        out_shape=outs,
        name=name,
        compiler_params=pltpu.CompilerParams(vmem_limit_bytes=megabytes << 20),
    )


def struct(shape, dtype):
    return jax.ShapeDtypeStruct(shape, dtype)


def decays(dt, a_log):
    step = jnp.maximum(dt, 0.0) + jnp.log1p(jnp.exp(-jnp.abs(dt)))
    rate = -step * jnp.exp(a_log)
    length = dt.shape[0]
    row = lax.broadcasted_iota(jnp.int32, (length, length), 0)
    col = lax.broadcasted_iota(jnp.int32, (length, length), 1)
    lower = (row >= col).astype(F32)
    cum = jnp.dot(lower, rate, precision=lax.Precision.HIGHEST, preferred_element_type=F32)
    return step, cum


def pair_lanes(values, pair):
    rows = values.shape[0]
    lane = lax.broadcasted_iota(jnp.int32, (rows, LANES), 1)
    left = jnp.broadcast_to(values[:, 2 * pair : 2 * pair + 1], (rows, LANES))
    right = jnp.broadcast_to(values[:, 2 * pair + 1 : 2 * pair + 2], (rows, LANES))
    return jnp.where(lane < HEAD_DIM, left, right)


def state_kernel(x_ref, b_ref, dt_ref, a_ref, packed_ref):
    step, cum = decays(dt_ref[...], a_ref[...])
    total = cum[-1:, :]
    tail = jnp.exp(total - cum) * step
    pairs = packed_ref.shape[0]
    groups = b_ref.shape[1] // STATE
    for pair in range(pairs):
        group = pair * groups // pairs
        x_pair = x_ref[:, pair * LANES : (pair + 1) * LANES].astype(F32)
        weighted = (pair_lanes(tail, pair) * x_pair).astype(BF16)
        b_group = b_ref[:, group * STATE : (group + 1) * STATE]
        state = lax.dot_general(
            b_group, weighted, (((0,), (0,)), ((), ())), preferred_element_type=F32
        )
        packed_ref[pair, 0:STATE, :] = state.astype(BF16)
        wide = jnp.broadcast_to(pair_lanes(total, pair), (TILE, LANES))
        high = wide.astype(BF16).astype(F32)
        row = lax.broadcasted_iota(jnp.int32, (TILE, LANES), 0)
        packed_ref[pair, STATE : STATE + TILE, :] = jnp.where(row == 0, high, wide - high).astype(BF16)


def inside_kernel(x_ref, b_ref, c_ref, dt_ref, a_ref, d_ref, out_ref):
    step, cum = decays(dt_ref[...], a_ref[...])
    cum_rows, step_rows = cum.T, step.T
    length = dt_ref.shape[0]
    pairs = x_ref.shape[1] // LANES
    groups = b_ref.shape[1] // STATE
    row = lax.broadcasted_iota(jnp.int32, (length, length), 0)
    col = lax.broadcasted_iota(jnp.int32, (length, length), 1)
    lane = lax.broadcasted_iota(jnp.int32, (length, LANES), 1)
    for group in range(groups):
        span = slice(group * STATE, (group + 1) * STATE)
        scores = lax.dot_general(
            c_ref[:, span], b_ref[:, span], (((1,), (1,)), ((), ())), preferred_element_type=F32
        )
        scores = jnp.where(row >= col, scores, 0.0)
        for pair in range(group * pairs // groups, (group + 1) * pairs // groups):
            x_pair = x_ref[:, pair * LANES : (pair + 1) * LANES]
            halves = []
            for head in (2 * pair, 2 * pair + 1):
                distance = cum[:, head : head + 1] - cum_rows[head : head + 1, :]
                decay = jnp.exp(jnp.where(row >= col, distance, FAR))
                mixing = (scores * (decay * step_rows[head : head + 1, :])).astype(BF16)
                halves.append(jnp.dot(mixing, x_pair, preferred_element_type=F32))
            inside = jnp.where(lane < HEAD_DIM, halves[0], halves[1])
            skip = pair_lanes(d_ref[...], pair) * x_pair.astype(F32)
            out_ref[:, pair * LANES : (pair + 1) * LANES] = inside + skip


def chain_kernel(packed_ref, out_ref):
    carry = jnp.zeros(packed_ref.shape[1:2] + (STATE, LANES), F32)
    for shard in range(packed_ref.shape[0]):
        out_ref[shard] = carry.astype(BF16)
        if shard < packed_ref.shape[0] - 1:
            block = packed_ref[shard].astype(F32)
            total = block[:, STATE : STATE + 1, :] + block[:, STATE + 1 : STATE + 2, :]
            carry = jnp.exp(total) * carry + block[:, 0:STATE, :]


def states_before(packed):
    pairs = packed.shape[0]
    seq, exp = lax.axis_size("seq"), lax.axis_size("exp")
    axes = ("seq", "exp") if pairs % (seq * exp) == 0 else ("exp",)
    shards = seq * exp if len(axes) == 2 else exp
    here = pairs // shards
    got = lax.all_to_all(packed, axes, split_axis=0, concat_axis=0, tiled=True)
    got = got.reshape(shards, here, STATE + TILE, LANES)
    if len(axes) == 2:
        before = call(chain_kernel, struct((shards, here, STATE, LANES), BF16), "chain")(got)
    else:
        block = got.astype(F32)
        totals, states = block[:, :, STATE : STATE + 1] + block[:, :, STATE + 1 : STATE + 2], block[:, :, :STATE]

        def walk(carry, item):
            return (carry[0] + item[0], jnp.exp(item[0]) * carry[1] + item[1]), carry

        zero = (jnp.zeros(totals.shape[1:], F32), jnp.zeros(states.shape[1:], F32))
        span, inner = lax.scan(walk, zero, (totals, states))
        everything = jax.tree.map(lambda part: lax.all_gather(part.astype(BF16), "seq").astype(F32), span)
        unused, outer = lax.scan(walk, zero, everything)
        chain = lax.dynamic_index_in_dim(outer[1], lax.axis_index("seq"), 0, keepdims=False)
        before = (jnp.exp(inner[0]) * chain[None] + inner[1]).astype(BF16)
    before = before.reshape(pairs, STATE, LANES)
    return lax.all_to_all(before, axes, split_axis=0, concat_axis=0, tiled=True)


def mixed_kernel(place_ref, local_ref, z_ref, c_ref, dt_ref, a_ref, norm_ref, before_ref, w_ref, *rest):
    outs, normed_ref = rest[:-1], rest[-1]
    step, cum = decays(dt_ref[...], a_ref[...])
    grown = jnp.exp(cum)
    pairs = before_ref.shape[0]
    groups = c_ref.shape[1] // STATE
    per_group = pairs // groups
    for group in range(groups):
        c_group = c_ref[:, group * STATE : (group + 1) * STATE]
        gated, squares = [], 0.0
        for pair in range(group * per_group, (group + 1) * per_group):
            span = slice(pair * LANES, (pair + 1) * LANES)
            carried = jnp.dot(c_group, before_ref[pair], preferred_element_type=F32)
            out = local_ref[:, span] + pair_lanes(grown, pair) * carried
            z = z_ref[:, span].astype(F32)
            value = out * (z / (1.0 + jnp.exp(-z)))
            gated.append(value)
            squares = squares + value * value
        mean = jnp.sum(squares, axis=1, keepdims=True) / (per_group * LANES)
        inverse = lax.rsqrt(mean + 1e-05)
        for offset, value in enumerate(gated):
            pair = group * per_group + offset
            span = slice(pair * LANES, (pair + 1) * LANES)
            normed_ref[:, span] = (value * inverse * norm_ref[:, span]).astype(BF16)
    count, rows = len(outs), outs[0].shape[0]
    blocks = []
    for shift in range(count):
        owner = lax.rem(place_ref[0] - shift + count, count)
        blocks.append(normed_ref[pl.ds(pl.multiple_of(owner * rows, rows), rows), :])
    product = jnp.dot(jnp.concatenate(blocks, axis=0), w_ref[...], preferred_element_type=F32)
    for shift in range(count):
        outs[shift][...] = product[shift * rows : (shift + 1) * rows].astype(BF16)


def rows_kernel(experts, resid_ref, routes_ref, gates_ref, gain_ref, *rest):
    parts, hidden_ref, rows_ref = rest[:-2], rest[-2], rest[-1]
    mixed = parts[0][...].astype(F32)
    for part in parts[1:]:
        mixed = mixed + part[...].astype(F32)
    hidden = (resid_ref[0].astype(F32) + mixed).astype(BF16)
    hidden_ref[...] = hidden
    value = hidden.astype(F32)
    scale = lax.rsqrt(jnp.mean(value * value, axis=1, keepdims=True) + 1e-05)
    width = value.shape[1]
    start = width // LANES * LANES
    extent = rows_ref.shape[1] - start
    count = value.shape[0]
    lane = lax.broadcasted_iota(jnp.int32, (count, extent), 1) + start - width
    expert = jnp.where(lane >= experts, lane - experts, lane)
    gate = jnp.zeros((count, extent), F32)
    for pick in range(routes_ref.shape[2]):
        same = routes_ref[0, :, pick : pick + 1] == expert
        gate = gate + jnp.where(same, gates_ref[0, :, pick : pick + 1], 0.0)
    high = gate.astype(BF16).astype(F32)
    gate = jnp.where(lane < experts, high, jnp.where(lane < 2 * experts, gate - high, 0.0))
    rows_ref[:, start:] = gate.astype(BF16)
    rows_ref[:, :width] = (value * scale * gain_ref[...]).astype(BF16)


def expert_kernel(experts, place_ref, rows_ref, up_ref, down_ref, near_ref, far_ref):
    width = up_ref.shape[1]
    start = width // LANES * LANES
    up = jnp.dot(rows_ref[:, :width], up_ref[0], preferred_element_type=F32)
    up = jnp.maximum(up, 0.0)
    activated = (up * up).astype(BF16)
    tail = rows_ref[:, start:].astype(F32)
    lane = lax.broadcasted_iota(jnp.int32, tail.shape, 1) + start - width
    mine = (lane == place_ref[1]) | (lane == place_ref[1] + experts)
    gate = jnp.sum(jnp.where(mine, tail, 0.0), axis=1, keepdims=True)
    out = jnp.dot(activated, down_ref[0], preferred_element_type=F32) * gate
    half = near_ref.shape[0]
    near_ref[...] = out[:half].astype(BF16)
    far_ref[...] = out[half:].astype(BF16)


def sum_kernel(kept_ref, got_ref, *outs):
    total = kept_ref[...].astype(F32) + got_ref[...].astype(F32)
    at = 0
    for out in outs:
        out[...] = total[at : at + out.shape[0]].astype(BF16)
        at += out.shape[0]


def last_kernel(hidden_ref, *rest):
    parts, out_ref = rest[:-1], rest[-1]
    total = parts[0][...].astype(F32)
    for part in parts[1:]:
        total = total + part[...].astype(F32)
    out_ref[0] = (hidden_ref[...].astype(F32) + total).astype(BF16)


def moved(value, axis, target):
    size = lax.axis_size(axis)
    return lax.ppermute(value, axis, [(i, target(i, size)) for i in range(size)])


def along_head(shift):
    return lambda i, size: (i + shift) % size


def along_chips(shift):
    return lambda i, size: (i // 2 + shift) % (size // 2) * 2 + i % 2


def partner(i, size):
    return i ^ 1


def per_device(
    x_in, z_in, b_in, c_in, dt_in, a_log, d_skip, norm_w, w_out, resid, routes, gates, moe_gain, w_up, w_down
):
    length, heads = dt_in.shape
    channels = x_in.shape[1]
    model = w_out.shape[1]
    head_size, exp_size = lax.axis_size("head"), lax.axis_size("exp")
    chips = exp_size // 2
    rows = resid.shape[1]
    experts = head_size * exp_size
    place = jnp.stack(
        [lax.axis_index("head"), lax.axis_index("head") * exp_size + lax.axis_index("exp")]
    ).astype(jnp.int32)
    a_row, d_row = a_log[None], d_skip[None]
    pairs = channels // LANES
    packed = call(state_kernel, struct((pairs, STATE + TILE, LANES), BF16), "state")(x_in, b_in, dt_in, a_row)
    local = call(inside_kernel, struct((length, channels), F32), "inside")(x_in, b_in, c_in, dt_in, a_row, d_row)
    before = states_before(packed)
    smem = pl.BlockSpec(memory_space=pltpu.SMEM)
    vmem = pl.BlockSpec(memory_space=pltpu.VMEM)
    mixed = pl.pallas_call(
        mixed_kernel,
        out_shape=[struct((rows, model), BF16)] * head_size,
        in_specs=[smem] + [vmem] * 8,
        scratch_shapes=[pltpu.VMEM((length, channels), BF16)],
        compiler_params=pltpu.CompilerParams(vmem_limit_bytes=24 << 20),
        name="mixed",
    )(place, local, z_in, c_in, dt_in, a_row, norm_w[None], before, w_out)
    parts = [mixed[0]] + [moved(mixed[s], "head", along_head(-s)) for s in range(1, head_size)]
    wide = -(-(model + 2 * experts) // LANES) * LANES
    hidden, own = call(
        functools.partial(rows_kernel, experts),
        [struct((rows, model), BF16), struct((rows, wide), BF16)],
        "rows",
    )(resid, routes, gates, moe_gain[None], *parts)
    by_head = jnp.concatenate([own] + [moved(own, "head", along_head(s)) for s in range(1, head_size)], axis=0)
    by_chip = jnp.concatenate(
        [by_head] + [moved(by_head, "exp", along_chips(s)) for s in range(1, chips)], axis=0
    )
    everything = jnp.concatenate([by_chip, moved(by_chip, "exp", partner)], axis=0)
    half = by_chip.shape[0]
    near, far = pl.pallas_call(
        functools.partial(expert_kernel, experts),
        out_shape=[struct((half, model), BF16)] * 2,
        in_specs=[smem] + [vmem] * 3,
        compiler_params=pltpu.CompilerParams(vmem_limit_bytes=32 << 20),
        name="experts",
    )(place, everything, w_up, w_down)
    quarter = half // chips
    sums = call(sum_kernel, [struct((quarter, model), BF16)] * chips, "sum")(near, moved(far, "exp", partner))
    kept = sums[0]
    for s in range(1, chips):
        got = moved(sums[s], "exp", along_chips(-s))
        count = head_size if s == chips - 1 else 1
        kept = call(sum_kernel, [struct((quarter // count, model), BF16)] * count, "sum")(kept, got)
        kept = kept[0] if count == 1 else kept
    back = [kept[0]] + [moved(kept[s], "head", along_head(-s)) for s in range(1, head_size)]
    return call(last_kernel, struct(resid.shape, BF16), "last")(hidden, *back)


def solution(mesh):
    placed = (
        P(("seq", "exp"), "head"),
        P(("seq", "exp"), "head"),
        P(("seq", "exp"), "head"),
        P(("seq", "exp"), "head"),
        P(("seq", "exp"), "head"),
        P("head"),
        P("head"),
        P("head"),
        P("head", None),
        P(("seq", "exp"), "head", None),
        P(("seq", "exp"), "head", None),
        P(("seq", "exp"), "head", None),
        P(),
        P(("head", "exp"), None, None),
        P(("head", "exp"), None, None),
    )
    return jax.shard_map(
        per_device,
        mesh=mesh,
        in_specs=placed,
        out_specs=P(("seq", "exp"), "head", None),
        check_vma=False,
    )
```

```python
import functools

import jax
import jax.numpy as jnp
from jax import lax
from jax.experimental import pallas as pl
from jax.experimental.pallas import tpu as pltpu
from jax.sharding import PartitionSpec as P

HEAD_DIM = 64
STATE = 128
LANES = 128
TILE = 16
FAR = -1e30
F32 = jnp.float32
BF16 = jnp.bfloat16
HBM = pl.BlockSpec(memory_space=pltpu.HBM)
VMEM = pl.BlockSpec(memory_space=pltpu.VMEM)
SMEM = pl.BlockSpec(memory_space=pltpu.SMEM)
NT = (((1,), (1,)), ((), ()))


def struct(shape, dtype):
    return jax.ShapeDtypeStruct(shape, dtype)


def call(kernel, name, outs, ins, scratch=(), megabytes=12, flops=0, moved_bytes=0):
    specs, args = [spec for spec, _ in ins], [arg for _, arg in ins]
    return pl.pallas_call(
        kernel,
        out_shape=outs,
        in_specs=specs,
        out_specs=jax.tree.map(lambda _: VMEM, outs),
        scratch_shapes=list(scratch),
        name=name,
        compiler_params=pltpu.CompilerParams(vmem_limit_bytes=megabytes << 20),
        cost_estimate=pl.CostEstimate(flops=flops, bytes_accessed=moved_bytes, transcendentals=0),
    )(*args)


def copies(sems, sources, targets):
    made = [pltpu.make_async_copy(s, t, sems.at[i]) for i, (s, t) in enumerate(zip(sources, targets))]
    for copy in made:
        copy.start()
    return made


def decays(dt_rows, a_log):
    heads, length = dt_rows.shape
    step = jnp.maximum(dt_rows, 0.0) + jnp.log1p(jnp.exp(-jnp.abs(dt_rows)))
    same = lax.broadcasted_iota(jnp.int32, (heads, heads), 0) == lax.broadcasted_iota(jnp.int32, (heads, heads), 1)
    a_column = jnp.sum(jnp.where(same, jnp.broadcast_to(a_log, (heads, heads)), 0.0), axis=1, keepdims=True)
    rate = -step * jnp.exp(a_column)
    row = lax.broadcasted_iota(jnp.int32, (length, length), 0)
    col = lax.broadcasted_iota(jnp.int32, (length, length), 1)
    upper = (row <= col).astype(F32)
    cum = jnp.dot(rate, upper, precision=lax.Precision.HIGHEST, preferred_element_type=F32)
    return step, cum


def pair_lanes(values, pair):
    rows = values.shape[0]
    lane = lax.broadcasted_iota(jnp.int32, (rows, LANES), 1)
    left = jnp.broadcast_to(values[:, 2 * pair : 2 * pair + 1], (rows, LANES))
    right = jnp.broadcast_to(values[:, 2 * pair + 1 : 2 * pair + 2], (rows, LANES))
    return jnp.where(lane < HEAD_DIM, left, right)


def state_kernel(place_ref, x_hbm, b_hbm, dt_hbm, a_hbm, *rest):
    outs, (x_ref, b_ref, dt_ref, a_ref, packed_ref, sems) = rest[:-6], rest[-6:]
    loads = copies(sems, (dt_hbm, a_hbm, x_hbm, b_hbm), (dt_ref, a_ref, x_ref, b_ref))
    loads[0].wait()
    loads[1].wait()
    step, cum = decays(dt_ref[...], a_ref[...])
    length = cum.shape[1]
    total = cum[:, length - 1 :]
    tail = (jnp.exp(total - cum) * step).T
    total = jnp.broadcast_to(total, cum.shape).T[0:1]
    loads[2].wait()
    loads[3].wait()
    pairs = packed_ref.shape[0]
    groups = b_ref.shape[1] // STATE
    for group in range(groups):
        turned = b_ref[:, group * STATE : (group + 1) * STATE].T
        for pair in range(group * pairs // groups, (group + 1) * pairs // groups):
            x_pair = x_ref[:, pair * LANES : (pair + 1) * LANES].astype(F32)
            weighted = (pair_lanes(tail, pair) * x_pair).astype(BF16)
            state = jnp.dot(turned, weighted, preferred_element_type=F32)
            packed_ref[pair, 0:STATE, :] = state.astype(BF16)
            wide = jnp.broadcast_to(pair_lanes(total, pair), (TILE, LANES))
            high = wide.astype(BF16).astype(F32)
            row = lax.broadcasted_iota(jnp.int32, (TILE, LANES), 0)
            packed_ref[pair, STATE : STATE + TILE, :] = jnp.where(row == 0, high, wide - high).astype(BF16)
    here = pairs // len(outs)
    for shift, out in enumerate(outs):
        out[...] = packed_ref[pl.ds((place_ref[2] ^ shift) * here, here)]


def inside_kernel(x_hbm, z_hbm, b_hbm, c_hbm, dt_hbm, a_hbm, d_hbm, norm_hbm, w_hbm, *rest):
    local_ref, grown_ref, c_ref, norm_ref, w_ref = rest[:5]
    x_ref, z_ref, b_ref, dt_ref, a_ref, d_ref, sems = rest[5:]
    loads = copies(
        sems,
        (dt_hbm, a_hbm, d_hbm, b_hbm, c_hbm, x_hbm, z_hbm, norm_hbm, w_hbm),
        (dt_ref, a_ref, d_ref, b_ref, c_ref, x_ref, z_ref, norm_ref, w_ref),
    )
    for load in loads[:7]:
        load.wait()
    step_rows, cum_rows = decays(dt_ref[...], a_ref[...])
    cum = cum_rows.T
    grown = jnp.exp(cum)
    length = cum.shape[0]
    pairs = x_ref.shape[1] // LANES
    groups = b_ref.shape[1] // STATE
    row = lax.broadcasted_iota(jnp.int32, (length, length), 0)
    col = lax.broadcasted_iota(jnp.int32, (length, length), 1)
    lane = lax.broadcasted_iota(jnp.int32, (length, LANES), 1)
    for group in range(groups):
        span = slice(group * STATE, (group + 1) * STATE)
        scores = lax.dot_general(c_ref[:, span], b_ref[:, span], NT, preferred_element_type=F32)
        scores = jnp.where(row >= col, scores, 0.0)
        for pair in range(group * pairs // groups, (group + 1) * pairs // groups):
            at = slice(pair * LANES, (pair + 1) * LANES)
            x_pair = x_ref[:, at]
            halves = []
            for head in (2 * pair, 2 * pair + 1):
                distance = cum[:, head : head + 1] - cum_rows[head : head + 1, :]
                decay = jnp.exp(jnp.where(row >= col, distance, FAR))
                mixing = (scores * (decay * step_rows[head : head + 1, :])).astype(BF16)
                halves.append(jnp.dot(mixing, x_pair, preferred_element_type=F32))
            inside = jnp.where(lane < HEAD_DIM, halves[0], halves[1])
            skip = pair_lanes(d_ref[...], pair) * x_pair.astype(F32)
            z = z_ref[:, at].astype(F32)
            gate = z / (1.0 + jnp.exp(-z))
            local_ref[:, at] = (inside + skip) * gate
            grown_ref[:, at] = pair_lanes(grown, pair) * gate
    loads[7].wait()
    loads[8].wait()


def prep_kernel(experts, width, resid_hbm, routes_hbm, gates_hbm, gain_hbm, up_hbm, down_hbm, *rest):
    gate_ref, resid_ref, gain_ref, up_ref, down_ref, routes_ref, gates_ref, sems = rest
    loads = copies(
        sems,
        (routes_hbm, gates_hbm, resid_hbm, gain_hbm, up_hbm, down_hbm),
        (routes_ref, gates_ref, resid_ref, gain_ref, up_ref, down_ref),
    )
    loads[0].wait()
    loads[1].wait()
    count, extent = gate_ref.shape
    start = width // LANES * LANES
    lane = lax.broadcasted_iota(jnp.int32, (extent, count), 0) + start - width
    expert = jnp.where(lane >= experts, lane - experts, lane)
    gate = jnp.zeros((extent, count), F32)
    for pick in range(routes_ref.shape[0]):
        gate = gate + jnp.where(routes_ref[pick] == expert, gates_ref[pick], 0.0)
    high = gate.astype(BF16).astype(F32)
    gate = jnp.where(lane < experts, high, jnp.where(lane < 2 * experts, gate - high, 0.0))
    gate_ref[...] = gate.T.astype(BF16)
    for load in loads[2:]:
        load.wait()


def chain_kernel(place_ref, *rest):
    count = (len(rest) - 1) // 2
    ins, outs, block_ref = rest[:count], rest[count : 2 * count], rest[-1]
    for shift in range(count):
        block_ref[place_ref[2] ^ shift] = ins[shift][...]
    carry = jnp.zeros(outs[0].shape, F32)
    for shard in range(count):
        block = block_ref[shard].astype(F32)
        block_ref[shard, :, 0:STATE, :] = carry.astype(BF16)
        total = block[:, STATE : STATE + 1, :] + block[:, STATE + 1 : STATE + 2, :]
        carry = jnp.exp(total) * carry + block[:, 0:STATE, :]
    for shift in range(count):
        outs[shift][...] = block_ref[place_ref[2] ^ shift, :, 0:STATE, :]


def chain_over_seq(place, got):
    mine = place[2]
    count = len(got)
    order = jnp.arange(count, dtype=jnp.int32) ^ mine
    block = jnp.stack(got)[order].astype(F32)
    totals = block[:, :, STATE : STATE + 1] + block[:, :, STATE + 1 : STATE + 2]

    def walk(carry, item):
        return (carry[0] + item[0], jnp.exp(item[0]) * carry[1] + item[1]), carry

    zero = (jnp.zeros(totals.shape[1:], F32), jnp.zeros(block[0, :, :STATE].shape, F32))
    span, inner = lax.scan(walk, zero, (totals, block[:, :, :STATE]))
    everything = jax.tree.map(lambda part: lax.all_gather(part.astype(BF16), "seq").astype(F32), span)
    unused, outer = lax.scan(walk, zero, everything)
    chain = lax.dynamic_index_in_dim(outer[1], lax.axis_index("seq"), 0, keepdims=False)
    before = (jnp.exp(inner[0]) * chain[None] + inner[1]).astype(BF16)[order]
    return [before[shift] for shift in range(count)]


def mixed_kernel(place_ref, local_ref, grown_ref, c_ref, norm_ref, w_ref, *rest):
    normed_ref, state_ref = rest[-2:]
    pairs = state_ref.shape[0]
    befores, outs = [], []
    held = 0
    for ref in rest[:-2]:
        if held < pairs:
            befores.append(ref)
            held += ref.shape[0]
        else:
            outs.append(ref)
    here = pairs // len(befores)
    for shift, before in enumerate(befores):
        state_ref[pl.ds((place_ref[2] ^ shift) * here, here)] = before[...]
    groups = c_ref.shape[1] // STATE
    per_group = pairs // groups
    for group in range(groups):
        c_group = c_ref[:, group * STATE : (group + 1) * STATE]
        gated, squares = [], 0.0
        for pair in range(group * per_group, (group + 1) * per_group):
            span = slice(pair * LANES, (pair + 1) * LANES)
            carried = jnp.dot(c_group, state_ref[pair], preferred_element_type=F32)
            value = local_ref[:, span] + grown_ref[:, span] * carried
            gated.append(value)
            squares = squares + value * value
        mean = jnp.sum(squares, axis=1, keepdims=True) / (per_group * LANES)
        inverse = lax.rsqrt(mean + 1e-05)
        for offset, value in enumerate(gated):
            pair = group * per_group + offset
            span = slice(pair * LANES, (pair + 1) * LANES)
            normed_ref[:, span] = (value * inverse * norm_ref[:, span]).astype(BF16)
    rows = outs[0].shape[0]
    blocks = []
    for shift in range(len(outs)):
        owner = place_ref[0] ^ shift
        blocks.append(normed_ref[pl.ds(pl.multiple_of(owner * rows, rows), rows), :])
    product = lax.dot_general(jnp.concatenate(blocks, axis=0), w_ref[...], NT, preferred_element_type=F32)
    for shift, out in enumerate(outs):
        out[...] = product[shift * rows : (shift + 1) * rows].astype(BF16)


def rows_kernel(resid_ref, gate_ref, gain_ref, *rest):
    parts, hidden_ref, rows_ref = rest[:-2], rest[-2], rest[-1]
    mixed = parts[0][...].astype(F32)
    for part in parts[1:]:
        mixed = mixed + part[...].astype(F32)
    hidden = (resid_ref[0].astype(F32) + mixed).astype(BF16)
    hidden_ref[...] = hidden
    value = hidden.astype(F32)
    scale = lax.rsqrt(jnp.mean(value * value, axis=1, keepdims=True) + 1e-05)
    width = value.shape[1]
    rows_ref[:, width // LANES * LANES :] = gate_ref[...]
    rows_ref[:, :width] = (value * scale * gain_ref[...]).astype(BF16)


def expert_kernel(experts, place_ref, up_ref, down_ref, mine_ref, partner_ref, kept_ref, sent_ref):
    width = up_ref.shape[2]
    start = width // LANES * LANES
    half = mine_ref.shape[0]
    rows = jnp.concatenate([mine_ref[:, :width], partner_ref[:, :width]], axis=0)
    up = lax.dot_general(rows, up_ref[0], NT, preferred_element_type=F32)
    up = jnp.maximum(up, 0.0)
    activated = (up * up).astype(BF16)
    tail = jnp.concatenate([mine_ref[:, start:], partner_ref[:, start:]], axis=0).astype(F32)
    lane = lax.broadcasted_iota(jnp.int32, tail.shape, 1) + start - width
    chosen = (lane == place_ref[1]) | (lane == place_ref[1] + experts)
    gate = jnp.sum(jnp.where(chosen, tail, 0.0), axis=1, keepdims=True)
    out = jnp.dot(activated, down_ref[0], preferred_element_type=F32) * gate
    kept_ref[...] = out[:half].astype(BF16)
    sent_ref[...] = out[half:].astype(BF16)


def split_sum_kernel(kept_ref, got_ref, *outs):
    rows = outs[0].shape[0]
    for at, out in enumerate(outs):
        span = slice(at * rows, (at + 1) * rows)
        out[...] = (kept_ref[span].astype(F32) + got_ref[span].astype(F32)).astype(BF16)


def piece_kernel(at, kept_ref, got_ref, *rest):
    parts, out_ref = rest[:-1], rest[-1]
    rows = out_ref.shape[0]
    span = slice(at * rows, (at + 1) * rows)
    total = kept_ref[span].astype(F32) + got_ref[span].astype(F32)
    for part in parts:
        total = total + part[...].astype(F32)
    out_ref[...] = total.astype(BF16)


def last_kernel(hidden_ref, *rest):
    parts, out_ref = rest[:-1], rest[-1]
    total = parts[0][...].astype(F32)
    for part in parts[1:]:
        total = total + part[...].astype(F32)
    out_ref[0] = (hidden_ref[...].astype(F32) + total).astype(BF16)


def swap(value, axis, mask):
    size = lax.axis_size(axis)
    return lax.ppermute(value, axis, [(i, i ^ mask) for i in range(size)])


def per_device(
    x_in, z_in, b_in, c_in, dt_in, a_log, d_skip, norm_w, w_out, resid, routes, gates, moe_gain, w_up, w_down
):
    length, heads = dt_in.shape
    channels = x_in.shape[1]
    model = w_out.shape[1]
    hidden_units = w_up.shape[2]
    seq_size, head_size, exp_size = lax.axis_size("seq"), lax.axis_size("head"), lax.axis_size("exp")
    chips = exp_size // 2
    rows = resid.shape[1]
    experts = head_size * exp_size
    pairs = channels // LANES
    axes = ("seq", "exp") if pairs % (seq_size * exp_size) == 0 else "exp"
    shards = lax.axis_size(axes)
    here = pairs // shards
    place = jnp.stack(
        [lax.axis_index("head"), lax.axis_index("head") * exp_size + lax.axis_index("exp"), lax.axis_index(axes)]
    ).astype(jnp.int32)
    dt_rows, a_row, d_row = dt_in.T, a_log[None], d_skip[None]
    dma = pltpu.SemaphoreType.DMA
    own = call(
        state_kernel,
        "state",
        [struct((here, STATE + TILE, LANES), BF16)] * shards,
        [(SMEM, place), (HBM, x_in), (HBM, b_in), (HBM, dt_rows), (HBM, a_row)],
        [pltpu.VMEM(x_in.shape, BF16), pltpu.VMEM(b_in.shape, BF16), pltpu.VMEM(dt_rows.shape, F32),
         pltpu.VMEM(a_row.shape, F32), pltpu.VMEM((pairs, STATE + TILE, LANES), BF16), dma((4,))],
        flops=1 << 25, moved_bytes=1 << 20,
    )
    got = [own[0]] + [swap(own[s], axes, s) for s in range(1, shards)]
    wide = -(-(model + 2 * experts) // LANES) * LANES
    local, grown, c_held, norm_held, w_held = call(
        inside_kernel,
        "inside",
        [struct((length, channels), F32), struct((length, channels), F32), struct(c_in.shape, BF16),
         struct((1, channels), F32), struct((model, channels), BF16)],
        [(HBM, value) for value in (x_in, z_in, b_in, c_in, dt_rows, a_row, d_row, norm_w[None], w_out.T)],
        [pltpu.VMEM(x_in.shape, BF16), pltpu.VMEM(z_in.shape, BF16), pltpu.VMEM(b_in.shape, BF16),
         pltpu.VMEM(dt_rows.shape, F32), pltpu.VMEM(a_row.shape, F32), pltpu.VMEM(d_row.shape, F32), dma((9,))],
        flops=1 << 27, moved_bytes=8 << 20,
    )
    turned = [jnp.transpose(value, (2, 0, 1)) for value in (routes, gates)]
    gate_lanes, resid_held, gain_held, up_held, down_held = call(
        functools.partial(prep_kernel, experts, model),
        "prep",
        [struct((rows, wide - model // LANES * LANES), BF16), struct(resid.shape, BF16), struct((1, model), F32),
         struct((1, hidden_units, model), BF16), struct(w_down.shape, BF16)],
        [(HBM, value) for value in (resid, *turned, moe_gain[None], jnp.swapaxes(w_up, 1, 2), w_down)],
        [pltpu.VMEM(turned[0].shape, jnp.int32), pltpu.VMEM(turned[1].shape, F32), dma((6,))],
        flops=1 << 20, moved_bytes=8 << 20,
    )
    if axes == "exp":
        before = chain_over_seq(place, got)
    else:
        before = call(
            chain_kernel,
            "chain",
            [struct((here, STATE, LANES), BF16)] * shards,
            [(SMEM, place)] + [(VMEM, value) for value in got],
            [pltpu.VMEM((shards, here, STATE + TILE, LANES), BF16)],
            flops=1 << 20, moved_bytes=1 << 19,
        )
    before = [before[0]] + [swap(before[s], axes, s) for s in range(1, shards)]
    mixed = call(
        mixed_kernel,
        "mixed",
        [struct((rows, model), BF16)] * head_size,
        [(SMEM, place)] + [(VMEM, value) for value in (local, grown, c_held, norm_held, w_held, *before)],
        [pltpu.VMEM((length, channels), BF16), pltpu.VMEM((pairs, STATE, LANES), BF16)],
        flops=1 << 29, moved_bytes=4 << 20,
    )
    order = list(range(head_size - 1, 0, -1))
    parts = [mixed[0]] + [swap(mixed[s], "head", s) for s in order]
    hidden, own_rows = call(
        rows_kernel,
        "rows",
        [struct((rows, model), BF16), struct((rows, wide), BF16)],
        [(VMEM, value) for value in (resid_held, gate_lanes, gain_held, *parts)],
    )
    near = {0: own_rows} | {s: swap(own_rows, "head", s) for s in order}
    sets = [near] + [{s: swap(near[s], "exp", 2 * d) for s in near} for d in range(1, chips)]
    produced = []
    for members in sets:
        mine = jnp.concatenate([members[s] for s in range(head_size)], axis=0)
        produced.append(
            call(
                functools.partial(expert_kernel, experts),
                "experts",
                [struct((head_size * rows, model), BF16)] * 2,
                [(SMEM, place)] + [(VMEM, value) for value in (up_held, down_held, mine, swap(mine, "exp", 1))],
                megabytes=16,
                flops=1 << 31, moved_bytes=8 << 20,
            )
        )
    returned = [(kept, swap(sent, "exp", 1)) for kept, sent in produced]
    arrived = {s: [] for s in range(head_size)}
    for d in range(1, chips):
        pieces = call(
            split_sum_kernel,
            "split",
            [struct((rows, model), BF16)] * head_size,
            [(VMEM, value) for value in returned[d]],
        )
        for s in order + [0]:
            arrived[s].append(swap(pieces[s], "exp", 2 * d))
    final = []
    for s in order + [0]:
        piece = call(
            functools.partial(piece_kernel, s),
            "piece",
            struct((rows, model), BF16),
            [(VMEM, value) for value in (*returned[0], *arrived[s])],
        )
        final.append(swap(piece, "head", s) if s else piece)
    return call(last_kernel, "last", struct(resid.shape, BF16), [(VMEM, value) for value in (hidden, *final)])


def solution(mesh):
    placed = (
        P(("seq", "exp"), "head"),
        P(("seq", "exp"), "head"),
        P(("seq", "exp"), "head"),
        P(("seq", "exp"), "head"),
        P(("seq", "exp"), "head"),
        P("head"),
        P("head"),
        P("head"),
        P("head", None),
        P(("seq", "exp"), "head", None),
        P(("seq", "exp"), "head", None),
        P(("seq", "exp"), "head", None),
        P(),
        P(("head", "exp"), None, None),
        P(("head", "exp"), None, None),
    )
    return jax.shard_map(
        per_device,
        mesh=mesh,
        in_specs=placed,
        out_specs=P(("seq", "exp"), "head", None),
        check_vma=False,
    )
```

```python
import functools

import jax
import jax.numpy as jnp
from jax import lax
from jax.experimental import pallas as pl
from jax.experimental.pallas import tpu as pltpu
from jax.sharding import PartitionSpec as P

HEAD_DIM = 64
STATE = 128
LANES = 128
TILE = 16
FAR = -1e30
F32 = jnp.float32
BF16 = jnp.bfloat16
HBM = pl.BlockSpec(memory_space=pltpu.HBM)
VMEM = pl.BlockSpec(memory_space=pltpu.VMEM)
ANY = pl.BlockSpec(memory_space=pl.ANY)
SMEM = pl.BlockSpec(memory_space=pltpu.SMEM)
NT = (((1,), (1,)), ((), ()))


def struct(shape, dtype):
    return jax.ShapeDtypeStruct(shape, dtype)


def call(kernel, name, outs, ins, scratch=(), megabytes=12, flops=0, moved_bytes=0):
    specs, args = [spec for spec, _ in ins], [arg for _, arg in ins]
    return pl.pallas_call(
        kernel,
        out_shape=outs,
        in_specs=specs,
        out_specs=jax.tree.map(lambda _: VMEM, outs),
        scratch_shapes=list(scratch),
        name=name,
        compiler_params=pltpu.CompilerParams(vmem_limit_bytes=megabytes << 20),
        cost_estimate=pl.CostEstimate(flops=flops, bytes_accessed=moved_bytes, transcendentals=0),
    )(*args)


def copies(sems, sources, targets):
    made = [pltpu.make_async_copy(s, t, sems.at[i]) for i, (s, t) in enumerate(zip(sources, targets))]
    for copy in made:
        copy.start()
    return made


def decays(dt_rows, a_log):
    heads, length = dt_rows.shape
    step = jnp.maximum(dt_rows, 0.0) + jnp.log1p(jnp.exp(-jnp.abs(dt_rows)))
    same = lax.broadcasted_iota(jnp.int32, (heads, heads), 0) == lax.broadcasted_iota(jnp.int32, (heads, heads), 1)
    a_column = jnp.sum(jnp.where(same, jnp.broadcast_to(a_log, (heads, heads)), 0.0), axis=1, keepdims=True)
    rate = -step * jnp.exp(a_column)
    row = lax.broadcasted_iota(jnp.int32, (length, length), 0)
    col = lax.broadcasted_iota(jnp.int32, (length, length), 1)
    upper = (row <= col).astype(F32)
    cum = jnp.dot(rate, upper, precision=lax.Precision.HIGHEST, preferred_element_type=F32)
    return step, cum


def pair_lanes(values, pair):
    rows = values.shape[0]
    lane = lax.broadcasted_iota(jnp.int32, (rows, LANES), 1)
    left = jnp.broadcast_to(values[:, 2 * pair : 2 * pair + 1], (rows, LANES))
    right = jnp.broadcast_to(values[:, 2 * pair + 1 : 2 * pair + 2], (rows, LANES))
    return jnp.where(lane < HEAD_DIM, left, right)


def unpacked(block):
    block = block.astype(F32)
    return block[:, STATE : STATE + 1, :] + block[:, STATE + 1 : STATE + 2, :], block[:, 0:STATE, :]


def pack(ref, total, state):
    ref[:, 0:STATE, :] = state.astype(BF16)
    wide = jnp.broadcast_to(total, (ref.shape[0], TILE, LANES))
    high = wide.astype(BF16).astype(F32)
    row = lax.broadcasted_iota(jnp.int32, wide.shape, 1)
    ref[:, STATE : STATE + TILE, :] = jnp.where(row == 0, high, wide - high).astype(BF16)


def state_kernel(place_ref, x_hbm, b_hbm, dt_hbm, a_hbm, keep_ref, send_ref, *scratch):
    x_ref, b_ref, dt_ref, a_ref, packed_ref, sems = scratch
    loads = copies(sems, (dt_hbm, a_hbm, x_hbm, b_hbm), (dt_ref, a_ref, x_ref, b_ref))
    loads[0].wait()
    loads[1].wait()
    step, cum = decays(dt_ref[...], a_ref[...])
    length = cum.shape[1]
    total = cum[:, length - 1 :]
    tail = (jnp.exp(total - cum) * step).T
    total = jnp.broadcast_to(total, cum.shape).T[0:1]
    loads[2].wait()
    loads[3].wait()
    pairs = packed_ref.shape[0]
    groups = b_ref.shape[1] // STATE
    for group in range(groups):
        turned = b_ref[:, group * STATE : (group + 1) * STATE].T
        for pair in range(group * pairs // groups, (group + 1) * pairs // groups):
            x_pair = x_ref[:, pair * LANES : (pair + 1) * LANES].astype(F32)
            weighted = (pair_lanes(tail, pair) * x_pair).astype(BF16)
            state = jnp.dot(turned, weighted, preferred_element_type=F32)
            pack(packed_ref.at[pair : pair + 1], pair_lanes(total, pair)[None], state[None])
    half = pairs // 2
    keep_ref[...] = packed_ref[pl.ds(place_ref[2] * half, half)]
    send_ref[...] = packed_ref[pl.ds((1 - place_ref[2]) * half, half)]


def chip_state_kernel(place_ref, keep_ref, got_ref, out_ref):
    first = place_ref[2] == 0
    keep, got = unpacked(keep_ref[...]), unpacked(got_ref[...])
    early = [jnp.where(first, mine, other) for mine, other in zip(keep, got)]
    late = [jnp.where(first, other, mine) for mine, other in zip(keep, got)]
    pack(out_ref, early[0] + late[0], jnp.exp(late[0]) * early[1] + late[1])


def span_kernel(place_ref, after_ref, *rest):
    ins, out_ref, block_ref = rest[:-2], rest[-2], rest[-1]
    for mask, part in enumerate(ins):
        block_ref[place_ref[3] ^ mask] = part[...]
    total, state = unpacked(block_ref[0])
    for chip in range(1, len(ins)):
        here, own = unpacked(block_ref[chip])
        total, state = total + here, jnp.exp(here) * state + own
    pack(out_ref, total, state)


def before_kernel(chips, place_ref, after_ref, keep_ref, got_ref, *rest):
    ins, (mine_ref, send_ref, chip_ref, part_ref) = rest[:-4], rest[-4:]
    for mask in range(chips):
        chip_ref[place_ref[3] ^ mask] = ins[mask][...]
    parts = len(ins) - chips
    for mask in range(parts):
        part_ref[place_ref[4] ^ mask] = ins[chips + mask][...]
    carry = jnp.zeros(mine_ref.shape, F32)
    for ref, count, own in ((part_ref, parts, place_ref[4]), (chip_ref, chips, place_ref[3])):
        for index in range(count - 1):
            total, state = unpacked(ref[index])
            carry = jnp.where(index < own, jnp.exp(total) * carry + state, carry)
    first = place_ref[2] == 0
    total, state = (jnp.where(first, k, g) for k, g in zip(unpacked(keep_ref[...]), unpacked(got_ref[...])))
    later = jnp.exp(total) * carry + state
    mine_ref[...] = jnp.where(first, carry, later).astype(BF16)
    send_ref[...] = jnp.where(first, later, carry).astype(BF16)


def inside_kernel(x_hbm, z_hbm, b_hbm, c_hbm, dt_hbm, a_hbm, d_hbm, local_ref, grown_ref, c_ref, *scratch):
    x_ref, z_ref, b_ref, dt_ref, a_ref, d_ref, sems = scratch
    loads = copies(
        sems,
        (dt_hbm, a_hbm, d_hbm, b_hbm, c_hbm, x_hbm, z_hbm),
        (dt_ref, a_ref, d_ref, b_ref, c_ref, x_ref, z_ref),
    )
    for load in loads:
        load.wait()
    step_rows, cum_rows = decays(dt_ref[...], a_ref[...])
    cum = cum_rows.T
    grown = jnp.exp(cum)
    length = cum.shape[0]
    pairs = x_ref.shape[1] // LANES
    groups = b_ref.shape[1] // STATE
    row = lax.broadcasted_iota(jnp.int32, (length, length), 0)
    col = lax.broadcasted_iota(jnp.int32, (length, length), 1)
    lane = lax.broadcasted_iota(jnp.int32, (length, LANES), 1)
    for group in range(groups):
        span = slice(group * STATE, (group + 1) * STATE)
        scores = lax.dot_general(c_ref[:, span], b_ref[:, span], NT, preferred_element_type=F32)
        scores = jnp.where(row >= col, scores, 0.0)
        for pair in range(group * pairs // groups, (group + 1) * pairs // groups):
            at = slice(pair * LANES, (pair + 1) * LANES)
            x_pair = x_ref[:, at]
            halves = []
            for head in (2 * pair, 2 * pair + 1):
                distance = cum[:, head : head + 1] - cum_rows[head : head + 1, :]
                decay = jnp.exp(jnp.where(row >= col, distance, FAR))
                mixing = (scores * (decay * step_rows[head : head + 1, :])).astype(BF16)
                halves.append(jnp.dot(mixing, x_pair, preferred_element_type=F32))
            inside = jnp.where(lane < HEAD_DIM, halves[0], halves[1])
            skip = pair_lanes(d_ref[...], pair) * x_pair.astype(F32)
            z = z_ref[:, at].astype(F32)
            gate = z / (1.0 + jnp.exp(-z))
            local_ref[:, at] = (inside + skip) * gate
            grown_ref[:, at] = pair_lanes(grown, pair) * gate


def prep_kernel(experts, width, resid_hbm, routes_hbm, gates_hbm, gain_hbm, norm_hbm, w_hbm, up_hbm, down_hbm, *rest):
    gate_ref, resid_ref, gain_ref, norm_ref, w_ref, up_ref, down_ref, routes_ref, gates_ref, sems = rest
    loads = copies(
        sems,
        (routes_hbm, gates_hbm, resid_hbm, gain_hbm, norm_hbm, w_hbm, up_hbm, down_hbm),
        (routes_ref, gates_ref, resid_ref, gain_ref, norm_ref, w_ref, up_ref, down_ref),
    )
    loads[0].wait()
    loads[1].wait()
    count, extent = gate_ref.shape
    start = width // LANES * LANES
    lane = lax.broadcasted_iota(jnp.int32, (extent, count), 0) + start - width
    expert = jnp.where(lane >= experts, lane - experts, lane)
    gate = jnp.zeros((extent, count), F32)
    for pick in range(routes_ref.shape[0]):
        gate = gate + jnp.where(routes_ref[pick] == expert, gates_ref[pick], 0.0)
    high = gate.astype(BF16).astype(F32)
    gate = jnp.where(lane < experts, high, jnp.where(lane < 2 * experts, gate - high, 0.0))
    gate_ref[...] = gate.T.astype(BF16)
    for load in loads[2:]:
        load.wait()


def mixed_kernel(place_ref, local_ref, grown_ref, c_ref, norm_ref, w_ref, mine_ref, got_ref, *rest):
    outs, (normed_ref, state_ref) = rest[:-2], rest[-2:]
    half = mine_ref.shape[0]
    pairs = 2 * half
    state_ref[pl.ds(place_ref[2] * half, half)] = mine_ref[...]
    state_ref[pl.ds((1 - place_ref[2]) * half, half)] = got_ref[...]
    groups = c_ref.shape[1] // STATE
    per_group = pairs // groups
    for group in range(groups):
        c_group = c_ref[:, group * STATE : (group + 1) * STATE]
        gated, squares = [], 0.0
        for pair in range(group * per_group, (group + 1) * per_group):
            span = slice(pair * LANES, (pair + 1) * LANES)
            carried = jnp.dot(c_group, state_ref[pair], preferred_element_type=F32)
            value = local_ref[:, span] + grown_ref[:, span] * carried
            gated.append(value)
            squares = squares + value * value
        mean = jnp.sum(squares, axis=1, keepdims=True) / (per_group * LANES)
        inverse = lax.rsqrt(mean + 1e-05)
        for offset, value in enumerate(gated):
            pair = group * per_group + offset
            span = slice(pair * LANES, (pair + 1) * LANES)
            normed_ref[:, span] = (value * inverse * norm_ref[:, span]).astype(BF16)
    rows = outs[0].shape[0]
    blocks = []
    for shift in range(len(outs)):
        owner = place_ref[0] ^ shift
        blocks.append(normed_ref[pl.ds(pl.multiple_of(owner * rows, rows), rows), :])
    product = lax.dot_general(jnp.concatenate(blocks, axis=0), w_ref[...], NT, preferred_element_type=F32)
    for shift, out in enumerate(outs):
        out[...] = product[shift * rows : (shift + 1) * rows].astype(BF16)


def rows_kernel(resid_ref, gate_ref, gain_ref, *rest):
    parts, hidden_ref, rows_ref = rest[:-2], rest[-2], rest[-1]
    mixed = parts[0][...].astype(F32)
    for part in parts[1:]:
        mixed = mixed + part[...].astype(F32)
    hidden = (resid_ref[0].astype(F32) + mixed).astype(BF16)
    hidden_ref[...] = hidden
    value = hidden.astype(F32)
    scale = lax.rsqrt(jnp.mean(value * value, axis=1, keepdims=True) + 1e-05)
    width = value.shape[1]
    rows_ref[:, width // LANES * LANES :] = gate_ref[...]
    rows_ref[:, :width] = (value * scale * gain_ref[...]).astype(BF16)


def expert_kernel(experts, place_ref, up_ref, down_ref, mine_ref, partner_ref, kept_ref, sent_ref):
    width = up_ref.shape[2]
    start = width // LANES * LANES
    half = mine_ref.shape[0]
    rows = jnp.concatenate([mine_ref[:, :width], partner_ref[:, :width]], axis=0)
    up = lax.dot_general(rows, up_ref[0], NT, preferred_element_type=F32)
    up = jnp.maximum(up, 0.0)
    activated = (up * up).astype(BF16)
    tail = jnp.concatenate([mine_ref[:, start:], partner_ref[:, start:]], axis=0).astype(F32)
    lane = lax.broadcasted_iota(jnp.int32, tail.shape, 1) + start - width
    chosen = (lane == place_ref[1]) | (lane == place_ref[1] + experts)
    gate = jnp.sum(jnp.where(chosen, tail, 0.0), axis=1, keepdims=True)
    out = jnp.dot(activated, down_ref[0], preferred_element_type=F32) * gate
    kept_ref[...] = out[:half].astype(BF16)
    sent_ref[...] = out[half:].astype(BF16)


def split_sum_kernel(kept_ref, got_ref, *outs):
    rows = outs[0].shape[0]
    for at, out in enumerate(outs):
        span = slice(at * rows, (at + 1) * rows)
        out[...] = (kept_ref[span].astype(F32) + got_ref[span].astype(F32)).astype(BF16)


def piece_kernel(at, kept_ref, got_ref, *rest):
    parts, out_ref = rest[:-1], rest[-1]
    rows = out_ref.shape[0]
    span = slice(at * rows, (at + 1) * rows)
    total = kept_ref[span].astype(F32) + got_ref[span].astype(F32)
    for part in parts:
        total = total + part[...].astype(F32)
    out_ref[...] = total.astype(BF16)


def last_kernel(hidden_ref, *rest):
    parts, out_ref = rest[:-1], rest[-1]
    total = parts[0][...].astype(F32)
    for part in parts[1:]:
        total = total + part[...].astype(F32)
    out_ref[0] = (hidden_ref[...].astype(F32) + total).astype(BF16)


def swap(value, axis, mask):
    size = lax.axis_size(axis)
    return lax.ppermute(value, axis, [(i, i ^ mask) for i in range(size)])


def per_device(
    x_in, z_in, b_in, c_in, dt_in, a_log, d_skip, norm_w, w_out, resid, routes, gates, moe_gain, w_up, w_down
):
    length, heads = dt_in.shape
    channels = x_in.shape[1]
    model = w_out.shape[1]
    hidden_units = w_up.shape[2]
    seq_size, head_size, exp_size = lax.axis_size("seq"), lax.axis_size("head"), lax.axis_size("exp")
    chips = exp_size // 2
    rows = resid.shape[1]
    experts = head_size * exp_size
    pairs = channels // LANES
    half = pairs // 2
    exp_index, head_index = lax.axis_index("exp"), lax.axis_index("head")
    place = jnp.stack(
        [head_index, head_index * exp_size + exp_index, exp_index % 2, exp_index // 2, lax.axis_index("seq")]
    ).astype(jnp.int32)
    dt_rows, a_row, d_row = dt_in.T, a_log[None], d_skip[None]
    dma = pltpu.SemaphoreType.DMA
    packed = struct((half, STATE + TILE, LANES), BF16)

    keep, send = call(
        state_kernel,
        "state",
        [packed, packed],
        [(SMEM, place), (HBM, x_in), (HBM, b_in), (HBM, dt_rows), (HBM, a_row)],
        [pltpu.VMEM(x_in.shape, BF16), pltpu.VMEM(b_in.shape, BF16), pltpu.VMEM(dt_rows.shape, F32),
         pltpu.VMEM(a_row.shape, F32), pltpu.VMEM((pairs, STATE + TILE, LANES), BF16), dma((4,))],
        megabytes=60, flops=1 << 25, moved_bytes=1 << 20,
    )
    local, grown, c_held = call(
        inside_kernel,
        "inside",
        [struct((length, channels), F32), struct((length, channels), F32), struct(c_in.shape, BF16)],
        [(HBM, value) for value in (x_in, z_in, b_in, c_in, dt_rows, a_row, d_row)],
        [pltpu.VMEM(x_in.shape, BF16), pltpu.VMEM(z_in.shape, BF16), pltpu.VMEM(b_in.shape, BF16),
         pltpu.VMEM(dt_rows.shape, F32), pltpu.VMEM(a_row.shape, F32), pltpu.VMEM(d_row.shape, F32), dma((7,))],
        megabytes=60, flops=1 << 27, moved_bytes=4 << 20,
    )
    wide = -(-(model + 2 * experts) // LANES) * LANES
    turned = [jnp.transpose(value, (2, 0, 1)) for value in (routes, gates)]
    gate_lanes, resid_held, gain_held, norm_held, w_held, up_held, down_held = call(
        functools.partial(prep_kernel, experts, model),
        "prep",
        [struct((rows, wide - model // LANES * LANES), BF16), struct(resid.shape, BF16), struct((1, model), F32),
         struct((1, channels), F32), struct((model, channels), BF16),
         struct((1, hidden_units, model), BF16), struct(w_down.shape, BF16)],
        [(HBM, value) for value in (resid, *turned, moe_gain[None], norm_w[None], w_out.T,
                                    jnp.swapaxes(w_up, 1, 2), w_down)],
        [pltpu.VMEM(turned[0].shape, jnp.int32), pltpu.VMEM(turned[1].shape, F32), dma((8,))],
        megabytes=48, flops=1 << 20, moved_bytes=8 << 20,
    )
    got = swap(send, "exp", 1)
    chip = call(chip_state_kernel, "chip_state", packed, [(SMEM, place), (VMEM, keep), (VMEM, got)])
    along_y = [chip] + [swap(chip, "exp", 2 * d) for d in range(1, chips)]
    span = call(
        span_kernel,
        "span",
        packed,
        [(SMEM, place), (ANY, c_held)] + [(VMEM, value) for value in along_y],
        [pltpu.VMEM((chips, *packed.shape), BF16)],
    )
    along_x = [span] + [swap(span, "seq", d) for d in range(1, seq_size)]
    before, before_send = call(
        functools.partial(before_kernel, chips),
        "before",
        [struct((half, STATE, LANES), BF16)] * 2,
        [(SMEM, place), (ANY, gate_lanes)] + [(VMEM, value) for value in (keep, got, *along_y, *along_x)],
        [pltpu.VMEM((chips, *packed.shape), BF16), pltpu.VMEM((seq_size, *packed.shape), BF16)],
        megabytes=24,
    )
    before_got = swap(before_send, "exp", 1)
    mixed = call(
        mixed_kernel,
        "mixed",
        [struct((rows, model), BF16)] * head_size,
        [(SMEM, place)] + [(VMEM, value) for value in (local, grown, c_held, norm_held, w_held, before, before_got)],
        [pltpu.VMEM((length, channels), BF16), pltpu.VMEM((pairs, STATE, LANES), BF16)],
        flops=1 << 29, moved_bytes=4 << 20,
    )
    order = list(range(head_size - 1, 0, -1))
    parts = [mixed[0]] + [swap(mixed[s], "head", s) for s in order]
    hidden, own_rows = call(
        rows_kernel,
        "rows",
        [struct((rows, model), BF16), struct((rows, wide), BF16)],
        [(VMEM, value) for value in (resid_held, gate_lanes, gain_held, *parts)],
    )

    def through_expert(members):
        mine = jnp.concatenate(members, axis=0)
        kept, sent = call(
            functools.partial(expert_kernel, experts),
            "experts",
            [struct((head_size * rows, model), BF16)] * 2,
            [(SMEM, place)] + [(VMEM, value) for value in (up_held, down_held, mine, swap(mine, "exp", 1))],
            megabytes=16, flops=1 << 31, moved_bytes=8 << 20,
        )
        return kept, sent

    near = [swap(own_rows, "head", s) for s in order] + [own_rows]
    far = [[swap(member, "exp", 2 * d) for member in near] for d in range(1, chips)]
    kept, sent = through_expert(near)
    kept, sent, far = lax.optimization_barrier((kept, sent, far))
    near_got = swap(sent, "exp", 1)
    arrived = [[] for _ in near]
    for d in range(1, chips):
        far_kept, far_sent = through_expert(far[d - 1])
        far_got = swap(far_sent, "exp", 1)
        pieces = call(
            split_sum_kernel,
            "split",
            [struct((rows, model), BF16)] * head_size,
            [(VMEM, far_kept), (VMEM, far_got)],
        )
        for at, piece in enumerate(pieces):
            arrived[at].append(swap(piece, "exp", 2 * d))
    final = []
    for at, mask in enumerate(order + [0]):
        piece = call(
            functools.partial(piece_kernel, at),
            "piece",
            struct((rows, model), BF16),
            [(VMEM, value) for value in (kept, near_got, *arrived[at])],
        )
        final.append(swap(piece, "head", mask) if mask else piece)
    return call(last_kernel, "last", struct(resid.shape, BF16), [(VMEM, value) for value in (hidden, *final)])


def solution(mesh):
    placed = (
        P(("seq", "exp"), "head"),
        P(("seq", "exp"), "head"),
        P(("seq", "exp"), "head"),
        P(("seq", "exp"), "head"),
        P(("seq", "exp"), "head"),
        P("head"),
        P("head"),
        P("head"),
        P("head", None),
        P(("seq", "exp"), "head", None),
        P(("seq", "exp"), "head", None),
        P(("seq", "exp"), "head", None),
        P(),
        P(("head", "exp"), None, None),
        P(("head", "exp"), None, None),
    )
    return jax.shard_map(
        per_device,
        mesh=mesh,
        in_specs=placed,
        out_specs=P(("seq", "exp"), "head", None),
        check_vma=False,
    )
```

```python
import functools

import jax
import jax.numpy as jnp
from jax import lax
from jax.experimental import pallas as pl
from jax.experimental.pallas import tpu as pltpu
from jax.sharding import PartitionSpec as P

HEAD_DIM = 64
STATE = 128
LANES = 128
TILE = 16
FAR = -1e30
F32 = jnp.float32
BF16 = jnp.bfloat16
HBM = pl.BlockSpec(memory_space=pltpu.HBM)
VMEM = pl.BlockSpec(memory_space=pltpu.VMEM)
ANY = pl.BlockSpec(memory_space=pl.ANY)
NT = (((1,), (1,)), ((), ()))


def struct(shape, dtype):
    return jax.ShapeDtypeStruct(shape, dtype)


def call(kernel, name, outs, ins, scratch=(), megabytes=12, pinned=True):
    args = [pltpu.with_memory_space_constraint(arg, pltpu.HBM) if spec is HBM else arg for spec, arg in ins]
    return pl.pallas_call(
        kernel,
        out_shape=jax.tree.map(lambda out: pltpu.VMEM(out.shape, out.dtype), outs) if pinned else outs,
        in_specs=[spec for spec, _ in ins],
        out_specs=jax.tree.map(lambda _: VMEM, outs),
        scratch_shapes=list(scratch),
        name=name,
        compiler_params=pltpu.CompilerParams(vmem_limit_bytes=megabytes << 20),
    )(*args)


def core_index():
    return lax.axis_index("exp") % 2


def chip_index():
    return lax.axis_index("exp") // 2


def copies(sems, sources, targets):
    made = [pltpu.make_async_copy(s, t, sems.at[i]) for i, (s, t) in enumerate(zip(sources, targets))]
    for copy in made:
        copy.start()
    return made


def decays(dt_rows, a_log):
    heads, length = dt_rows.shape
    step = jnp.maximum(dt_rows, 0.0) + jnp.log1p(jnp.exp(-jnp.abs(dt_rows)))
    same = lax.broadcasted_iota(jnp.int32, (heads, heads), 0) == lax.broadcasted_iota(jnp.int32, (heads, heads), 1)
    a_column = jnp.sum(jnp.where(same, jnp.broadcast_to(a_log, (heads, heads)), 0.0), axis=1, keepdims=True)
    rate = -step * jnp.exp(a_column)
    row = lax.broadcasted_iota(jnp.int32, (length, length), 0)
    col = lax.broadcasted_iota(jnp.int32, (length, length), 1)
    upper = (row <= col).astype(F32)
    cum = jnp.dot(rate, upper, precision=lax.Precision.HIGHEST, preferred_element_type=F32)
    return step, cum


def pair_lanes(values, pair):
    rows = values.shape[0]
    lane = lax.broadcasted_iota(jnp.int32, (rows, LANES), 1)
    left = jnp.broadcast_to(values[:, 2 * pair : 2 * pair + 1], (rows, LANES))
    right = jnp.broadcast_to(values[:, 2 * pair + 1 : 2 * pair + 2], (rows, LANES))
    return jnp.where(lane < HEAD_DIM, left, right)


def unpacked(block):
    block = block.astype(F32)
    return block[:, STATE : STATE + 1, :] + block[:, STATE + 1 : STATE + 2, :], block[:, 0:STATE, :]


def pack(ref, total, state):
    ref[:, 0:STATE, :] = state.astype(BF16)
    wide = jnp.broadcast_to(total, (ref.shape[0], TILE, LANES))
    high = wide.astype(BF16).astype(F32)
    row = lax.broadcasted_iota(jnp.int32, wide.shape, 1)
    ref[:, STATE : STATE + TILE, :] = jnp.where(row == 0, high, wide - high).astype(BF16)


def state_kernel(x_hbm, b_hbm, dt_hbm, a_hbm, keep_ref, send_ref, *scratch):
    x_ref, b_ref, dt_ref, a_ref, packed_ref, sems = scratch
    loads = copies(sems, (dt_hbm, a_hbm, x_hbm, b_hbm), (dt_ref, a_ref, x_ref, b_ref))
    loads[0].wait()
    loads[1].wait()
    step, cum = decays(dt_ref[...], a_ref[...])
    length = cum.shape[1]
    total = cum[:, length - 1 :]
    tail = (jnp.exp(total - cum) * step).T
    total = jnp.broadcast_to(total, cum.shape).T[0:1]
    loads[2].wait()
    loads[3].wait()
    pairs = packed_ref.shape[0]
    groups = b_ref.shape[1] // STATE
    for group in range(groups):
        turned = b_ref[:, group * STATE : (group + 1) * STATE].T
        for pair in range(group * pairs // groups, (group + 1) * pairs // groups):
            x_pair = x_ref[:, pair * LANES : (pair + 1) * LANES].astype(F32)
            weighted = (pair_lanes(tail, pair) * x_pair).astype(BF16)
            state = jnp.dot(turned, weighted, preferred_element_type=F32)
            pack(packed_ref.at[pair : pair + 1], pair_lanes(total, pair)[None], state[None])
    half = pairs // 2
    keep_ref[...] = packed_ref[pl.ds(core_index() * half, half)]
    send_ref[...] = packed_ref[pl.ds((1 - core_index()) * half, half)]


def chip_state_kernel(keep_ref, got_ref, out_ref):
    first = core_index() == 0
    keep, got = unpacked(keep_ref[...]), unpacked(got_ref[...])
    early = [jnp.where(first, mine, other) for mine, other in zip(keep, got)]
    late = [jnp.where(first, other, mine) for mine, other in zip(keep, got)]
    pack(out_ref, early[0] + late[0], jnp.exp(late[0]) * early[1] + late[1])


def weights_kernel(after_ref, up_hbm, down_hbm, up_ref, down_ref, sems):
    for load in copies(sems, (up_hbm, down_hbm), (up_ref, down_ref)):
        load.wait()


def span_kernel(after_ref, *rest):
    ins, out_ref, block_ref = rest[:-2], rest[-2], rest[-1]
    for mask, part in enumerate(ins):
        block_ref[chip_index() ^ mask] = part[...]
    total, state = unpacked(block_ref[0])
    for chip in range(1, len(ins)):
        here, own = unpacked(block_ref[chip])
        total, state = total + here, jnp.exp(here) * state + own
    pack(out_ref, total, state)


def before_kernel(chips, after_ref, keep_ref, got_ref, *rest):
    ins, (mine_ref, send_ref, chip_ref, part_ref) = rest[:-4], rest[-4:]
    for mask in range(chips):
        chip_ref[chip_index() ^ mask] = ins[mask][...]
    parts = len(ins) - chips
    for mask in range(parts):
        part_ref[lax.axis_index("seq") ^ mask] = ins[chips + mask][...]
    carry = jnp.zeros(mine_ref.shape, F32)
    for ref, count, own in ((part_ref, parts, lax.axis_index("seq")), (chip_ref, chips, chip_index())):
        for index in range(count - 1):
            total, state = unpacked(ref[index])
            carry = jnp.where(index < own, jnp.exp(total) * carry + state, carry)
    first = core_index() == 0
    total, state = (jnp.where(first, k, g) for k, g in zip(unpacked(keep_ref[...]), unpacked(got_ref[...])))
    later = jnp.exp(total) * carry + state
    mine_ref[...] = jnp.where(first, carry, later).astype(BF16)
    send_ref[...] = jnp.where(first, later, carry).astype(BF16)


def inside_kernel(x_hbm, z_hbm, b_hbm, c_hbm, dt_hbm, a_hbm, d_hbm, local_ref, grown_ref, c_ref, *scratch):
    x_ref, z_ref, b_ref, dt_ref, a_ref, d_ref, sems = scratch
    loads = copies(
        sems,
        (dt_hbm, a_hbm, d_hbm, b_hbm, c_hbm, x_hbm, z_hbm),
        (dt_ref, a_ref, d_ref, b_ref, c_ref, x_ref, z_ref),
    )
    for load in loads:
        load.wait()
    step_rows, cum_rows = decays(dt_ref[...], a_ref[...])
    cum = cum_rows.T
    grown = jnp.exp(cum)
    length = cum.shape[0]
    pairs = x_ref.shape[1] // LANES
    groups = b_ref.shape[1] // STATE
    row = lax.broadcasted_iota(jnp.int32, (length, length), 0)
    col = lax.broadcasted_iota(jnp.int32, (length, length), 1)
    lane = lax.broadcasted_iota(jnp.int32, (length, LANES), 1)
    for group in range(groups):
        span = slice(group * STATE, (group + 1) * STATE)
        scores = lax.dot_general(c_ref[:, span], b_ref[:, span], NT, preferred_element_type=F32)
        scores = jnp.where(row >= col, scores, 0.0)
        for pair in range(group * pairs // groups, (group + 1) * pairs // groups):
            at = slice(pair * LANES, (pair + 1) * LANES)
            x_pair = x_ref[:, at]
            halves = []
            for head in (2 * pair, 2 * pair + 1):
                distance = cum[:, head : head + 1] - cum_rows[head : head + 1, :]
                decay = jnp.exp(jnp.where(row >= col, distance, FAR))
                mixing = (scores * (decay * step_rows[head : head + 1, :])).astype(BF16)
                halves.append(jnp.dot(mixing, x_pair, preferred_element_type=F32))
            inside = jnp.where(lane < HEAD_DIM, halves[0], halves[1])
            skip = pair_lanes(d_ref[...], pair) * x_pair.astype(F32)
            z = z_ref[:, at].astype(F32)
            gate = z / (1.0 + jnp.exp(-z))
            local_ref[:, at] = (inside + skip) * gate
            grown_ref[:, at] = pair_lanes(grown, pair) * gate


def prep_kernel(experts, width, resid_hbm, routes_hbm, gates_hbm, gain_hbm, norm_hbm, w_hbm, *rest):
    gate_ref, resid_ref, gain_ref, norm_ref, w_ref, routes_ref, gates_ref, sems = rest
    loads = copies(
        sems,
        (routes_hbm, gates_hbm, resid_hbm, gain_hbm, norm_hbm, w_hbm),
        (routes_ref, gates_ref, resid_ref, gain_ref, norm_ref, w_ref),
    )
    loads[0].wait()
    loads[1].wait()
    count, extent = gate_ref.shape
    start = width // LANES * LANES
    lane = lax.broadcasted_iota(jnp.int32, (extent, count), 0) + start - width
    expert = jnp.where(lane >= experts, lane - experts, lane)
    gate = jnp.zeros((extent, count), F32)
    for pick in range(routes_ref.shape[0]):
        gate = gate + jnp.where(routes_ref[pick] == expert, gates_ref[pick], 0.0)
    high = gate.astype(BF16).astype(F32)
    gate = jnp.where(lane < experts, high, jnp.where(lane < 2 * experts, gate - high, 0.0))
    gate_ref[...] = gate.T.astype(BF16)
    for load in loads[2:]:
        load.wait()


def mixed_kernel(local_ref, grown_ref, c_ref, norm_ref, w_ref, mine_ref, got_ref, *rest):
    outs, (normed_ref, state_ref) = rest[:-2], rest[-2:]
    half = mine_ref.shape[0]
    pairs = 2 * half
    state_ref[pl.ds(core_index() * half, half)] = mine_ref[...]
    state_ref[pl.ds((1 - core_index()) * half, half)] = got_ref[...]
    groups = c_ref.shape[1] // STATE
    per_group = pairs // groups
    for group in range(groups):
        c_group = c_ref[:, group * STATE : (group + 1) * STATE]
        gated, squares = [], 0.0
        for pair in range(group * per_group, (group + 1) * per_group):
            span = slice(pair * LANES, (pair + 1) * LANES)
            carried = jnp.dot(c_group, state_ref[pair], preferred_element_type=F32)
            value = local_ref[:, span] + grown_ref[:, span] * carried
            gated.append(value)
            squares = squares + value * value
        mean = jnp.sum(squares, axis=1, keepdims=True) / (per_group * LANES)
        inverse = lax.rsqrt(mean + 1e-05)
        for offset, value in enumerate(gated):
            pair = group * per_group + offset
            span = slice(pair * LANES, (pair + 1) * LANES)
            normed_ref[:, span] = (value * inverse * norm_ref[:, span]).astype(BF16)
    rows = outs[0].shape[0]
    blocks = []
    for shift in range(len(outs)):
        owner = lax.axis_index("head") ^ shift
        blocks.append(normed_ref[pl.ds(pl.multiple_of(owner * rows, rows), rows), :])
    product = lax.dot_general(jnp.concatenate(blocks, axis=0), w_ref[...], NT, preferred_element_type=F32)
    for shift, out in enumerate(outs):
        out[...] = product[shift * rows : (shift + 1) * rows].astype(BF16)


def rows_kernel(after_ref, resid_ref, gate_ref, gain_ref, *rest):
    parts, hidden_ref, rows_ref = rest[:-2], rest[-2], rest[-1]
    mixed = parts[0][...].astype(F32)
    for part in parts[1:]:
        mixed = mixed + part[...].astype(F32)
    hidden = (resid_ref[0].astype(F32) + mixed).astype(BF16)
    hidden_ref[...] = hidden
    value = hidden.astype(F32)
    scale = lax.rsqrt(jnp.mean(value * value, axis=1, keepdims=True) + 1e-05)
    width = value.shape[1]
    rows_ref[:, width // LANES * LANES :] = gate_ref[...]
    rows_ref[:, :width] = (value * scale * gain_ref[...]).astype(BF16)


def expert_kernel(experts, up_ref, down_ref, mine_ref, partner_ref, kept_ref, sent_ref):
    width = up_ref.shape[2]
    start = width // LANES * LANES
    half = mine_ref.shape[0]
    rows = jnp.concatenate([mine_ref[:, :width], partner_ref[:, :width]], axis=0)
    up = lax.dot_general(rows, up_ref[0], NT, preferred_element_type=F32)
    up = jnp.maximum(up, 0.0)
    activated = (up * up).astype(BF16)
    tail = jnp.concatenate([mine_ref[:, start:], partner_ref[:, start:]], axis=0).astype(F32)
    lane = lax.broadcasted_iota(jnp.int32, tail.shape, 1) + start - width
    own = lax.axis_index("head") * lax.axis_size("exp") + lax.axis_index("exp")
    chosen = (lane == own) | (lane == own + experts)
    gate = jnp.sum(jnp.where(chosen, tail, 0.0), axis=1, keepdims=True)
    out = jnp.dot(activated, down_ref[0], preferred_element_type=F32) * gate
    kept_ref[...] = out[:half].astype(BF16)
    sent_ref[...] = out[half:].astype(BF16)


def split_sum_kernel(kept_ref, got_ref, *outs):
    rows = outs[0].shape[0]
    for at, out in enumerate(outs):
        span = slice(at * rows, (at + 1) * rows)
        out[...] = (kept_ref[span].astype(F32) + got_ref[span].astype(F32)).astype(BF16)


def piece_kernel(at, kept_ref, got_ref, *rest):
    parts, out_ref = rest[:-1], rest[-1]
    rows = out_ref.shape[0]
    span = slice(at * rows, (at + 1) * rows)
    total = kept_ref[span].astype(F32) + got_ref[span].astype(F32)
    for part in parts:
        total = total + part[...].astype(F32)
    out_ref[...] = total.astype(BF16)


def last_kernel(hidden_ref, *rest):
    parts, out_ref = rest[:-1], rest[-1]
    total = parts[0][...].astype(F32)
    for part in parts[1:]:
        total = total + part[...].astype(F32)
    out_ref[0] = (hidden_ref[...].astype(F32) + total).astype(BF16)


def swap(value, axis, mask):
    size = lax.axis_size(axis)
    return lax.ppermute(value, axis, [(i, i ^ mask) for i in range(size)])


def per_device(
    x_in, z_in, b_in, c_in, dt_in, a_log, d_skip, norm_w, w_out, resid, routes, gates, moe_gain, w_up, w_down
):
    length, heads = dt_in.shape
    channels = x_in.shape[1]
    model = w_out.shape[1]
    hidden_units = w_up.shape[2]
    seq_size, head_size, exp_size = lax.axis_size("seq"), lax.axis_size("head"), lax.axis_size("exp")
    chips = exp_size // 2
    rows = resid.shape[1]
    experts = head_size * exp_size
    pairs = channels // LANES
    half = pairs // 2
    dt_rows, a_row, d_row = dt_in.T, a_log[None], d_skip[None]
    dma = pltpu.SemaphoreType.DMA
    packed = struct((half, STATE + TILE, LANES), BF16)

    keep, send = call(
        state_kernel,
        "state",
        [packed, packed],
        [(HBM, x_in), (HBM, b_in), (HBM, dt_rows), (HBM, a_row)],
        [pltpu.VMEM(x_in.shape, BF16), pltpu.VMEM(b_in.shape, BF16), pltpu.VMEM(dt_rows.shape, F32),
         pltpu.VMEM(a_row.shape, F32), pltpu.VMEM((pairs, STATE + TILE, LANES), BF16), dma((4,))],
        megabytes=16,
    )
    local, grown, c_held = call(
        inside_kernel,
        "inside",
        [struct((length, channels), F32), struct((length, channels), F32), struct(c_in.shape, BF16)],
        [(HBM, value) for value in (x_in, z_in, b_in, c_in, dt_rows, a_row, d_row)],
        [pltpu.VMEM(x_in.shape, BF16), pltpu.VMEM(z_in.shape, BF16), pltpu.VMEM(b_in.shape, BF16),
         pltpu.VMEM(dt_rows.shape, F32), pltpu.VMEM(a_row.shape, F32), pltpu.VMEM(d_row.shape, F32), dma((7,))],
        megabytes=16,
    )
    wide = -(-(model + 2 * experts) // LANES) * LANES
    turned = [jnp.transpose(value, (2, 0, 1)) for value in (routes, gates)]
    gate_lanes, resid_held, gain_held, norm_held, w_held = call(
        functools.partial(prep_kernel, experts, model),
        "prep",
        [struct((rows, wide - model // LANES * LANES), BF16), struct(resid.shape, BF16), struct((1, model), F32),
         struct((1, channels), F32), struct((model, channels), BF16)],
        [(HBM, value) for value in (resid, *turned, moe_gain[None], norm_w[None], w_out.T)],
        [pltpu.VMEM(turned[0].shape, jnp.int32), pltpu.VMEM(turned[1].shape, F32), dma((6,))],
        megabytes=16,
    )
    got = swap(send, "exp", 1)
    chip = call(chip_state_kernel, "chip_state", packed, [(VMEM, keep), (VMEM, got)])
    along_y = [chip] + [swap(chip, "exp", 2 * d) for d in range(1, chips)]
    span = call(
        span_kernel,
        "span",
        packed,
        [(ANY, c_held)] + [(VMEM, value) for value in along_y],
        [pltpu.VMEM((chips, *packed.shape), BF16)],
    )
    along_x = [span] + [swap(span, "seq", d) for d in range(1, seq_size)]
    before, before_send = call(
        functools.partial(before_kernel, chips),
        "before",
        [struct((half, STATE, LANES), BF16)] * 2,
        [(ANY, gate_lanes)] + [(VMEM, value) for value in (keep, got, *along_y, *along_x)],
        [pltpu.VMEM((chips, *packed.shape), BF16), pltpu.VMEM((seq_size, *packed.shape), BF16)],
        megabytes=24,
    )
    before_got = swap(before_send, "exp", 1)
    mixed = call(
        mixed_kernel,
        "mixed",
        [struct((rows, model), BF16)] * head_size,
        [(VMEM, value) for value in (local, grown, c_held, norm_held, w_held, before, before_got)],
        [pltpu.VMEM((length, channels), BF16), pltpu.VMEM((pairs, STATE, LANES), BF16)],
    )
    up_turned = jnp.swapaxes(w_up, 1, 2)
    up_held, down_held = call(
        weights_kernel,
        "weights",
        [struct(up_turned.shape, BF16), struct(w_down.shape, BF16)],
        [(ANY, mixed[0]), (HBM, up_turned), (HBM, w_down)],
        [dma((2,))],
    )
    order = list(range(head_size - 1, 0, -1))
    parts = [mixed[0]] + [swap(mixed[s], "head", s) for s in order]
    hidden, own_rows = call(
        rows_kernel,
        "rows",
        [struct((rows, model), BF16), struct((rows, wide), BF16)],
        [(ANY, up_held)] + [(VMEM, value) for value in (resid_held, gate_lanes, gain_held, *parts)],
    )

    def through_expert(members):
        mine = jnp.concatenate(members, axis=0)
        kept, sent = call(
            functools.partial(expert_kernel, experts),
            "experts",
            [struct((head_size * rows, model), BF16)] * 2,
            [(VMEM, value) for value in (up_held, down_held, mine, swap(mine, "exp", 1))],
            megabytes=16,
        )
        return kept, sent

    near = [own_rows] + [swap(own_rows, "head", s) for s in reversed(order)]
    far = [[swap(member, "exp", 2 * d) for member in near] for d in range(1, chips)]
    near, early = lax.optimization_barrier((near, [members[:-1] for members in far]))
    far = [members + others[-1:] for members, others in zip(early, far)]
    near, far = near[::-1], [members[::-1] for members in far]
    kept, sent = through_expert(near)
    kept, sent, far = lax.optimization_barrier((kept, sent, far))
    near_got = swap(sent, "exp", 1)
    arrived = [[] for _ in near]
    for d in range(1, chips):
        far_kept, far_sent = through_expert(far[d - 1])
        far_got = swap(far_sent, "exp", 1)
        pieces = call(
            split_sum_kernel,
            "split",
            [struct((rows, model), BF16)] * head_size,
            [(VMEM, far_kept), (VMEM, far_got)],
        )
        for at, piece in enumerate(pieces):
            arrived[at].append(swap(piece, "exp", 2 * d))
    final = []
    for at, mask in enumerate(order + [0]):
        piece = call(
            functools.partial(piece_kernel, at),
            "piece",
            struct((rows, model), BF16),
            [(VMEM, value) for value in (kept, near_got, *arrived[at])],
        )
        final.append(swap(piece, "head", mask) if mask else piece)
    return call(
        last_kernel,
        "last",
        struct(resid.shape, BF16),
        [(VMEM, value) for value in (hidden, *final)],
        pinned=False,
    )


def solution(mesh):
    placed = (
        P(("seq", "exp"), "head"),
        P(("seq", "exp"), "head"),
        P(("seq", "exp"), "head"),
        P(("seq", "exp"), "head"),
        P(("seq", "exp"), "head"),
        P("head"),
        P("head"),
        P("head"),
        P("head", None),
        P(("seq", "exp"), "head", None),
        P(("seq", "exp"), "head", None),
        P(("seq", "exp"), "head", None),
        P(),
        P(("head", "exp"), None, None),
        P(("head", "exp"), None, None),
    )
    return jax.shard_map(
        per_device,
        mesh=mesh,
        in_specs=placed,
        out_specs=P(("seq", "exp"), "head", None),
        check_vma=False,
    )
```

```python
import functools

import jax
import jax.numpy as jnp
from jax import lax
from jax.experimental import pallas as pl
from jax.experimental.pallas import tpu as pltpu
from jax.sharding import PartitionSpec as P

HEAD_DIM = 64
STATE = 128
LANES = 128
TILE = 16
FAR = -1e30
F32 = jnp.float32
BF16 = jnp.bfloat16
HBM = pl.BlockSpec(memory_space=pltpu.HBM)
VMEM = pl.BlockSpec(memory_space=pltpu.VMEM)
ANY = pl.BlockSpec(memory_space=pl.ANY)
NT = (((1,), (1,)), ((), ()))


def struct(shape, dtype):
    return jax.ShapeDtypeStruct(shape, dtype)


def call(kernel, name, outs, ins, scratch=(), megabytes=12, pinned=True):
    args = [pltpu.with_memory_space_constraint(arg, pltpu.HBM) if spec is HBM else arg for spec, arg in ins]
    return pl.pallas_call(
        kernel,
        out_shape=jax.tree.map(lambda out: pltpu.VMEM(out.shape, out.dtype), outs) if pinned else outs,
        in_specs=[spec for spec, _ in ins],
        out_specs=jax.tree.map(lambda _: VMEM, outs),
        scratch_shapes=list(scratch),
        name=name,
        compiler_params=pltpu.CompilerParams(vmem_limit_bytes=megabytes << 20),
    )(*args)


def core_index():
    return lax.axis_index("exp") % 2


def chip_index():
    return lax.axis_index("exp") // 2


def copies(sems, sources, targets):
    made = [pltpu.make_async_copy(s, t, sems.at[i]) for i, (s, t) in enumerate(zip(sources, targets))]
    for copy in made:
        copy.start()
    return made


def decays(dt_rows, a_log):
    heads, length = dt_rows.shape
    step = jnp.maximum(dt_rows, 0.0) + jnp.log1p(jnp.exp(-jnp.abs(dt_rows)))
    same = lax.broadcasted_iota(jnp.int32, (heads, heads), 0) == lax.broadcasted_iota(jnp.int32, (heads, heads), 1)
    a_column = jnp.sum(jnp.where(same, jnp.broadcast_to(a_log, (heads, heads)), 0.0), axis=1, keepdims=True)
    rate = -step * jnp.exp(a_column)
    row = lax.broadcasted_iota(jnp.int32, (length, length), 0)
    col = lax.broadcasted_iota(jnp.int32, (length, length), 1)
    upper = (row <= col).astype(F32)
    cum = jnp.dot(rate, upper, precision=lax.Precision.HIGHEST, preferred_element_type=F32)
    return step, cum


def pair_lanes(values, pair):
    rows = values.shape[0]
    lane = lax.broadcasted_iota(jnp.int32, (rows, LANES), 1)
    left = jnp.broadcast_to(values[:, 2 * pair : 2 * pair + 1], (rows, LANES))
    right = jnp.broadcast_to(values[:, 2 * pair + 1 : 2 * pair + 2], (rows, LANES))
    return jnp.where(lane < HEAD_DIM, left, right)


def unpacked(block):
    block = block.astype(F32)
    return block[:, STATE : STATE + 1, :] + block[:, STATE + 1 : STATE + 2, :], block[:, 0:STATE, :]


def pack(ref, total, state):
    ref[:, 0:STATE, :] = state.astype(BF16)
    wide = jnp.broadcast_to(total, (ref.shape[0], TILE, LANES))
    high = wide.astype(BF16).astype(F32)
    row = lax.broadcasted_iota(jnp.int32, wide.shape, 1)
    ref[:, STATE : STATE + TILE, :] = jnp.where(row == 0, high, wide - high).astype(BF16)


def state_kernel(x_hbm, b_hbm, dt_hbm, a_hbm, keep_ref, send_ref, *scratch):
    x_ref, b_ref, dt_ref, a_ref, packed_ref, sems = scratch
    loads = copies(sems, (dt_hbm, a_hbm, x_hbm, b_hbm), (dt_ref, a_ref, x_ref, b_ref))
    loads[0].wait()
    loads[1].wait()
    step, cum = decays(dt_ref[...], a_ref[...])
    length = cum.shape[1]
    total = cum[:, length - 1 :]
    tail = (jnp.exp(total - cum) * step).T
    total = jnp.broadcast_to(total, cum.shape).T[0:1]
    loads[2].wait()
    loads[3].wait()
    pairs = packed_ref.shape[0]
    groups = b_ref.shape[1] // STATE
    for group in range(groups):
        turned = b_ref[:, group * STATE : (group + 1) * STATE].T
        for pair in range(group * pairs // groups, (group + 1) * pairs // groups):
            x_pair = x_ref[:, pair * LANES : (pair + 1) * LANES].astype(F32)
            weighted = (pair_lanes(tail, pair) * x_pair).astype(BF16)
            state = jnp.dot(turned, weighted, preferred_element_type=F32)
            pack(packed_ref.at[pair : pair + 1], pair_lanes(total, pair)[None], state[None])
    half = pairs // 2
    keep_ref[...] = packed_ref[pl.ds(core_index() * half, half)]
    send_ref[...] = packed_ref[pl.ds((1 - core_index()) * half, half)]


def chip_state_kernel(keep_ref, got_ref, out_ref):
    first = core_index() == 0
    keep, got = unpacked(keep_ref[...]), unpacked(got_ref[...])
    early = [jnp.where(first, mine, other) for mine, other in zip(keep, got)]
    late = [jnp.where(first, other, mine) for mine, other in zip(keep, got)]
    pack(out_ref, early[0] + late[0], jnp.exp(late[0]) * early[1] + late[1])


def weights_kernel(after_ref, up_hbm, down_hbm, up_ref, down_ref, sems):
    for load in copies(sems, (up_hbm, down_hbm), (up_ref, down_ref)):
        load.wait()


def span_kernel(after_ref, *rest):
    ins, out_ref, block_ref = rest[:-2], rest[-2], rest[-1]
    for mask, part in enumerate(ins):
        block_ref[chip_index() ^ mask] = part[...]
    total, state = unpacked(block_ref[0])
    for chip in range(1, len(ins)):
        here, own = unpacked(block_ref[chip])
        total, state = total + here, jnp.exp(here) * state + own
    pack(out_ref, total, state)


def before_kernel(chips, after_ref, keep_ref, got_ref, *rest):
    ins, (mine_ref, send_ref, chip_ref, part_ref) = rest[:-4], rest[-4:]
    for mask in range(chips):
        chip_ref[chip_index() ^ mask] = ins[mask][...]
    parts = len(ins) - chips
    for mask in range(parts):
        part_ref[lax.axis_index("seq") ^ mask] = ins[chips + mask][...]
    carry = jnp.zeros(mine_ref.shape, F32)
    for ref, count, own in ((part_ref, parts, lax.axis_index("seq")), (chip_ref, chips, chip_index())):
        for index in range(count - 1):
            total, state = unpacked(ref[index])
            carry = jnp.where(index < own, jnp.exp(total) * carry + state, carry)
    first = core_index() == 0
    total, state = (jnp.where(first, k, g) for k, g in zip(unpacked(keep_ref[...]), unpacked(got_ref[...])))
    later = jnp.exp(total) * carry + state
    mine_ref[...] = jnp.where(first, carry, later).astype(BF16)
    send_ref[...] = jnp.where(first, later, carry).astype(BF16)


def inside_kernel(x_hbm, z_hbm, b_hbm, c_hbm, dt_hbm, a_hbm, d_hbm, local_ref, grown_ref, c_ref, *scratch):
    x_ref, z_ref, b_ref, dt_ref, a_ref, d_ref, sems = scratch
    loads = copies(
        sems,
        (dt_hbm, a_hbm, d_hbm, b_hbm, c_hbm, x_hbm, z_hbm),
        (dt_ref, a_ref, d_ref, b_ref, c_ref, x_ref, z_ref),
    )
    for load in loads:
        load.wait()
    step_rows, cum_rows = decays(dt_ref[...], a_ref[...])
    cum = cum_rows.T
    grown = jnp.exp(cum)
    length = cum.shape[0]
    pairs = x_ref.shape[1] // LANES
    groups = b_ref.shape[1] // STATE
    row = lax.broadcasted_iota(jnp.int32, (length, length), 0)
    col = lax.broadcasted_iota(jnp.int32, (length, length), 1)
    lane = lax.broadcasted_iota(jnp.int32, (length, LANES), 1)
    for group in range(groups):
        span = slice(group * STATE, (group + 1) * STATE)
        scores = lax.dot_general(c_ref[:, span], b_ref[:, span], NT, preferred_element_type=F32)
        scores = jnp.where(row >= col, scores, 0.0)
        for pair in range(group * pairs // groups, (group + 1) * pairs // groups):
            at = slice(pair * LANES, (pair + 1) * LANES)
            x_pair = x_ref[:, at]
            halves = []
            for head in (2 * pair, 2 * pair + 1):
                distance = cum[:, head : head + 1] - cum_rows[head : head + 1, :]
                decay = jnp.exp(jnp.where(row >= col, distance, FAR))
                mixing = (scores * (decay * step_rows[head : head + 1, :])).astype(BF16)
                halves.append(jnp.dot(mixing, x_pair, preferred_element_type=F32))
            inside = jnp.where(lane < HEAD_DIM, halves[0], halves[1])
            skip = pair_lanes(d_ref[...], pair) * x_pair.astype(F32)
            z = z_ref[:, at].astype(F32)
            gate = z / (1.0 + jnp.exp(-z))
            local_ref[:, at] = (inside + skip) * gate
            grown_ref[:, at] = pair_lanes(grown, pair) * gate


def prep_kernel(experts, width, resid_hbm, routes_hbm, gates_hbm, gain_hbm, norm_hbm, w_hbm, *rest):
    gate_ref, resid_ref, gain_ref, norm_ref, w_ref, routes_ref, gates_ref, sems = rest
    loads = copies(
        sems,
        (routes_hbm, gates_hbm, resid_hbm, gain_hbm, norm_hbm, w_hbm),
        (routes_ref, gates_ref, resid_ref, gain_ref, norm_ref, w_ref),
    )
    loads[0].wait()
    loads[1].wait()
    count, extent = gate_ref.shape
    start = width // LANES * LANES
    lane = lax.broadcasted_iota(jnp.int32, (extent, count), 0) + start - width
    expert = jnp.where(lane >= experts, lane - experts, lane)
    gate = jnp.zeros((extent, count), F32)
    for pick in range(routes_ref.shape[0]):
        gate = gate + jnp.where(routes_ref[pick] == expert, gates_ref[pick], 0.0)
    high = gate.astype(BF16).astype(F32)
    gate = jnp.where(lane < experts, high, jnp.where(lane < 2 * experts, gate - high, 0.0))
    gate_ref[...] = gate.T.astype(BF16)
    for load in loads[2:]:
        load.wait()


def mixed_kernel(after_up, after_down, local_ref, grown_ref, c_ref, norm_ref, w_ref, mine_ref, got_ref, *rest):
    outs, (normed_ref, state_ref) = rest[:-2], rest[-2:]
    half = mine_ref.shape[0]
    pairs = 2 * half
    state_ref[pl.ds(core_index() * half, half)] = mine_ref[...]
    state_ref[pl.ds((1 - core_index()) * half, half)] = got_ref[...]
    groups = c_ref.shape[1] // STATE
    per_group = pairs // groups
    for group in range(groups):
        c_group = c_ref[:, group * STATE : (group + 1) * STATE]
        gated, squares = [], 0.0
        for pair in range(group * per_group, (group + 1) * per_group):
            span = slice(pair * LANES, (pair + 1) * LANES)
            carried = jnp.dot(c_group, state_ref[pair], preferred_element_type=F32)
            value = local_ref[:, span] + grown_ref[:, span] * carried
            gated.append(value)
            squares = squares + value * value
        mean = jnp.sum(squares, axis=1, keepdims=True) / (per_group * LANES)
        inverse = lax.rsqrt(mean + 1e-05)
        for offset, value in enumerate(gated):
            pair = group * per_group + offset
            span = slice(pair * LANES, (pair + 1) * LANES)
            normed_ref[:, span] = (value * inverse * norm_ref[:, span]).astype(BF16)
    rows = outs[0].shape[0]
    blocks = []
    for shift in range(len(outs)):
        owner = lax.axis_index("head") ^ shift
        blocks.append(normed_ref[pl.ds(pl.multiple_of(owner * rows, rows), rows), :])
    product = lax.dot_general(jnp.concatenate(blocks, axis=0), w_ref[...], NT, preferred_element_type=F32)
    for shift, out in enumerate(outs):
        out[...] = product[shift * rows : (shift + 1) * rows].astype(BF16)


def rows_kernel(after_ref, resid_ref, gate_ref, gain_ref, *rest):
    parts, hidden_ref, rows_ref = rest[:-2], rest[-2], rest[-1]
    mixed = parts[0][...].astype(F32)
    for part in parts[1:]:
        mixed = mixed + part[...].astype(F32)
    hidden = (resid_ref[0].astype(F32) + mixed).astype(BF16)
    hidden_ref[...] = hidden
    value = hidden.astype(F32)
    scale = lax.rsqrt(jnp.mean(value * value, axis=1, keepdims=True) + 1e-05)
    width = value.shape[1]
    rows_ref[:, width // LANES * LANES :] = gate_ref[...]
    rows_ref[:, :width] = (value * scale * gain_ref[...]).astype(BF16)


def expert_kernel(experts, up_ref, down_ref, other_up_ref, other_down_ref, *rest):
    count = len(rest) // 2
    ins, outs = rest[:count], rest[count:]
    width = up_ref.shape[2]
    start = width // LANES * LANES
    rows = jnp.concatenate([ref[:, :width] for ref in ins], axis=0)
    tail = jnp.concatenate([ref[:, start:] for ref in ins], axis=0).astype(F32)
    lane = lax.broadcasted_iota(jnp.int32, tail.shape, 1) + start - width
    own = lax.axis_index("head") * lax.axis_size("exp") + lax.axis_index("exp")
    other = own + 1 - 2 * core_index()
    total = 0.0
    for expert, up_of, down_of in ((own, up_ref, down_ref), (other, other_up_ref, other_down_ref)):
        up = lax.dot_general(rows, up_of[0], NT, preferred_element_type=F32)
        up = jnp.maximum(up, 0.0)
        activated = (up * up).astype(BF16)
        chosen = (lane == expert) | (lane == expert + experts)
        gate = jnp.sum(jnp.where(chosen, tail, 0.0), axis=1, keepdims=True)
        total = total + jnp.dot(activated, down_of[0], preferred_element_type=F32) * gate
    size = outs[0].shape[0]
    for at, out in enumerate(outs):
        out[...] = total[at * size : (at + 1) * size].astype(BF16)


def sum_kernel(*refs):
    total = refs[0][...].astype(F32)
    for ref in refs[1:-1]:
        total = total + ref[...].astype(F32)
    refs[-1][...] = total.astype(BF16)


def last_kernel(hidden_ref, *rest):
    parts, out_ref = rest[:-1], rest[-1]
    total = parts[0][...].astype(F32)
    for part in parts[1:]:
        total = total + part[...].astype(F32)
    out_ref[0] = (hidden_ref[...].astype(F32) + total).astype(BF16)


def swap(value, axis, mask):
    size = lax.axis_size(axis)
    return lax.ppermute(value, axis, [(i, i ^ mask) for i in range(size)])


def per_device(
    x_in, z_in, b_in, c_in, dt_in, a_log, d_skip, norm_w, w_out, resid, routes, gates, moe_gain, w_up, w_down
):
    length, heads = dt_in.shape
    channels = x_in.shape[1]
    model = w_out.shape[1]
    hidden_units = w_up.shape[2]
    seq_size, head_size, exp_size = lax.axis_size("seq"), lax.axis_size("head"), lax.axis_size("exp")
    chips = exp_size // 2
    rows = resid.shape[1]
    experts = head_size * exp_size
    pairs = channels // LANES
    half = pairs // 2
    dt_rows, a_row, d_row = dt_in.T, a_log[None], d_skip[None]
    dma = pltpu.SemaphoreType.DMA
    packed = struct((half, STATE + TILE, LANES), BF16)

    keep, send = call(
        state_kernel,
        "state",
        [packed, packed],
        [(HBM, x_in), (HBM, b_in), (HBM, dt_rows), (HBM, a_row)],
        [pltpu.VMEM(x_in.shape, BF16), pltpu.VMEM(b_in.shape, BF16), pltpu.VMEM(dt_rows.shape, F32),
         pltpu.VMEM(a_row.shape, F32), pltpu.VMEM((pairs, STATE + TILE, LANES), BF16), dma((4,))],
        megabytes=16,
    )
    local, grown, c_held = call(
        inside_kernel,
        "inside",
        [struct((length, channels), F32), struct((length, channels), F32), struct(c_in.shape, BF16)],
        [(HBM, value) for value in (x_in, z_in, b_in, c_in, dt_rows, a_row, d_row)],
        [pltpu.VMEM(x_in.shape, BF16), pltpu.VMEM(z_in.shape, BF16), pltpu.VMEM(b_in.shape, BF16),
         pltpu.VMEM(dt_rows.shape, F32), pltpu.VMEM(a_row.shape, F32), pltpu.VMEM(d_row.shape, F32), dma((7,))],
        megabytes=16,
    )
    wide = -(-(model + 2 * experts) // LANES) * LANES
    turned = [jnp.transpose(value, (2, 0, 1)) for value in (routes, gates)]
    gate_lanes, resid_held, gain_held, norm_held, w_held = call(
        functools.partial(prep_kernel, experts, model),
        "prep",
        [struct((rows, wide - model // LANES * LANES), BF16), struct(resid.shape, BF16), struct((1, model), F32),
         struct((1, channels), F32), struct((model, channels), BF16)],
        [(HBM, value) for value in (resid, *turned, moe_gain[None], norm_w[None], w_out.T)],
        [pltpu.VMEM(turned[0].shape, jnp.int32), pltpu.VMEM(turned[1].shape, F32), dma((6,))],
        megabytes=16,
    )
    up_turned = jnp.swapaxes(w_up, 1, 2)
    other_up, other_down = swap(up_turned, "exp", 1), swap(w_down, "exp", 1)
    got = swap(send, "exp", 1)
    chip = call(chip_state_kernel, "chip_state", packed, [(VMEM, keep), (VMEM, got)])
    along_y = [chip] + [swap(chip, "exp", 2 * d) for d in range(1, chips)]
    span = call(
        span_kernel,
        "span",
        packed,
        [(ANY, c_held)] + [(VMEM, value) for value in along_y],
        [pltpu.VMEM((chips, *packed.shape), BF16)],
    )
    along_x = [span] + [swap(span, "seq", d) for d in range(1, seq_size)]
    before, before_send = call(
        functools.partial(before_kernel, chips),
        "before",
        [struct((half, STATE, LANES), BF16)] * 2,
        [(ANY, gate_lanes)] + [(VMEM, value) for value in (keep, got, *along_y, *along_x)],
        [pltpu.VMEM((chips, *packed.shape), BF16), pltpu.VMEM((seq_size, *packed.shape), BF16)],
        megabytes=24,
    )
    before_got = swap(before_send, "exp", 1)
    mixed = call(
        mixed_kernel,
        "mixed",
        [struct((rows, model), BF16)] * head_size,
        [(ANY, other_up), (ANY, other_down)]
        + [(VMEM, value) for value in (local, grown, c_held, norm_held, w_held, before, before_got)],
        [pltpu.VMEM((length, channels), BF16), pltpu.VMEM((pairs, STATE, LANES), BF16)],
    )
    up_held, down_held = call(
        weights_kernel,
        "weights",
        [struct(up_turned.shape, BF16), struct(w_down.shape, BF16)],
        [(ANY, mixed[0]), (HBM, up_turned), (HBM, w_down)],
        [dma((2,))],
    )
    order = list(range(head_size - 1, 0, -1))
    parts = [mixed[0]] + [swap(mixed[s], "head", s) for s in order]
    hidden, own_rows = call(
        rows_kernel,
        "rows",
        [struct((rows, model), BF16), struct((rows, wide), BF16)],
        [(ANY, up_held)] + [(VMEM, value) for value in (resid_held, gate_lanes, gain_held, *parts)],
    )

    def through_experts(members):
        produced = call(
            functools.partial(expert_kernel, experts),
            "experts",
            [struct((rows, model), BF16)] * len(members),
            [(VMEM, value) for value in (up_held, down_held, other_up, other_down, *members.values())],
            megabytes=16,
        )
        return dict(zip(members, produced))

    near = {0: own_rows} | {s: swap(own_rows, "head", s) for s in range(1, head_size)}
    far = [{s: swap(near[s], "exp", 2 * d) for s in near} for d in range(1, chips)]
    early = [{s: members[s] for s in members if s != head_size - 1} for members in far]
    near, early = lax.optimization_barrier((near, early))
    far = [others | members for others, members in zip(far, early)]
    back_near = through_experts(near)
    back_near, far = lax.optimization_barrier((back_near, far))
    back_far = [through_experts(members) for members in far]
    relayed, direct = [s for s in order if s % 2 == 0], [s for s in order if s % 2 == 1]
    later = [0] + direct[1:]

    def diagonal(s):
        return [swap(members[s], ("head", "exp"), s * exp_size + 2 * d) for d, members in enumerate(back_far, 1)]

    arrived = [swap(back_near[s], "head", s) for s in direct]
    got = {s: [swap(members[s], "exp", 2 * d) for d, members in enumerate(back_far, 1)] for s in relayed}
    arrived, got = lax.optimization_barrier((arrived, got))
    arrived += [part for s in direct[:1] for part in diagonal(s)]
    totals = {
        s: call(sum_kernel, "sum", struct((rows, model), BF16), [(VMEM, v) for v in (back_near[s], *got[s])])
        for s in relayed
    }
    totals, rest = lax.optimization_barrier((totals, [{s: members[s] for s in later} for members in back_far]))
    back_far = rest
    arrived += [swap(totals[s], "head", s) for s in relayed]
    for s in later:
        arrived += diagonal(s)
    return call(
        last_kernel,
        "last",
        struct(resid.shape, BF16),
        [(VMEM, value) for value in (hidden, back_near[0], *arrived)],
        pinned=False,
    )


def solution(mesh):
    placed = (
        P(("seq", "exp"), "head"),
        P(("seq", "exp"), "head"),
        P(("seq", "exp"), "head"),
        P(("seq", "exp"), "head"),
        P(("seq", "exp"), "head"),
        P("head"),
        P("head"),
        P("head"),
        P("head", None),
        P(("seq", "exp"), "head", None),
        P(("seq", "exp"), "head", None),
        P(("seq", "exp"), "head", None),
        P(),
        P(("head", "exp"), None, None),
        P(("head", "exp"), None, None),
    )
    return jax.shard_map(
        per_device,
        mesh=mesh,
        in_specs=placed,
        out_specs=P(("seq", "exp"), "head", None),
        check_vma=False,
    )
```

```python
import functools

import jax
import jax.numpy as jnp
from jax import lax
from jax.experimental import pallas as pl
from jax.experimental.pallas import tpu as pltpu
from jax.sharding import PartitionSpec as P

HEAD_DIM = 64
STATE = 128
LANES = 128
TILE = 16
OWN = -1
FAR = -1e30
F32 = jnp.float32
BF16 = jnp.bfloat16
HBM = pl.BlockSpec(memory_space=pltpu.HBM)
VMEM = pl.BlockSpec(memory_space=pltpu.VMEM)
ANY = pl.BlockSpec(memory_space=pl.ANY)
NT = (((1,), (1,)), ((), ()))


def struct(shape, dtype):
    return jax.ShapeDtypeStruct(shape, dtype)


def call(kernel, name, outs, ins, scratch=(), megabytes=12, pinned=True):
    args = [pltpu.with_memory_space_constraint(arg, pltpu.HBM) if spec is HBM else arg for spec, arg in ins]
    return pl.pallas_call(
        kernel,
        out_shape=jax.tree.map(lambda out: pltpu.VMEM(out.shape, out.dtype), outs) if pinned else outs,
        in_specs=[spec for spec, _ in ins],
        out_specs=jax.tree.map(lambda _: VMEM, outs),
        scratch_shapes=list(scratch),
        name=name,
        compiler_params=pltpu.CompilerParams(vmem_limit_bytes=megabytes << 20),
    )(*args)


def offsets(count):
    down = list(range(count - 1, 0, -1))
    return [down, down[-1:] + down[:-1]]


def head_offset(slot, count):
    first, second = (order[slot] for order in offsets(count))
    return jnp.where(core_index() == 0, first, second)


def core_index():
    return lax.axis_index("exp") % 2


def chip_index():
    return lax.axis_index("exp") // 2


def copies(sems, sources, targets):
    made = [pltpu.make_async_copy(s, t, sems.at[i]) for i, (s, t) in enumerate(zip(sources, targets))]
    for copy in made:
        copy.start()
    return made


def decays(dt_rows, a_log):
    heads, length = dt_rows.shape
    step = jnp.maximum(dt_rows, 0.0) + jnp.log1p(jnp.exp(-jnp.abs(dt_rows)))
    same = lax.broadcasted_iota(jnp.int32, (heads, heads), 0) == lax.broadcasted_iota(jnp.int32, (heads, heads), 1)
    a_column = jnp.sum(jnp.where(same, jnp.broadcast_to(a_log, (heads, heads)), 0.0), axis=1, keepdims=True)
    rate = -step * jnp.exp(a_column)
    row = lax.broadcasted_iota(jnp.int32, (length, length), 0)
    col = lax.broadcasted_iota(jnp.int32, (length, length), 1)
    upper = (row <= col).astype(F32)
    cum = jnp.dot(rate, upper, precision=lax.Precision.HIGHEST, preferred_element_type=F32)
    return step, cum


def pair_lanes(values, pair):
    rows = values.shape[0]
    lane = lax.broadcasted_iota(jnp.int32, (rows, LANES), 1)
    left = jnp.broadcast_to(values[:, 2 * pair : 2 * pair + 1], (rows, LANES))
    right = jnp.broadcast_to(values[:, 2 * pair + 1 : 2 * pair + 2], (rows, LANES))
    return jnp.where(lane < HEAD_DIM, left, right)


def unpacked(block):
    block = block.astype(F32)
    return block[:, STATE : STATE + 1, :] + block[:, STATE + 1 : STATE + 2, :], block[:, 0:STATE, :]


def pack(ref, total, state):
    ref[:, 0:STATE, :] = state.astype(BF16)
    wide = jnp.broadcast_to(total, (ref.shape[0], TILE, LANES))
    high = wide.astype(BF16).astype(F32)
    row = lax.broadcasted_iota(jnp.int32, wide.shape, 1)
    ref[:, STATE : STATE + TILE, :] = jnp.where(row == 0, high, wide - high).astype(BF16)


def state_kernel(x_hbm, b_hbm, dt_hbm, a_hbm, keep_ref, send_ref, *scratch):
    x_ref, b_ref, dt_ref, a_ref, packed_ref, sems = scratch
    loads = copies(sems, (dt_hbm, a_hbm, x_hbm, b_hbm), (dt_ref, a_ref, x_ref, b_ref))
    loads[0].wait()
    loads[1].wait()
    step, cum = decays(dt_ref[...], a_ref[...])
    length = cum.shape[1]
    total = cum[:, length - 1 :]
    tail = (jnp.exp(total - cum) * step).T
    total = jnp.broadcast_to(total, cum.shape).T[0:1]
    loads[2].wait()
    loads[3].wait()
    pairs = packed_ref.shape[0]
    groups = b_ref.shape[1] // STATE
    for group in range(groups):
        turned = b_ref[:, group * STATE : (group + 1) * STATE].T
        for pair in range(group * pairs // groups, (group + 1) * pairs // groups):
            x_pair = x_ref[:, pair * LANES : (pair + 1) * LANES].astype(F32)
            weighted = (pair_lanes(tail, pair) * x_pair).astype(BF16)
            state = jnp.dot(turned, weighted, preferred_element_type=F32)
            pack(packed_ref.at[pair : pair + 1], pair_lanes(total, pair)[None], state[None])
    half = pairs // 2
    keep_ref[...] = packed_ref[pl.ds(core_index() * half, half)]
    send_ref[...] = packed_ref[pl.ds((1 - core_index()) * half, half)]


def chip_state_kernel(keep_ref, got_ref, out_ref):
    first = core_index() == 0
    keep, got = unpacked(keep_ref[...]), unpacked(got_ref[...])
    early = [jnp.where(first, mine, other) for mine, other in zip(keep, got)]
    late = [jnp.where(first, other, mine) for mine, other in zip(keep, got)]
    pack(out_ref, early[0] + late[0], jnp.exp(late[0]) * early[1] + late[1])


def weights_kernel(after_ref, up_hbm, down_hbm, up_ref, down_ref, sems):
    for load in copies(sems, (up_hbm, down_hbm), (up_ref, down_ref)):
        load.wait()


def span_kernel(after_ref, *rest):
    ins, out_ref, block_ref = rest[:-2], rest[-2], rest[-1]
    for mask, part in enumerate(ins):
        block_ref[chip_index() ^ mask] = part[...]
    total, state = unpacked(block_ref[0])
    for chip in range(1, len(ins)):
        here, own = unpacked(block_ref[chip])
        total, state = total + here, jnp.exp(here) * state + own
    pack(out_ref, total, state)


def before_kernel(chips, after_ref, keep_ref, got_ref, *rest):
    ins, (mine_ref, send_ref, chip_ref, part_ref) = rest[:-4], rest[-4:]
    for mask in range(chips):
        chip_ref[chip_index() ^ mask] = ins[mask][...]
    parts = len(ins) - chips
    for mask in range(parts):
        part_ref[lax.axis_index("seq") ^ mask] = ins[chips + mask][...]
    carry = jnp.zeros(mine_ref.shape, F32)
    for ref, count, own in ((part_ref, parts, lax.axis_index("seq")), (chip_ref, chips, chip_index())):
        for index in range(count - 1):
            total, state = unpacked(ref[index])
            carry = jnp.where(index < own, jnp.exp(total) * carry + state, carry)
    first = core_index() == 0
    total, state = (jnp.where(first, k, g) for k, g in zip(unpacked(keep_ref[...]), unpacked(got_ref[...])))
    later = jnp.exp(total) * carry + state
    mine_ref[...] = jnp.where(first, carry, later).astype(BF16)
    send_ref[...] = jnp.where(first, later, carry).astype(BF16)


def inside_kernel(x_hbm, z_hbm, b_hbm, c_hbm, dt_hbm, a_hbm, d_hbm, local_ref, grown_ref, c_ref, *scratch):
    x_ref, z_ref, b_ref, dt_ref, a_ref, d_ref, sems = scratch
    loads = copies(
        sems,
        (dt_hbm, a_hbm, d_hbm, b_hbm, c_hbm, x_hbm, z_hbm),
        (dt_ref, a_ref, d_ref, b_ref, c_ref, x_ref, z_ref),
    )
    for load in loads:
        load.wait()
    step_rows, cum_rows = decays(dt_ref[...], a_ref[...])
    cum = cum_rows.T
    grown = jnp.exp(cum)
    length = cum.shape[0]
    pairs = x_ref.shape[1] // LANES
    groups = b_ref.shape[1] // STATE
    row = lax.broadcasted_iota(jnp.int32, (length, length), 0)
    col = lax.broadcasted_iota(jnp.int32, (length, length), 1)
    lane = lax.broadcasted_iota(jnp.int32, (length, LANES), 1)
    for group in range(groups):
        span = slice(group * STATE, (group + 1) * STATE)
        scores = lax.dot_general(c_ref[:, span], b_ref[:, span], NT, preferred_element_type=F32)
        scores = jnp.where(row >= col, scores, 0.0)
        for pair in range(group * pairs // groups, (group + 1) * pairs // groups):
            at = slice(pair * LANES, (pair + 1) * LANES)
            x_pair = x_ref[:, at]
            halves = []
            for head in (2 * pair, 2 * pair + 1):
                distance = cum[:, head : head + 1] - cum_rows[head : head + 1, :]
                decay = jnp.exp(jnp.where(row >= col, distance, FAR))
                mixing = (scores * (decay * step_rows[head : head + 1, :])).astype(BF16)
                halves.append(jnp.dot(mixing, x_pair, preferred_element_type=F32))
            inside = jnp.where(lane < HEAD_DIM, halves[0], halves[1])
            skip = pair_lanes(d_ref[...], pair) * x_pair.astype(F32)
            z = z_ref[:, at].astype(F32)
            gate = z / (1.0 + jnp.exp(-z))
            local_ref[:, at] = (inside + skip) * gate
            grown_ref[:, at] = pair_lanes(grown, pair) * gate


def prep_kernel(experts, width, resid_hbm, routes_hbm, gates_hbm, gain_hbm, norm_hbm, w_hbm, *rest):
    gate_ref, resid_ref, gain_ref, norm_ref, w_ref, routes_ref, gates_ref, sems = rest
    loads = copies(
        sems,
        (routes_hbm, gates_hbm, resid_hbm, gain_hbm, norm_hbm, w_hbm),
        (routes_ref, gates_ref, resid_ref, gain_ref, norm_ref, w_ref),
    )
    loads[0].wait()
    loads[1].wait()
    count, extent = gate_ref.shape
    start = width // LANES * LANES
    lane = lax.broadcasted_iota(jnp.int32, (extent, count), 0) + start - width
    expert = jnp.where(lane >= experts, lane - experts, lane)
    gate = jnp.zeros((extent, count), F32)
    for pick in range(routes_ref.shape[0]):
        gate = gate + jnp.where(routes_ref[pick] == expert, gates_ref[pick], 0.0)
    high = gate.astype(BF16).astype(F32)
    gate = jnp.where(lane < experts, high, jnp.where(lane < 2 * experts, gate - high, 0.0))
    gate_ref[...] = gate.T.astype(BF16)
    for load in loads[2:]:
        load.wait()


def mixed_kernel(after_up, after_down, local_ref, grown_ref, c_ref, norm_ref, w_ref, mine_ref, got_ref, *rest):
    outs, (normed_ref, state_ref) = rest[:-2], rest[-2:]
    half = mine_ref.shape[0]
    pairs = 2 * half
    state_ref[pl.ds(core_index() * half, half)] = mine_ref[...]
    state_ref[pl.ds((1 - core_index()) * half, half)] = got_ref[...]
    groups = c_ref.shape[1] // STATE
    per_group = pairs // groups
    for group in range(groups):
        c_group = c_ref[:, group * STATE : (group + 1) * STATE]
        gated, squares = [], 0.0
        for pair in range(group * per_group, (group + 1) * per_group):
            span = slice(pair * LANES, (pair + 1) * LANES)
            carried = jnp.dot(c_group, state_ref[pair], preferred_element_type=F32)
            value = local_ref[:, span] + grown_ref[:, span] * carried
            gated.append(value)
            squares = squares + value * value
        mean = jnp.sum(squares, axis=1, keepdims=True) / (per_group * LANES)
        inverse = lax.rsqrt(mean + 1e-05)
        for offset, value in enumerate(gated):
            pair = group * per_group + offset
            span = slice(pair * LANES, (pair + 1) * LANES)
            normed_ref[:, span] = (value * inverse * norm_ref[:, span]).astype(BF16)
    rows = outs[0].shape[0]
    blocks = []
    for shift in range(len(outs)):
        owner = lax.axis_index("head") ^ (head_offset(shift - 1, len(outs)) if shift else 0)
        blocks.append(normed_ref[pl.ds(pl.multiple_of(owner * rows, rows), rows), :])
    product = lax.dot_general(jnp.concatenate(blocks, axis=0), w_ref[...], NT, preferred_element_type=F32)
    for shift, out in enumerate(outs):
        out[...] = product[shift * rows : (shift + 1) * rows].astype(BF16)


def rows_kernel(after_ref, resid_ref, gate_ref, gain_ref, *rest):
    parts, hidden_ref, rows_ref = rest[:-2], rest[-2], rest[-1]
    mixed = parts[0][...].astype(F32)
    for part in parts[1:]:
        mixed = mixed + part[...].astype(F32)
    hidden = (resid_ref[0].astype(F32) + mixed).astype(BF16)
    hidden_ref[...] = hidden
    value = hidden.astype(F32)
    scale = lax.rsqrt(jnp.mean(value * value, axis=1, keepdims=True) + 1e-05)
    width = value.shape[1]
    rows_ref[:, width // LANES * LANES :] = gate_ref[...]
    rows_ref[:, :width] = (value * scale * gain_ref[...]).astype(BF16)


def expert_kernel(experts, up_ref, down_ref, other_up_ref, other_down_ref, *rest):
    count = len(rest) // 2
    ins, outs = rest[:count], rest[count:]
    width = up_ref.shape[2]
    start = width // LANES * LANES
    rows = jnp.concatenate([ref[:, :width] for ref in ins], axis=0)
    tail = jnp.concatenate([ref[:, start:] for ref in ins], axis=0).astype(F32)
    lane = lax.broadcasted_iota(jnp.int32, tail.shape, 1) + start - width
    own = lax.axis_index("head") * lax.axis_size("exp") + lax.axis_index("exp")
    other = own + 1 - 2 * core_index()
    total = 0.0
    for expert, up_of, down_of in ((own, up_ref, down_ref), (other, other_up_ref, other_down_ref)):
        up = lax.dot_general(rows, up_of[0], NT, preferred_element_type=F32)
        up = jnp.maximum(up, 0.0)
        activated = (up * up).astype(BF16)
        chosen = (lane == expert) | (lane == expert + experts)
        gate = jnp.sum(jnp.where(chosen, tail, 0.0), axis=1, keepdims=True)
        total = total + jnp.dot(activated, down_of[0], preferred_element_type=F32) * gate
    size = outs[0].shape[0]
    for at, out in enumerate(outs):
        out[...] = total[at * size : (at + 1) * size].astype(BF16)


def sum_kernel(*refs):
    total = refs[0][...].astype(F32)
    for ref in refs[1:-1]:
        total = total + ref[...].astype(F32)
    refs[-1][...] = total.astype(BF16)


def last_kernel(hidden_ref, *rest):
    parts, out_ref = rest[:-1], rest[-1]
    total = parts[0][...].astype(F32)
    for part in parts[1:]:
        total = total + part[...].astype(F32)
    out_ref[0] = (hidden_ref[...].astype(F32) + total).astype(BF16)


def swap(value, axis, mask):
    size = lax.axis_size(axis)
    return lax.ppermute(value, axis, [(i, i ^ mask) for i in range(size)])


def swap_slot(value, slot, chip_mask=0):
    heads, size = lax.axis_size("head"), lax.axis_size("exp")
    order = offsets(heads)
    pairs = []
    for i in range(heads * size):
        head, exp = i // size, i % size
        pairs.append((i, (head ^ order[exp % 2][slot]) * size + (exp ^ (2 * chip_mask))))
    return lax.ppermute(value, ("head", "exp"), pairs)


def per_device(
    x_in, z_in, b_in, c_in, dt_in, a_log, d_skip, norm_w, w_out, resid, routes, gates, moe_gain, w_up, w_down
):
    length, heads = dt_in.shape
    channels = x_in.shape[1]
    model = w_out.shape[1]
    hidden_units = w_up.shape[2]
    seq_size, head_size, exp_size = lax.axis_size("seq"), lax.axis_size("head"), lax.axis_size("exp")
    chips = exp_size // 2
    rows = resid.shape[1]
    experts = head_size * exp_size
    pairs = channels // LANES
    half = pairs // 2
    dt_rows, a_row, d_row = dt_in.T, a_log[None], d_skip[None]
    dma = pltpu.SemaphoreType.DMA
    packed = struct((half, STATE + TILE, LANES), BF16)

    keep, send = call(
        state_kernel,
        "state",
        [packed, packed],
        [(HBM, x_in), (HBM, b_in), (HBM, dt_rows), (HBM, a_row)],
        [pltpu.VMEM(x_in.shape, BF16), pltpu.VMEM(b_in.shape, BF16), pltpu.VMEM(dt_rows.shape, F32),
         pltpu.VMEM(a_row.shape, F32), pltpu.VMEM((pairs, STATE + TILE, LANES), BF16), dma((4,))],
        megabytes=16,
    )
    local, grown, c_held = call(
        inside_kernel,
        "inside",
        [struct((length, channels), F32), struct((length, channels), F32), struct(c_in.shape, BF16)],
        [(HBM, value) for value in (x_in, z_in, b_in, c_in, dt_rows, a_row, d_row)],
        [pltpu.VMEM(x_in.shape, BF16), pltpu.VMEM(z_in.shape, BF16), pltpu.VMEM(b_in.shape, BF16),
         pltpu.VMEM(dt_rows.shape, F32), pltpu.VMEM(a_row.shape, F32), pltpu.VMEM(d_row.shape, F32), dma((7,))],
        megabytes=16,
    )
    wide = -(-(model + 2 * experts) // LANES) * LANES
    turned = [jnp.transpose(value, (2, 0, 1)) for value in (routes, gates)]
    gate_lanes, resid_held, gain_held, norm_held, w_held = call(
        functools.partial(prep_kernel, experts, model),
        "prep",
        [struct((rows, wide - model // LANES * LANES), BF16), struct(resid.shape, BF16), struct((1, model), F32),
         struct((1, channels), F32), struct((model, channels), BF16)],
        [(HBM, value) for value in (resid, *turned, moe_gain[None], norm_w[None], w_out.T)],
        [pltpu.VMEM(turned[0].shape, jnp.int32), pltpu.VMEM(turned[1].shape, F32), dma((6,))],
        megabytes=16,
    )
    up_turned = jnp.swapaxes(w_up, 1, 2)
    other_up, other_down = swap(up_turned, "exp", 1), swap(w_down, "exp", 1)
    got = swap(send, "exp", 1)
    chip = call(chip_state_kernel, "chip_state", packed, [(VMEM, keep), (VMEM, got)])
    along_y = [chip] + [swap(chip, "exp", 2 * d) for d in range(1, chips)]
    span = call(
        span_kernel,
        "span",
        packed,
        [(ANY, c_held)] + [(VMEM, value) for value in along_y],
        [pltpu.VMEM((chips, *packed.shape), BF16)],
    )
    along_x = [span] + [swap(span, "seq", d) for d in range(1, seq_size)]
    before, before_send = call(
        functools.partial(before_kernel, chips),
        "before",
        [struct((half, STATE, LANES), BF16)] * 2,
        [(ANY, gate_lanes)] + [(VMEM, value) for value in (keep, got, *along_y, *along_x)],
        [pltpu.VMEM((chips, *packed.shape), BF16), pltpu.VMEM((seq_size, *packed.shape), BF16)],
        megabytes=24,
    )
    before_got = swap(before_send, "exp", 1)
    mixed = call(
        mixed_kernel,
        "mixed",
        [struct((rows, model), BF16)] * head_size,
        [(ANY, other_up), (ANY, other_down)]
        + [(VMEM, value) for value in (local, grown, c_held, norm_held, w_held, before, before_got)],
        [pltpu.VMEM((length, channels), BF16), pltpu.VMEM((pairs, STATE, LANES), BF16)],
    )
    up_held, down_held = call(
        weights_kernel,
        "weights",
        [struct(up_turned.shape, BF16), struct(w_down.shape, BF16)],
        [(ANY, mixed[0]), (HBM, up_turned), (HBM, w_down)],
        [dma((2,))],
    )
    slots = list(range(head_size - 1))
    parts = [mixed[0]] + [swap_slot(mixed[k + 1], k) for k in slots]
    hidden, own_rows = call(
        rows_kernel,
        "rows",
        [struct((rows, model), BF16), struct((rows, wide), BF16)],
        [(ANY, up_held)] + [(VMEM, value) for value in (resid_held, gate_lanes, gain_held, *parts)],
    )

    def through_experts(members):
        produced = call(
            functools.partial(expert_kernel, experts),
            "experts",
            [struct((rows, model), BF16)] * len(members),
            [(VMEM, value) for value in (up_held, down_held, other_up, other_down, *members.values())],
            megabytes=16,
        )
        return dict(zip(members, produced))

    near = {k: swap_slot(own_rows, slots[-1 - k]) for k in slots} | {OWN: own_rows}
    far = [{k: swap(near[k], "exp", 2 * d) for k in near} for d in range(1, chips)]
    early = [{k: members[k] for k in (OWN,)} for members in far]
    near, early = lax.optimization_barrier((near, early))
    far = [members | others for members, others in zip(far, early)]
    back_near = through_experts(near)
    back_near, far = lax.optimization_barrier((back_near, far))
    back_far = [through_experts(members) for members in far]
    relayed, direct = slots[1:2], slots[2:] + slots[0:1]

    def diagonal(k):
        return [swap_slot(members[k], slots[-1 - k], d) for d, members in enumerate(back_far, 1)]

    def across(members, k):
        return [swap(results[k], "exp", 2 * d) for d, results in enumerate(members, 1)]

    arrived = [swap_slot(back_near[k], slots[-1 - k]) for k in direct]
    got = {k: across(back_far, k) for k in relayed}
    arrived, got = lax.optimization_barrier((arrived, got))
    arrived += diagonal(direct[0])
    totals = {
        k: call(sum_kernel, "sum", struct((rows, model), BF16), [(VMEM, v) for v in (back_near[k], *got[k])])
        for k in relayed
    }
    totals, back_far = lax.optimization_barrier((totals, back_far))
    arrived += [swap_slot(totals[k], slots[-1 - k]) for k in relayed]
    for k in direct[1:]:
        arrived += diagonal(k)
    arrived += across(back_far, OWN)
    return call(
        last_kernel,
        "last",
        struct(resid.shape, BF16),
        [(VMEM, value) for value in (hidden, back_near[OWN], *arrived)],
        pinned=False,
    )


def solution(mesh):
    placed = (
        P(("seq", "exp"), "head"),
        P(("seq", "exp"), "head"),
        P(("seq", "exp"), "head"),
        P(("seq", "exp"), "head"),
        P(("seq", "exp"), "head"),
        P("head"),
        P("head"),
        P("head"),
        P("head", None),
        P(("seq", "exp"), "head", None),
        P(("seq", "exp"), "head", None),
        P(("seq", "exp"), "head", None),
        P(),
        P(("head", "exp"), None, None),
        P(("head", "exp"), None, None),
    )
    return jax.shard_map(
        per_device,
        mesh=mesh,
        in_specs=placed,
        out_specs=P(("seq", "exp"), "head", None),
        check_vma=False,
    )
```

```python
import functools

import jax
import jax.numpy as jnp
from jax import lax
from jax.experimental import pallas as pl
from jax.experimental.pallas import tpu as pltpu
from jax.sharding import PartitionSpec as P

HEAD_DIM = 64
STATE = 128
LANES = 128
TILE = 16
FAR = -1e30
F32 = jnp.float32
BF16 = jnp.bfloat16
HBM = pl.BlockSpec(memory_space=pltpu.HBM)
VMEM = pl.BlockSpec(memory_space=pltpu.VMEM)
ANY = pl.BlockSpec(memory_space=pl.ANY)
NT = (((1,), (1,)), ((), ()))


def struct(shape, dtype):
    return jax.ShapeDtypeStruct(shape, dtype)


def call(kernel, name, outs, ins, scratch=(), megabytes=12, pinned=True):
    args = [pltpu.with_memory_space_constraint(arg, pltpu.HBM) if spec is HBM else arg for spec, arg in ins]
    return pl.pallas_call(
        kernel,
        out_shape=jax.tree.map(lambda out: pltpu.VMEM(out.shape, out.dtype), outs) if pinned else outs,
        in_specs=[spec for spec, _ in ins],
        out_specs=jax.tree.map(lambda _: VMEM, outs),
        scratch_shapes=list(scratch),
        name=name,
        compiler_params=pltpu.CompilerParams(vmem_limit_bytes=megabytes << 20),
    )(*args)


def offsets(count):
    down = list(range(count - 1, 0, -1))
    return [down, down[-1:] + down[:-1]]


def head_offset(slot, count):
    first, second = (order[slot] for order in offsets(count))
    return jnp.where(core_index() == 0, first, second)


def core_index():
    return lax.axis_index("exp") % 2


def chip_index():
    return lax.axis_index("exp") // 2


def copies(sems, sources, targets):
    made = [pltpu.make_async_copy(s, t, sems.at[i]) for i, (s, t) in enumerate(zip(sources, targets))]
    for copy in made:
        copy.start()
    return made


def decays(dt_rows, a_log):
    heads, length = dt_rows.shape
    step = jnp.maximum(dt_rows, 0.0) + jnp.log1p(jnp.exp(-jnp.abs(dt_rows)))
    same = lax.broadcasted_iota(jnp.int32, (heads, heads), 0) == lax.broadcasted_iota(jnp.int32, (heads, heads), 1)
    a_column = jnp.sum(jnp.where(same, jnp.broadcast_to(a_log, (heads, heads)), 0.0), axis=1, keepdims=True)
    rate = -step * jnp.exp(a_column)
    row = lax.broadcasted_iota(jnp.int32, (length, length), 0)
    col = lax.broadcasted_iota(jnp.int32, (length, length), 1)
    upper = (row <= col).astype(F32)
    cum = jnp.dot(rate, upper, precision=lax.Precision.HIGHEST, preferred_element_type=F32)
    return step, cum


def pair_lanes(values, pair):
    rows = values.shape[0]
    lane = lax.broadcasted_iota(jnp.int32, (rows, LANES), 1)
    left = jnp.broadcast_to(values[:, 2 * pair : 2 * pair + 1], (rows, LANES))
    right = jnp.broadcast_to(values[:, 2 * pair + 1 : 2 * pair + 2], (rows, LANES))
    return jnp.where(lane < HEAD_DIM, left, right)


def unpacked(block):
    block = block.astype(F32)
    return block[:, STATE : STATE + 1, :] + block[:, STATE + 1 : STATE + 2, :], block[:, 0:STATE, :]


def pack(ref, total, state):
    ref[:, 0:STATE, :] = state.astype(BF16)
    wide = jnp.broadcast_to(total, (ref.shape[0], TILE, LANES))
    high = wide.astype(BF16).astype(F32)
    row = lax.broadcasted_iota(jnp.int32, wide.shape, 1)
    ref[:, STATE : STATE + TILE, :] = jnp.where(row == 0, high, wide - high).astype(BF16)


def state_kernel(x_hbm, b_hbm, dt_hbm, a_hbm, keep_ref, send_ref, *scratch):
    x_ref, b_ref, dt_ref, a_ref, packed_ref, sems = scratch
    loads = copies(sems, (dt_hbm, a_hbm, x_hbm, b_hbm), (dt_ref, a_ref, x_ref, b_ref))
    loads[0].wait()
    loads[1].wait()
    step, cum = decays(dt_ref[...], a_ref[...])
    length = cum.shape[1]
    total = cum[:, length - 1 :]
    tail = (jnp.exp(total - cum) * step).T
    total = jnp.broadcast_to(total, cum.shape).T[0:1]
    loads[2].wait()
    loads[3].wait()
    pairs = packed_ref.shape[0]
    groups = b_ref.shape[1] // STATE
    for group in range(groups):
        turned = b_ref[:, group * STATE : (group + 1) * STATE].T
        for pair in range(group * pairs // groups, (group + 1) * pairs // groups):
            x_pair = x_ref[:, pair * LANES : (pair + 1) * LANES].astype(F32)
            weighted = (pair_lanes(tail, pair) * x_pair).astype(BF16)
            state = jnp.dot(turned, weighted, preferred_element_type=F32)
            pack(packed_ref.at[pair : pair + 1], pair_lanes(total, pair)[None], state[None])
    half = pairs // 2
    keep_ref[...] = packed_ref[pl.ds(core_index() * half, half)]
    send_ref[...] = packed_ref[pl.ds((1 - core_index()) * half, half)]


def chip_state_kernel(keep_ref, got_ref, out_ref):
    first = core_index() == 0
    keep, got = unpacked(keep_ref[...]), unpacked(got_ref[...])
    early = [jnp.where(first, mine, other) for mine, other in zip(keep, got)]
    late = [jnp.where(first, other, mine) for mine, other in zip(keep, got)]
    pack(out_ref, early[0] + late[0], jnp.exp(late[0]) * early[1] + late[1])


def weights_kernel(after_ref, up_hbm, down_hbm, up_ref, down_ref, sems):
    for load in copies(sems, (up_hbm, down_hbm), (up_ref, down_ref)):
        load.wait()


def span_kernel(after_ref, *rest):
    ins, out_ref, block_ref = rest[:-2], rest[-2], rest[-1]
    for mask, part in enumerate(ins):
        block_ref[chip_index() ^ mask] = part[...]
    total, state = unpacked(block_ref[0])
    for chip in range(1, len(ins)):
        here, own = unpacked(block_ref[chip])
        total, state = total + here, jnp.exp(here) * state + own
    pack(out_ref, total, state)


def before_kernel(chips, after_ref, keep_ref, got_ref, *rest):
    ins, (mine_ref, send_ref, chip_ref, part_ref) = rest[:-4], rest[-4:]
    for mask in range(chips):
        chip_ref[chip_index() ^ mask] = ins[mask][...]
    parts = len(ins) - chips
    for mask in range(parts):
        part_ref[lax.axis_index("seq") ^ mask] = ins[chips + mask][...]
    carry = jnp.zeros(mine_ref.shape, F32)
    for ref, count, own in ((part_ref, parts, lax.axis_index("seq")), (chip_ref, chips, chip_index())):
        for index in range(count - 1):
            total, state = unpacked(ref[index])
            carry = jnp.where(index < own, jnp.exp(total) * carry + state, carry)
    first = core_index() == 0
    total, state = (jnp.where(first, k, g) for k, g in zip(unpacked(keep_ref[...]), unpacked(got_ref[...])))
    later = jnp.exp(total) * carry + state
    mine_ref[...] = jnp.where(first, carry, later).astype(BF16)
    send_ref[...] = jnp.where(first, later, carry).astype(BF16)


def inside_kernel(x_hbm, z_hbm, b_hbm, c_hbm, dt_hbm, a_hbm, d_hbm, local_ref, grown_ref, c_ref, *scratch):
    x_ref, z_ref, b_ref, dt_ref, a_ref, d_ref, sems = scratch
    loads = copies(
        sems,
        (dt_hbm, a_hbm, d_hbm, b_hbm, c_hbm, x_hbm, z_hbm),
        (dt_ref, a_ref, d_ref, b_ref, c_ref, x_ref, z_ref),
    )
    for load in loads:
        load.wait()
    step_rows, cum_rows = decays(dt_ref[...], a_ref[...])
    cum = cum_rows.T
    grown = jnp.exp(cum)
    length = cum.shape[0]
    pairs = x_ref.shape[1] // LANES
    groups = b_ref.shape[1] // STATE
    row = lax.broadcasted_iota(jnp.int32, (length, length), 0)
    col = lax.broadcasted_iota(jnp.int32, (length, length), 1)
    lane = lax.broadcasted_iota(jnp.int32, (length, LANES), 1)
    for group in range(groups):
        span = slice(group * STATE, (group + 1) * STATE)
        scores = lax.dot_general(c_ref[:, span], b_ref[:, span], NT, preferred_element_type=F32)
        scores = jnp.where(row >= col, scores, 0.0)
        for pair in range(group * pairs // groups, (group + 1) * pairs // groups):
            at = slice(pair * LANES, (pair + 1) * LANES)
            x_pair = x_ref[:, at]
            halves = []
            for head in (2 * pair, 2 * pair + 1):
                distance = cum[:, head : head + 1] - cum_rows[head : head + 1, :]
                decay = jnp.exp(jnp.where(row >= col, distance, FAR))
                mixing = (scores * (decay * step_rows[head : head + 1, :])).astype(BF16)
                halves.append(jnp.dot(mixing, x_pair, preferred_element_type=F32))
            inside = jnp.where(lane < HEAD_DIM, halves[0], halves[1])
            skip = pair_lanes(d_ref[...], pair) * x_pair.astype(F32)
            z = z_ref[:, at].astype(F32)
            gate = z / (1.0 + jnp.exp(-z))
            local_ref[:, at] = (inside + skip) * gate
            grown_ref[:, at] = pair_lanes(grown, pair) * gate


def prep_kernel(experts, width, resid_hbm, routes_hbm, gates_hbm, gain_hbm, norm_hbm, w_hbm, *rest):
    gate_ref, resid_ref, gain_ref, norm_ref, w_ref, routes_ref, gates_ref, sems = rest
    loads = copies(
        sems,
        (routes_hbm, gates_hbm, resid_hbm, gain_hbm, norm_hbm, w_hbm),
        (routes_ref, gates_ref, resid_ref, gain_ref, norm_ref, w_ref),
    )
    loads[0].wait()
    loads[1].wait()
    count, extent = gate_ref.shape
    start = width // LANES * LANES
    lane = lax.broadcasted_iota(jnp.int32, (extent, count), 0) + start - width
    expert = jnp.where(lane >= experts, lane - experts, lane)
    gate = jnp.zeros((extent, count), F32)
    for pick in range(routes_ref.shape[0]):
        gate = gate + jnp.where(routes_ref[pick] == expert, gates_ref[pick], 0.0)
    high = gate.astype(BF16).astype(F32)
    gate = jnp.where(lane < experts, high, jnp.where(lane < 2 * experts, gate - high, 0.0))
    gate_ref[...] = gate.T.astype(BF16)
    for load in loads[2:]:
        load.wait()


def mixed_kernel(after_up, after_down, local_ref, grown_ref, c_ref, norm_ref, w_ref, mine_ref, got_ref, *rest):
    outs, (normed_ref, state_ref) = rest[:-2], rest[-2:]
    half = mine_ref.shape[0]
    pairs = 2 * half
    state_ref[pl.ds(core_index() * half, half)] = mine_ref[...]
    state_ref[pl.ds((1 - core_index()) * half, half)] = got_ref[...]
    groups = c_ref.shape[1] // STATE
    per_group = pairs // groups
    for group in range(groups):
        c_group = c_ref[:, group * STATE : (group + 1) * STATE]
        gated, squares = [], 0.0
        for pair in range(group * per_group, (group + 1) * per_group):
            span = slice(pair * LANES, (pair + 1) * LANES)
            carried = jnp.dot(c_group, state_ref[pair], preferred_element_type=F32)
            value = local_ref[:, span] + grown_ref[:, span] * carried
            gated.append(value)
            squares = squares + value * value
        mean = jnp.sum(squares, axis=1, keepdims=True) / (per_group * LANES)
        inverse = lax.rsqrt(mean + 1e-05)
        for offset, value in enumerate(gated):
            pair = group * per_group + offset
            span = slice(pair * LANES, (pair + 1) * LANES)
            normed_ref[:, span] = (value * inverse * norm_ref[:, span]).astype(BF16)
    rows = outs[0].shape[0]
    blocks = []
    for shift in range(len(outs)):
        owner = lax.axis_index("head") ^ (head_offset(shift - 1, len(outs)) if shift else 0)
        blocks.append(normed_ref[pl.ds(pl.multiple_of(owner * rows, rows), rows), :])
    product = lax.dot_general(jnp.concatenate(blocks, axis=0), w_ref[...], NT, preferred_element_type=F32)
    for shift, out in enumerate(outs):
        out[...] = product[shift * rows : (shift + 1) * rows].astype(BF16)


def rows_kernel(after_ref, resid_ref, gate_ref, gain_ref, *rest):
    parts, hidden_ref, rows_ref = rest[:-2], rest[-2], rest[-1]
    mixed = parts[0][...].astype(F32)
    for part in parts[1:]:
        mixed = mixed + part[...].astype(F32)
    hidden = (resid_ref[0].astype(F32) + mixed).astype(BF16)
    hidden_ref[...] = hidden
    value = hidden.astype(F32)
    scale = lax.rsqrt(jnp.mean(value * value, axis=1, keepdims=True) + 1e-05)
    width = value.shape[1]
    rows_ref[:, width // LANES * LANES :] = gate_ref[...]
    rows_ref[:, :width] = (value * scale * gain_ref[...]).astype(BF16)


def expert_kernel(experts, count, up_ref, down_ref, other_up_ref, other_down_ref, *rest):
    ins, outs = rest[:count], rest[count:]
    width = up_ref.shape[2]
    start = width // LANES * LANES
    rows = jnp.concatenate([ref[:, :width] for ref in ins], axis=0)
    tail = jnp.concatenate([ref[:, start:] for ref in ins], axis=0).astype(F32)
    lane = lax.broadcasted_iota(jnp.int32, tail.shape, 1) + start - width
    own = lax.axis_index("head") * lax.axis_size("exp") + lax.axis_index("exp")
    other = own + 1 - 2 * core_index()
    total = 0.0
    for expert, up_of, down_of in ((own, up_ref, down_ref), (other, other_up_ref, other_down_ref)):
        up = lax.dot_general(rows, up_of[0], NT, preferred_element_type=F32)
        up = jnp.maximum(up, 0.0)
        activated = (up * up).astype(BF16)
        chosen = (lane == expert) | (lane == expert + experts)
        gate = jnp.sum(jnp.where(chosen, tail, 0.0), axis=1, keepdims=True)
        total = total + jnp.dot(activated, down_of[0], preferred_element_type=F32) * gate
    at = 0
    for out in outs:
        out[...] = total[at : at + out.shape[0]].astype(BF16)
        at += out.shape[0]


def sum_kernel(*refs):
    total = refs[0][...].astype(F32)
    for ref in refs[1:-1]:
        total = total + ref[...].astype(F32)
    refs[-1][...] = total.astype(BF16)


def last_kernel(hidden_ref, *rest):
    parts, out_ref = rest[:-1], rest[-1]
    total = parts[0][...].astype(F32)
    for part in parts[1:]:
        total = total + part[...].astype(F32)
    out_ref[0] = (hidden_ref[...].astype(F32) + total).astype(BF16)


def swap(value, axis, mask):
    size = lax.axis_size(axis)
    return lax.ppermute(value, axis, [(i, i ^ mask) for i in range(size)])


def swap_slot(value, slot, chip_mask=0):
    heads, size = lax.axis_size("head"), lax.axis_size("exp")
    order = offsets(heads)
    pairs = []
    for i in range(heads * size):
        head, exp = i // size, i % size
        pairs.append((i, (head ^ order[exp % 2][slot]) * size + (exp ^ (2 * chip_mask))))
    return lax.ppermute(value, ("head", "exp"), pairs)


def per_device(
    x_in, z_in, b_in, c_in, dt_in, a_log, d_skip, norm_w, w_out, resid, routes, gates, moe_gain, w_up, w_down
):
    length, heads = dt_in.shape
    channels = x_in.shape[1]
    model = w_out.shape[1]
    hidden_units = w_up.shape[2]
    seq_size, head_size, exp_size = lax.axis_size("seq"), lax.axis_size("head"), lax.axis_size("exp")
    chips = exp_size // 2
    rows = resid.shape[1]
    experts = head_size * exp_size
    pairs = channels // LANES
    half = pairs // 2
    dt_rows, a_row, d_row = dt_in.T, a_log[None], d_skip[None]
    dma = pltpu.SemaphoreType.DMA
    packed = struct((half, STATE + TILE, LANES), BF16)

    keep, send = call(
        state_kernel,
        "state",
        [packed, packed],
        [(HBM, x_in), (HBM, b_in), (HBM, dt_rows), (HBM, a_row)],
        [pltpu.VMEM(x_in.shape, BF16), pltpu.VMEM(b_in.shape, BF16), pltpu.VMEM(dt_rows.shape, F32),
         pltpu.VMEM(a_row.shape, F32), pltpu.VMEM((pairs, STATE + TILE, LANES), BF16), dma((4,))],
        megabytes=16,
    )
    local, grown, c_held = call(
        inside_kernel,
        "inside",
        [struct((length, channels), F32), struct((length, channels), F32), struct(c_in.shape, BF16)],
        [(HBM, value) for value in (x_in, z_in, b_in, c_in, dt_rows, a_row, d_row)],
        [pltpu.VMEM(x_in.shape, BF16), pltpu.VMEM(z_in.shape, BF16), pltpu.VMEM(b_in.shape, BF16),
         pltpu.VMEM(dt_rows.shape, F32), pltpu.VMEM(a_row.shape, F32), pltpu.VMEM(d_row.shape, F32), dma((7,))],
        megabytes=16,
    )
    wide = -(-(model + 2 * experts) // LANES) * LANES
    turned = [jnp.transpose(value, (2, 0, 1)) for value in (routes, gates)]
    gate_lanes, resid_held, gain_held, norm_held, w_held = call(
        functools.partial(prep_kernel, experts, model),
        "prep",
        [struct((rows, wide - model // LANES * LANES), BF16), struct(resid.shape, BF16), struct((1, model), F32),
         struct((1, channels), F32), struct((model, channels), BF16)],
        [(HBM, value) for value in (resid, *turned, moe_gain[None], norm_w[None], w_out.T)],
        [pltpu.VMEM(turned[0].shape, jnp.int32), pltpu.VMEM(turned[1].shape, F32), dma((6,))],
        megabytes=16,
    )
    up_turned = jnp.swapaxes(w_up, 1, 2)
    other_up, other_down = swap(up_turned, "exp", 1), swap(w_down, "exp", 1)
    got = swap(send, "exp", 1)
    chip = call(chip_state_kernel, "chip_state", packed, [(VMEM, keep), (VMEM, got)])
    along_y = [chip] + [swap(chip, "exp", 2 * d) for d in range(1, chips)]
    span = call(
        span_kernel,
        "span",
        packed,
        [(ANY, c_held)] + [(VMEM, value) for value in along_y],
        [pltpu.VMEM((chips, *packed.shape), BF16)],
    )
    along_x = [span] + [swap(span, "seq", d) for d in range(1, seq_size)]
    before, before_send = call(
        functools.partial(before_kernel, chips),
        "before",
        [struct((half, STATE, LANES), BF16)] * 2,
        [(ANY, gate_lanes)] + [(VMEM, value) for value in (keep, got, *along_y, *along_x)],
        [pltpu.VMEM((chips, *packed.shape), BF16), pltpu.VMEM((seq_size, *packed.shape), BF16)],
        megabytes=24,
    )
    before_got = swap(before_send, "exp", 1)
    mixed = call(
        mixed_kernel,
        "mixed",
        [struct((rows, model), BF16)] * head_size,
        [(ANY, other_up), (ANY, other_down)]
        + [(VMEM, value) for value in (local, grown, c_held, norm_held, w_held, before, before_got)],
        [pltpu.VMEM((length, channels), BF16), pltpu.VMEM((pairs, STATE, LANES), BF16)],
    )
    up_held, down_held = call(
        weights_kernel,
        "weights",
        [struct(up_turned.shape, BF16), struct(w_down.shape, BF16)],
        [(ANY, mixed[0]), (HBM, up_turned), (HBM, w_down)],
        [dma((2,))],
    )
    slots = list(range(head_size - 1))
    parts = [mixed[0]] + [swap_slot(mixed[k + 1], k) for k in slots]
    hidden, own_rows = call(
        rows_kernel,
        "rows",
        [struct((rows, model), BF16), struct((rows, wide), BF16)],
        [(ANY, up_held)] + [(VMEM, value) for value in (resid_held, gate_lanes, gain_held, *parts)],
    )

    def through_experts(members, sizes):
        return call(
            functools.partial(expert_kernel, experts, len(members)),
            "experts",
            [struct((size * rows, model), BF16) for size in sizes],
            [(VMEM, value) for value in (up_held, down_held, other_up, other_down, *members)],
            megabytes=16,
        )

    near = [swap_slot(own_rows, k) for k in slots]
    far = [
        [swap(near[k], "exp", 2 * d) for k in slots[:-1]]
        + [swap_slot(own_rows, slots[-1], d), swap(own_rows, "exp", 2 * d)]
        for d in range(1, chips)
    ]
    near, whole = lax.optimization_barrier((near + [own_rows], [members[-1] for members in far]))
    far = [members[:-1] + [last] for members, last in zip(far, whole)]
    back_near = through_experts(near, [1] * head_size)
    back_near, far = lax.optimization_barrier((back_near, far))
    back_far = [through_experts(members, [1] * head_size) for members in far]
    totals = []
    for k in slots:
        got = [swap(pieces[k], "exp", 2 * d) for d, pieces in enumerate(back_far, 1)]
        totals.append(
            call(sum_kernel, "sum", struct((rows, model), BF16), [(VMEM, v) for v in (back_near[k], *got)])
        )
    totals[1], mine = lax.optimization_barrier((totals[1], [pieces[-1] for pieces in back_far]))
    arrived = [swap_slot(total, k) for k, total in enumerate(totals)]
    arrived += [swap(piece, "exp", 2 * d) for d, piece in enumerate(mine, 1)]
    return call(
        last_kernel,
        "last",
        struct(resid.shape, BF16),
        [(VMEM, value) for value in (hidden, back_near[-1], *arrived)],
        pinned=False,
    )


def solution(mesh):
    placed = (
        P(("seq", "exp"), "head"),
        P(("seq", "exp"), "head"),
        P(("seq", "exp"), "head"),
        P(("seq", "exp"), "head"),
        P(("seq", "exp"), "head"),
        P("head"),
        P("head"),
        P("head"),
        P("head", None),
        P(("seq", "exp"), "head", None),
        P(("seq", "exp"), "head", None),
        P(("seq", "exp"), "head", None),
        P(),
        P(("head", "exp"), None, None),
        P(("head", "exp"), None, None),
    )
    return jax.shard_map(
        per_device,
        mesh=mesh,
        in_specs=placed,
        out_specs=P(("seq", "exp"), "head", None),
        check_vma=False,
    )
```

```python
import functools

import jax
import jax.numpy as jnp
from jax import lax
from jax.experimental import pallas as pl
from jax.experimental.pallas import tpu as pltpu
from jax.sharding import PartitionSpec as P

HEAD_DIM = 64
STATE = 128
LANES = 128
TILE = 16
FAR = -1e30
F32 = jnp.float32
BF16 = jnp.bfloat16
HBM = pl.BlockSpec(memory_space=pltpu.HBM)
VMEM = pl.BlockSpec(memory_space=pltpu.VMEM)
ANY = pl.BlockSpec(memory_space=pl.ANY)
NT = (((1,), (1,)), ((), ()))


def struct(shape, dtype):
    return jax.ShapeDtypeStruct(shape, dtype)


def call(kernel, name, outs, ins, scratch=(), megabytes=12, pinned=True):
    args = [pltpu.with_memory_space_constraint(arg, pltpu.HBM) if spec is HBM else arg for spec, arg in ins]
    return pl.pallas_call(
        kernel,
        out_shape=jax.tree.map(lambda out: pltpu.VMEM(out.shape, out.dtype), outs) if pinned else outs,
        in_specs=[spec for spec, _ in ins],
        out_specs=jax.tree.map(lambda _: VMEM, outs),
        scratch_shapes=list(scratch),
        name=name,
        compiler_params=pltpu.CompilerParams(vmem_limit_bytes=megabytes << 20),
    )(*args)


def offsets(count):
    down = list(range(count - 1, 0, -1))
    return [down, down[-1:] + down[:-1]]


def head_offset(slot, count):
    first, second = (order[slot] for order in offsets(count))
    return jnp.where(core_index() == 0, first, second)


def core_index():
    return lax.axis_index("exp") % 2


def chip_index():
    return lax.axis_index("exp") // 2


def copies(sems, sources, targets):
    made = [pltpu.make_async_copy(s, t, sems.at[i]) for i, (s, t) in enumerate(zip(sources, targets))]
    for copy in made:
        copy.start()
    return made


def decays(dt_rows, a_log):
    heads, length = dt_rows.shape
    step = jnp.maximum(dt_rows, 0.0) + jnp.log1p(jnp.exp(-jnp.abs(dt_rows)))
    same = lax.broadcasted_iota(jnp.int32, (heads, heads), 0) == lax.broadcasted_iota(jnp.int32, (heads, heads), 1)
    a_column = jnp.sum(jnp.where(same, jnp.broadcast_to(a_log, (heads, heads)), 0.0), axis=1, keepdims=True)
    rate = -step * jnp.exp(a_column)
    row = lax.broadcasted_iota(jnp.int32, (length, length), 0)
    col = lax.broadcasted_iota(jnp.int32, (length, length), 1)
    upper = (row <= col).astype(F32)
    cum = jnp.dot(rate, upper, precision=lax.Precision.HIGHEST, preferred_element_type=F32)
    return step, cum


def pair_lanes(values, pair):
    rows = values.shape[0]
    lane = lax.broadcasted_iota(jnp.int32, (rows, LANES), 1)
    left = jnp.broadcast_to(values[:, 2 * pair : 2 * pair + 1], (rows, LANES))
    right = jnp.broadcast_to(values[:, 2 * pair + 1 : 2 * pair + 2], (rows, LANES))
    return jnp.where(lane < HEAD_DIM, left, right)


def unpacked(block):
    block = block.astype(F32)
    return block[:, STATE : STATE + 1, :] + block[:, STATE + 1 : STATE + 2, :], block[:, 0:STATE, :]


def pack(ref, total, state):
    ref[:, 0:STATE, :] = state.astype(BF16)
    wide = jnp.broadcast_to(total, (ref.shape[0], TILE, LANES))
    high = wide.astype(BF16).astype(F32)
    row = lax.broadcasted_iota(jnp.int32, wide.shape, 1)
    ref[:, STATE : STATE + TILE, :] = jnp.where(row == 0, high, wide - high).astype(BF16)


def state_kernel(x_hbm, b_hbm, dt_hbm, a_hbm, keep_ref, send_ref, *scratch):
    x_ref, b_ref, dt_ref, a_ref, packed_ref, sems = scratch
    loads = copies(sems, (dt_hbm, a_hbm, x_hbm, b_hbm), (dt_ref, a_ref, x_ref, b_ref))
    loads[0].wait()
    loads[1].wait()
    step, cum = decays(dt_ref[...], a_ref[...])
    length = cum.shape[1]
    total = cum[:, length - 1 :]
    tail = (jnp.exp(total - cum) * step).T
    total = jnp.broadcast_to(total, cum.shape).T[0:1]
    loads[2].wait()
    loads[3].wait()
    pairs = packed_ref.shape[0]
    groups = b_ref.shape[1] // STATE
    for group in range(groups):
        turned = b_ref[:, group * STATE : (group + 1) * STATE].T
        for pair in range(group * pairs // groups, (group + 1) * pairs // groups):
            x_pair = x_ref[:, pair * LANES : (pair + 1) * LANES].astype(F32)
            weighted = (pair_lanes(tail, pair) * x_pair).astype(BF16)
            state = jnp.dot(turned, weighted, preferred_element_type=F32)
            pack(packed_ref.at[pair : pair + 1], pair_lanes(total, pair)[None], state[None])
    half = pairs // 2
    keep_ref[...] = packed_ref[pl.ds(core_index() * half, half)]
    send_ref[...] = packed_ref[pl.ds((1 - core_index()) * half, half)]


def chip_state_kernel(keep_ref, got_ref, out_ref):
    first = core_index() == 0
    keep, got = unpacked(keep_ref[...]), unpacked(got_ref[...])
    early = [jnp.where(first, mine, other) for mine, other in zip(keep, got)]
    late = [jnp.where(first, other, mine) for mine, other in zip(keep, got)]
    pack(out_ref, early[0] + late[0], jnp.exp(late[0]) * early[1] + late[1])


def weights_kernel(after_ref, up_hbm, down_hbm, up_ref, down_ref, sems):
    for load in copies(sems, (up_hbm, down_hbm), (up_ref, down_ref)):
        load.wait()


def span_kernel(after_ref, *rest):
    ins, out_ref, block_ref = rest[:-2], rest[-2], rest[-1]
    for mask, part in enumerate(ins):
        block_ref[chip_index() ^ mask] = part[...]
    total, state = unpacked(block_ref[0])
    for chip in range(1, len(ins)):
        here, own = unpacked(block_ref[chip])
        total, state = total + here, jnp.exp(here) * state + own
    pack(out_ref, total, state)


def before_kernel(chips, after_ref, keep_ref, got_ref, *rest):
    ins, (mine_ref, send_ref, chip_ref, part_ref) = rest[:-4], rest[-4:]
    for mask in range(chips):
        chip_ref[chip_index() ^ mask] = ins[mask][...]
    parts = len(ins) - chips
    for mask in range(parts):
        part_ref[lax.axis_index("seq") ^ mask] = ins[chips + mask][...]
    carry = jnp.zeros(mine_ref.shape, F32)
    for ref, count, own in ((part_ref, parts, lax.axis_index("seq")), (chip_ref, chips, chip_index())):
        for index in range(count - 1):
            total, state = unpacked(ref[index])
            carry = jnp.where(index < own, jnp.exp(total) * carry + state, carry)
    first = core_index() == 0
    total, state = (jnp.where(first, k, g) for k, g in zip(unpacked(keep_ref[...]), unpacked(got_ref[...])))
    later = jnp.exp(total) * carry + state
    mine_ref[...] = jnp.where(first, carry, later).astype(BF16)
    send_ref[...] = jnp.where(first, later, carry).astype(BF16)


def inside_kernel(x_hbm, z_hbm, b_hbm, c_hbm, dt_hbm, a_hbm, d_hbm, local_ref, grown_ref, c_ref, *scratch):
    x_ref, z_ref, b_ref, dt_ref, a_ref, d_ref, sems = scratch
    loads = copies(
        sems,
        (dt_hbm, a_hbm, d_hbm, b_hbm, c_hbm, x_hbm, z_hbm),
        (dt_ref, a_ref, d_ref, b_ref, c_ref, x_ref, z_ref),
    )
    for load in loads:
        load.wait()
    step_rows, cum_rows = decays(dt_ref[...], a_ref[...])
    cum = cum_rows.T
    grown = jnp.exp(cum)
    length = cum.shape[0]
    pairs = x_ref.shape[1] // LANES
    groups = b_ref.shape[1] // STATE
    row = lax.broadcasted_iota(jnp.int32, (length, length), 0)
    col = lax.broadcasted_iota(jnp.int32, (length, length), 1)
    lane = lax.broadcasted_iota(jnp.int32, (length, LANES), 1)
    for group in range(groups):
        span = slice(group * STATE, (group + 1) * STATE)
        scores = lax.dot_general(c_ref[:, span], b_ref[:, span], NT, preferred_element_type=F32)
        scores = jnp.where(row >= col, scores, 0.0)
        for pair in range(group * pairs // groups, (group + 1) * pairs // groups):
            at = slice(pair * LANES, (pair + 1) * LANES)
            x_pair = x_ref[:, at]
            halves = []
            for head in (2 * pair, 2 * pair + 1):
                distance = cum[:, head : head + 1] - cum_rows[head : head + 1, :]
                decay = jnp.exp(jnp.where(row >= col, distance, FAR))
                mixing = (scores * (decay * step_rows[head : head + 1, :])).astype(BF16)
                halves.append(jnp.dot(mixing, x_pair, preferred_element_type=F32))
            inside = jnp.where(lane < HEAD_DIM, halves[0], halves[1])
            skip = pair_lanes(d_ref[...], pair) * x_pair.astype(F32)
            z = z_ref[:, at].astype(F32)
            gate = z / (1.0 + jnp.exp(-z))
            local_ref[:, at] = (inside + skip) * gate
            grown_ref[:, at] = pair_lanes(grown, pair) * gate


def prep_kernel(experts, width, resid_hbm, routes_hbm, gates_hbm, gain_hbm, norm_hbm, w_hbm, *rest):
    gate_ref, resid_ref, gain_ref, norm_ref, w_ref, routes_ref, gates_ref, sems = rest
    loads = copies(
        sems,
        (routes_hbm, gates_hbm, resid_hbm, gain_hbm, norm_hbm, w_hbm),
        (routes_ref, gates_ref, resid_ref, gain_ref, norm_ref, w_ref),
    )
    loads[0].wait()
    loads[1].wait()
    count, extent = gate_ref.shape
    start = width // LANES * LANES
    lane = lax.broadcasted_iota(jnp.int32, (extent, count), 0) + start - width
    expert = jnp.where(lane >= experts, lane - experts, lane)
    gate = jnp.zeros((extent, count), F32)
    for pick in range(routes_ref.shape[0]):
        gate = gate + jnp.where(routes_ref[pick] == expert, gates_ref[pick], 0.0)
    high = gate.astype(BF16).astype(F32)
    gate = jnp.where(lane < experts, high, jnp.where(lane < 2 * experts, gate - high, 0.0))
    gate_ref[...] = gate.T.astype(BF16)
    for load in loads[2:]:
        load.wait()


def half_product(half, local_ref, grown_ref, c_ref, norm_ref, w_ref, state_ref, normed_ref, count):
    pairs = state_ref.shape[0]
    width = pairs * LANES
    base = pl.multiple_of(half * width, width)
    groups = c_ref.shape[1] // STATE // 2
    per_group = pairs // groups
    for group in range(groups):
        c_group = c_ref[:, pl.ds(pl.multiple_of((half * groups + group) * STATE, STATE), STATE)]
        gated, squares = [], 0.0
        for pair in range(group * per_group, (group + 1) * per_group):
            span = pl.ds(pl.multiple_of(base + pair * LANES, LANES), LANES)
            carried = jnp.dot(c_group, state_ref[pair], preferred_element_type=F32)
            value = local_ref[:, span] + grown_ref[:, span] * carried
            gated.append(value)
            squares = squares + value * value
        mean = jnp.sum(squares, axis=1, keepdims=True) / (per_group * LANES)
        inverse = lax.rsqrt(mean + 1e-05)
        for offset, value in enumerate(gated):
            pair = group * per_group + offset
            gain = norm_ref[:, pl.ds(pl.multiple_of(base + pair * LANES, LANES), LANES)]
            normed_ref[:, pair * LANES : (pair + 1) * LANES] = (value * inverse * gain).astype(BF16)
    rows = normed_ref.shape[0] // count
    blocks = []
    for shift in range(count):
        owner = lax.axis_index("head") ^ (head_offset(shift - 1, count) if shift else 0)
        blocks.append(normed_ref[pl.ds(pl.multiple_of(owner * rows, rows), rows), :])
    weight = w_ref[:, pl.ds(base, width)]
    return lax.dot_general(jnp.concatenate(blocks, axis=0), weight, NT, preferred_element_type=F32)


def first_half_kernel(count, local_ref, grown_ref, c_ref, norm_ref, w_ref, mine_ref, out_ref, normed_ref):
    out_ref[...] = half_product(
        core_index(), local_ref, grown_ref, c_ref, norm_ref, w_ref, mine_ref, normed_ref, count
    )


def mixed_kernel(after_up, after_down, local_ref, grown_ref, c_ref, norm_ref, w_ref, got_ref, first_ref, *rest):
    outs, normed_ref = rest[:-1], rest[-1]
    product = first_ref[...] + half_product(
        1 - core_index(), local_ref, grown_ref, c_ref, norm_ref, w_ref, got_ref, normed_ref, len(outs)
    )
    rows = outs[0].shape[0]
    for shift, out in enumerate(outs):
        out[...] = product[shift * rows : (shift + 1) * rows].astype(BF16)


def rows_kernel(after_ref, resid_ref, gate_ref, gain_ref, *rest):
    parts, hidden_ref, rows_ref = rest[:-2], rest[-2], rest[-1]
    mixed = parts[0][...].astype(F32)
    for part in parts[1:]:
        mixed = mixed + part[...].astype(F32)
    hidden = (resid_ref[0].astype(F32) + mixed).astype(BF16)
    hidden_ref[...] = hidden
    value = hidden.astype(F32)
    scale = lax.rsqrt(jnp.mean(value * value, axis=1, keepdims=True) + 1e-05)
    width = value.shape[1]
    rows_ref[:, width // LANES * LANES :] = gate_ref[...]
    rows_ref[:, :width] = (value * scale * gain_ref[...]).astype(BF16)


def expert_kernel(experts, count, up_ref, down_ref, other_up_ref, other_down_ref, *rest):
    ins, outs = rest[:count], rest[count:]
    width = up_ref.shape[2]
    start = width // LANES * LANES
    rows = jnp.concatenate([ref[:, :width] for ref in ins], axis=0)
    tail = jnp.concatenate([ref[:, start:] for ref in ins], axis=0).astype(F32)
    lane = lax.broadcasted_iota(jnp.int32, tail.shape, 1) + start - width
    own = lax.axis_index("head") * lax.axis_size("exp") + lax.axis_index("exp")
    other = own + 1 - 2 * core_index()
    total = 0.0
    for expert, up_of, down_of in ((own, up_ref, down_ref), (other, other_up_ref, other_down_ref)):
        up = lax.dot_general(rows, up_of[0], NT, preferred_element_type=F32)
        up = jnp.maximum(up, 0.0)
        activated = (up * up).astype(BF16)
        chosen = (lane == expert) | (lane == expert + experts)
        gate = jnp.sum(jnp.where(chosen, tail, 0.0), axis=1, keepdims=True)
        total = total + jnp.dot(activated, down_of[0], preferred_element_type=F32) * gate
    at = 0
    for out in outs:
        out[...] = total[at : at + out.shape[0]].astype(BF16)
        at += out.shape[0]


def sum_kernel(*refs):
    total = refs[0][...].astype(F32)
    for ref in refs[1:-1]:
        total = total + ref[...].astype(F32)
    refs[-1][...] = total.astype(BF16)


def last_kernel(hidden_ref, *rest):
    parts, out_ref = rest[:-1], rest[-1]
    total = parts[0][...].astype(F32)
    for part in parts[1:]:
        total = total + part[...].astype(F32)
    out_ref[0] = (hidden_ref[...].astype(F32) + total).astype(BF16)


def swap(value, axis, mask):
    size = lax.axis_size(axis)
    return lax.ppermute(value, axis, [(i, i ^ mask) for i in range(size)])


def swap_slot(value, slot, chip_mask=0):
    heads, size = lax.axis_size("head"), lax.axis_size("exp")
    order = offsets(heads)
    pairs = []
    for i in range(heads * size):
        head, exp = i // size, i % size
        pairs.append((i, (head ^ order[exp % 2][slot]) * size + (exp ^ (2 * chip_mask))))
    return lax.ppermute(value, ("head", "exp"), pairs)


def per_device(
    x_in, z_in, b_in, c_in, dt_in, a_log, d_skip, norm_w, w_out, resid, routes, gates, moe_gain, w_up, w_down
):
    length, heads = dt_in.shape
    channels = x_in.shape[1]
    model = w_out.shape[1]
    hidden_units = w_up.shape[2]
    seq_size, head_size, exp_size = lax.axis_size("seq"), lax.axis_size("head"), lax.axis_size("exp")
    chips = exp_size // 2
    rows = resid.shape[1]
    experts = head_size * exp_size
    pairs = channels // LANES
    half = pairs // 2
    dt_rows, a_row, d_row = dt_in.T, a_log[None], d_skip[None]
    dma = pltpu.SemaphoreType.DMA
    packed = struct((half, STATE + TILE, LANES), BF16)

    keep, send = call(
        state_kernel,
        "state",
        [packed, packed],
        [(HBM, x_in), (HBM, b_in), (HBM, dt_rows), (HBM, a_row)],
        [pltpu.VMEM(x_in.shape, BF16), pltpu.VMEM(b_in.shape, BF16), pltpu.VMEM(dt_rows.shape, F32),
         pltpu.VMEM(a_row.shape, F32), pltpu.VMEM((pairs, STATE + TILE, LANES), BF16), dma((4,))],
        megabytes=16,
    )
    local, grown, c_held = call(
        inside_kernel,
        "inside",
        [struct((length, channels), F32), struct((length, channels), F32), struct(c_in.shape, BF16)],
        [(HBM, value) for value in (x_in, z_in, b_in, c_in, dt_rows, a_row, d_row)],
        [pltpu.VMEM(x_in.shape, BF16), pltpu.VMEM(z_in.shape, BF16), pltpu.VMEM(b_in.shape, BF16),
         pltpu.VMEM(dt_rows.shape, F32), pltpu.VMEM(a_row.shape, F32), pltpu.VMEM(d_row.shape, F32), dma((7,))],
        megabytes=16,
    )
    wide = -(-(model + 2 * experts) // LANES) * LANES
    turned = [jnp.transpose(value, (2, 0, 1)) for value in (routes, gates)]
    gate_lanes, resid_held, gain_held, norm_held, w_held = call(
        functools.partial(prep_kernel, experts, model),
        "prep",
        [struct((rows, wide - model // LANES * LANES), BF16), struct(resid.shape, BF16), struct((1, model), F32),
         struct((1, channels), F32), struct((model, channels), BF16)],
        [(HBM, value) for value in (resid, *turned, moe_gain[None], norm_w[None], w_out.T)],
        [pltpu.VMEM(turned[0].shape, jnp.int32), pltpu.VMEM(turned[1].shape, F32), dma((6,))],
        megabytes=16,
    )
    up_turned = jnp.swapaxes(w_up, 1, 2)
    got = swap(send, "exp", 1)
    chip = call(chip_state_kernel, "chip_state", packed, [(VMEM, keep), (VMEM, got)])
    chip, up_after, down_after = lax.optimization_barrier((chip, up_turned, w_down))
    other_up, other_down = swap(up_after, "exp", 1), swap(down_after, "exp", 1)
    along_y = [chip] + [swap(chip, "exp", 2 * d) for d in range(1, chips)]
    span = call(
        span_kernel,
        "span",
        packed,
        [(ANY, c_held)] + [(VMEM, value) for value in along_y],
        [pltpu.VMEM((chips, *packed.shape), BF16)],
    )
    along_x = [span] + [swap(span, "seq", d) for d in range(1, seq_size)]
    before, before_send = call(
        functools.partial(before_kernel, chips),
        "before",
        [struct((half, STATE, LANES), BF16)] * 2,
        [(ANY, gate_lanes)] + [(VMEM, value) for value in (keep, got, *along_y, *along_x)],
        [pltpu.VMEM((chips, *packed.shape), BF16), pltpu.VMEM((seq_size, *packed.shape), BF16)],
        megabytes=24,
    )
    before_got = swap(before_send, "exp", 1)
    shared = [(VMEM, value) for value in (local, grown, c_held, norm_held, w_held)]
    normed_half = pltpu.VMEM((length, channels // 2), BF16)
    first = call(
        functools.partial(first_half_kernel, head_size),
        "first_half",
        struct((length, model), F32),
        shared + [(VMEM, before)],
        [normed_half],
    )
    mixed = call(
        mixed_kernel,
        "mixed",
        [struct((rows, model), BF16)] * head_size,
        [(ANY, other_up), (ANY, other_down)] + shared + [(VMEM, before_got), (VMEM, first)],
        [normed_half],
    )
    up_held, down_held = call(
        weights_kernel,
        "weights",
        [struct(up_turned.shape, BF16), struct(w_down.shape, BF16)],
        [(ANY, mixed[0]), (HBM, up_turned), (HBM, w_down)],
        [dma((2,))],
    )
    slots = list(range(head_size - 1))
    parts = [mixed[0]] + [swap_slot(mixed[k + 1], k) for k in slots]
    hidden, own_rows = call(
        rows_kernel,
        "rows",
        [struct((rows, model), BF16), struct((rows, wide), BF16)],
        [(ANY, up_held)] + [(VMEM, value) for value in (resid_held, gate_lanes, gain_held, *parts)],
    )

    def through_experts(members, sizes):
        return call(
            functools.partial(expert_kernel, experts, len(members)),
            "experts",
            [struct((size * rows, model), BF16) for size in sizes],
            [(VMEM, value) for value in (up_held, down_held, other_up, other_down, *members)],
            megabytes=16,
        )

    near = [swap_slot(own_rows, k) for k in slots]
    far = [
        [swap(near[k], "exp", 2 * d) for k in slots[:-1]]
        + [swap_slot(own_rows, slots[-1], d), swap(own_rows, "exp", 2 * d)]
        for d in range(1, chips)
    ]
    near, whole = lax.optimization_barrier((near + [own_rows], [members[-1] for members in far]))
    far = [members[:-1] + [last] for members, last in zip(far, whole)]
    back_near = through_experts(near, [1] * head_size)
    back_near, far = lax.optimization_barrier((back_near, far))
    back_far = [through_experts(members, [1] * head_size) for members in far]
    totals = []
    for k in slots:
        got = [swap(pieces[k], "exp", 2 * d) for d, pieces in enumerate(back_far, 1)]
        totals.append(
            call(sum_kernel, "sum", struct((rows, model), BF16), [(VMEM, v) for v in (back_near[k], *got)])
        )
    totals[-2], mine = lax.optimization_barrier((totals[-2], [pieces[-1] for pieces in back_far]))
    arrived = [swap_slot(total, k) for k, total in enumerate(totals)]
    arrived += [swap(piece, "exp", 2 * d) for d, piece in enumerate(mine, 1)]
    return call(
        last_kernel,
        "last",
        struct(resid.shape, BF16),
        [(VMEM, value) for value in (hidden, back_near[-1], *arrived)],
        pinned=False,
    )


def solution(mesh):
    placed = (
        P(("seq", "exp"), "head"),
        P(("seq", "exp"), "head"),
        P(("seq", "exp"), "head"),
        P(("seq", "exp"), "head"),
        P(("seq", "exp"), "head"),
        P("head"),
        P("head"),
        P("head"),
        P("head", None),
        P(("seq", "exp"), "head", None),
        P(("seq", "exp"), "head", None),
        P(("seq", "exp"), "head", None),
        P(),
        P(("head", "exp"), None, None),
        P(("head", "exp"), None, None),
    )
    return jax.shard_map(
        per_device,
        mesh=mesh,
        in_specs=placed,
        out_specs=P(("seq", "exp"), "head", None),
        check_vma=False,
    )
```

```python
import functools

import jax
import jax.numpy as jnp
from jax import lax
from jax.experimental import pallas as pl
from jax.experimental.pallas import tpu as pltpu
from jax.sharding import PartitionSpec as P

HEAD_DIM = 64
STATE = 128
LANES = 128
TILE = 16
FAR = -1e30
F32 = jnp.float32
BF16 = jnp.bfloat16
HBM = pl.BlockSpec(memory_space=pltpu.HBM)
VMEM = pl.BlockSpec(memory_space=pltpu.VMEM)
ANY = pl.BlockSpec(memory_space=pl.ANY)
NT = (((1,), (1,)), ((), ()))


def struct(shape, dtype):
    return jax.ShapeDtypeStruct(shape, dtype)


def call(kernel, name, outs, ins, scratch=(), megabytes=12, pinned=True):
    args = [pltpu.with_memory_space_constraint(arg, pltpu.HBM) if spec is HBM else arg for spec, arg in ins]
    return pl.pallas_call(
        kernel,
        out_shape=jax.tree.map(lambda out: pltpu.VMEM(out.shape, out.dtype), outs) if pinned else outs,
        in_specs=[spec for spec, _ in ins],
        out_specs=jax.tree.map(lambda _: VMEM, outs),
        scratch_shapes=list(scratch),
        name=name,
        compiler_params=pltpu.CompilerParams(vmem_limit_bytes=megabytes << 20),
    )(*args)


def offsets(count):
    down = list(range(count - 1, 0, -1))
    return [down, down[-2::-1] + down[-1:]]


def head_offset(slot, count):
    first, second = (order[slot] for order in offsets(count))
    return jnp.where(core_index() == 0, first, second)


def core_index():
    return lax.axis_index("exp") % 2


def chip_index():
    return lax.axis_index("exp") // 2


def copies(sems, sources, targets):
    made = [pltpu.make_async_copy(s, t, sems.at[i]) for i, (s, t) in enumerate(zip(sources, targets))]
    for copy in made:
        copy.start()
    return made


def decays(dt_rows, a_log):
    heads, length = dt_rows.shape
    step = jnp.maximum(dt_rows, 0.0) + jnp.log1p(jnp.exp(-jnp.abs(dt_rows)))
    same = lax.broadcasted_iota(jnp.int32, (heads, heads), 0) == lax.broadcasted_iota(jnp.int32, (heads, heads), 1)
    a_column = jnp.sum(jnp.where(same, jnp.broadcast_to(a_log, (heads, heads)), 0.0), axis=1, keepdims=True)
    rate = -step * jnp.exp(a_column)
    row = lax.broadcasted_iota(jnp.int32, (length, length), 0)
    col = lax.broadcasted_iota(jnp.int32, (length, length), 1)
    upper = (row <= col).astype(F32)
    cum = jnp.dot(rate, upper, precision=lax.Precision.HIGHEST, preferred_element_type=F32)
    return step, cum


def pair_lanes(values, pair):
    rows = values.shape[0]
    lane = lax.broadcasted_iota(jnp.int32, (rows, LANES), 1)
    left = jnp.broadcast_to(values[:, 2 * pair : 2 * pair + 1], (rows, LANES))
    right = jnp.broadcast_to(values[:, 2 * pair + 1 : 2 * pair + 2], (rows, LANES))
    return jnp.where(lane < HEAD_DIM, left, right)


def unpacked(block):
    block = block.astype(F32)
    return block[:, STATE : STATE + 1, :] + block[:, STATE + 1 : STATE + 2, :], block[:, 0:STATE, :]


def pack(ref, total, state):
    ref[:, 0:STATE, :] = state.astype(BF16)
    wide = jnp.broadcast_to(total, (ref.shape[0], TILE, LANES))
    high = wide.astype(BF16).astype(F32)
    row = lax.broadcasted_iota(jnp.int32, wide.shape, 1)
    ref[:, STATE : STATE + TILE, :] = jnp.where(row == 0, high, wide - high).astype(BF16)


def state_kernel(x_hbm, b_hbm, dt_hbm, a_hbm, keep_ref, send_ref, *scratch):
    x_ref, b_ref, dt_ref, a_ref, packed_ref, sems = scratch
    loads = copies(sems, (dt_hbm, a_hbm, x_hbm, b_hbm), (dt_ref, a_ref, x_ref, b_ref))
    loads[0].wait()
    loads[1].wait()
    step, cum = decays(dt_ref[...], a_ref[...])
    length = cum.shape[1]
    total = cum[:, length - 1 :]
    tail = (jnp.exp(total - cum) * step).T
    total = jnp.broadcast_to(total, cum.shape).T[0:1]
    loads[2].wait()
    loads[3].wait()
    pairs = packed_ref.shape[0]
    groups = b_ref.shape[1] // STATE
    for group in range(groups):
        turned = b_ref[:, group * STATE : (group + 1) * STATE].T
        for pair in range(group * pairs // groups, (group + 1) * pairs // groups):
            x_pair = x_ref[:, pair * LANES : (pair + 1) * LANES].astype(F32)
            weighted = (pair_lanes(tail, pair) * x_pair).astype(BF16)
            state = jnp.dot(turned, weighted, preferred_element_type=F32)
            pack(packed_ref.at[pair : pair + 1], pair_lanes(total, pair)[None], state[None])
    half = pairs // 2
    keep_ref[...] = packed_ref[pl.ds(core_index() * half, half)]
    send_ref[...] = packed_ref[pl.ds((1 - core_index()) * half, half)]


def chip_state_kernel(keep_ref, got_ref, out_ref):
    first = core_index() == 0
    keep, got = unpacked(keep_ref[...]), unpacked(got_ref[...])
    early = [jnp.where(first, mine, other) for mine, other in zip(keep, got)]
    late = [jnp.where(first, other, mine) for mine, other in zip(keep, got)]
    pack(out_ref, early[0] + late[0], jnp.exp(late[0]) * early[1] + late[1])


def weights_kernel(after_ref, up_hbm, down_hbm, up_ref, down_ref, sems):
    for load in copies(sems, (up_hbm, down_hbm), (up_ref, down_ref)):
        load.wait()


def span_kernel(after_ref, *rest):
    ins, out_ref, block_ref = rest[:-2], rest[-2], rest[-1]
    for mask, part in enumerate(ins):
        block_ref[chip_index() ^ mask] = part[...]
    total, state = unpacked(block_ref[0])
    for chip in range(1, len(ins)):
        here, own = unpacked(block_ref[chip])
        total, state = total + here, jnp.exp(here) * state + own
    pack(out_ref, total, state)


def before_kernel(chips, after_ref, keep_ref, got_ref, *rest):
    ins, (mine_ref, send_ref, chip_ref, part_ref) = rest[:-4], rest[-4:]
    for mask in range(chips):
        chip_ref[chip_index() ^ mask] = ins[mask][...]
    parts = len(ins) - chips
    for mask in range(parts):
        part_ref[lax.axis_index("seq") ^ mask] = ins[chips + mask][...]
    carry = jnp.zeros(mine_ref.shape, F32)
    for ref, count, own in ((part_ref, parts, lax.axis_index("seq")), (chip_ref, chips, chip_index())):
        for index in range(count - 1):
            total, state = unpacked(ref[index])
            carry = jnp.where(index < own, jnp.exp(total) * carry + state, carry)
    first = core_index() == 0
    total, state = (jnp.where(first, k, g) for k, g in zip(unpacked(keep_ref[...]), unpacked(got_ref[...])))
    later = jnp.exp(total) * carry + state
    mine_ref[...] = jnp.where(first, carry, later).astype(BF16)
    send_ref[...] = jnp.where(first, later, carry).astype(BF16)


def inside_kernel(x_hbm, z_hbm, b_hbm, c_hbm, dt_hbm, a_hbm, d_hbm, local_ref, grown_ref, c_ref, *scratch):
    x_ref, z_ref, b_ref, dt_ref, a_ref, d_ref, sems = scratch
    loads = copies(
        sems,
        (dt_hbm, a_hbm, d_hbm, b_hbm, c_hbm, x_hbm, z_hbm),
        (dt_ref, a_ref, d_ref, b_ref, c_ref, x_ref, z_ref),
    )
    for load in loads:
        load.wait()
    step_rows, cum_rows = decays(dt_ref[...], a_ref[...])
    cum = cum_rows.T
    grown = jnp.exp(cum)
    length = cum.shape[0]
    pairs = x_ref.shape[1] // LANES
    groups = b_ref.shape[1] // STATE
    row = lax.broadcasted_iota(jnp.int32, (length, length), 0)
    col = lax.broadcasted_iota(jnp.int32, (length, length), 1)
    lane = lax.broadcasted_iota(jnp.int32, (length, LANES), 1)
    for group in range(groups):
        span = slice(group * STATE, (group + 1) * STATE)
        scores = lax.dot_general(c_ref[:, span], b_ref[:, span], NT, preferred_element_type=F32)
        scores = jnp.where(row >= col, scores, 0.0)
        for pair in range(group * pairs // groups, (group + 1) * pairs // groups):
            at = slice(pair * LANES, (pair + 1) * LANES)
            x_pair = x_ref[:, at]
            halves = []
            for head in (2 * pair, 2 * pair + 1):
                distance = cum[:, head : head + 1] - cum_rows[head : head + 1, :]
                decay = jnp.exp(jnp.where(row >= col, distance, FAR))
                mixing = (scores * (decay * step_rows[head : head + 1, :])).astype(BF16)
                halves.append(jnp.dot(mixing, x_pair, preferred_element_type=F32))
            inside = jnp.where(lane < HEAD_DIM, halves[0], halves[1])
            skip = pair_lanes(d_ref[...], pair) * x_pair.astype(F32)
            z = z_ref[:, at].astype(F32)
            gate = z / (1.0 + jnp.exp(-z))
            local_ref[:, at] = (inside + skip) * gate
            grown_ref[:, at] = pair_lanes(grown, pair) * gate


def prep_kernel(experts, width, resid_hbm, routes_hbm, gates_hbm, gain_hbm, norm_hbm, w_hbm, *rest):
    gate_ref, resid_ref, gain_ref, norm_ref, w_ref, routes_ref, gates_ref, sems = rest
    loads = copies(
        sems,
        (routes_hbm, gates_hbm, resid_hbm, gain_hbm, norm_hbm, w_hbm),
        (routes_ref, gates_ref, resid_ref, gain_ref, norm_ref, w_ref),
    )
    loads[0].wait()
    loads[1].wait()
    count, extent = gate_ref.shape
    start = width // LANES * LANES
    lane = lax.broadcasted_iota(jnp.int32, (extent, count), 0) + start - width
    expert = jnp.where(lane >= experts, lane - experts, lane)
    gate = jnp.zeros((extent, count), F32)
    for pick in range(routes_ref.shape[0]):
        gate = gate + jnp.where(routes_ref[pick] == expert, gates_ref[pick], 0.0)
    high = gate.astype(BF16).astype(F32)
    gate = jnp.where(lane < experts, high, jnp.where(lane < 2 * experts, gate - high, 0.0))
    gate_ref[...] = gate.T.astype(BF16)
    for load in loads[2:]:
        load.wait()


def half_product(half, local_ref, grown_ref, c_ref, norm_ref, w_ref, state_ref, normed_ref, count):
    pairs = state_ref.shape[0]
    width = pairs * LANES
    base = pl.multiple_of(half * width, width)
    groups = c_ref.shape[1] // STATE // 2
    per_group = pairs // groups
    for group in range(groups):
        c_group = c_ref[:, pl.ds(pl.multiple_of((half * groups + group) * STATE, STATE), STATE)]
        gated, squares = [], 0.0
        for pair in range(group * per_group, (group + 1) * per_group):
            span = pl.ds(pl.multiple_of(base + pair * LANES, LANES), LANES)
            carried = jnp.dot(c_group, state_ref[pair], preferred_element_type=F32)
            value = local_ref[:, span] + grown_ref[:, span] * carried
            gated.append(value)
            squares = squares + value * value
        mean = jnp.sum(squares, axis=1, keepdims=True) / (per_group * LANES)
        inverse = lax.rsqrt(mean + 1e-05)
        for offset, value in enumerate(gated):
            pair = group * per_group + offset
            gain = norm_ref[:, pl.ds(pl.multiple_of(base + pair * LANES, LANES), LANES)]
            normed_ref[:, pair * LANES : (pair + 1) * LANES] = (value * inverse * gain).astype(BF16)
    rows = normed_ref.shape[0] // count
    blocks = []
    for shift in range(count):
        owner = lax.axis_index("head") ^ (head_offset(shift - 1, count) if shift else 0)
        blocks.append(normed_ref[pl.ds(pl.multiple_of(owner * rows, rows), rows), :])
    weight = w_ref[:, pl.ds(base, width)]
    return lax.dot_general(jnp.concatenate(blocks, axis=0), weight, NT, preferred_element_type=F32)


def first_half_kernel(count, local_ref, grown_ref, c_ref, norm_ref, w_ref, mine_ref, out_ref, normed_ref):
    out_ref[...] = half_product(
        core_index(), local_ref, grown_ref, c_ref, norm_ref, w_ref, mine_ref, normed_ref, count
    )


def mixed_kernel(after_up, after_down, local_ref, grown_ref, c_ref, norm_ref, w_ref, got_ref, first_ref, *rest):
    outs, normed_ref = rest[:-1], rest[-1]
    product = first_ref[...] + half_product(
        1 - core_index(), local_ref, grown_ref, c_ref, norm_ref, w_ref, got_ref, normed_ref, len(outs)
    )
    rows = outs[0].shape[0]
    for shift, out in enumerate(outs):
        out[...] = product[shift * rows : (shift + 1) * rows].astype(BF16)


def rows_kernel(after_ref, resid_ref, gate_ref, gain_ref, *rest):
    parts, hidden_ref, rows_ref = rest[:-2], rest[-2], rest[-1]
    mixed = parts[0][...].astype(F32)
    for part in parts[1:]:
        mixed = mixed + part[...].astype(F32)
    hidden = (resid_ref[0].astype(F32) + mixed).astype(BF16)
    hidden_ref[...] = hidden
    value = hidden.astype(F32)
    scale = lax.rsqrt(jnp.mean(value * value, axis=1, keepdims=True) + 1e-05)
    width = value.shape[1]
    rows_ref[:, width // LANES * LANES :] = gate_ref[...]
    rows_ref[:, :width] = (value * scale * gain_ref[...]).astype(BF16)


def expert_kernel(experts, count, up_ref, down_ref, other_up_ref, other_down_ref, *rest):
    ins, outs = rest[:count], rest[count:]
    width = up_ref.shape[2]
    start = width // LANES * LANES
    rows = jnp.concatenate([ref[:, :width] for ref in ins], axis=0)
    tail = jnp.concatenate([ref[:, start:] for ref in ins], axis=0).astype(F32)
    lane = lax.broadcasted_iota(jnp.int32, tail.shape, 1) + start - width
    own = lax.axis_index("head") * lax.axis_size("exp") + lax.axis_index("exp")
    other = own + 1 - 2 * core_index()
    total = 0.0
    for expert, up_of, down_of in ((own, up_ref, down_ref), (other, other_up_ref, other_down_ref)):
        up = lax.dot_general(rows, up_of[0], NT, preferred_element_type=F32)
        up = jnp.maximum(up, 0.0)
        activated = (up * up).astype(BF16)
        chosen = (lane == expert) | (lane == expert + experts)
        gate = jnp.sum(jnp.where(chosen, tail, 0.0), axis=1, keepdims=True)
        total = total + jnp.dot(activated, down_of[0], preferred_element_type=F32) * gate
    at = 0
    for out in outs:
        out[...] = total[at : at + out.shape[0]].astype(BF16)
        at += out.shape[0]


def sum_kernel(*refs):
    total = refs[0][...].astype(F32)
    for ref in refs[1:-1]:
        total = total + ref[...].astype(F32)
    refs[-1][...] = total.astype(BF16)


def last_kernel(hidden_ref, *rest):
    parts, out_ref = rest[:-1], rest[-1]
    total = parts[0][...].astype(F32)
    for part in parts[1:]:
        total = total + part[...].astype(F32)
    out_ref[0] = (hidden_ref[...].astype(F32) + total).astype(BF16)


def swap(value, axis, mask):
    size = lax.axis_size(axis)
    return lax.ppermute(value, axis, [(i, i ^ mask) for i in range(size)])


def swap_slot(value, slot, chip_mask=0):
    heads, size = lax.axis_size("head"), lax.axis_size("exp")
    order = offsets(heads)
    pairs = []
    for i in range(heads * size):
        head, exp = i // size, i % size
        pairs.append((i, (head ^ order[exp % 2][slot]) * size + (exp ^ (2 * chip_mask))))
    return lax.ppermute(value, ("head", "exp"), pairs)


def per_device(
    x_in, z_in, b_in, c_in, dt_in, a_log, d_skip, norm_w, w_out, resid, routes, gates, moe_gain, w_up, w_down
):
    length, heads = dt_in.shape
    channels = x_in.shape[1]
    model = w_out.shape[1]
    hidden_units = w_up.shape[2]
    seq_size, head_size, exp_size = lax.axis_size("seq"), lax.axis_size("head"), lax.axis_size("exp")
    chips = exp_size // 2
    rows = resid.shape[1]
    experts = head_size * exp_size
    pairs = channels // LANES
    half = pairs // 2
    dt_rows, a_row, d_row = dt_in.T, a_log[None], d_skip[None]
    dma = pltpu.SemaphoreType.DMA
    packed = struct((half, STATE + TILE, LANES), BF16)

    keep, send = call(
        state_kernel,
        "state",
        [packed, packed],
        [(HBM, x_in), (HBM, b_in), (HBM, dt_rows), (HBM, a_row)],
        [pltpu.VMEM(x_in.shape, BF16), pltpu.VMEM(b_in.shape, BF16), pltpu.VMEM(dt_rows.shape, F32),
         pltpu.VMEM(a_row.shape, F32), pltpu.VMEM((pairs, STATE + TILE, LANES), BF16), dma((4,))],
        megabytes=16,
    )
    local, grown, c_held = call(
        inside_kernel,
        "inside",
        [struct((length, channels), F32), struct((length, channels), F32), struct(c_in.shape, BF16)],
        [(HBM, value) for value in (x_in, z_in, b_in, c_in, dt_rows, a_row, d_row)],
        [pltpu.VMEM(x_in.shape, BF16), pltpu.VMEM(z_in.shape, BF16), pltpu.VMEM(b_in.shape, BF16),
         pltpu.VMEM(dt_rows.shape, F32), pltpu.VMEM(a_row.shape, F32), pltpu.VMEM(d_row.shape, F32), dma((7,))],
        megabytes=16,
    )
    wide = -(-(model + 2 * experts) // LANES) * LANES
    turned = [jnp.transpose(value, (2, 0, 1)) for value in (routes, gates)]
    gate_lanes, resid_held, gain_held, norm_held, w_held = call(
        functools.partial(prep_kernel, experts, model),
        "prep",
        [struct((rows, wide - model // LANES * LANES), BF16), struct(resid.shape, BF16), struct((1, model), F32),
         struct((1, channels), F32), struct((model, channels), BF16)],
        [(HBM, value) for value in (resid, *turned, moe_gain[None], norm_w[None], w_out.T)],
        [pltpu.VMEM(turned[0].shape, jnp.int32), pltpu.VMEM(turned[1].shape, F32), dma((6,))],
        megabytes=16,
    )
    up_turned = jnp.swapaxes(w_up, 1, 2)
    got = swap(send, "exp", 1)
    chip = call(chip_state_kernel, "chip_state", packed, [(VMEM, keep), (VMEM, got)])
    chip, up_after, down_after = lax.optimization_barrier((chip, up_turned, w_down))
    other_up, other_down = swap(up_after, "exp", 1), swap(down_after, "exp", 1)
    along_y = [chip] + [swap(chip, "exp", 2 * d) for d in range(1, chips)]
    span = call(
        span_kernel,
        "span",
        packed,
        [(ANY, c_held)] + [(VMEM, value) for value in along_y],
        [pltpu.VMEM((chips, *packed.shape), BF16)],
    )
    along_x = [span] + [swap(span, "seq", d) for d in range(1, seq_size)]
    before, before_send = call(
        functools.partial(before_kernel, chips),
        "before",
        [struct((half, STATE, LANES), BF16)] * 2,
        [(ANY, gate_lanes)] + [(VMEM, value) for value in (keep, got, *along_y, *along_x)],
        [pltpu.VMEM((chips, *packed.shape), BF16), pltpu.VMEM((seq_size, *packed.shape), BF16)],
        megabytes=24,
    )
    before_got = swap(before_send, "exp", 1)
    shared = [(VMEM, value) for value in (local, grown, c_held, norm_held, w_held)]
    normed_half = pltpu.VMEM((length, channels // 2), BF16)
    first = call(
        functools.partial(first_half_kernel, head_size),
        "first_half",
        struct((length, model), F32),
        shared + [(VMEM, before)],
        [normed_half],
    )
    mixed = call(
        mixed_kernel,
        "mixed",
        [struct((rows, model), BF16)] * head_size,
        [(ANY, other_up), (ANY, other_down)] + shared + [(VMEM, before_got), (VMEM, first)],
        [normed_half],
    )
    up_held, down_held = call(
        weights_kernel,
        "weights",
        [struct(up_turned.shape, BF16), struct(w_down.shape, BF16)],
        [(ANY, mixed[0]), (HBM, up_turned), (HBM, w_down)],
        [dma((2,))],
    )
    slots = list(range(head_size - 1))
    parts = [mixed[0]] + [swap_slot(mixed[k + 1], k) for k in slots]
    hidden, own_rows = call(
        rows_kernel,
        "rows",
        [struct((rows, model), BF16), struct((rows, wide), BF16)],
        [(ANY, up_held)] + [(VMEM, value) for value in (resid_held, gate_lanes, gain_held, *parts)],
    )

    def through_experts(members, sizes):
        return call(
            functools.partial(expert_kernel, experts, len(members)),
            "experts",
            [struct((size * rows, model), BF16) for size in sizes],
            [(VMEM, value) for value in (up_held, down_held, other_up, other_down, *members)],
            megabytes=16,
        )

    near = [swap_slot(own_rows, k) for k in slots]
    far = [
        [swap(near[k], "exp", 2 * d) for k in slots[:-1]]
        + [swap_slot(own_rows, slots[-1], d), swap(own_rows, "exp", 2 * d)]
        for d in range(1, chips)
    ]
    near, whole = lax.optimization_barrier((near + [own_rows], [members[-1] for members in far]))
    far = [members[:-1] + [last] for members, last in zip(far, whole)]
    back_near = through_experts(near, [1] * head_size)
    back_near, far = lax.optimization_barrier((back_near, far))
    back_far = [through_experts(members, [1] * head_size) for members in far]
    totals = []
    for k in slots:
        got = [swap(pieces[k], "exp", 2 * d) for d, pieces in enumerate(back_far, 1)]
        totals.append(
            call(sum_kernel, "sum", struct((rows, model), BF16), [(VMEM, v) for v in (back_near[k], *got)])
        )
    totals[-2], mine = lax.optimization_barrier((totals[-2], [pieces[-1] for pieces in back_far]))
    arrived = [swap_slot(total, k) for k, total in enumerate(totals)]
    arrived += [swap(piece, "exp", 2 * d) for d, piece in enumerate(mine, 1)]
    return call(
        last_kernel,
        "last",
        struct(resid.shape, BF16),
        [(VMEM, value) for value in (hidden, back_near[-1], *arrived)],
        pinned=False,
    )


def solution(mesh):
    placed = (
        P(("seq", "exp"), "head"),
        P(("seq", "exp"), "head"),
        P(("seq", "exp"), "head"),
        P(("seq", "exp"), "head"),
        P(("seq", "exp"), "head"),
        P("head"),
        P("head"),
        P("head"),
        P("head", None),
        P(("seq", "exp"), "head", None),
        P(("seq", "exp"), "head", None),
        P(("seq", "exp"), "head", None),
        P(),
        P(("head", "exp"), None, None),
        P(("head", "exp"), None, None),
    )
    return jax.shard_map(
        per_device,
        mesh=mesh,
        in_specs=placed,
        out_specs=P(("seq", "exp"), "head", None),
        check_vma=False,
    )
```

```python
import functools

import jax
import jax.numpy as jnp
from jax import lax
from jax.experimental import pallas as pl
from jax.experimental.pallas import tpu as pltpu
from jax.sharding import PartitionSpec as P

HEAD_DIM = 64
STATE = 128
LANES = 128
TILE = 16
FAR = -1e30
F32 = jnp.float32
BF16 = jnp.bfloat16
HBM = pl.BlockSpec(memory_space=pltpu.HBM)
VMEM = pl.BlockSpec(memory_space=pltpu.VMEM)
ANY = pl.BlockSpec(memory_space=pl.ANY)
NT = (((1,), (1,)), ((), ()))


def struct(shape, dtype):
    return jax.ShapeDtypeStruct(shape, dtype)


def call(kernel, name, outs, ins, scratch=(), megabytes=12, pinned=True):
    args = [pltpu.with_memory_space_constraint(arg, pltpu.HBM) if spec is HBM else arg for spec, arg in ins]
    return pl.pallas_call(
        kernel,
        out_shape=jax.tree.map(lambda out: pltpu.VMEM(out.shape, out.dtype), outs) if pinned else outs,
        in_specs=[spec for spec, _ in ins],
        out_specs=jax.tree.map(lambda _: VMEM, outs),
        scratch_shapes=list(scratch),
        name=name,
        compiler_params=pltpu.CompilerParams(vmem_limit_bytes=megabytes << 20),
    )(*args)


def offsets(count):
    down = list(range(count - 1, 0, -1))
    return [down, down[-2::-1] + down[-1:]]


def head_offset(slot, count):
    first, second = (order[slot] for order in offsets(count))
    return jnp.where(core_index() == 0, first, second)


def core_index():
    return lax.axis_index("exp") % 2


def chip_index():
    return lax.axis_index("exp") // 2


def copies(sems, sources, targets):
    made = [pltpu.make_async_copy(s, t, sems.at[i]) for i, (s, t) in enumerate(zip(sources, targets))]
    for copy in made:
        copy.start()
    return made


def decays(dt_rows, a_log):
    heads, length = dt_rows.shape
    step = jnp.maximum(dt_rows, 0.0) + jnp.log1p(jnp.exp(-jnp.abs(dt_rows)))
    same = lax.broadcasted_iota(jnp.int32, (heads, heads), 0) == lax.broadcasted_iota(jnp.int32, (heads, heads), 1)
    a_column = jnp.sum(jnp.where(same, jnp.broadcast_to(a_log, (heads, heads)), 0.0), axis=1, keepdims=True)
    rate = -step * jnp.exp(a_column)
    row = lax.broadcasted_iota(jnp.int32, (length, length), 0)
    col = lax.broadcasted_iota(jnp.int32, (length, length), 1)
    upper = (row <= col).astype(F32)
    cum = jnp.dot(rate, upper, precision=lax.Precision.HIGHEST, preferred_element_type=F32)
    return step, cum


def pair_lanes(values, pair):
    rows = values.shape[0]
    lane = lax.broadcasted_iota(jnp.int32, (rows, LANES), 1)
    left = jnp.broadcast_to(values[:, 2 * pair : 2 * pair + 1], (rows, LANES))
    right = jnp.broadcast_to(values[:, 2 * pair + 1 : 2 * pair + 2], (rows, LANES))
    return jnp.where(lane < HEAD_DIM, left, right)


def unpacked(block):
    block = block.astype(F32)
    return block[:, STATE : STATE + 1, :] + block[:, STATE + 1 : STATE + 2, :], block[:, 0:STATE, :]


def pack(ref, total, state):
    ref[:, 0:STATE, :] = state.astype(BF16)
    wide = jnp.broadcast_to(total, (ref.shape[0], TILE, LANES))
    high = wide.astype(BF16).astype(F32)
    row = lax.broadcasted_iota(jnp.int32, wide.shape, 1)
    ref[:, STATE : STATE + TILE, :] = jnp.where(row == 0, high, wide - high).astype(BF16)


def state_kernel(x_hbm, b_hbm, dt_hbm, a_hbm, keep_ref, send_ref, *scratch):
    x_ref, b_ref, dt_ref, a_ref, packed_ref, sems = scratch
    loads = copies(sems, (dt_hbm, a_hbm, x_hbm, b_hbm), (dt_ref, a_ref, x_ref, b_ref))
    loads[0].wait()
    loads[1].wait()
    step, cum = decays(dt_ref[...], a_ref[...])
    length = cum.shape[1]
    total = cum[:, length - 1 :]
    tail = (jnp.exp(total - cum) * step).T
    total = jnp.broadcast_to(total, cum.shape).T[0:1]
    loads[2].wait()
    loads[3].wait()
    pairs = packed_ref.shape[0]
    groups = b_ref.shape[1] // STATE
    for group in range(groups):
        turned = b_ref[:, group * STATE : (group + 1) * STATE].T
        for pair in range(group * pairs // groups, (group + 1) * pairs // groups):
            x_pair = x_ref[:, pair * LANES : (pair + 1) * LANES].astype(F32)
            weighted = (pair_lanes(tail, pair) * x_pair).astype(BF16)
            state = jnp.dot(turned, weighted, preferred_element_type=F32)
            pack(packed_ref.at[pair : pair + 1], pair_lanes(total, pair)[None], state[None])
    half = pairs // 2
    keep_ref[...] = packed_ref[pl.ds(core_index() * half, half)]
    send_ref[...] = packed_ref[pl.ds((1 - core_index()) * half, half)]


def chip_state_kernel(keep_ref, got_ref, out_ref):
    first = core_index() == 0
    keep, got = unpacked(keep_ref[...]), unpacked(got_ref[...])
    early = [jnp.where(first, mine, other) for mine, other in zip(keep, got)]
    late = [jnp.where(first, other, mine) for mine, other in zip(keep, got)]
    pack(out_ref, early[0] + late[0], jnp.exp(late[0]) * early[1] + late[1])


def weights_kernel(after_ref, up_hbm, down_hbm, up_ref, down_ref, sems):
    for load in copies(sems, (up_hbm, down_hbm), (up_ref, down_ref)):
        load.wait()


def span_kernel(after_ref, *rest):
    ins, out_ref, block_ref = rest[:-2], rest[-2], rest[-1]
    for mask, part in enumerate(ins):
        block_ref[chip_index() ^ mask] = part[...]
    total, state = unpacked(block_ref[0])
    for chip in range(1, len(ins)):
        here, own = unpacked(block_ref[chip])
        total, state = total + here, jnp.exp(here) * state + own
    pack(out_ref, total, state)


def before_kernel(chips, after_ref, keep_ref, got_ref, *rest):
    ins, (mine_ref, send_ref, chip_ref, part_ref) = rest[:-4], rest[-4:]
    for mask in range(chips):
        chip_ref[chip_index() ^ mask] = ins[mask][...]
    parts = len(ins) - chips
    for mask in range(parts):
        part_ref[lax.axis_index("seq") ^ mask] = ins[chips + mask][...]
    carry = jnp.zeros(mine_ref.shape, F32)
    for ref, count, own in ((part_ref, parts, lax.axis_index("seq")), (chip_ref, chips, chip_index())):
        for index in range(count - 1):
            total, state = unpacked(ref[index])
            carry = jnp.where(index < own, jnp.exp(total) * carry + state, carry)
    first = core_index() == 0
    total, state = (jnp.where(first, k, g) for k, g in zip(unpacked(keep_ref[...]), unpacked(got_ref[...])))
    later = jnp.exp(total) * carry + state
    mine_ref[...] = jnp.where(first, carry, later).astype(BF16)
    send_ref[...] = jnp.where(first, later, carry).astype(BF16)


def inside_kernel(x_hbm, z_hbm, b_hbm, c_hbm, dt_hbm, a_hbm, d_hbm, local_ref, grown_ref, c_ref, *scratch):
    x_ref, z_ref, b_ref, dt_ref, a_ref, d_ref, sems = scratch
    loads = copies(
        sems,
        (dt_hbm, a_hbm, d_hbm, b_hbm, c_hbm, x_hbm, z_hbm),
        (dt_ref, a_ref, d_ref, b_ref, c_ref, x_ref, z_ref),
    )
    for load in loads:
        load.wait()
    step_rows, cum_rows = decays(dt_ref[...], a_ref[...])
    cum = cum_rows.T
    grown = jnp.exp(cum)
    length = cum.shape[0]
    pairs = x_ref.shape[1] // LANES
    groups = b_ref.shape[1] // STATE
    row = lax.broadcasted_iota(jnp.int32, (length, length), 0)
    col = lax.broadcasted_iota(jnp.int32, (length, length), 1)
    lane = lax.broadcasted_iota(jnp.int32, (length, LANES), 1)
    for group in range(groups):
        span = slice(group * STATE, (group + 1) * STATE)
        scores = lax.dot_general(c_ref[:, span], b_ref[:, span], NT, preferred_element_type=F32)
        scores = jnp.where(row >= col, scores, 0.0)
        for pair in range(group * pairs // groups, (group + 1) * pairs // groups):
            at = slice(pair * LANES, (pair + 1) * LANES)
            x_pair = x_ref[:, at]
            halves = []
            for head in (2 * pair, 2 * pair + 1):
                distance = cum[:, head : head + 1] - cum_rows[head : head + 1, :]
                decay = jnp.exp(jnp.where(row >= col, distance, FAR))
                mixing = (scores * (decay * step_rows[head : head + 1, :])).astype(BF16)
                halves.append(jnp.dot(mixing, x_pair, preferred_element_type=F32))
            inside = jnp.where(lane < HEAD_DIM, halves[0], halves[1])
            skip = pair_lanes(d_ref[...], pair) * x_pair.astype(F32)
            z = z_ref[:, at].astype(F32)
            gate = z / (1.0 + jnp.exp(-z))
            local_ref[:, at] = (inside + skip) * gate
            grown_ref[:, at] = pair_lanes(grown, pair) * gate


def prep_kernel(experts, width, resid_hbm, routes_hbm, gates_hbm, gain_hbm, norm_hbm, w_hbm, *rest):
    gate_ref, resid_ref, gain_ref, norm_ref, w_ref, routes_ref, gates_ref, sems = rest
    loads = copies(
        sems,
        (routes_hbm, gates_hbm, resid_hbm, gain_hbm, norm_hbm, w_hbm),
        (routes_ref, gates_ref, resid_ref, gain_ref, norm_ref, w_ref),
    )
    loads[0].wait()
    loads[1].wait()
    count, extent = gate_ref.shape
    start = width // LANES * LANES
    lane = lax.broadcasted_iota(jnp.int32, (extent, count), 0) + start - width
    expert = jnp.where(lane >= experts, lane - experts, lane)
    gate = jnp.zeros((extent, count), F32)
    for pick in range(routes_ref.shape[0]):
        gate = gate + jnp.where(routes_ref[pick] == expert, gates_ref[pick], 0.0)
    high = gate.astype(BF16).astype(F32)
    gate = jnp.where(lane < experts, high, jnp.where(lane < 2 * experts, gate - high, 0.0))
    gate_ref[...] = gate.T.astype(BF16)
    for load in loads[2:]:
        load.wait()


def half_product(half, local_ref, grown_ref, c_ref, norm_ref, w_ref, state_ref, normed_ref, count):
    pairs = state_ref.shape[0]
    width = pairs * LANES
    base = pl.multiple_of(half * width, width)
    groups = c_ref.shape[1] // STATE // 2
    per_group = pairs // groups
    for group in range(groups):
        c_group = c_ref[:, pl.ds(pl.multiple_of((half * groups + group) * STATE, STATE), STATE)]
        gated, squares = [], 0.0
        for pair in range(group * per_group, (group + 1) * per_group):
            span = pl.ds(pl.multiple_of(base + pair * LANES, LANES), LANES)
            carried = jnp.dot(c_group, state_ref[pair], preferred_element_type=F32)
            value = local_ref[:, span] + grown_ref[:, span] * carried
            gated.append(value)
            squares = squares + value * value
        mean = jnp.sum(squares, axis=1, keepdims=True) / (per_group * LANES)
        inverse = lax.rsqrt(mean + 1e-05)
        for offset, value in enumerate(gated):
            pair = group * per_group + offset
            gain = norm_ref[:, pl.ds(pl.multiple_of(base + pair * LANES, LANES), LANES)]
            normed_ref[:, pair * LANES : (pair + 1) * LANES] = (value * inverse * gain).astype(BF16)
    rows = normed_ref.shape[0] // count
    blocks = []
    for shift in range(count):
        owner = lax.axis_index("head") ^ (head_offset(shift - 1, count) if shift else 0)
        blocks.append(normed_ref[pl.ds(pl.multiple_of(owner * rows, rows), rows), :])
    weight = w_ref[:, pl.ds(base, width)]
    return lax.dot_general(jnp.concatenate(blocks, axis=0), weight, NT, preferred_element_type=F32)


def first_half_kernel(count, local_ref, grown_ref, c_ref, norm_ref, w_ref, mine_ref, out_ref, normed_ref):
    out_ref[...] = half_product(
        core_index(), local_ref, grown_ref, c_ref, norm_ref, w_ref, mine_ref, normed_ref, count
    )


def mixed_kernel(after_up, after_down, local_ref, grown_ref, c_ref, norm_ref, w_ref, got_ref, first_ref, *rest):
    outs, normed_ref = rest[:-1], rest[-1]
    product = first_ref[...] + half_product(
        1 - core_index(), local_ref, grown_ref, c_ref, norm_ref, w_ref, got_ref, normed_ref, len(outs)
    )
    rows = outs[0].shape[0]
    for shift, out in enumerate(outs):
        out[...] = product[shift * rows : (shift + 1) * rows].astype(BF16)


def rows_kernel(after_ref, resid_ref, gate_ref, gain_ref, *rest):
    parts, hidden_ref, rows_ref = rest[:-2], rest[-2], rest[-1]
    mixed = parts[0][...].astype(F32)
    for part in parts[1:]:
        mixed = mixed + part[...].astype(F32)
    hidden = (resid_ref[0].astype(F32) + mixed).astype(BF16)
    hidden_ref[...] = hidden
    value = hidden.astype(F32)
    scale = lax.rsqrt(jnp.mean(value * value, axis=1, keepdims=True) + 1e-05)
    width = value.shape[1]
    rows_ref[:, width // LANES * LANES :] = gate_ref[...]
    rows_ref[:, :width] = (value * scale * gain_ref[...]).astype(BF16)


def expert_kernel(experts, count, up_ref, down_ref, other_up_ref, other_down_ref, *rest):
    ins, outs = rest[:count], rest[count:]
    width = up_ref.shape[2]
    start = width // LANES * LANES
    rows = jnp.concatenate([ref[:, :width] for ref in ins], axis=0)
    tail = jnp.concatenate([ref[:, start:] for ref in ins], axis=0).astype(F32)
    lane = lax.broadcasted_iota(jnp.int32, tail.shape, 1) + start - width
    own = lax.axis_index("head") * lax.axis_size("exp") + lax.axis_index("exp")
    other = own + 1 - 2 * core_index()
    total = 0.0
    for expert, up_of, down_of in ((own, up_ref, down_ref), (other, other_up_ref, other_down_ref)):
        up = lax.dot_general(rows, up_of[0], NT, preferred_element_type=F32)
        up = jnp.maximum(up, 0.0)
        activated = (up * up).astype(BF16)
        chosen = (lane == expert) | (lane == expert + experts)
        gate = jnp.sum(jnp.where(chosen, tail, 0.0), axis=1, keepdims=True)
        total = total + jnp.dot(activated, down_of[0], preferred_element_type=F32) * gate
    at = 0
    for out in outs:
        out[...] = total[at : at + out.shape[0]].astype(BF16)
        at += out.shape[0]


def sum_kernel(*refs):
    total = refs[0][...].astype(F32)
    for ref in refs[1:-1]:
        total = total + ref[...].astype(F32)
    refs[-1][...] = total.astype(BF16)


def last_kernel(hidden_ref, *rest):
    parts, out_ref = rest[:-1], rest[-1]
    total = parts[0][...].astype(F32)
    for part in parts[1:]:
        total = total + part[...].astype(F32)
    out_ref[0] = (hidden_ref[...].astype(F32) + total).astype(BF16)


def swap(value, axis, mask):
    size = lax.axis_size(axis)
    return lax.ppermute(value, axis, [(i, i ^ mask) for i in range(size)])


def swap_slot(value, slot, chip_mask=0):
    heads, size = lax.axis_size("head"), lax.axis_size("exp")
    order = offsets(heads)
    pairs = []
    for i in range(heads * size):
        head, exp = i // size, i % size
        pairs.append((i, (head ^ order[exp % 2][slot]) * size + (exp ^ (2 * chip_mask))))
    return lax.ppermute(value, ("head", "exp"), pairs)


def per_device(
    x_in, z_in, b_in, c_in, dt_in, a_log, d_skip, norm_w, w_out, resid, routes, gates, moe_gain, w_up, w_down
):
    length, heads = dt_in.shape
    channels = x_in.shape[1]
    model = w_out.shape[1]
    hidden_units = w_up.shape[2]
    seq_size, head_size, exp_size = lax.axis_size("seq"), lax.axis_size("head"), lax.axis_size("exp")
    chips = exp_size // 2
    rows = resid.shape[1]
    experts = head_size * exp_size
    pairs = channels // LANES
    half = pairs // 2
    dt_rows, a_row, d_row = dt_in.T, a_log[None], d_skip[None]
    dma = pltpu.SemaphoreType.DMA
    packed = struct((half, STATE + TILE, LANES), BF16)

    keep, send = call(
        state_kernel,
        "state",
        [packed, packed],
        [(HBM, x_in), (HBM, b_in), (HBM, dt_rows), (HBM, a_row)],
        [pltpu.VMEM(x_in.shape, BF16), pltpu.VMEM(b_in.shape, BF16), pltpu.VMEM(dt_rows.shape, F32),
         pltpu.VMEM(a_row.shape, F32), pltpu.VMEM((pairs, STATE + TILE, LANES), BF16), dma((4,))],
        megabytes=16,
    )
    local, grown, c_held = call(
        inside_kernel,
        "inside",
        [struct((length, channels), F32), struct((length, channels), F32), struct(c_in.shape, BF16)],
        [(HBM, value) for value in (x_in, z_in, b_in, c_in, dt_rows, a_row, d_row)],
        [pltpu.VMEM(x_in.shape, BF16), pltpu.VMEM(z_in.shape, BF16), pltpu.VMEM(b_in.shape, BF16),
         pltpu.VMEM(dt_rows.shape, F32), pltpu.VMEM(a_row.shape, F32), pltpu.VMEM(d_row.shape, F32), dma((7,))],
        megabytes=16,
    )
    wide = -(-(model + 2 * experts) // LANES) * LANES
    turned = [jnp.transpose(value, (2, 0, 1)) for value in (routes, gates)]
    gate_lanes, resid_held, gain_held, norm_held, w_held = call(
        functools.partial(prep_kernel, experts, model),
        "prep",
        [struct((rows, wide - model // LANES * LANES), BF16), struct(resid.shape, BF16), struct((1, model), F32),
         struct((1, channels), F32), struct((model, channels), BF16)],
        [(HBM, value) for value in (resid, *turned, moe_gain[None], norm_w[None], w_out.T)],
        [pltpu.VMEM(turned[0].shape, jnp.int32), pltpu.VMEM(turned[1].shape, F32), dma((6,))],
        megabytes=16,
    )
    up_turned = jnp.swapaxes(w_up, 1, 2)
    got = swap(send, "exp", 1)
    chip = call(chip_state_kernel, "chip_state", packed, [(VMEM, keep), (VMEM, got)])
    chip, up_after, down_after = lax.optimization_barrier((chip, up_turned, w_down))
    other_up, other_down = swap(up_after, "exp", 1), swap(down_after, "exp", 1)
    along_y = [chip] + [swap(chip, "exp", 2 * d) for d in range(1, chips)]
    span = call(
        span_kernel,
        "span",
        packed,
        [(ANY, c_held)] + [(VMEM, value) for value in along_y],
        [pltpu.VMEM((chips, *packed.shape), BF16)],
    )
    along_x = [span] + [swap(span, "seq", d) for d in range(1, seq_size)]
    before, before_send = call(
        functools.partial(before_kernel, chips),
        "before",
        [struct((half, STATE, LANES), BF16)] * 2,
        [(ANY, gate_lanes)] + [(VMEM, value) for value in (keep, got, *along_y, *along_x)],
        [pltpu.VMEM((chips, *packed.shape), BF16), pltpu.VMEM((seq_size, *packed.shape), BF16)],
        megabytes=24,
    )
    before_got = swap(before_send, "exp", 1)
    shared = [(VMEM, value) for value in (local, grown, c_held, norm_held, w_held)]
    normed_half = pltpu.VMEM((length, channels // 2), BF16)
    first = call(
        functools.partial(first_half_kernel, head_size),
        "first_half",
        struct((length, model), F32),
        shared + [(VMEM, before)],
        [normed_half],
    )
    mixed = call(
        mixed_kernel,
        "mixed",
        [struct((rows, model), BF16)] * head_size,
        [(ANY, other_up), (ANY, other_down)] + shared + [(VMEM, before_got), (VMEM, first)],
        [normed_half],
    )
    up_held, down_held = call(
        weights_kernel,
        "weights",
        [struct(up_turned.shape, BF16), struct(w_down.shape, BF16)],
        [(ANY, mixed[0]), (HBM, up_turned), (HBM, w_down)],
        [dma((2,))],
    )
    slots = list(range(head_size - 1))
    parts = [mixed[0]] + [swap_slot(mixed[k + 1], k) for k in slots]
    hidden, own_rows = call(
        rows_kernel,
        "rows",
        [struct((rows, model), BF16), struct((rows, wide), BF16)],
        [(ANY, up_held)] + [(VMEM, value) for value in (resid_held, gate_lanes, gain_held, *parts)],
    )

    def through_experts(members, sizes):
        return call(
            functools.partial(expert_kernel, experts, len(members)),
            "experts",
            [struct((size * rows, model), BF16) for size in sizes],
            [(VMEM, value) for value in (up_held, down_held, other_up, other_down, *members)],
            megabytes=16,
        )

    near = [swap_slot(own_rows, k) for k in slots]
    far = [
        [swap(near[k], "exp", 2 * d) for k in slots[:-1]]
        + [swap_slot(own_rows, slots[-1], d), swap(own_rows, "exp", 2 * d)]
        for d in range(1, chips)
    ]
    near, whole = lax.optimization_barrier((near + [own_rows], [members[-1] for members in far]))
    far = [members[:-1] + [last] for members, last in zip(far, whole)]
    back_near = through_experts(near, [1] * head_size)
    back_near, far = lax.optimization_barrier((back_near, far))
    back_far = [through_experts(members, [1] * head_size) for members in far]
    arrived = [swap_slot(back_near[0], 0)]
    got = {k: [swap(pieces[k], "exp", 2 * d) for d, pieces in enumerate(back_far, 1)] for k in slots[1:]}
    arrived, got[1] = lax.optimization_barrier((arrived, got[1]))
    arrived += [swap_slot(pieces[0], 0, d) for d, pieces in enumerate(back_far, 1)]
    mine = [pieces[-1] for pieces in back_far]
    for k in slots[1:]:
        total = call(sum_kernel, "sum", struct((rows, model), BF16), [(VMEM, v) for v in (back_near[k], *got[k])])
        if k == 1:
            total, mine = lax.optimization_barrier((total, mine))
        arrived.append(swap_slot(total, k))
    arrived += [swap(piece, "exp", 2 * d) for d, piece in enumerate(mine, 1)]
    return call(
        last_kernel,
        "last",
        struct(resid.shape, BF16),
        [(VMEM, value) for value in (hidden, back_near[-1], *arrived)],
        pinned=False,
    )


def solution(mesh):
    placed = (
        P(("seq", "exp"), "head"),
        P(("seq", "exp"), "head"),
        P(("seq", "exp"), "head"),
        P(("seq", "exp"), "head"),
        P(("seq", "exp"), "head"),
        P("head"),
        P("head"),
        P("head"),
        P("head", None),
        P(("seq", "exp"), "head", None),
        P(("seq", "exp"), "head", None),
        P(("seq", "exp"), "head", None),
        P(),
        P(("head", "exp"), None, None),
        P(("head", "exp"), None, None),
    )
    return jax.shard_map(
        per_device,
        mesh=mesh,
        in_specs=placed,
        out_specs=P(("seq", "exp"), "head", None),
        check_vma=False,
    )
```

```python
import functools

import jax
import jax.numpy as jnp
from jax import lax
from jax.experimental import pallas as pl
from jax.experimental.pallas import tpu as pltpu
from jax.sharding import PartitionSpec as P

HEAD_DIM = 64
STATE = 128
LANES = 128
TILE = 16
FAR = -1e30
F32 = jnp.float32
BF16 = jnp.bfloat16
HBM = pl.BlockSpec(memory_space=pltpu.HBM)
VMEM = pl.BlockSpec(memory_space=pltpu.VMEM)
ANY = pl.BlockSpec(memory_space=pl.ANY)
NT = (((1,), (1,)), ((), ()))


def struct(shape, dtype):
    return jax.ShapeDtypeStruct(shape, dtype)


def call(kernel, name, outs, ins, scratch=(), megabytes=12, pinned=True):
    args = [pltpu.with_memory_space_constraint(arg, pltpu.HBM) if spec is HBM else arg for spec, arg in ins]
    return pl.pallas_call(
        kernel,
        out_shape=jax.tree.map(lambda out: pltpu.VMEM(out.shape, out.dtype), outs) if pinned else outs,
        in_specs=[spec for spec, _ in ins],
        out_specs=jax.tree.map(lambda _: VMEM, outs),
        scratch_shapes=list(scratch),
        name=name,
        compiler_params=pltpu.CompilerParams(vmem_limit_bytes=megabytes << 20),
    )(*args)


def offsets(count):
    down = list(range(count - 1, 0, -1))
    return [down, down[-2::-1] + down[-1:]]


def head_offset(slot, count):
    first, second = (order[slot] for order in offsets(count))
    return jnp.where(core_index() == 0, first, second)


def core_index():
    return lax.axis_index("exp") % 2


def chip_index():
    return lax.axis_index("exp") // 2


def copies(sems, sources, targets):
    made = [pltpu.make_async_copy(s, t, sems.at[i]) for i, (s, t) in enumerate(zip(sources, targets))]
    for copy in made:
        copy.start()
    return made


def decays(dt_rows, a_log):
    heads, length = dt_rows.shape
    step = jnp.maximum(dt_rows, 0.0) + jnp.log1p(jnp.exp(-jnp.abs(dt_rows)))
    same = lax.broadcasted_iota(jnp.int32, (heads, heads), 0) == lax.broadcasted_iota(jnp.int32, (heads, heads), 1)
    a_column = jnp.sum(jnp.where(same, jnp.broadcast_to(a_log, (heads, heads)), 0.0), axis=1, keepdims=True)
    rate = -step * jnp.exp(a_column)
    row = lax.broadcasted_iota(jnp.int32, (length, length), 0)
    col = lax.broadcasted_iota(jnp.int32, (length, length), 1)
    upper = (row <= col).astype(F32)
    cum = jnp.dot(rate, upper, precision=lax.Precision.HIGHEST, preferred_element_type=F32)
    return step, cum


def pair_lanes(values, pair):
    rows = values.shape[0]
    lane = lax.broadcasted_iota(jnp.int32, (rows, LANES), 1)
    left = jnp.broadcast_to(values[:, 2 * pair : 2 * pair + 1], (rows, LANES))
    right = jnp.broadcast_to(values[:, 2 * pair + 1 : 2 * pair + 2], (rows, LANES))
    return jnp.where(lane < HEAD_DIM, left, right)


def unpacked(block):
    block = block.astype(F32)
    return block[:, STATE : STATE + 1, :] + block[:, STATE + 1 : STATE + 2, :], block[:, 0:STATE, :]


def pack(ref, total, state):
    ref[:, 0:STATE, :] = state.astype(BF16)
    wide = jnp.broadcast_to(total, (ref.shape[0], TILE, LANES))
    high = wide.astype(BF16).astype(F32)
    row = lax.broadcasted_iota(jnp.int32, wide.shape, 1)
    ref[:, STATE : STATE + TILE, :] = jnp.where(row == 0, high, wide - high).astype(BF16)


def state_kernel(x_hbm, b_hbm, dt_hbm, a_hbm, keep_ref, send_ref, *scratch):
    x_ref, b_ref, dt_ref, a_ref, packed_ref, sems = scratch
    loads = copies(sems, (dt_hbm, a_hbm, x_hbm, b_hbm), (dt_ref, a_ref, x_ref, b_ref))
    loads[0].wait()
    loads[1].wait()
    step, cum = decays(dt_ref[...], a_ref[...])
    length = cum.shape[1]
    total = cum[:, length - 1 :]
    tail = (jnp.exp(total - cum) * step).T
    total = jnp.broadcast_to(total, cum.shape).T[0:1]
    loads[2].wait()
    loads[3].wait()
    pairs = packed_ref.shape[0]
    groups = b_ref.shape[1] // STATE
    for group in range(groups):
        turned = b_ref[:, group * STATE : (group + 1) * STATE].T
        for pair in range(group * pairs // groups, (group + 1) * pairs // groups):
            x_pair = x_ref[:, pair * LANES : (pair + 1) * LANES].astype(F32)
            weighted = (pair_lanes(tail, pair) * x_pair).astype(BF16)
            state = jnp.dot(turned, weighted, preferred_element_type=F32)
            pack(packed_ref.at[pair : pair + 1], pair_lanes(total, pair)[None], state[None])
    half = pairs // 2
    keep_ref[...] = packed_ref[pl.ds(core_index() * half, half)]
    send_ref[...] = packed_ref[pl.ds((1 - core_index()) * half, half)]


def chip_state_kernel(keep_ref, got_ref, out_ref):
    first = core_index() == 0
    keep, got = unpacked(keep_ref[...]), unpacked(got_ref[...])
    early = [jnp.where(first, mine, other) for mine, other in zip(keep, got)]
    late = [jnp.where(first, other, mine) for mine, other in zip(keep, got)]
    pack(out_ref, early[0] + late[0], jnp.exp(late[0]) * early[1] + late[1])


def weights_kernel(after_ref, up_hbm, down_hbm, up_ref, down_ref, sems):
    for load in copies(sems, (up_hbm, down_hbm), (up_ref, down_ref)):
        load.wait()


def span_kernel(after_ref, *rest):
    ins, out_ref, block_ref = rest[:-2], rest[-2], rest[-1]
    for mask, part in enumerate(ins):
        block_ref[chip_index() ^ mask] = part[...]
    total, state = unpacked(block_ref[0])
    for chip in range(1, len(ins)):
        here, own = unpacked(block_ref[chip])
        total, state = total + here, jnp.exp(here) * state + own
    pack(out_ref, total, state)


def before_kernel(chips, after_ref, keep_ref, got_ref, *rest):
    ins, (mine_ref, send_ref, chip_ref, part_ref) = rest[:-4], rest[-4:]
    for mask in range(chips):
        chip_ref[chip_index() ^ mask] = ins[mask][...]
    parts = len(ins) - chips
    for mask in range(parts):
        part_ref[lax.axis_index("seq") ^ mask] = ins[chips + mask][...]
    carry = jnp.zeros(mine_ref.shape, F32)
    for ref, count, own in ((part_ref, parts, lax.axis_index("seq")), (chip_ref, chips, chip_index())):
        for index in range(count - 1):
            total, state = unpacked(ref[index])
            carry = jnp.where(index < own, jnp.exp(total) * carry + state, carry)
    first = core_index() == 0
    total, state = (jnp.where(first, k, g) for k, g in zip(unpacked(keep_ref[...]), unpacked(got_ref[...])))
    later = jnp.exp(total) * carry + state
    mine_ref[...] = jnp.where(first, carry, later).astype(BF16)
    send_ref[...] = jnp.where(first, later, carry).astype(BF16)


def inside_kernel(x_hbm, z_hbm, b_hbm, c_hbm, dt_hbm, a_hbm, d_hbm, local_ref, grown_ref, c_ref, *scratch):
    x_ref, z_ref, b_ref, dt_ref, a_ref, d_ref, sems = scratch
    loads = copies(
        sems,
        (dt_hbm, a_hbm, d_hbm, b_hbm, c_hbm, x_hbm, z_hbm),
        (dt_ref, a_ref, d_ref, b_ref, c_ref, x_ref, z_ref),
    )
    for load in loads:
        load.wait()
    step_rows, cum_rows = decays(dt_ref[...], a_ref[...])
    cum = cum_rows.T
    grown = jnp.exp(cum)
    length = cum.shape[0]
    pairs = x_ref.shape[1] // LANES
    groups = b_ref.shape[1] // STATE
    row = lax.broadcasted_iota(jnp.int32, (length, length), 0)
    col = lax.broadcasted_iota(jnp.int32, (length, length), 1)
    lane = lax.broadcasted_iota(jnp.int32, (length, LANES), 1)
    for group in range(groups):
        span = slice(group * STATE, (group + 1) * STATE)
        scores = lax.dot_general(c_ref[:, span], b_ref[:, span], NT, preferred_element_type=F32)
        scores = jnp.where(row >= col, scores, 0.0)
        for pair in range(group * pairs // groups, (group + 1) * pairs // groups):
            at = slice(pair * LANES, (pair + 1) * LANES)
            x_pair = x_ref[:, at]
            halves = []
            for head in (2 * pair, 2 * pair + 1):
                distance = cum[:, head : head + 1] - cum_rows[head : head + 1, :]
                decay = jnp.exp(jnp.where(row >= col, distance, FAR))
                mixing = (scores * (decay * step_rows[head : head + 1, :])).astype(BF16)
                halves.append(jnp.dot(mixing, x_pair, preferred_element_type=F32))
            inside = jnp.where(lane < HEAD_DIM, halves[0], halves[1])
            skip = pair_lanes(d_ref[...], pair) * x_pair.astype(F32)
            z = z_ref[:, at].astype(F32)
            gate = z / (1.0 + jnp.exp(-z))
            local_ref[:, at] = (inside + skip) * gate
            grown_ref[:, at] = pair_lanes(grown, pair) * gate


def prep_kernel(experts, width, resid_hbm, routes_hbm, gates_hbm, gain_hbm, norm_hbm, w_hbm, *rest):
    gate_ref, resid_ref, gain_ref, norm_ref, w_ref, routes_ref, gates_ref, sems = rest
    loads = copies(
        sems,
        (routes_hbm, gates_hbm, resid_hbm, gain_hbm, norm_hbm, w_hbm),
        (routes_ref, gates_ref, resid_ref, gain_ref, norm_ref, w_ref),
    )
    loads[0].wait()
    loads[1].wait()
    count, extent = gate_ref.shape
    start = width // LANES * LANES
    lane = lax.broadcasted_iota(jnp.int32, (extent, count), 0) + start - width
    expert = jnp.where(lane >= experts, lane - experts, lane)
    gate = jnp.zeros((extent, count), F32)
    for pick in range(routes_ref.shape[0]):
        gate = gate + jnp.where(routes_ref[pick] == expert, gates_ref[pick], 0.0)
    high = gate.astype(BF16).astype(F32)
    gate = jnp.where(lane < experts, high, jnp.where(lane < 2 * experts, gate - high, 0.0))
    gate_ref[...] = gate.T.astype(BF16)
    for load in loads[2:]:
        load.wait()


def half_product(half, local_ref, grown_ref, c_ref, norm_ref, w_ref, state_ref, normed_ref, count):
    pairs = state_ref.shape[0]
    width = pairs * LANES
    base = pl.multiple_of(half * width, width)
    groups = c_ref.shape[1] // STATE // 2
    per_group = pairs // groups
    for group in range(groups):
        c_group = c_ref[:, pl.ds(pl.multiple_of((half * groups + group) * STATE, STATE), STATE)]
        gated, squares = [], 0.0
        for pair in range(group * per_group, (group + 1) * per_group):
            span = pl.ds(pl.multiple_of(base + pair * LANES, LANES), LANES)
            carried = jnp.dot(c_group, state_ref[pair], preferred_element_type=F32)
            value = local_ref[:, span] + grown_ref[:, span] * carried
            gated.append(value)
            squares = squares + value * value
        mean = jnp.sum(squares, axis=1, keepdims=True) / (per_group * LANES)
        inverse = lax.rsqrt(mean + 1e-05)
        for offset, value in enumerate(gated):
            pair = group * per_group + offset
            gain = norm_ref[:, pl.ds(pl.multiple_of(base + pair * LANES, LANES), LANES)]
            normed_ref[:, pair * LANES : (pair + 1) * LANES] = (value * inverse * gain).astype(BF16)
    rows = normed_ref.shape[0] // count
    blocks = []
    for shift in range(count):
        owner = lax.axis_index("head") ^ (head_offset(shift - 1, count) if shift else 0)
        blocks.append(normed_ref[pl.ds(pl.multiple_of(owner * rows, rows), rows), :])
    weight = w_ref[:, pl.ds(base, width)]
    return lax.dot_general(jnp.concatenate(blocks, axis=0), weight, NT, preferred_element_type=F32)


def first_half_kernel(count, local_ref, grown_ref, c_ref, norm_ref, w_ref, mine_ref, out_ref, normed_ref):
    out_ref[...] = half_product(
        core_index(), local_ref, grown_ref, c_ref, norm_ref, w_ref, mine_ref, normed_ref, count
    )


def mixed_kernel(after_up, after_down, local_ref, grown_ref, c_ref, norm_ref, w_ref, got_ref, first_ref, *rest):
    outs, normed_ref = rest[:-1], rest[-1]
    product = first_ref[...] + half_product(
        1 - core_index(), local_ref, grown_ref, c_ref, norm_ref, w_ref, got_ref, normed_ref, len(outs)
    )
    rows = outs[0].shape[0]
    for shift, out in enumerate(outs):
        out[...] = product[shift * rows : (shift + 1) * rows].astype(BF16)


def rows_kernel(after_ref, resid_ref, gate_ref, gain_ref, *rest):
    parts, hidden_ref, rows_ref = rest[:-2], rest[-2], rest[-1]
    mixed = parts[0][...].astype(F32)
    for part in parts[1:]:
        mixed = mixed + part[...].astype(F32)
    hidden = (resid_ref[0].astype(F32) + mixed).astype(BF16)
    hidden_ref[...] = hidden
    value = hidden.astype(F32)
    scale = lax.rsqrt(jnp.mean(value * value, axis=1, keepdims=True) + 1e-05)
    width = value.shape[1]
    rows_ref[:, width // LANES * LANES :] = gate_ref[...]
    rows_ref[:, :width] = (value * scale * gain_ref[...]).astype(BF16)


def expert_kernel(experts, count, up_ref, down_ref, other_up_ref, other_down_ref, *rest):
    ins, outs = rest[:count], rest[count:]
    width = up_ref.shape[2]
    start = width // LANES * LANES
    rows = jnp.concatenate([ref[:, :width] for ref in ins], axis=0)
    tail = jnp.concatenate([ref[:, start:] for ref in ins], axis=0).astype(F32)
    lane = lax.broadcasted_iota(jnp.int32, tail.shape, 1) + start - width
    own = lax.axis_index("head") * lax.axis_size("exp") + lax.axis_index("exp")
    other = own + 1 - 2 * core_index()
    total = 0.0
    for expert, up_of, down_of in ((own, up_ref, down_ref), (other, other_up_ref, other_down_ref)):
        up = lax.dot_general(rows, up_of[0], NT, preferred_element_type=F32)
        up = jnp.maximum(up, 0.0)
        activated = (up * up).astype(BF16)
        chosen = (lane == expert) | (lane == expert + experts)
        gate = jnp.sum(jnp.where(chosen, tail, 0.0), axis=1, keepdims=True)
        total = total + jnp.dot(activated, down_of[0], preferred_element_type=F32) * gate
    at = 0
    for out in outs:
        out[...] = total[at : at + out.shape[0]].astype(BF16)
        at += out.shape[0]


def sum_kernel(*refs):
    total = refs[0][...].astype(F32)
    for ref in refs[1:-1]:
        total = total + ref[...].astype(F32)
    refs[-1][...] = total.astype(BF16)


def last_kernel(hidden_ref, *rest):
    parts, out_ref = rest[:-1], rest[-1]
    total = parts[0][...].astype(F32)
    for part in parts[1:]:
        total = total + part[...].astype(F32)
    out_ref[0] = (hidden_ref[...].astype(F32) + total).astype(BF16)


def swap(value, axis, mask):
    size = lax.axis_size(axis)
    return lax.ppermute(value, axis, [(i, i ^ mask) for i in range(size)])


def swap_slot(value, slot, chip_mask=0):
    heads, size = lax.axis_size("head"), lax.axis_size("exp")
    order = offsets(heads)
    pairs = []
    for i in range(heads * size):
        head, exp = i // size, i % size
        pairs.append((i, (head ^ order[exp % 2][slot]) * size + (exp ^ (2 * chip_mask))))
    return lax.ppermute(value, ("head", "exp"), pairs)


def per_device(
    x_in, z_in, b_in, c_in, dt_in, a_log, d_skip, norm_w, w_out, resid, routes, gates, moe_gain, w_up, w_down
):
    length, heads = dt_in.shape
    channels = x_in.shape[1]
    model = w_out.shape[1]
    hidden_units = w_up.shape[2]
    seq_size, head_size, exp_size = lax.axis_size("seq"), lax.axis_size("head"), lax.axis_size("exp")
    chips = exp_size // 2
    rows = resid.shape[1]
    experts = head_size * exp_size
    pairs = channels // LANES
    half = pairs // 2
    dt_rows, a_row, d_row = dt_in.T, a_log[None], d_skip[None]
    dma = pltpu.SemaphoreType.DMA
    packed = struct((half, STATE + TILE, LANES), BF16)

    keep, send = call(
        state_kernel,
        "state",
        [packed, packed],
        [(HBM, x_in), (HBM, b_in), (HBM, dt_rows), (HBM, a_row)],
        [pltpu.VMEM(x_in.shape, BF16), pltpu.VMEM(b_in.shape, BF16), pltpu.VMEM(dt_rows.shape, F32),
         pltpu.VMEM(a_row.shape, F32), pltpu.VMEM((pairs, STATE + TILE, LANES), BF16), dma((4,))],
        megabytes=16,
    )
    local, grown, c_held = call(
        inside_kernel,
        "inside",
        [struct((length, channels), F32), struct((length, channels), F32), struct(c_in.shape, BF16)],
        [(HBM, value) for value in (x_in, z_in, b_in, c_in, dt_rows, a_row, d_row)],
        [pltpu.VMEM(x_in.shape, BF16), pltpu.VMEM(z_in.shape, BF16), pltpu.VMEM(b_in.shape, BF16),
         pltpu.VMEM(dt_rows.shape, F32), pltpu.VMEM(a_row.shape, F32), pltpu.VMEM(d_row.shape, F32), dma((7,))],
        megabytes=16,
    )
    wide = -(-(model + 2 * experts) // LANES) * LANES
    turned = [jnp.transpose(value, (2, 0, 1)) for value in (routes, gates)]
    gate_lanes, resid_held, gain_held, norm_held, w_held = call(
        functools.partial(prep_kernel, experts, model),
        "prep",
        [struct((rows, wide - model // LANES * LANES), BF16), struct(resid.shape, BF16), struct((1, model), F32),
         struct((1, channels), F32), struct((model, channels), BF16)],
        [(HBM, value) for value in (resid, *turned, moe_gain[None], norm_w[None], w_out.T)],
        [pltpu.VMEM(turned[0].shape, jnp.int32), pltpu.VMEM(turned[1].shape, F32), dma((6,))],
        megabytes=16,
    )
    up_turned = jnp.swapaxes(w_up, 1, 2)
    got = swap(send, "exp", 1)
    chip = call(chip_state_kernel, "chip_state", packed, [(VMEM, keep), (VMEM, got)])
    chip, up_after, down_after = lax.optimization_barrier((chip, up_turned, w_down))
    other_up, other_down = swap(up_after, "exp", 1), swap(down_after, "exp", 1)
    along_y = [chip] + [swap(chip, "exp", 2 * d) for d in range(1, chips)]
    span = call(
        span_kernel,
        "span",
        packed,
        [(ANY, c_held)] + [(VMEM, value) for value in along_y],
        [pltpu.VMEM((chips, *packed.shape), BF16)],
    )
    along_x = [span] + [swap(span, "seq", d) for d in range(1, seq_size)]
    before, before_send = call(
        functools.partial(before_kernel, chips),
        "before",
        [struct((half, STATE, LANES), BF16)] * 2,
        [(ANY, gate_lanes)] + [(VMEM, value) for value in (keep, got, *along_y, *along_x)],
        [pltpu.VMEM((chips, *packed.shape), BF16), pltpu.VMEM((seq_size, *packed.shape), BF16)],
        megabytes=24,
    )
    before_got = swap(before_send, "exp", 1)
    shared = [(VMEM, value) for value in (local, grown, c_held, norm_held, w_held)]
    normed_half = pltpu.VMEM((length, channels // 2), BF16)
    first = call(
        functools.partial(first_half_kernel, head_size),
        "first_half",
        struct((length, model), F32),
        shared + [(VMEM, before)],
        [normed_half],
    )
    mixed = call(
        mixed_kernel,
        "mixed",
        [struct((rows, model), BF16)] * head_size,
        [(ANY, other_up), (ANY, other_down)] + shared + [(VMEM, before_got), (VMEM, first)],
        [normed_half],
    )
    up_held, down_held = call(
        weights_kernel,
        "weights",
        [struct(up_turned.shape, BF16), struct(w_down.shape, BF16)],
        [(ANY, mixed[0]), (HBM, up_turned), (HBM, w_down)],
        [dma((2,))],
    )
    slots = list(range(head_size - 1))
    parts = [mixed[0]] + [swap_slot(mixed[k + 1], k) for k in slots]
    hidden, own_rows = call(
        rows_kernel,
        "rows",
        [struct((rows, model), BF16), struct((rows, wide), BF16)],
        [(ANY, up_held)] + [(VMEM, value) for value in (resid_held, gate_lanes, gain_held, *parts)],
    )

    def through_experts(members):
        return call(
            functools.partial(expert_kernel, experts, len(members)),
            "experts",
            [struct((rows, model), BF16)] * len(members),
            [(VMEM, value) for value in (up_held, down_held, other_up, other_down, *members)],
            megabytes=16,
        )

    both = ("head", "exp")
    group = [z * exp_size + 2 * d for z in (1, 0) for d in reversed(range(chips))][:-1]

    def spread(block):
        return [block] + [swap(block, both, mask) for mask in group]

    sets = [spread(swap(own_rows, "head", high)) for high in range(2, head_size, 2)]
    near = through_experts(spread(own_rows))
    near, sets = lax.optimization_barrier((near, sets))
    far = [through_experts(members) for members in sets]
    arrived = []
    for high, pieces in zip(range(2, head_size, 2), far):
        got = [swap(piece, both, mask) for piece, mask in zip(pieces[1:], group)]
        total = call(sum_kernel, "sum", struct((rows, model), BF16), [(VMEM, v) for v in (pieces[0], *got)])
        arrived.append(swap(total, "head", high))
    arrived += [swap(piece, both, mask) for piece, mask in zip(near[1:], group)]
    return call(
        last_kernel,
        "last",
        struct(resid.shape, BF16),
        [(VMEM, value) for value in (hidden, near[0], *arrived)],
        pinned=False,
    )


def solution(mesh):
    placed = (
        P(("seq", "exp"), "head"),
        P(("seq", "exp"), "head"),
        P(("seq", "exp"), "head"),
        P(("seq", "exp"), "head"),
        P(("seq", "exp"), "head"),
        P("head"),
        P("head"),
        P("head"),
        P("head", None),
        P(("seq", "exp"), "head", None),
        P(("seq", "exp"), "head", None),
        P(("seq", "exp"), "head", None),
        P(),
        P(("head", "exp"), None, None),
        P(("head", "exp"), None, None),
    )
    return jax.shard_map(
        per_device,
        mesh=mesh,
        in_specs=placed,
        out_specs=P(("seq", "exp"), "head", None),
        check_vma=False,
    )
```

```python
import functools

import jax
import jax.numpy as jnp
from jax import lax
from jax.experimental import pallas as pl
from jax.experimental.pallas import tpu as pltpu
from jax.sharding import PartitionSpec as P

HEAD_DIM = 64
STATE = 128
LANES = 128
TILE = 16
FAR = -1e30
F32 = jnp.float32
BF16 = jnp.bfloat16
HBM = pl.BlockSpec(memory_space=pltpu.HBM)
VMEM = pl.BlockSpec(memory_space=pltpu.VMEM)
ANY = pl.BlockSpec(memory_space=pl.ANY)
NT = (((1,), (1,)), ((), ()))


def struct(shape, dtype):
    return jax.ShapeDtypeStruct(shape, dtype)


def call(kernel, name, outs, ins, scratch=(), megabytes=12, pinned=True):
    args = [pltpu.with_memory_space_constraint(arg, pltpu.HBM) if spec is HBM else arg for spec, arg in ins]
    return pl.pallas_call(
        kernel,
        out_shape=jax.tree.map(lambda out: pltpu.VMEM(out.shape, out.dtype), outs) if pinned else outs,
        in_specs=[spec for spec, _ in ins],
        out_specs=jax.tree.map(lambda _: VMEM, outs),
        scratch_shapes=list(scratch),
        name=name,
        compiler_params=pltpu.CompilerParams(vmem_limit_bytes=megabytes << 20),
    )(*args)


def offsets(count):
    down = list(range(count - 1, 0, -1))
    return [down, down[-2::-1] + down[-1:]]


def head_offset(slot, count):
    first, second = (order[slot] for order in offsets(count))
    return jnp.where(core_index() == 0, first, second)


def core_index():
    return lax.axis_index("exp") % 2


def chip_index():
    return lax.axis_index("exp") // 2


def copies(sems, sources, targets):
    made = [pltpu.make_async_copy(s, t, sems.at[i]) for i, (s, t) in enumerate(zip(sources, targets))]
    for copy in made:
        copy.start()
    return made


def decays(dt_rows, a_log):
    heads, length = dt_rows.shape
    step = jnp.maximum(dt_rows, 0.0) + jnp.log1p(jnp.exp(-jnp.abs(dt_rows)))
    same = lax.broadcasted_iota(jnp.int32, (heads, heads), 0) == lax.broadcasted_iota(jnp.int32, (heads, heads), 1)
    a_column = jnp.sum(jnp.where(same, jnp.broadcast_to(a_log, (heads, heads)), 0.0), axis=1, keepdims=True)
    rate = -step * jnp.exp(a_column)
    row = lax.broadcasted_iota(jnp.int32, (length, length), 0)
    col = lax.broadcasted_iota(jnp.int32, (length, length), 1)
    upper = (row <= col).astype(F32)
    cum = jnp.dot(rate, upper, precision=lax.Precision.HIGHEST, preferred_element_type=F32)
    return step, cum


def pair_lanes(values, pair):
    rows = values.shape[0]
    lane = lax.broadcasted_iota(jnp.int32, (rows, LANES), 1)
    left = jnp.broadcast_to(values[:, 2 * pair : 2 * pair + 1], (rows, LANES))
    right = jnp.broadcast_to(values[:, 2 * pair + 1 : 2 * pair + 2], (rows, LANES))
    return jnp.where(lane < HEAD_DIM, left, right)


def unpacked(block):
    block = block.astype(F32)
    return block[:, STATE : STATE + 1, :] + block[:, STATE + 1 : STATE + 2, :], block[:, 0:STATE, :]


def pack(ref, total, state):
    ref[:, 0:STATE, :] = state.astype(BF16)
    wide = jnp.broadcast_to(total, (ref.shape[0], TILE, LANES))
    high = wide.astype(BF16).astype(F32)
    row = lax.broadcasted_iota(jnp.int32, wide.shape, 1)
    ref[:, STATE : STATE + TILE, :] = jnp.where(row == 0, high, wide - high).astype(BF16)


def state_kernel(x_hbm, b_hbm, dt_hbm, a_hbm, keep_ref, send_ref, *scratch):
    x_ref, b_ref, dt_ref, a_ref, packed_ref, sems = scratch
    loads = copies(sems, (dt_hbm, a_hbm, x_hbm, b_hbm), (dt_ref, a_ref, x_ref, b_ref))
    loads[0].wait()
    loads[1].wait()
    step, cum = decays(dt_ref[...], a_ref[...])
    length = cum.shape[1]
    total = cum[:, length - 1 :]
    tail = (jnp.exp(total - cum) * step).T
    total = jnp.broadcast_to(total, cum.shape).T[0:1]
    loads[2].wait()
    loads[3].wait()
    pairs = packed_ref.shape[0]
    groups = b_ref.shape[1] // STATE
    for group in range(groups):
        turned = b_ref[:, group * STATE : (group + 1) * STATE].T
        for pair in range(group * pairs // groups, (group + 1) * pairs // groups):
            x_pair = x_ref[:, pair * LANES : (pair + 1) * LANES].astype(F32)
            weighted = (pair_lanes(tail, pair) * x_pair).astype(BF16)
            state = jnp.dot(turned, weighted, preferred_element_type=F32)
            pack(packed_ref.at[pair : pair + 1], pair_lanes(total, pair)[None], state[None])
    half = pairs // 2
    keep_ref[...] = packed_ref[pl.ds(core_index() * half, half)]
    send_ref[...] = packed_ref[pl.ds((1 - core_index()) * half, half)]


def chip_state_kernel(keep_ref, got_ref, out_ref):
    first = core_index() == 0
    keep, got = unpacked(keep_ref[...]), unpacked(got_ref[...])
    early = [jnp.where(first, mine, other) for mine, other in zip(keep, got)]
    late = [jnp.where(first, other, mine) for mine, other in zip(keep, got)]
    pack(out_ref, early[0] + late[0], jnp.exp(late[0]) * early[1] + late[1])


def weights_kernel(after_ref, up_hbm, down_hbm, up_ref, down_ref, sems):
    for load in copies(sems, (up_hbm, down_hbm), (up_ref, down_ref)):
        load.wait()


def span_kernel(after_ref, *rest):
    ins, out_ref, block_ref = rest[:-2], rest[-2], rest[-1]
    for mask, part in enumerate(ins):
        block_ref[chip_index() ^ mask] = part[...]
    total, state = unpacked(block_ref[0])
    for chip in range(1, len(ins)):
        here, own = unpacked(block_ref[chip])
        total, state = total + here, jnp.exp(here) * state + own
    pack(out_ref, total, state)


def before_kernel(chips, after_ref, keep_ref, got_ref, *rest):
    ins, (mine_ref, send_ref, chip_ref, part_ref) = rest[:-4], rest[-4:]
    for mask in range(chips):
        chip_ref[chip_index() ^ mask] = ins[mask][...]
    parts = len(ins) - chips
    for mask in range(parts):
        part_ref[lax.axis_index("seq") ^ mask] = ins[chips + mask][...]
    carry = jnp.zeros(mine_ref.shape, F32)
    for ref, count, own in ((part_ref, parts, lax.axis_index("seq")), (chip_ref, chips, chip_index())):
        for index in range(count - 1):
            total, state = unpacked(ref[index])
            carry = jnp.where(index < own, jnp.exp(total) * carry + state, carry)
    first = core_index() == 0
    total, state = (jnp.where(first, k, g) for k, g in zip(unpacked(keep_ref[...]), unpacked(got_ref[...])))
    later = jnp.exp(total) * carry + state
    mine_ref[...] = jnp.where(first, carry, later).astype(BF16)
    send_ref[...] = jnp.where(first, later, carry).astype(BF16)


def inside_kernel(x_hbm, z_hbm, b_hbm, c_hbm, dt_hbm, a_hbm, d_hbm, local_ref, grown_ref, c_ref, *scratch):
    x_ref, z_ref, b_ref, dt_ref, a_ref, d_ref, sems = scratch
    loads = copies(
        sems,
        (dt_hbm, a_hbm, d_hbm, b_hbm, c_hbm, x_hbm, z_hbm),
        (dt_ref, a_ref, d_ref, b_ref, c_ref, x_ref, z_ref),
    )
    for load in loads:
        load.wait()
    step_rows, cum_rows = decays(dt_ref[...], a_ref[...])
    cum = cum_rows.T
    grown = jnp.exp(cum)
    length = cum.shape[0]
    pairs = x_ref.shape[1] // LANES
    groups = b_ref.shape[1] // STATE
    row = lax.broadcasted_iota(jnp.int32, (length, length), 0)
    col = lax.broadcasted_iota(jnp.int32, (length, length), 1)
    lane = lax.broadcasted_iota(jnp.int32, (length, LANES), 1)
    for group in range(groups):
        span = slice(group * STATE, (group + 1) * STATE)
        scores = lax.dot_general(c_ref[:, span], b_ref[:, span], NT, preferred_element_type=F32)
        scores = jnp.where(row >= col, scores, 0.0)
        for pair in range(group * pairs // groups, (group + 1) * pairs // groups):
            at = slice(pair * LANES, (pair + 1) * LANES)
            x_pair = x_ref[:, at]
            halves = []
            for head in (2 * pair, 2 * pair + 1):
                distance = cum[:, head : head + 1] - cum_rows[head : head + 1, :]
                decay = jnp.exp(jnp.where(row >= col, distance, FAR))
                mixing = (scores * (decay * step_rows[head : head + 1, :])).astype(BF16)
                halves.append(jnp.dot(mixing, x_pair, preferred_element_type=F32))
            inside = jnp.where(lane < HEAD_DIM, halves[0], halves[1])
            skip = pair_lanes(d_ref[...], pair) * x_pair.astype(F32)
            z = z_ref[:, at].astype(F32)
            gate = z / (1.0 + jnp.exp(-z))
            local_ref[:, at] = (inside + skip) * gate
            grown_ref[:, at] = pair_lanes(grown, pair) * gate


def prep_kernel(experts, width, resid_hbm, routes_hbm, gates_hbm, gain_hbm, norm_hbm, w_hbm, *rest):
    gate_ref, resid_ref, gain_ref, norm_ref, w_ref, routes_ref, gates_ref, sems = rest
    loads = copies(
        sems,
        (routes_hbm, gates_hbm, resid_hbm, gain_hbm, norm_hbm, w_hbm),
        (routes_ref, gates_ref, resid_ref, gain_ref, norm_ref, w_ref),
    )
    loads[0].wait()
    loads[1].wait()
    count, extent = gate_ref.shape
    start = width // LANES * LANES
    lane = lax.broadcasted_iota(jnp.int32, (extent, count), 0) + start - width
    expert = jnp.where(lane >= experts, lane - experts, lane)
    gate = jnp.zeros((extent, count), F32)
    for pick in range(routes_ref.shape[0]):
        gate = gate + jnp.where(routes_ref[pick] == expert, gates_ref[pick], 0.0)
    high = gate.astype(BF16).astype(F32)
    gate = jnp.where(lane < experts, high, jnp.where(lane < 2 * experts, gate - high, 0.0))
    gate_ref[...] = gate.T.astype(BF16)
    for load in loads[2:]:
        load.wait()


def half_product(half, local_ref, grown_ref, c_ref, norm_ref, w_ref, state_ref, normed_ref, count):
    pairs = state_ref.shape[0]
    width = pairs * LANES
    base = pl.multiple_of(half * width, width)
    groups = c_ref.shape[1] // STATE // 2
    per_group = pairs // groups
    for group in range(groups):
        c_group = c_ref[:, pl.ds(pl.multiple_of((half * groups + group) * STATE, STATE), STATE)]
        gated, squares = [], 0.0
        for pair in range(group * per_group, (group + 1) * per_group):
            span = pl.ds(pl.multiple_of(base + pair * LANES, LANES), LANES)
            carried = jnp.dot(c_group, state_ref[pair], preferred_element_type=F32)
            value = local_ref[:, span] + grown_ref[:, span] * carried
            gated.append(value)
            squares = squares + value * value
        mean = jnp.sum(squares, axis=1, keepdims=True) / (per_group * LANES)
        inverse = lax.rsqrt(mean + 1e-05)
        for offset, value in enumerate(gated):
            pair = group * per_group + offset
            gain = norm_ref[:, pl.ds(pl.multiple_of(base + pair * LANES, LANES), LANES)]
            normed_ref[:, pair * LANES : (pair + 1) * LANES] = (value * inverse * gain).astype(BF16)
    rows = normed_ref.shape[0] // count
    blocks = []
    for shift in range(count):
        owner = lax.axis_index("head") ^ (head_offset(shift - 1, count) if shift else 0)
        blocks.append(normed_ref[pl.ds(pl.multiple_of(owner * rows, rows), rows), :])
    weight = w_ref[:, pl.ds(base, width)]
    return lax.dot_general(jnp.concatenate(blocks, axis=0), weight, NT, preferred_element_type=F32)


def first_half_kernel(count, local_ref, grown_ref, c_ref, norm_ref, w_ref, mine_ref, out_ref, normed_ref):
    out_ref[...] = half_product(
        core_index(), local_ref, grown_ref, c_ref, norm_ref, w_ref, mine_ref, normed_ref, count
    )


def mixed_kernel(after_up, after_down, local_ref, grown_ref, c_ref, norm_ref, w_ref, got_ref, first_ref, *rest):
    outs, normed_ref = rest[:-1], rest[-1]
    product = first_ref[...] + half_product(
        1 - core_index(), local_ref, grown_ref, c_ref, norm_ref, w_ref, got_ref, normed_ref, len(outs)
    )
    rows = outs[0].shape[0]
    for shift, out in enumerate(outs):
        out[...] = product[shift * rows : (shift + 1) * rows].astype(BF16)


def rows_kernel(after_ref, resid_ref, gate_ref, gain_ref, *rest):
    parts, hidden_ref, rows_ref = rest[:-2], rest[-2], rest[-1]
    mixed = parts[0][...].astype(F32)
    for part in parts[1:]:
        mixed = mixed + part[...].astype(F32)
    hidden = (resid_ref[0].astype(F32) + mixed).astype(BF16)
    hidden_ref[...] = hidden
    value = hidden.astype(F32)
    scale = lax.rsqrt(jnp.mean(value * value, axis=1, keepdims=True) + 1e-05)
    width = value.shape[1]
    rows_ref[:, width // LANES * LANES :] = gate_ref[...]
    rows_ref[:, :width] = (value * scale * gain_ref[...]).astype(BF16)


def expert_kernel(experts, count, up_ref, down_ref, other_up_ref, other_down_ref, *rest):
    ins, outs = rest[:count], rest[count:]
    width = up_ref.shape[2]
    start = width // LANES * LANES
    rows = jnp.concatenate([ref[:, :width] for ref in ins], axis=0)
    tail = jnp.concatenate([ref[:, start:] for ref in ins], axis=0).astype(F32)
    lane = lax.broadcasted_iota(jnp.int32, tail.shape, 1) + start - width
    own = lax.axis_index("head") * lax.axis_size("exp") + lax.axis_index("exp")
    other = own + 1 - 2 * core_index()
    total = 0.0
    for expert, up_of, down_of in ((own, up_ref, down_ref), (other, other_up_ref, other_down_ref)):
        up = lax.dot_general(rows, up_of[0], NT, preferred_element_type=F32)
        up = jnp.maximum(up, 0.0)
        activated = (up * up).astype(BF16)
        chosen = (lane == expert) | (lane == expert + experts)
        gate = jnp.sum(jnp.where(chosen, tail, 0.0), axis=1, keepdims=True)
        total = total + jnp.dot(activated, down_of[0], preferred_element_type=F32) * gate
    at = 0
    for out in outs:
        out[...] = total[at : at + out.shape[0]].astype(BF16)
        at += out.shape[0]


def sum_kernel(*refs):
    total = refs[0][...].astype(F32)
    for ref in refs[1:-1]:
        total = total + ref[...].astype(F32)
    refs[-1][...] = total.astype(BF16)


def last_kernel(hidden_ref, *rest):
    parts, out_ref = rest[:-1], rest[-1]
    total = parts[0][...].astype(F32)
    for part in parts[1:]:
        total = total + part[...].astype(F32)
    out_ref[0] = (hidden_ref[...].astype(F32) + total).astype(BF16)


def swap(value, axis, mask):
    size = lax.axis_size(axis)
    return lax.ppermute(value, axis, [(i, i ^ mask) for i in range(size)])


def swap_slot(value, slot, chip_mask=0):
    heads, size = lax.axis_size("head"), lax.axis_size("exp")
    order = offsets(heads)
    pairs = []
    for i in range(heads * size):
        head, exp = i // size, i % size
        pairs.append((i, (head ^ order[exp % 2][slot]) * size + (exp ^ (2 * chip_mask))))
    return lax.ppermute(value, ("head", "exp"), pairs)


def per_device(
    x_in, z_in, b_in, c_in, dt_in, a_log, d_skip, norm_w, w_out, resid, routes, gates, moe_gain, w_up, w_down
):
    length, heads = dt_in.shape
    channels = x_in.shape[1]
    model = w_out.shape[1]
    hidden_units = w_up.shape[2]
    seq_size, head_size, exp_size = lax.axis_size("seq"), lax.axis_size("head"), lax.axis_size("exp")
    chips = exp_size // 2
    rows = resid.shape[1]
    experts = head_size * exp_size
    pairs = channels // LANES
    half = pairs // 2
    dt_rows, a_row, d_row = dt_in.T, a_log[None], d_skip[None]
    dma = pltpu.SemaphoreType.DMA
    packed = struct((half, STATE + TILE, LANES), BF16)

    keep, send = call(
        state_kernel,
        "state",
        [packed, packed],
        [(HBM, x_in), (HBM, b_in), (HBM, dt_rows), (HBM, a_row)],
        [pltpu.VMEM(x_in.shape, BF16), pltpu.VMEM(b_in.shape, BF16), pltpu.VMEM(dt_rows.shape, F32),
         pltpu.VMEM(a_row.shape, F32), pltpu.VMEM((pairs, STATE + TILE, LANES), BF16), dma((4,))],
        megabytes=16,
    )
    local, grown, c_held = call(
        inside_kernel,
        "inside",
        [struct((length, channels), F32), struct((length, channels), F32), struct(c_in.shape, BF16)],
        [(HBM, value) for value in (x_in, z_in, b_in, c_in, dt_rows, a_row, d_row)],
        [pltpu.VMEM(x_in.shape, BF16), pltpu.VMEM(z_in.shape, BF16), pltpu.VMEM(b_in.shape, BF16),
         pltpu.VMEM(dt_rows.shape, F32), pltpu.VMEM(a_row.shape, F32), pltpu.VMEM(d_row.shape, F32), dma((7,))],
        megabytes=16,
    )
    wide = -(-(model + 2 * experts) // LANES) * LANES
    turned = [jnp.transpose(value, (2, 0, 1)) for value in (routes, gates)]
    gate_lanes, resid_held, gain_held, norm_held, w_held = call(
        functools.partial(prep_kernel, experts, model),
        "prep",
        [struct((rows, wide - model // LANES * LANES), BF16), struct(resid.shape, BF16), struct((1, model), F32),
         struct((1, channels), F32), struct((model, channels), BF16)],
        [(HBM, value) for value in (resid, *turned, moe_gain[None], norm_w[None], w_out.T)],
        [pltpu.VMEM(turned[0].shape, jnp.int32), pltpu.VMEM(turned[1].shape, F32), dma((6,))],
        megabytes=16,
    )
    up_turned = jnp.swapaxes(w_up, 1, 2)
    got = swap(send, "exp", 1)
    chip = call(chip_state_kernel, "chip_state", packed, [(VMEM, keep), (VMEM, got)])
    chip, up_after, down_after = lax.optimization_barrier((chip, up_turned, w_down))
    other_up, other_down = swap(up_after, "exp", 1), swap(down_after, "exp", 1)
    along_y = [chip] + [swap(chip, "exp", 2 * d) for d in range(1, chips)]
    span = call(
        span_kernel,
        "span",
        packed,
        [(ANY, c_held)] + [(VMEM, value) for value in along_y],
        [pltpu.VMEM((chips, *packed.shape), BF16)],
    )
    along_x = [span] + [swap(span, "seq", d) for d in range(1, seq_size)]
    before, before_send = call(
        functools.partial(before_kernel, chips),
        "before",
        [struct((half, STATE, LANES), BF16)] * 2,
        [(ANY, gate_lanes)] + [(VMEM, value) for value in (keep, got, *along_y, *along_x)],
        [pltpu.VMEM((chips, *packed.shape), BF16), pltpu.VMEM((seq_size, *packed.shape), BF16)],
        megabytes=24,
    )
    before_got = swap(before_send, "exp", 1)
    shared = [(VMEM, value) for value in (local, grown, c_held, norm_held, w_held)]
    normed_half = pltpu.VMEM((length, channels // 2), BF16)
    first = call(
        functools.partial(first_half_kernel, head_size),
        "first_half",
        struct((length, model), F32),
        shared + [(VMEM, before)],
        [normed_half],
    )
    mixed = call(
        mixed_kernel,
        "mixed",
        [struct((rows, model), BF16)] * head_size,
        [(ANY, other_up), (ANY, other_down)] + shared + [(VMEM, before_got), (VMEM, first)],
        [normed_half],
    )
    up_held, down_held = call(
        weights_kernel,
        "weights",
        [struct(up_turned.shape, BF16), struct(w_down.shape, BF16)],
        [(ANY, mixed[0]), (HBM, up_turned), (HBM, w_down)],
        [dma((2,))],
    )
    slots = list(range(head_size - 1))
    parts = [mixed[0]] + [swap_slot(mixed[k + 1], k) for k in slots]
    hidden, own_rows = call(
        rows_kernel,
        "rows",
        [struct((rows, model), BF16), struct((rows, wide), BF16)],
        [(ANY, up_held)] + [(VMEM, value) for value in (resid_held, gate_lanes, gain_held, *parts)],
    )

    def through_experts(members):
        return call(
            functools.partial(expert_kernel, experts, len(members)),
            "experts",
            [struct((rows, model), BF16)] * len(members),
            [(VMEM, value) for value in (up_held, down_held, other_up, other_down, *members)],
            megabytes=16,
        )

    both = ("head", "exp")
    group = [z * exp_size + 2 * d for z in (1, 0) for d in reversed(range(chips))][:-1]

    def spread(block):
        return [block] + [swap(block, both, mask) for mask in reversed(group)]

    sets = [spread(swap(own_rows, "head", high)) for high in range(2, head_size, 2)]
    near = through_experts(spread(own_rows))
    near, sets = lax.optimization_barrier((near, sets))
    far = [through_experts(members) for members in sets]
    arrived, near = [], list(near)
    for high, pieces in zip(range(2, head_size, 2), far):
        got = [swap(piece, both, mask) for piece, mask in zip(pieces[:0:-1], group)]
        total = call(sum_kernel, "sum", struct((rows, model), BF16), [(VMEM, v) for v in (pieces[0], *got)])
        if high == 2:
            total, near[1:-1] = lax.optimization_barrier((total, near[1:-1]))
        arrived.append(swap(total, "head", high))
    arrived += [swap(piece, both, mask) for piece, mask in zip(near[:0:-1], group)]
    return call(
        last_kernel,
        "last",
        struct(resid.shape, BF16),
        [(VMEM, value) for value in (hidden, near[0], *arrived)],
        pinned=False,
    )


def solution(mesh):
    placed = (
        P(("seq", "exp"), "head"),
        P(("seq", "exp"), "head"),
        P(("seq", "exp"), "head"),
        P(("seq", "exp"), "head"),
        P(("seq", "exp"), "head"),
        P("head"),
        P("head"),
        P("head"),
        P("head", None),
        P(("seq", "exp"), "head", None),
        P(("seq", "exp"), "head", None),
        P(("seq", "exp"), "head", None),
        P(),
        P(("head", "exp"), None, None),
        P(("head", "exp"), None, None),
    )
    return jax.shard_map(
        per_device,
        mesh=mesh,
        in_specs=placed,
        out_specs=P(("seq", "exp"), "head", None),
        check_vma=False,
    )
```

```python
import functools

import jax
import jax.numpy as jnp
from jax import lax
from jax.experimental import pallas as pl
from jax.experimental.pallas import tpu as pltpu
from jax.sharding import PartitionSpec as P

HEAD_DIM = 64
STATE = 128
LANES = 128
TILE = 16
FAR = -1e30
F32 = jnp.float32
BF16 = jnp.bfloat16
HBM = pl.BlockSpec(memory_space=pltpu.HBM)
VMEM = pl.BlockSpec(memory_space=pltpu.VMEM)
ANY = pl.BlockSpec(memory_space=pl.ANY)
NT = (((1,), (1,)), ((), ()))


def struct(shape, dtype):
    return jax.ShapeDtypeStruct(shape, dtype)


def call(kernel, name, outs, ins, scratch=(), megabytes=12, pinned=True):
    args = [pltpu.with_memory_space_constraint(arg, pltpu.HBM) if spec is HBM else arg for spec, arg in ins]
    return pl.pallas_call(
        kernel,
        out_shape=jax.tree.map(lambda out: pltpu.VMEM(out.shape, out.dtype), outs) if pinned else outs,
        in_specs=[spec for spec, _ in ins],
        out_specs=jax.tree.map(lambda _: VMEM, outs),
        scratch_shapes=list(scratch),
        name=name,
        compiler_params=pltpu.CompilerParams(vmem_limit_bytes=megabytes << 20),
    )(*args)


def offsets(count):
    down = list(range(count - 1, 0, -1))
    return [[2, 3, 1], [3, 1, 2]] if count == 4 else [down, down]


def targets(count):
    return [[2, 3, 1], [1, 1, 2]] if count == 4 else offsets(count)


def head_offset(slot, count):
    first, second = (order[slot] for order in offsets(count))
    return jnp.where(core_index() == 0, first, second)


def core_index():
    return lax.axis_index("exp") % 2


def chip_index():
    return lax.axis_index("exp") // 2


def copies(sems, sources, targets):
    made = [pltpu.make_async_copy(s, t, sems.at[i]) for i, (s, t) in enumerate(zip(sources, targets))]
    for copy in made:
        copy.start()
    return made


def decays(dt_rows, a_log):
    heads, length = dt_rows.shape
    step = jnp.maximum(dt_rows, 0.0) + jnp.log1p(jnp.exp(-jnp.abs(dt_rows)))
    same = lax.broadcasted_iota(jnp.int32, (heads, heads), 0) == lax.broadcasted_iota(jnp.int32, (heads, heads), 1)
    a_column = jnp.sum(jnp.where(same, jnp.broadcast_to(a_log, (heads, heads)), 0.0), axis=1, keepdims=True)
    rate = -step * jnp.exp(a_column)
    row = lax.broadcasted_iota(jnp.int32, (length, length), 0)
    col = lax.broadcasted_iota(jnp.int32, (length, length), 1)
    upper = (row <= col).astype(F32)
    cum = jnp.dot(rate, upper, precision=lax.Precision.HIGHEST, preferred_element_type=F32)
    return step, cum


def pair_lanes(values, pair):
    rows = values.shape[0]
    lane = lax.broadcasted_iota(jnp.int32, (rows, LANES), 1)
    left = jnp.broadcast_to(values[:, 2 * pair : 2 * pair + 1], (rows, LANES))
    right = jnp.broadcast_to(values[:, 2 * pair + 1 : 2 * pair + 2], (rows, LANES))
    return jnp.where(lane < HEAD_DIM, left, right)


def unpacked(block):
    pairs = block.shape[0] // STATE
    tail = block[pairs * STATE :].astype(F32)
    totals = [tail[pair : pair + 1] + tail[pairs + pair : pairs + pair + 1] for pair in range(pairs)]
    return jnp.stack(totals), block[: pairs * STATE].astype(F32).reshape(pairs, STATE, LANES)


def pack(ref, total, state):
    pairs = state.shape[0]
    ref[0 : pairs * STATE, :] = state.reshape(pairs * STATE, LANES).astype(BF16)
    row = lax.broadcasted_iota(jnp.int32, (TILE, LANES), 0)
    tail = jnp.zeros((TILE, LANES), F32)
    for pair in range(pairs):
        wide = jnp.broadcast_to(total[pair], (TILE, LANES))
        high = wide.astype(BF16).astype(F32)
        tail = jnp.where(row == pair, high, jnp.where(row == pairs + pair, wide - high, tail))
    ref[pairs * STATE :, :] = tail.astype(BF16)


def state_kernel(x_hbm, b_hbm, dt_hbm, a_hbm, keep_ref, send_ref, *scratch):
    x_ref, b_ref, dt_ref, a_ref, packed_ref, sems = scratch
    loads = copies(sems, (dt_hbm, a_hbm, x_hbm, b_hbm), (dt_ref, a_ref, x_ref, b_ref))
    loads[0].wait()
    loads[1].wait()
    step, cum = decays(dt_ref[...], a_ref[...])
    length = cum.shape[1]
    total = cum[:, length - 1 :]
    tail = (jnp.exp(total - cum) * step).T
    total = jnp.broadcast_to(total, cum.shape).T[0:1]
    loads[2].wait()
    loads[3].wait()
    pairs = x_ref.shape[1] // LANES
    half = pairs // 2
    groups = b_ref.shape[1] // STATE
    totals, states = [], []
    for group in range(groups):
        turned = b_ref[:, group * STATE : (group + 1) * STATE].T
        for pair in range(group * pairs // groups, (group + 1) * pairs // groups):
            x_pair = x_ref[:, pair * LANES : (pair + 1) * LANES].astype(F32)
            weighted = (pair_lanes(tail, pair) * x_pair).astype(BF16)
            state = jnp.dot(turned, weighted, preferred_element_type=F32)
            totals.append(pair_lanes(total, pair))
            states.append(state)
    for at in range(2):
        span = slice(at * half, (at + 1) * half)
        pack(packed_ref.at[at], totals[span], jnp.stack(states[span]))
    keep_ref[...] = packed_ref[core_index()]
    send_ref[...] = packed_ref[1 - core_index()]


def chip_state_kernel(keep_ref, got_ref, out_ref):
    first = core_index() == 0
    keep, got = unpacked(keep_ref[...]), unpacked(got_ref[...])
    early = [jnp.where(first, mine, other) for mine, other in zip(keep, got)]
    late = [jnp.where(first, other, mine) for mine, other in zip(keep, got)]
    pack(out_ref, early[0] + late[0], jnp.exp(late[0]) * early[1] + late[1])


def weights_kernel(after_ref, up_hbm, down_hbm, up_ref, down_ref, sems):
    for load in copies(sems, (up_hbm, down_hbm), (up_ref, down_ref)):
        load.wait()


def span_kernel(after_ref, *rest):
    ins, out_ref, block_ref = rest[:-2], rest[-2], rest[-1]
    for mask, part in enumerate(ins):
        block_ref[chip_index() ^ mask] = part[...]
    total, state = unpacked(block_ref[0])
    for chip in range(1, len(ins)):
        here, own = unpacked(block_ref[chip])
        total, state = total + here, jnp.exp(here) * state + own
    pack(out_ref, total, state)


def before_kernel(chips, after_ref, keep_ref, got_ref, *rest):
    ins, (mine_ref, send_ref, chip_ref, part_ref) = rest[:-4], rest[-4:]
    for mask in range(chips):
        chip_ref[chip_index() ^ mask] = ins[mask][...]
    parts = len(ins) - chips
    for mask in range(parts):
        part_ref[lax.axis_index("seq") ^ mask] = ins[chips + mask][...]
    carry = jnp.zeros(mine_ref.shape, F32)
    for ref, count, own in ((part_ref, parts, lax.axis_index("seq")), (chip_ref, chips, chip_index())):
        for index in range(count - 1):
            total, state = unpacked(ref[index])
            carry = jnp.where(index < own, jnp.exp(total) * carry + state, carry)
    first = core_index() == 0
    total, state = (jnp.where(first, k, g) for k, g in zip(unpacked(keep_ref[...]), unpacked(got_ref[...])))
    later = jnp.exp(total) * carry + state
    mine_ref[...] = jnp.where(first, carry, later).astype(BF16)
    send_ref[...] = jnp.where(first, later, carry).astype(BF16)


def inside_kernel(x_hbm, z_hbm, b_hbm, c_hbm, dt_hbm, a_hbm, d_hbm, local_ref, grown_ref, c_ref, *scratch):
    x_ref, z_ref, b_ref, dt_ref, a_ref, d_ref, sems = scratch
    loads = copies(
        sems,
        (dt_hbm, a_hbm, d_hbm, b_hbm, c_hbm, x_hbm, z_hbm),
        (dt_ref, a_ref, d_ref, b_ref, c_ref, x_ref, z_ref),
    )
    for load in loads:
        load.wait()
    step_rows, cum_rows = decays(dt_ref[...], a_ref[...])
    cum = cum_rows.T
    grown = jnp.exp(cum)
    length = cum.shape[0]
    pairs = x_ref.shape[1] // LANES
    groups = b_ref.shape[1] // STATE
    row = lax.broadcasted_iota(jnp.int32, (length, length), 0)
    col = lax.broadcasted_iota(jnp.int32, (length, length), 1)
    lane = lax.broadcasted_iota(jnp.int32, (length, LANES), 1)
    for group in range(groups):
        span = slice(group * STATE, (group + 1) * STATE)
        scores = lax.dot_general(c_ref[:, span], b_ref[:, span], NT, preferred_element_type=F32)
        scores = jnp.where(row >= col, scores, 0.0)
        for pair in range(group * pairs // groups, (group + 1) * pairs // groups):
            at = slice(pair * LANES, (pair + 1) * LANES)
            x_pair = x_ref[:, at]
            halves = []
            for head in (2 * pair, 2 * pair + 1):
                distance = cum[:, head : head + 1] - cum_rows[head : head + 1, :]
                decay = jnp.exp(jnp.where(row >= col, distance, FAR))
                mixing = (scores * (decay * step_rows[head : head + 1, :])).astype(BF16)
                halves.append(jnp.dot(mixing, x_pair, preferred_element_type=F32))
            inside = jnp.where(lane < HEAD_DIM, halves[0], halves[1])
            skip = pair_lanes(d_ref[...], pair) * x_pair.astype(F32)
            z = z_ref[:, at].astype(F32)
            gate = z / (1.0 + jnp.exp(-z))
            local_ref[:, at] = (inside + skip) * gate
            grown_ref[:, at] = pair_lanes(grown, pair) * gate


def prep_kernel(experts, width, resid_hbm, routes_hbm, gates_hbm, gain_hbm, norm_hbm, w_hbm, *rest):
    gate_ref, resid_ref, gain_ref, norm_ref, w_ref, routes_ref, gates_ref, sems = rest
    loads = copies(
        sems,
        (routes_hbm, gates_hbm, resid_hbm, gain_hbm, norm_hbm, w_hbm),
        (routes_ref, gates_ref, resid_ref, gain_ref, norm_ref, w_ref),
    )
    loads[0].wait()
    loads[1].wait()
    count, extent = gate_ref.shape
    start = width // LANES * LANES
    lane = lax.broadcasted_iota(jnp.int32, (extent, count), 0) + start - width
    expert = jnp.where(lane >= experts, lane - experts, lane)
    gate = jnp.zeros((extent, count), F32)
    for pick in range(routes_ref.shape[0]):
        gate = gate + jnp.where(routes_ref[pick] == expert, gates_ref[pick], 0.0)
    high = gate.astype(BF16).astype(F32)
    gate = jnp.where(lane < experts, high, jnp.where(lane < 2 * experts, gate - high, 0.0))
    gate_ref[...] = gate.T.astype(BF16)
    for load in loads[2:]:
        load.wait()


def half_product(half, local_ref, grown_ref, c_ref, norm_ref, w_ref, state_ref, normed_ref, count):
    pairs = state_ref.shape[0]
    width = pairs * LANES
    base = pl.multiple_of(half * width, width)
    groups = c_ref.shape[1] // STATE // 2
    per_group = pairs // groups
    for group in range(groups):
        c_group = c_ref[:, pl.ds(pl.multiple_of((half * groups + group) * STATE, STATE), STATE)]
        gated, squares = [], 0.0
        for pair in range(group * per_group, (group + 1) * per_group):
            span = pl.ds(pl.multiple_of(base + pair * LANES, LANES), LANES)
            carried = jnp.dot(c_group, state_ref[pair], preferred_element_type=F32)
            value = local_ref[:, span] + grown_ref[:, span] * carried
            gated.append(value)
            squares = squares + value * value
        mean = jnp.sum(squares, axis=1, keepdims=True) / (per_group * LANES)
        inverse = lax.rsqrt(mean + 1e-05)
        for offset, value in enumerate(gated):
            pair = group * per_group + offset
            gain = norm_ref[:, pl.ds(pl.multiple_of(base + pair * LANES, LANES), LANES)]
            normed_ref[:, pair * LANES : (pair + 1) * LANES] = (value * inverse * gain).astype(BF16)
    rows = normed_ref.shape[0] // count
    blocks = []
    for shift in range(count):
        owner = lax.axis_index("head") ^ (head_offset(shift - 1, count) if shift else 0)
        blocks.append(normed_ref[pl.ds(pl.multiple_of(owner * rows, rows), rows), :])
    weight = w_ref[:, pl.ds(base, width)]
    return lax.dot_general(jnp.concatenate(blocks, axis=0), weight, NT, preferred_element_type=F32)


def first_half_kernel(count, local_ref, grown_ref, c_ref, norm_ref, w_ref, mine_ref, out_ref, normed_ref):
    out_ref[...] = half_product(
        core_index(), local_ref, grown_ref, c_ref, norm_ref, w_ref, mine_ref, normed_ref, count
    )


def mixed_kernel(after_up, after_down, local_ref, grown_ref, c_ref, norm_ref, w_ref, got_ref, first_ref, *rest):
    outs, normed_ref = rest[:-1], rest[-1]
    product = first_ref[...] + half_product(
        1 - core_index(), local_ref, grown_ref, c_ref, norm_ref, w_ref, got_ref, normed_ref, len(outs)
    )
    rows = outs[0].shape[0]
    for shift, out in enumerate(outs):
        out[...] = product[shift * rows : (shift + 1) * rows].astype(BF16)


def relay_kernel(own_ref, got_ref, out_ref):
    got = jnp.where(core_index() == 1, got_ref[...].astype(F32), 0.0)
    out_ref[...] = (own_ref[...].astype(F32) + got).astype(BF16)


def rows_kernel(after_ref, resid_ref, gate_ref, gain_ref, *rest):
    parts, hidden_ref, rows_ref = rest[:-2], rest[-2], rest[-1]
    mixed = parts[0][...].astype(F32)
    for at, part in enumerate(parts[1:]):
        value = part[...].astype(F32)
        if at == 0 and len(parts) == 4:
            value = jnp.where(core_index() == 0, value, 0.0)
        mixed = mixed + value
    hidden = (resid_ref[0].astype(F32) + mixed).astype(BF16)
    hidden_ref[...] = hidden
    value = hidden.astype(F32)
    scale = lax.rsqrt(jnp.mean(value * value, axis=1, keepdims=True) + 1e-05)
    width = value.shape[1]
    rows_ref[:, width // LANES * LANES :] = gate_ref[...]
    rows_ref[:, :width] = (value * scale * gain_ref[...]).astype(BF16)


def expert_kernel(experts, count, up_ref, down_ref, other_up_ref, other_down_ref, *rest):
    ins, outs = rest[:count], rest[count:]
    width = up_ref.shape[2]
    start = width // LANES * LANES
    rows = jnp.concatenate([ref[:, :width] for ref in ins], axis=0)
    tail = jnp.concatenate([ref[:, start:] for ref in ins], axis=0).astype(F32)
    lane = lax.broadcasted_iota(jnp.int32, tail.shape, 1) + start - width
    own = lax.axis_index("head") * lax.axis_size("exp") + lax.axis_index("exp")
    other = own + 1 - 2 * core_index()
    total = 0.0
    for expert, up_of, down_of in ((own, up_ref, down_ref), (other, other_up_ref, other_down_ref)):
        up = lax.dot_general(rows, up_of[0], NT, preferred_element_type=F32)
        up = jnp.maximum(up, 0.0)
        activated = (up * up).astype(BF16)
        chosen = (lane == expert) | (lane == expert + experts)
        gate = jnp.sum(jnp.where(chosen, tail, 0.0), axis=1, keepdims=True)
        total = total + jnp.dot(activated, down_of[0], preferred_element_type=F32) * gate
    at = 0
    for out in outs:
        out[...] = total[at : at + out.shape[0]].astype(BF16)
        at += out.shape[0]


def sum_kernel(*refs):
    total = refs[0][...].astype(F32)
    for ref in refs[1:-1]:
        total = total + ref[...].astype(F32)
    refs[-1][...] = total.astype(BF16)


def last_kernel(hidden_ref, *rest):
    parts, out_ref = rest[:-1], rest[-1]
    total = parts[0][...].astype(F32)
    for part in parts[1:]:
        total = total + part[...].astype(F32)
    out_ref[0] = (hidden_ref[...].astype(F32) + total).astype(BF16)


def swap(value, axis, mask):
    size = lax.axis_size(axis)
    return lax.ppermute(value, axis, [(i, i ^ mask) for i in range(size)])


def swap_slot(value, slot):
    heads, size = lax.axis_size("head"), lax.axis_size("exp")
    order = targets(heads)
    pairs = []
    for i in range(heads * size):
        head, exp = i // size, i % size
        pairs.append((i, (head ^ order[exp % 2][slot]) * size + exp))
    return lax.ppermute(value, ("head", "exp"), pairs)


def per_device(
    x_in, z_in, b_in, c_in, dt_in, a_log, d_skip, norm_w, w_out, resid, routes, gates, moe_gain, w_up, w_down
):
    length, heads = dt_in.shape
    channels = x_in.shape[1]
    model = w_out.shape[1]
    hidden_units = w_up.shape[2]
    seq_size, head_size, exp_size = lax.axis_size("seq"), lax.axis_size("head"), lax.axis_size("exp")
    chips = exp_size // 2
    rows = resid.shape[1]
    experts = head_size * exp_size
    pairs = channels // LANES
    half = pairs // 2
    dt_rows, a_row, d_row = dt_in.T, a_log[None], d_skip[None]
    dma = pltpu.SemaphoreType.DMA
    packed = struct((half * STATE + TILE, LANES), BF16)

    keep, send = call(
        state_kernel,
        "state",
        [packed, packed],
        [(HBM, x_in), (HBM, b_in), (HBM, dt_rows), (HBM, a_row)],
        [pltpu.VMEM(x_in.shape, BF16), pltpu.VMEM(b_in.shape, BF16), pltpu.VMEM(dt_rows.shape, F32),
         pltpu.VMEM(a_row.shape, F32), pltpu.VMEM((2, half * STATE + TILE, LANES), BF16), dma((4,))],
        megabytes=16,
    )
    local, grown, c_held = call(
        inside_kernel,
        "inside",
        [struct((length, channels), F32), struct((length, channels), F32), struct(c_in.shape, BF16)],
        [(HBM, value) for value in (x_in, z_in, b_in, c_in, dt_rows, a_row, d_row)],
        [pltpu.VMEM(x_in.shape, BF16), pltpu.VMEM(z_in.shape, BF16), pltpu.VMEM(b_in.shape, BF16),
         pltpu.VMEM(dt_rows.shape, F32), pltpu.VMEM(a_row.shape, F32), pltpu.VMEM(d_row.shape, F32), dma((7,))],
        megabytes=16,
    )
    wide = -(-(model + 2 * experts) // LANES) * LANES
    turned = [jnp.transpose(value, (2, 0, 1)) for value in (routes, gates)]
    gate_lanes, resid_held, gain_held, norm_held, w_held = call(
        functools.partial(prep_kernel, experts, model),
        "prep",
        [struct((rows, wide - model // LANES * LANES), BF16), struct(resid.shape, BF16), struct((1, model), F32),
         struct((1, channels), F32), struct((model, channels), BF16)],
        [(HBM, value) for value in (resid, *turned, moe_gain[None], norm_w[None], w_out.T)],
        [pltpu.VMEM(turned[0].shape, jnp.int32), pltpu.VMEM(turned[1].shape, F32), dma((6,))],
        megabytes=16,
    )
    up_turned = jnp.swapaxes(w_up, 1, 2)
    got = swap(send, "exp", 1)
    chip = call(chip_state_kernel, "chip_state", packed, [(VMEM, keep), (VMEM, got)])
    chip, up_after, down_after = lax.optimization_barrier((chip, up_turned, w_down))
    other_up, other_down = swap(up_after, "exp", 1), swap(down_after, "exp", 1)
    along_y = [chip] + [swap(chip, "exp", 2 * d) for d in range(1, chips)]
    span = call(
        span_kernel,
        "span",
        packed,
        [(ANY, c_held)] + [(VMEM, value) for value in along_y],
        [pltpu.VMEM((chips, *packed.shape), BF16)],
    )
    along_x = [span] + [swap(span, "seq", d) for d in range(1, seq_size)]
    before, before_send = call(
        functools.partial(before_kernel, chips),
        "before",
        [struct((half, STATE, LANES), BF16)] * 2,
        [(ANY, gate_lanes)] + [(VMEM, value) for value in (keep, got, *along_y, *along_x)],
        [pltpu.VMEM((chips, *packed.shape), BF16), pltpu.VMEM((seq_size, *packed.shape), BF16)],
        megabytes=24,
    )
    before_got = swap(before_send, "exp", 1)
    shared = [(VMEM, value) for value in (local, grown, c_held, norm_held, w_held)]
    normed_half = pltpu.VMEM((length, channels // 2), BF16)
    first = call(
        functools.partial(first_half_kernel, head_size),
        "first_half",
        struct((length, model), F32),
        shared + [(VMEM, before)],
        [normed_half],
    )
    mixed = call(
        mixed_kernel,
        "mixed",
        [struct((rows, model), BF16)] * head_size,
        [(ANY, other_up), (ANY, other_down)] + shared + [(VMEM, before_got), (VMEM, first)],
        [normed_half],
    )
    up_held, down_held = call(
        weights_kernel,
        "weights",
        [struct(up_turned.shape, BF16), struct(w_down.shape, BF16)],
        [(ANY, mixed[0]), (HBM, up_turned), (HBM, w_down)],
        [dma((2,))],
    )
    slots = list(range(head_size - 1))
    parts, last = [swap_slot(mixed[k + 1], k) for k in slots[:-1]], mixed[-1]
    if head_size == 4:
        last = call(relay_kernel, "relay", struct((rows, model), BF16), [(VMEM, last), (VMEM, parts[0])])
    parts = [mixed[0]] + parts + [swap_slot(last, slots[-1])]
    hidden, own_rows = call(
        rows_kernel,
        "rows",
        [struct((rows, model), BF16), struct((rows, wide), BF16)],
        [(ANY, up_held)] + [(VMEM, value) for value in (resid_held, gate_lanes, gain_held, *parts)],
    )

    def through_experts(members):
        return call(
            functools.partial(expert_kernel, experts, len(members)),
            "experts",
            [struct((rows, model), BF16)] * len(members),
            [(VMEM, value) for value in (up_held, down_held, other_up, other_down, *members)],
            megabytes=16,
        )

    both = ("head", "exp")
    group = [z * exp_size + 2 * d for z in (1, 0) for d in reversed(range(chips))][:-1]

    def spread(block):
        return [block] + [swap(block, both, mask) for mask in reversed(group)]

    sets = [spread(swap(own_rows, "head", high)) for high in range(2, head_size, 2)]
    near = through_experts(spread(own_rows))
    near, sets = lax.optimization_barrier((near, sets))
    far = [through_experts(members) for members in sets]
    arrived, near = [], list(near)
    for high, pieces in zip(range(2, head_size, 2), far):
        got = [swap(piece, both, mask) for piece, mask in zip(pieces[:0:-1], group)]
        total = call(sum_kernel, "sum", struct((rows, model), BF16), [(VMEM, v) for v in (pieces[0], *got)])
        if high == 2:
            total, near[1:-1] = lax.optimization_barrier((total, near[1:-1]))
        arrived.append(swap(total, "head", high))
    arrived += [swap(piece, both, mask) for piece, mask in zip(near[:0:-1], group)]
    return call(
        last_kernel,
        "last",
        struct(resid.shape, BF16),
        [(VMEM, value) for value in (hidden, near[0], *arrived)],
        pinned=False,
    )


def solution(mesh):
    placed = (
        P(("seq", "exp"), "head"),
        P(("seq", "exp"), "head"),
        P(("seq", "exp"), "head"),
        P(("seq", "exp"), "head"),
        P(("seq", "exp"), "head"),
        P("head"),
        P("head"),
        P("head"),
        P("head", None),
        P(("seq", "exp"), "head", None),
        P(("seq", "exp"), "head", None),
        P(("seq", "exp"), "head", None),
        P(),
        P(("head", "exp"), None, None),
        P(("head", "exp"), None, None),
    )
    return jax.shard_map(
        per_device,
        mesh=mesh,
        in_specs=placed,
        out_specs=P(("seq", "exp"), "head", None),
        check_vma=False,
    )
```

```python
import functools

import jax
import jax.numpy as jnp
from jax import lax
from jax.experimental import pallas as pl
from jax.experimental.pallas import tpu as pltpu
from jax.sharding import PartitionSpec as P

HEAD_DIM = 64
STATE = 128
LANES = 128
TILE = 16
FAR = -1e30
F32 = jnp.float32
BF16 = jnp.bfloat16
HBM = pl.BlockSpec(memory_space=pltpu.HBM)
VMEM = pl.BlockSpec(memory_space=pltpu.VMEM)
ANY = pl.BlockSpec(memory_space=pl.ANY)
NT = (((1,), (1,)), ((), ()))


def struct(shape, dtype):
    return jax.ShapeDtypeStruct(shape, dtype)


def call(kernel, name, outs, ins, scratch=(), megabytes=12, pinned=True):
    args = [pltpu.with_memory_space_constraint(arg, pltpu.HBM) if spec is HBM else arg for spec, arg in ins]
    return pl.pallas_call(
        kernel,
        out_shape=jax.tree.map(lambda out: pltpu.VMEM(out.shape, out.dtype), outs) if pinned else outs,
        in_specs=[spec for spec, _ in ins],
        out_specs=jax.tree.map(lambda _: VMEM, outs),
        scratch_shapes=list(scratch),
        name=name,
        compiler_params=pltpu.CompilerParams(vmem_limit_bytes=megabytes << 20),
    )(*args)


def offsets(count):
    down = list(range(count - 1, 0, -1))
    return [[3, 1, 2], [2, 3, 1]] if count == 4 else [down, down]


def targets(count):
    return [[1, 1, 2], [2, 3, 1]] if count == 4 else offsets(count)


def head_offset(slot, count):
    first, second = (order[slot] for order in offsets(count))
    return jnp.where(core_index() == 0, first, second)


def core_index():
    return lax.axis_index("exp") % 2


def chip_index():
    return lax.axis_index("exp") // 2


def copies(sems, sources, targets):
    made = [pltpu.make_async_copy(s, t, sems.at[i]) for i, (s, t) in enumerate(zip(sources, targets))]
    for copy in made:
        copy.start()
    return made


def decays(dt_rows, a_log):
    heads, length = dt_rows.shape
    step = jnp.maximum(dt_rows, 0.0) + jnp.log1p(jnp.exp(-jnp.abs(dt_rows)))
    same = lax.broadcasted_iota(jnp.int32, (heads, heads), 0) == lax.broadcasted_iota(jnp.int32, (heads, heads), 1)
    a_column = jnp.sum(jnp.where(same, jnp.broadcast_to(a_log, (heads, heads)), 0.0), axis=1, keepdims=True)
    rate = -step * jnp.exp(a_column)
    row = lax.broadcasted_iota(jnp.int32, (length, length), 0)
    col = lax.broadcasted_iota(jnp.int32, (length, length), 1)
    upper = (row <= col).astype(F32)
    cum = jnp.dot(rate, upper, precision=lax.Precision.HIGHEST, preferred_element_type=F32)
    return step, cum


def pair_lanes(values, pair):
    rows = values.shape[0]
    lane = lax.broadcasted_iota(jnp.int32, (rows, LANES), 1)
    left = jnp.broadcast_to(values[:, 2 * pair : 2 * pair + 1], (rows, LANES))
    right = jnp.broadcast_to(values[:, 2 * pair + 1 : 2 * pair + 2], (rows, LANES))
    return jnp.where(lane < HEAD_DIM, left, right)


def unpacked(block):
    pairs = block.shape[0] // STATE
    tail = block[pairs * STATE :].astype(F32)
    totals = [tail[pair : pair + 1] + tail[pairs + pair : pairs + pair + 1] for pair in range(pairs)]
    return jnp.stack(totals), block[: pairs * STATE].astype(F32).reshape(pairs, STATE, LANES)


def pack(ref, total, state):
    pairs = state.shape[0]
    ref[0 : pairs * STATE, :] = state.reshape(pairs * STATE, LANES).astype(BF16)
    row = lax.broadcasted_iota(jnp.int32, (TILE, LANES), 0)
    tail = jnp.zeros((TILE, LANES), F32)
    for pair in range(pairs):
        wide = jnp.broadcast_to(total[pair], (TILE, LANES))
        high = wide.astype(BF16).astype(F32)
        tail = jnp.where(row == pair, high, jnp.where(row == pairs + pair, wide - high, tail))
    ref[pairs * STATE :, :] = tail.astype(BF16)


def state_kernel(x_hbm, b_hbm, dt_hbm, a_hbm, keep_ref, send_ref, *scratch):
    x_ref, b_ref, dt_ref, a_ref, packed_ref, sems = scratch
    loads = copies(sems, (dt_hbm, a_hbm, x_hbm, b_hbm), (dt_ref, a_ref, x_ref, b_ref))
    loads[0].wait()
    loads[1].wait()
    step, cum = decays(dt_ref[...], a_ref[...])
    length = cum.shape[1]
    total = cum[:, length - 1 :]
    tail = (jnp.exp(total - cum) * step).T
    total = jnp.broadcast_to(total, cum.shape).T[0:1]
    loads[2].wait()
    loads[3].wait()
    pairs = x_ref.shape[1] // LANES
    half = pairs // 2
    groups = b_ref.shape[1] // STATE
    totals, states = [], []
    for group in range(groups):
        turned = b_ref[:, group * STATE : (group + 1) * STATE].T
        for pair in range(group * pairs // groups, (group + 1) * pairs // groups):
            x_pair = x_ref[:, pair * LANES : (pair + 1) * LANES].astype(F32)
            weighted = (pair_lanes(tail, pair) * x_pair).astype(BF16)
            state = jnp.dot(turned, weighted, preferred_element_type=F32)
            totals.append(pair_lanes(total, pair))
            states.append(state)
    for at in range(2):
        span = slice(at * half, (at + 1) * half)
        pack(packed_ref.at[at], totals[span], jnp.stack(states[span]))
    keep_ref[...] = packed_ref[core_index()]
    send_ref[...] = packed_ref[1 - core_index()]


def chip_state_kernel(keep_ref, got_ref, out_ref):
    first = core_index() == 0
    keep, got = unpacked(keep_ref[...]), unpacked(got_ref[...])
    early = [jnp.where(first, mine, other) for mine, other in zip(keep, got)]
    late = [jnp.where(first, other, mine) for mine, other in zip(keep, got)]
    pack(out_ref, early[0] + late[0], jnp.exp(late[0]) * early[1] + late[1])


def weights_kernel(after_ref, up_hbm, down_hbm, up_ref, down_ref, sems):
    for load in copies(sems, (up_hbm, down_hbm), (up_ref, down_ref)):
        load.wait()


def span_kernel(after_ref, *rest):
    ins, out_ref, block_ref = rest[:-2], rest[-2], rest[-1]
    for mask, part in enumerate(ins):
        block_ref[chip_index() ^ mask] = part[...]
    total, state = unpacked(block_ref[0])
    for chip in range(1, len(ins)):
        here, own = unpacked(block_ref[chip])
        total, state = total + here, jnp.exp(here) * state + own
    pack(out_ref, total, state)


def before_kernel(chips, after_ref, keep_ref, got_ref, *rest):
    ins, (mine_ref, send_ref, chip_ref, part_ref) = rest[:-4], rest[-4:]
    for mask in range(chips):
        chip_ref[chip_index() ^ mask] = ins[mask][...]
    parts = len(ins) - chips
    for mask in range(parts):
        part_ref[lax.axis_index("seq") ^ mask] = ins[chips + mask][...]
    carry = jnp.zeros(mine_ref.shape, F32)
    for ref, count, own in ((part_ref, parts, lax.axis_index("seq")), (chip_ref, chips, chip_index())):
        for index in range(count - 1):
            total, state = unpacked(ref[index])
            carry = jnp.where(index < own, jnp.exp(total) * carry + state, carry)
    first = core_index() == 0
    total, state = (jnp.where(first, k, g) for k, g in zip(unpacked(keep_ref[...]), unpacked(got_ref[...])))
    later = jnp.exp(total) * carry + state
    mine_ref[...] = jnp.where(first, carry, later).astype(BF16)
    send_ref[...] = jnp.where(first, later, carry).astype(BF16)


def inside_kernel(x_hbm, z_hbm, b_hbm, c_hbm, dt_hbm, a_hbm, d_hbm, local_ref, grown_ref, c_ref, *scratch):
    x_ref, z_ref, b_ref, dt_ref, a_ref, d_ref, sems = scratch
    loads = copies(
        sems,
        (dt_hbm, a_hbm, d_hbm, b_hbm, c_hbm, x_hbm, z_hbm),
        (dt_ref, a_ref, d_ref, b_ref, c_ref, x_ref, z_ref),
    )
    for load in loads:
        load.wait()
    step_rows, cum_rows = decays(dt_ref[...], a_ref[...])
    cum = cum_rows.T
    grown = jnp.exp(cum)
    length = cum.shape[0]
    pairs = x_ref.shape[1] // LANES
    groups = b_ref.shape[1] // STATE
    row = lax.broadcasted_iota(jnp.int32, (length, length), 0)
    col = lax.broadcasted_iota(jnp.int32, (length, length), 1)
    lane = lax.broadcasted_iota(jnp.int32, (length, LANES), 1)
    for group in range(groups):
        span = slice(group * STATE, (group + 1) * STATE)
        scores = lax.dot_general(c_ref[:, span], b_ref[:, span], NT, preferred_element_type=F32)
        scores = jnp.where(row >= col, scores, 0.0)
        for pair in range(group * pairs // groups, (group + 1) * pairs // groups):
            at = slice(pair * LANES, (pair + 1) * LANES)
            x_pair = x_ref[:, at]
            halves = []
            for head in (2 * pair, 2 * pair + 1):
                distance = cum[:, head : head + 1] - cum_rows[head : head + 1, :]
                decay = jnp.exp(jnp.where(row >= col, distance, FAR))
                mixing = (scores * (decay * step_rows[head : head + 1, :])).astype(BF16)
                halves.append(jnp.dot(mixing, x_pair, preferred_element_type=F32))
            inside = jnp.where(lane < HEAD_DIM, halves[0], halves[1])
            skip = pair_lanes(d_ref[...], pair) * x_pair.astype(F32)
            z = z_ref[:, at].astype(F32)
            gate = z / (1.0 + jnp.exp(-z))
            local_ref[:, at] = (inside + skip) * gate
            grown_ref[:, at] = pair_lanes(grown, pair) * gate


def prep_kernel(experts, width, resid_hbm, routes_hbm, gates_hbm, gain_hbm, norm_hbm, w_hbm, *rest):
    gate_ref, resid_ref, gain_ref, norm_ref, w_ref, routes_ref, gates_ref, sems = rest
    loads = copies(
        sems,
        (routes_hbm, gates_hbm, resid_hbm, gain_hbm, norm_hbm, w_hbm),
        (routes_ref, gates_ref, resid_ref, gain_ref, norm_ref, w_ref),
    )
    loads[0].wait()
    loads[1].wait()
    count, extent = gate_ref.shape
    start = width // LANES * LANES
    lane = lax.broadcasted_iota(jnp.int32, (extent, count), 0) + start - width
    expert = jnp.where(lane >= experts, lane - experts, lane)
    gate = jnp.zeros((extent, count), F32)
    for pick in range(routes_ref.shape[0]):
        gate = gate + jnp.where(routes_ref[pick] == expert, gates_ref[pick], 0.0)
    high = gate.astype(BF16).astype(F32)
    gate = jnp.where(lane < experts, high, jnp.where(lane < 2 * experts, gate - high, 0.0))
    gate_ref[...] = gate.T.astype(BF16)
    for load in loads[2:]:
        load.wait()


def half_product(half, local_ref, grown_ref, c_ref, norm_ref, w_ref, state_ref, normed_ref, count):
    pairs = state_ref.shape[0]
    width = pairs * LANES
    base = pl.multiple_of(half * width, width)
    groups = c_ref.shape[1] // STATE // 2
    per_group = pairs // groups
    for group in range(groups):
        c_group = c_ref[:, pl.ds(pl.multiple_of((half * groups + group) * STATE, STATE), STATE)]
        gated, squares = [], 0.0
        for pair in range(group * per_group, (group + 1) * per_group):
            span = pl.ds(pl.multiple_of(base + pair * LANES, LANES), LANES)
            carried = jnp.dot(c_group, state_ref[pair], preferred_element_type=F32)
            value = local_ref[:, span] + grown_ref[:, span] * carried
            gated.append(value)
            squares = squares + value * value
        mean = jnp.sum(squares, axis=1, keepdims=True) / (per_group * LANES)
        inverse = lax.rsqrt(mean + 1e-05)
        for offset, value in enumerate(gated):
            pair = group * per_group + offset
            gain = norm_ref[:, pl.ds(pl.multiple_of(base + pair * LANES, LANES), LANES)]
            normed_ref[:, pair * LANES : (pair + 1) * LANES] = (value * inverse * gain).astype(BF16)
    rows = normed_ref.shape[0] // count
    blocks = []
    for shift in range(count):
        owner = lax.axis_index("head") ^ (head_offset(shift - 1, count) if shift else 0)
        blocks.append(normed_ref[pl.ds(pl.multiple_of(owner * rows, rows), rows), :])
    weight = w_ref[:, pl.ds(base, width)]
    return lax.dot_general(jnp.concatenate(blocks, axis=0), weight, NT, preferred_element_type=F32)


def first_half_kernel(count, local_ref, grown_ref, c_ref, norm_ref, w_ref, mine_ref, out_ref, normed_ref):
    out_ref[...] = half_product(
        core_index(), local_ref, grown_ref, c_ref, norm_ref, w_ref, mine_ref, normed_ref, count
    )


def mixed_kernel(after_up, after_down, local_ref, grown_ref, c_ref, norm_ref, w_ref, got_ref, first_ref, *rest):
    outs, normed_ref = rest[:-1], rest[-1]
    product = first_ref[...] + half_product(
        1 - core_index(), local_ref, grown_ref, c_ref, norm_ref, w_ref, got_ref, normed_ref, len(outs)
    )
    rows = outs[0].shape[0]
    for shift, out in enumerate(outs):
        out[...] = product[shift * rows : (shift + 1) * rows].astype(BF16)


def relay_kernel(own_ref, got_ref, out_ref):
    got = jnp.where(core_index() == 0, got_ref[...].astype(F32), 0.0)
    out_ref[...] = (own_ref[...].astype(F32) + got).astype(BF16)


def rows_kernel(after_ref, resid_ref, gate_ref, gain_ref, *rest):
    parts, hidden_ref, rows_ref = rest[:-2], rest[-2], rest[-1]
    mixed = parts[0][...].astype(F32)
    for at, part in enumerate(parts[1:]):
        value = part[...].astype(F32)
        if at == 0 and len(parts) == 4:
            value = jnp.where(core_index() == 1, value, 0.0)
        mixed = mixed + value
    hidden = (resid_ref[0].astype(F32) + mixed).astype(BF16)
    hidden_ref[...] = hidden
    value = hidden.astype(F32)
    scale = lax.rsqrt(jnp.mean(value * value, axis=1, keepdims=True) + 1e-05)
    width = value.shape[1]
    rows_ref[:, width // LANES * LANES :] = gate_ref[...]
    rows_ref[:, :width] = (value * scale * gain_ref[...]).astype(BF16)


def expert_kernel(experts, count, up_ref, down_ref, other_up_ref, other_down_ref, *rest):
    ins, outs = rest[:count], rest[count:]
    width = up_ref.shape[2]
    start = width // LANES * LANES
    rows = jnp.concatenate([ref[:, :width] for ref in ins], axis=0)
    tail = jnp.concatenate([ref[:, start:] for ref in ins], axis=0).astype(F32)
    lane = lax.broadcasted_iota(jnp.int32, tail.shape, 1) + start - width
    own = lax.axis_index("head") * lax.axis_size("exp") + lax.axis_index("exp")
    other = own + 1 - 2 * core_index()
    total = 0.0
    for expert, up_of, down_of in ((own, up_ref, down_ref), (other, other_up_ref, other_down_ref)):
        up = lax.dot_general(rows, up_of[0], NT, preferred_element_type=F32)
        up = jnp.maximum(up, 0.0)
        activated = (up * up).astype(BF16)
        chosen = (lane == expert) | (lane == expert + experts)
        gate = jnp.sum(jnp.where(chosen, tail, 0.0), axis=1, keepdims=True)
        total = total + jnp.dot(activated, down_of[0], preferred_element_type=F32) * gate
    at = 0
    for out in outs:
        out[...] = total[at : at + out.shape[0]].astype(BF16)
        at += out.shape[0]


def sum_kernel(*refs):
    total = refs[0][...].astype(F32)
    for ref in refs[1:-1]:
        total = total + ref[...].astype(F32)
    refs[-1][...] = total.astype(BF16)


def last_kernel(hidden_ref, *rest):
    parts, out_ref = rest[:-1], rest[-1]
    total = parts[0][...].astype(F32)
    for part in parts[1:]:
        total = total + part[...].astype(F32)
    out_ref[0] = (hidden_ref[...].astype(F32) + total).astype(BF16)


def swap(value, axis, mask):
    size = lax.axis_size(axis)
    return lax.ppermute(value, axis, [(i, i ^ mask) for i in range(size)])


def swap_slot(value, slot):
    heads, size = lax.axis_size("head"), lax.axis_size("exp")
    order = targets(heads)
    pairs = []
    for i in range(heads * size):
        head, exp = i // size, i % size
        pairs.append((i, (head ^ order[exp % 2][slot]) * size + exp))
    return lax.ppermute(value, ("head", "exp"), pairs)


def per_device(
    x_in, z_in, b_in, c_in, dt_in, a_log, d_skip, norm_w, w_out, resid, routes, gates, moe_gain, w_up, w_down
):
    length, heads = dt_in.shape
    channels = x_in.shape[1]
    model = w_out.shape[1]
    hidden_units = w_up.shape[2]
    seq_size, head_size, exp_size = lax.axis_size("seq"), lax.axis_size("head"), lax.axis_size("exp")
    chips = exp_size // 2
    rows = resid.shape[1]
    experts = head_size * exp_size
    pairs = channels // LANES
    half = pairs // 2
    dt_rows, a_row, d_row = dt_in.T, a_log[None], d_skip[None]
    dma = pltpu.SemaphoreType.DMA
    packed = struct((half * STATE + TILE, LANES), BF16)

    keep, send = call(
        state_kernel,
        "state",
        [packed, packed],
        [(HBM, x_in), (HBM, b_in), (HBM, dt_rows), (HBM, a_row)],
        [pltpu.VMEM(x_in.shape, BF16), pltpu.VMEM(b_in.shape, BF16), pltpu.VMEM(dt_rows.shape, F32),
         pltpu.VMEM(a_row.shape, F32), pltpu.VMEM((2, half * STATE + TILE, LANES), BF16), dma((4,))],
        megabytes=16,
    )
    local, grown, c_held = call(
        inside_kernel,
        "inside",
        [struct((length, channels), F32), struct((length, channels), F32), struct(c_in.shape, BF16)],
        [(HBM, value) for value in (x_in, z_in, b_in, c_in, dt_rows, a_row, d_row)],
        [pltpu.VMEM(x_in.shape, BF16), pltpu.VMEM(z_in.shape, BF16), pltpu.VMEM(b_in.shape, BF16),
         pltpu.VMEM(dt_rows.shape, F32), pltpu.VMEM(a_row.shape, F32), pltpu.VMEM(d_row.shape, F32), dma((7,))],
        megabytes=16,
    )
    wide = -(-(model + 2 * experts) // LANES) * LANES
    turned = [jnp.transpose(value, (2, 0, 1)) for value in (routes, gates)]
    gate_lanes, resid_held, gain_held, norm_held, w_held = call(
        functools.partial(prep_kernel, experts, model),
        "prep",
        [struct((rows, wide - model // LANES * LANES), BF16), struct(resid.shape, BF16), struct((1, model), F32),
         struct((1, channels), F32), struct((model, channels), BF16)],
        [(HBM, value) for value in (resid, *turned, moe_gain[None], norm_w[None], w_out.T)],
        [pltpu.VMEM(turned[0].shape, jnp.int32), pltpu.VMEM(turned[1].shape, F32), dma((6,))],
        megabytes=16,
    )
    up_turned = jnp.swapaxes(w_up, 1, 2)
    got = swap(send, "exp", 1)
    chip = call(chip_state_kernel, "chip_state", packed, [(VMEM, keep), (VMEM, got)])
    chip, up_after, down_after = lax.optimization_barrier((chip, up_turned, w_down))
    other_up, other_down = swap(up_after, "exp", 1), swap(down_after, "exp", 1)
    along_y = [chip] + [swap(chip, "exp", 2 * d) for d in range(1, chips)]
    span = call(
        span_kernel,
        "span",
        packed,
        [(ANY, c_held)] + [(VMEM, value) for value in along_y],
        [pltpu.VMEM((chips, *packed.shape), BF16)],
    )
    along_x = [span] + [swap(span, "seq", d) for d in range(1, seq_size)]
    before, before_send = call(
        functools.partial(before_kernel, chips),
        "before",
        [struct((half, STATE, LANES), BF16)] * 2,
        [(ANY, gate_lanes)] + [(VMEM, value) for value in (keep, got, *along_y, *along_x)],
        [pltpu.VMEM((chips, *packed.shape), BF16), pltpu.VMEM((seq_size, *packed.shape), BF16)],
        megabytes=24,
    )
    before_got = swap(before_send, "exp", 1)
    shared = [(VMEM, value) for value in (local, grown, c_held, norm_held, w_held)]
    normed_half = pltpu.VMEM((length, channels // 2), BF16)
    first = call(
        functools.partial(first_half_kernel, head_size),
        "first_half",
        struct((length, model), F32),
        shared + [(VMEM, before)],
        [normed_half],
    )
    mixed = call(
        mixed_kernel,
        "mixed",
        [struct((rows, model), BF16)] * head_size,
        [(ANY, other_up), (ANY, other_down)] + shared + [(VMEM, before_got), (VMEM, first)],
        [normed_half],
    )
    up_held, down_held = call(
        weights_kernel,
        "weights",
        [struct(up_turned.shape, BF16), struct(w_down.shape, BF16)],
        [(ANY, mixed[0]), (HBM, up_turned), (HBM, w_down)],
        [dma((2,))],
    )
    slots = list(range(head_size - 1))
    parts, last = [swap_slot(mixed[k + 1], k) for k in slots[:-1]], mixed[-1]
    if head_size == 4:
        last = call(relay_kernel, "relay", struct((rows, model), BF16), [(VMEM, last), (VMEM, parts[0])])
    parts = [mixed[0]] + parts + [swap_slot(last, slots[-1])]
    hidden, own_rows = call(
        rows_kernel,
        "rows",
        [struct((rows, model), BF16), struct((rows, wide), BF16)],
        [(ANY, up_held)] + [(VMEM, value) for value in (resid_held, gate_lanes, gain_held, *parts)],
    )

    def through_experts(members):
        return call(
            functools.partial(expert_kernel, experts, len(members)),
            "experts",
            [struct((rows, model), BF16)] * len(members),
            [(VMEM, value) for value in (up_held, down_held, other_up, other_down, *members)],
            megabytes=16,
        )

    both = ("head", "exp")
    group = [z * exp_size + 2 * d for z in (1, 0) for d in reversed(range(chips))][:-1]

    def spread(block):
        return [block] + [swap(block, both, mask) for mask in reversed(group)]

    sets = [spread(swap(own_rows, "head", high)) for high in range(2, head_size, 2)]
    near = through_experts(spread(own_rows))
    near, sets = lax.optimization_barrier((near, sets))
    far = [through_experts(members) for members in sets]
    arrived, near = [], list(near)
    for high, pieces in zip(range(2, head_size, 2), far):
        got = [swap(piece, both, mask) for piece, mask in zip(pieces[:0:-1], group)]
        total = call(sum_kernel, "sum", struct((rows, model), BF16), [(VMEM, v) for v in (pieces[0], *got)])
        if high == 2:
            total, near[1:-1] = lax.optimization_barrier((total, near[1:-1]))
        arrived.append(swap(total, "head", high))
    arrived += [swap(piece, both, mask) for piece, mask in zip(near[:0:-1], group)]
    return call(
        last_kernel,
        "last",
        struct(resid.shape, BF16),
        [(VMEM, value) for value in (hidden, near[0], *arrived)],
        pinned=False,
    )


def solution(mesh):
    placed = (
        P(("seq", "exp"), "head"),
        P(("seq", "exp"), "head"),
        P(("seq", "exp"), "head"),
        P(("seq", "exp"), "head"),
        P(("seq", "exp"), "head"),
        P("head"),
        P("head"),
        P("head"),
        P("head", None),
        P(("seq", "exp"), "head", None),
        P(("seq", "exp"), "head", None),
        P(("seq", "exp"), "head", None),
        P(),
        P(("head", "exp"), None, None),
        P(("head", "exp"), None, None),
    )
    return jax.shard_map(
        per_device,
        mesh=mesh,
        in_specs=placed,
        out_specs=P(("seq", "exp"), "head", None),
        check_vma=False,
    )
```

```python
import functools

import jax
import jax.numpy as jnp
from jax import lax
from jax.experimental import pallas as pl
from jax.experimental.pallas import tpu as pltpu
from jax.sharding import PartitionSpec as P

HEAD_DIM = 64
STATE = 128
LANES = 128
TILE = 16
FAR = -1e30
F32 = jnp.float32
BF16 = jnp.bfloat16
HBM = pl.BlockSpec(memory_space=pltpu.HBM)
VMEM = pl.BlockSpec(memory_space=pltpu.VMEM)
ANY = pl.BlockSpec(memory_space=pl.ANY)
NT = (((1,), (1,)), ((), ()))


def struct(shape, dtype):
    return jax.ShapeDtypeStruct(shape, dtype)


def call(kernel, name, outs, ins, scratch=(), megabytes=12, pinned=True):
    args = [pltpu.with_memory_space_constraint(arg, pltpu.HBM) if spec is HBM else arg for spec, arg in ins]
    return pl.pallas_call(
        kernel,
        out_shape=jax.tree.map(lambda out: pltpu.VMEM(out.shape, out.dtype), outs) if pinned else outs,
        in_specs=[spec for spec, _ in ins],
        out_specs=jax.tree.map(lambda _: VMEM, outs),
        scratch_shapes=list(scratch),
        name=name,
        compiler_params=pltpu.CompilerParams(vmem_limit_bytes=megabytes << 20),
    )(*args)


def offsets(count):
    down = list(range(count - 1, 0, -1))
    return [[2, 3, 1], [3, 1, 2]] if count == 4 else [down, down]


def head_offset(slot, count):
    first, second = (order[slot] for order in offsets(count))
    return jnp.where(core_index() == 0, first, second)


def core_index():
    return lax.axis_index("exp") % 2


def chip_index():
    return lax.axis_index("exp") // 2


def copies(sems, sources, targets):
    made = [pltpu.make_async_copy(s, t, sems.at[i]) for i, (s, t) in enumerate(zip(sources, targets))]
    for copy in made:
        copy.start()
    return made


def decays(dt_rows, a_log):
    heads, length = dt_rows.shape
    step = jnp.maximum(dt_rows, 0.0) + jnp.log1p(jnp.exp(-jnp.abs(dt_rows)))
    same = lax.broadcasted_iota(jnp.int32, (heads, heads), 0) == lax.broadcasted_iota(jnp.int32, (heads, heads), 1)
    a_column = jnp.sum(jnp.where(same, jnp.broadcast_to(a_log, (heads, heads)), 0.0), axis=1, keepdims=True)
    rate = -step * jnp.exp(a_column)
    row = lax.broadcasted_iota(jnp.int32, (length, length), 0)
    col = lax.broadcasted_iota(jnp.int32, (length, length), 1)
    upper = (row <= col).astype(F32)
    cum = jnp.dot(rate, upper, precision=lax.Precision.HIGHEST, preferred_element_type=F32)
    return step, cum


def pair_lanes(values, pair):
    rows = values.shape[0]
    lane = lax.broadcasted_iota(jnp.int32, (rows, LANES), 1)
    left = jnp.broadcast_to(values[:, 2 * pair : 2 * pair + 1], (rows, LANES))
    right = jnp.broadcast_to(values[:, 2 * pair + 1 : 2 * pair + 2], (rows, LANES))
    return jnp.where(lane < HEAD_DIM, left, right)


def unpacked(block):
    pairs = block.shape[0] // STATE
    tail = block[pairs * STATE :].astype(F32)
    totals = [tail[pair : pair + 1] + tail[pairs + pair : pairs + pair + 1] for pair in range(pairs)]
    return jnp.stack(totals), block[: pairs * STATE].astype(F32).reshape(pairs, STATE, LANES)


def pack(ref, total, state):
    pairs = state.shape[0]
    ref[0 : pairs * STATE, :] = state.reshape(pairs * STATE, LANES).astype(BF16)
    row = lax.broadcasted_iota(jnp.int32, (TILE, LANES), 0)
    tail = jnp.zeros((TILE, LANES), F32)
    for pair in range(pairs):
        wide = jnp.broadcast_to(total[pair], (TILE, LANES))
        high = wide.astype(BF16).astype(F32)
        tail = jnp.where(row == pair, high, jnp.where(row == pairs + pair, wide - high, tail))
    ref[pairs * STATE :, :] = tail.astype(BF16)


def state_kernel(x_hbm, b_hbm, dt_hbm, a_hbm, keep_ref, send_ref, *scratch):
    x_ref, b_ref, dt_ref, a_ref, packed_ref, sems = scratch
    loads = copies(sems, (dt_hbm, a_hbm, x_hbm, b_hbm), (dt_ref, a_ref, x_ref, b_ref))
    loads[0].wait()
    loads[1].wait()
    step, cum = decays(dt_ref[...], a_ref[...])
    length = cum.shape[1]
    total = cum[:, length - 1 :]
    tail = (jnp.exp(total - cum) * step).T
    total = jnp.broadcast_to(total, cum.shape).T[0:1]
    loads[2].wait()
    loads[3].wait()
    pairs = x_ref.shape[1] // LANES
    half = pairs // 2
    groups = b_ref.shape[1] // STATE
    totals, states = [], []
    for group in range(groups):
        turned = b_ref[:, group * STATE : (group + 1) * STATE].T
        for pair in range(group * pairs // groups, (group + 1) * pairs // groups):
            x_pair = x_ref[:, pair * LANES : (pair + 1) * LANES].astype(F32)
            weighted = (pair_lanes(tail, pair) * x_pair).astype(BF16)
            state = jnp.dot(turned, weighted, preferred_element_type=F32)
            totals.append(pair_lanes(total, pair))
            states.append(state)
    for at in range(2):
        span = slice(at * half, (at + 1) * half)
        pack(packed_ref.at[at], totals[span], jnp.stack(states[span]))
    keep_ref[...] = packed_ref[core_index()]
    send_ref[...] = packed_ref[1 - core_index()]


def chip_state_kernel(keep_ref, got_ref, out_ref):
    first = core_index() == 0
    keep, got = unpacked(keep_ref[...]), unpacked(got_ref[...])
    early = [jnp.where(first, mine, other) for mine, other in zip(keep, got)]
    late = [jnp.where(first, other, mine) for mine, other in zip(keep, got)]
    pack(out_ref, early[0] + late[0], jnp.exp(late[0]) * early[1] + late[1])


def weights_kernel(after_ref, up_hbm, down_hbm, up_ref, down_ref, sems):
    for load in copies(sems, (up_hbm, down_hbm), (up_ref, down_ref)):
        load.wait()


def span_kernel(after_ref, *rest):
    ins, out_ref, block_ref = rest[:-2], rest[-2], rest[-1]
    for mask, part in enumerate(ins):
        block_ref[chip_index() ^ mask] = part[...]
    total, state = unpacked(block_ref[0])
    for chip in range(1, len(ins)):
        here, own = unpacked(block_ref[chip])
        total, state = total + here, jnp.exp(here) * state + own
    pack(out_ref, total, state)


def before_kernel(chips, after_ref, keep_ref, got_ref, *rest):
    ins, (mine_ref, send_ref, chip_ref, part_ref) = rest[:-4], rest[-4:]
    for mask in range(chips):
        chip_ref[chip_index() ^ mask] = ins[mask][...]
    parts = len(ins) - chips
    for mask in range(parts):
        part_ref[lax.axis_index("seq") ^ mask] = ins[chips + mask][...]
    carry = jnp.zeros(mine_ref.shape, F32)
    for ref, count, own in ((part_ref, parts, lax.axis_index("seq")), (chip_ref, chips, chip_index())):
        for index in range(count - 1):
            total, state = unpacked(ref[index])
            carry = jnp.where(index < own, jnp.exp(total) * carry + state, carry)
    first = core_index() == 0
    total, state = (jnp.where(first, k, g) for k, g in zip(unpacked(keep_ref[...]), unpacked(got_ref[...])))
    later = jnp.exp(total) * carry + state
    mine_ref[...] = jnp.where(first, carry, later).astype(BF16)
    send_ref[...] = jnp.where(first, later, carry).astype(BF16)


def inside_kernel(x_hbm, z_hbm, b_hbm, c_hbm, dt_hbm, a_hbm, d_hbm, local_ref, grown_ref, c_ref, *scratch):
    x_ref, z_ref, b_ref, dt_ref, a_ref, d_ref, sems = scratch
    loads = copies(
        sems,
        (dt_hbm, a_hbm, d_hbm, b_hbm, c_hbm, x_hbm, z_hbm),
        (dt_ref, a_ref, d_ref, b_ref, c_ref, x_ref, z_ref),
    )
    for load in loads:
        load.wait()
    step_rows, cum_rows = decays(dt_ref[...], a_ref[...])
    cum = cum_rows.T
    grown = jnp.exp(cum)
    length = cum.shape[0]
    pairs = x_ref.shape[1] // LANES
    groups = b_ref.shape[1] // STATE
    row = lax.broadcasted_iota(jnp.int32, (length, length), 0)
    col = lax.broadcasted_iota(jnp.int32, (length, length), 1)
    lane = lax.broadcasted_iota(jnp.int32, (length, LANES), 1)
    for group in range(groups):
        span = slice(group * STATE, (group + 1) * STATE)
        scores = lax.dot_general(c_ref[:, span], b_ref[:, span], NT, preferred_element_type=F32)
        scores = jnp.where(row >= col, scores, 0.0)
        for pair in range(group * pairs // groups, (group + 1) * pairs // groups):
            at = slice(pair * LANES, (pair + 1) * LANES)
            x_pair = x_ref[:, at]
            halves = []
            for head in (2 * pair, 2 * pair + 1):
                distance = cum[:, head : head + 1] - cum_rows[head : head + 1, :]
                decay = jnp.exp(jnp.where(row >= col, distance, FAR))
                mixing = (scores * (decay * step_rows[head : head + 1, :])).astype(BF16)
                halves.append(jnp.dot(mixing, x_pair, preferred_element_type=F32))
            inside = jnp.where(lane < HEAD_DIM, halves[0], halves[1])
            skip = pair_lanes(d_ref[...], pair) * x_pair.astype(F32)
            z = z_ref[:, at].astype(F32)
            gate = z / (1.0 + jnp.exp(-z))
            local_ref[:, at] = (inside + skip) * gate
            grown_ref[:, at] = pair_lanes(grown, pair) * gate


def prep_kernel(experts, width, resid_hbm, routes_hbm, gates_hbm, gain_hbm, norm_hbm, w_hbm, *rest):
    gate_ref, resid_ref, gain_ref, norm_ref, w_ref, routes_ref, gates_ref, sems = rest
    loads = copies(
        sems,
        (routes_hbm, gates_hbm, resid_hbm, gain_hbm, norm_hbm, w_hbm),
        (routes_ref, gates_ref, resid_ref, gain_ref, norm_ref, w_ref),
    )
    loads[0].wait()
    loads[1].wait()
    count, extent = gate_ref.shape
    start = width // LANES * LANES
    lane = lax.broadcasted_iota(jnp.int32, (extent, count), 0) + start - width
    expert = jnp.where(lane >= experts, lane - experts, lane)
    gate = jnp.zeros((extent, count), F32)
    for pick in range(routes_ref.shape[0]):
        gate = gate + jnp.where(routes_ref[pick] == expert, gates_ref[pick], 0.0)
    high = gate.astype(BF16).astype(F32)
    gate = jnp.where(lane < experts, high, jnp.where(lane < 2 * experts, gate - high, 0.0))
    gate_ref[...] = gate.T.astype(BF16)
    for load in loads[2:]:
        load.wait()


def half_product(half, local_ref, grown_ref, c_ref, norm_ref, w_ref, state_ref, normed_ref, count):
    pairs = state_ref.shape[0]
    width = pairs * LANES
    base = pl.multiple_of(half * width, width)
    groups = c_ref.shape[1] // STATE // 2
    per_group = pairs // groups
    for group in range(groups):
        c_group = c_ref[:, pl.ds(pl.multiple_of((half * groups + group) * STATE, STATE), STATE)]
        gated, squares = [], 0.0
        for pair in range(group * per_group, (group + 1) * per_group):
            span = pl.ds(pl.multiple_of(base + pair * LANES, LANES), LANES)
            carried = jnp.dot(c_group, state_ref[pair], preferred_element_type=F32)
            value = local_ref[:, span] + grown_ref[:, span] * carried
            gated.append(value)
            squares = squares + value * value
        mean = jnp.sum(squares, axis=1, keepdims=True) / (per_group * LANES)
        inverse = lax.rsqrt(mean + 1e-05)
        for offset, value in enumerate(gated):
            pair = group * per_group + offset
            gain = norm_ref[:, pl.ds(pl.multiple_of(base + pair * LANES, LANES), LANES)]
            normed_ref[:, pair * LANES : (pair + 1) * LANES] = (value * inverse * gain).astype(BF16)
    rows = normed_ref.shape[0] // count
    blocks = []
    for shift in range(count):
        owner = lax.axis_index("head") ^ (head_offset(shift - 1, count) if shift else 0)
        blocks.append(normed_ref[pl.ds(pl.multiple_of(owner * rows, rows), rows), :])
    weight = w_ref[:, pl.ds(base, width)]
    return lax.dot_general(jnp.concatenate(blocks, axis=0), weight, NT, preferred_element_type=F32)


def first_half_kernel(count, local_ref, grown_ref, c_ref, norm_ref, w_ref, mine_ref, out_ref, normed_ref):
    out_ref[...] = half_product(
        core_index(), local_ref, grown_ref, c_ref, norm_ref, w_ref, mine_ref, normed_ref, count
    )


def mixed_kernel(after_up, after_down, local_ref, grown_ref, c_ref, norm_ref, w_ref, got_ref, first_ref, *rest):
    outs, normed_ref = rest[:-1], rest[-1]
    product = first_ref[...] + half_product(
        1 - core_index(), local_ref, grown_ref, c_ref, norm_ref, w_ref, got_ref, normed_ref, len(outs)
    )
    rows = outs[0].shape[0]
    for shift, out in enumerate(outs):
        out[...] = product[shift * rows : (shift + 1) * rows].astype(BF16)


def rows_kernel(relay, after_ref, resid_ref, gate_ref, gain_ref, *rest):
    parts, hidden_ref, rows_ref = rest[:-2], rest[-2], rest[-1]
    mixed = parts[0][...].astype(F32)
    for at, part in enumerate(parts[1:]):
        value = part[...].astype(F32)
        if at == 0 and relay:
            value = jnp.where(core_index() == 0, value, 0.0)
        mixed = mixed + value
    hidden = (resid_ref[0].astype(F32) + mixed).astype(BF16)
    hidden_ref[...] = hidden
    value = hidden.astype(F32)
    scale = lax.rsqrt(jnp.mean(value * value, axis=1, keepdims=True) + 1e-05)
    width = value.shape[1]
    rows_ref[:, width // LANES * LANES :] = gate_ref[...]
    rows_ref[:, :width] = (value * scale * gain_ref[...]).astype(BF16)


def expert_kernel(experts, count, up_ref, down_ref, other_up_ref, other_down_ref, *rest):
    ins, outs = rest[:count], rest[count:]
    width = up_ref.shape[2]
    start = width // LANES * LANES
    rows = jnp.concatenate([ref[:, :width] for ref in ins], axis=0)
    tail = jnp.concatenate([ref[:, start:] for ref in ins], axis=0).astype(F32)
    lane = lax.broadcasted_iota(jnp.int32, tail.shape, 1) + start - width
    own = lax.axis_index("head") * lax.axis_size("exp") + lax.axis_index("exp")
    other = own + 1 - 2 * core_index()
    total = 0.0
    for expert, up_of, down_of in ((own, up_ref, down_ref), (other, other_up_ref, other_down_ref)):
        up = lax.dot_general(rows, up_of[0], NT, preferred_element_type=F32)
        up = jnp.maximum(up, 0.0)
        activated = (up * up).astype(BF16)
        chosen = (lane == expert) | (lane == expert + experts)
        gate = jnp.sum(jnp.where(chosen, tail, 0.0), axis=1, keepdims=True)
        total = total + jnp.dot(activated, down_of[0], preferred_element_type=F32) * gate
    at = 0
    for out in outs:
        out[...] = total[at : at + out.shape[0]].astype(BF16)
        at += out.shape[0]


def sum_kernel(*refs):
    total = refs[0][...].astype(F32)
    for ref in refs[1:-1]:
        total = total + ref[...].astype(F32)
    refs[-1][...] = total.astype(BF16)


def last_kernel(hidden_ref, *rest):
    parts, out_ref = rest[:-1], rest[-1]
    total = parts[0][...].astype(F32)
    for part in parts[1:]:
        total = total + part[...].astype(F32)
    out_ref[0] = (hidden_ref[...].astype(F32) + total).astype(BF16)


def swap(value, axis, mask):
    size = lax.axis_size(axis)
    return lax.ppermute(value, axis, [(i, i ^ mask) for i in range(size)])


def swap_by_core(value, masks):
    heads, size = lax.axis_size("head"), lax.axis_size("exp")
    pairs = []
    for i in range(heads * size):
        mask = masks[i % size % 2]
        if mask:
            pairs.append((i, i ^ (mask * size)))
    return lax.ppermute(value, ("head", "exp"), pairs)


def projection_parts(pieces):
    orders = list(zip(*offsets(len(pieces))))
    if len(pieces) != 4:
        return [pieces[0]] + [swap_by_core(piece, masks) for piece, masks in zip(pieces[1:], orders)]
    first = swap_by_core(pieces[1], (2, 1))
    second = swap_by_core(pieces[2], orders[1])
    third = swap_by_core(pieces[3], (1, 0))
    relayed = call(sum_kernel, "relay", struct(pieces[3].shape, BF16), [(VMEM, pieces[3]), (VMEM, first)])
    return [pieces[0], first, second, third, swap_by_core(relayed, (0, 2))]


def per_device(
    x_in, z_in, b_in, c_in, dt_in, a_log, d_skip, norm_w, w_out, resid, routes, gates, moe_gain, w_up, w_down
):
    length, heads = dt_in.shape
    channels = x_in.shape[1]
    model = w_out.shape[1]
    hidden_units = w_up.shape[2]
    seq_size, head_size, exp_size = lax.axis_size("seq"), lax.axis_size("head"), lax.axis_size("exp")
    chips = exp_size // 2
    rows = resid.shape[1]
    experts = head_size * exp_size
    pairs = channels // LANES
    half = pairs // 2
    dt_rows, a_row, d_row = dt_in.T, a_log[None], d_skip[None]
    dma = pltpu.SemaphoreType.DMA
    packed = struct((half * STATE + TILE, LANES), BF16)

    keep, send = call(
        state_kernel,
        "state",
        [packed, packed],
        [(HBM, x_in), (HBM, b_in), (HBM, dt_rows), (HBM, a_row)],
        [pltpu.VMEM(x_in.shape, BF16), pltpu.VMEM(b_in.shape, BF16), pltpu.VMEM(dt_rows.shape, F32),
         pltpu.VMEM(a_row.shape, F32), pltpu.VMEM((2, half * STATE + TILE, LANES), BF16), dma((4,))],
        megabytes=16,
    )
    local, grown, c_held = call(
        inside_kernel,
        "inside",
        [struct((length, channels), F32), struct((length, channels), F32), struct(c_in.shape, BF16)],
        [(HBM, value) for value in (x_in, z_in, b_in, c_in, dt_rows, a_row, d_row)],
        [pltpu.VMEM(x_in.shape, BF16), pltpu.VMEM(z_in.shape, BF16), pltpu.VMEM(b_in.shape, BF16),
         pltpu.VMEM(dt_rows.shape, F32), pltpu.VMEM(a_row.shape, F32), pltpu.VMEM(d_row.shape, F32), dma((7,))],
        megabytes=16,
    )
    wide = -(-(model + 2 * experts) // LANES) * LANES
    turned = [jnp.transpose(value, (2, 0, 1)) for value in (routes, gates)]
    gate_lanes, resid_held, gain_held, norm_held, w_held = call(
        functools.partial(prep_kernel, experts, model),
        "prep",
        [struct((rows, wide - model // LANES * LANES), BF16), struct(resid.shape, BF16), struct((1, model), F32),
         struct((1, channels), F32), struct((model, channels), BF16)],
        [(HBM, value) for value in (resid, *turned, moe_gain[None], norm_w[None], w_out.T)],
        [pltpu.VMEM(turned[0].shape, jnp.int32), pltpu.VMEM(turned[1].shape, F32), dma((6,))],
        megabytes=16,
    )
    up_turned = jnp.swapaxes(w_up, 1, 2)
    got = swap(send, "exp", 1)
    chip = call(chip_state_kernel, "chip_state", packed, [(VMEM, keep), (VMEM, got)])
    chip, up_after, down_after = lax.optimization_barrier((chip, up_turned, w_down))
    other_up, other_down = swap(up_after, "exp", 1), swap(down_after, "exp", 1)
    along_y = [chip] + [swap(chip, "exp", 2 * d) for d in range(1, chips)]
    span = call(
        span_kernel,
        "span",
        packed,
        [(ANY, c_held)] + [(VMEM, value) for value in along_y],
        [pltpu.VMEM((chips, *packed.shape), BF16)],
    )
    along_x = [span] + [swap(span, "seq", d) for d in range(1, seq_size)]
    before, before_send = call(
        functools.partial(before_kernel, chips),
        "before",
        [struct((half, STATE, LANES), BF16)] * 2,
        [(ANY, gate_lanes)] + [(VMEM, value) for value in (keep, got, *along_y, *along_x)],
        [pltpu.VMEM((chips, *packed.shape), BF16), pltpu.VMEM((seq_size, *packed.shape), BF16)],
        megabytes=24,
    )
    before_got = swap(before_send, "exp", 1)
    shared = [(VMEM, value) for value in (local, grown, c_held, norm_held, w_held)]
    normed_half = pltpu.VMEM((length, channels // 2), BF16)
    first = call(
        functools.partial(first_half_kernel, head_size),
        "first_half",
        struct((length, model), F32),
        shared + [(VMEM, before)],
        [normed_half],
    )
    mixed = call(
        mixed_kernel,
        "mixed",
        [struct((rows, model), BF16)] * head_size,
        [(ANY, other_up), (ANY, other_down)] + shared + [(VMEM, before_got), (VMEM, first)],
        [normed_half],
    )
    up_held, down_held = call(
        weights_kernel,
        "weights",
        [struct(up_turned.shape, BF16), struct(w_down.shape, BF16)],
        [(ANY, mixed[0]), (HBM, up_turned), (HBM, w_down)],
        [dma((2,))],
    )
    parts = projection_parts(mixed)
    hidden, own_rows = call(
        functools.partial(rows_kernel, head_size == 4),
        "rows",
        [struct((rows, model), BF16), struct((rows, wide), BF16)],
        [(ANY, up_held)] + [(VMEM, value) for value in (resid_held, gate_lanes, gain_held, *parts)],
    )

    def through_experts(members):
        return call(
            functools.partial(expert_kernel, experts, len(members)),
            "experts",
            [struct((rows, model), BF16)] * len(members),
            [(VMEM, value) for value in (up_held, down_held, other_up, other_down, *members)],
            megabytes=16,
        )

    both = ("head", "exp")
    group = [z * exp_size + 2 * d for z in (1, 0) for d in reversed(range(chips))][:-1]

    def spread(block):
        return [block] + [swap(block, both, mask) for mask in reversed(group)]

    sets = [spread(swap(own_rows, "head", high)) for high in range(2, head_size, 2)]
    near = through_experts(spread(own_rows))
    near, sets = lax.optimization_barrier((near, sets))
    far = [through_experts(members) for members in sets]
    arrived, near = [], list(near)
    for high, pieces in zip(range(2, head_size, 2), far):
        got = [swap(piece, both, mask) for piece, mask in zip(pieces[:0:-1], group)]
        total = call(sum_kernel, "sum", struct((rows, model), BF16), [(VMEM, v) for v in (pieces[0], *got)])
        if high == 2:
            total, near[1:-1] = lax.optimization_barrier((total, near[1:-1]))
        arrived.append(swap(total, "head", high))
    arrived += [swap(piece, both, mask) for piece, mask in zip(near[:0:-1], group)]
    return call(
        last_kernel,
        "last",
        struct(resid.shape, BF16),
        [(VMEM, value) for value in (hidden, near[0], *arrived)],
        pinned=False,
    )


def solution(mesh):
    placed = (
        P(("seq", "exp"), "head"),
        P(("seq", "exp"), "head"),
        P(("seq", "exp"), "head"),
        P(("seq", "exp"), "head"),
        P(("seq", "exp"), "head"),
        P("head"),
        P("head"),
        P("head"),
        P("head", None),
        P(("seq", "exp"), "head", None),
        P(("seq", "exp"), "head", None),
        P(("seq", "exp"), "head", None),
        P(),
        P(("head", "exp"), None, None),
        P(("head", "exp"), None, None),
    )
    return jax.shard_map(
        per_device,
        mesh=mesh,
        in_specs=placed,
        out_specs=P(("seq", "exp"), "head", None),
        check_vma=False,
    )
```

```python
import functools

import jax
import jax.numpy as jnp
from jax import lax
from jax.experimental import pallas as pl
from jax.experimental.pallas import tpu as pltpu
from jax.sharding import PartitionSpec as P

HEAD_DIM = 64
STATE = 128
LANES = 128
TILE = 16
FAR = -1e30
F32 = jnp.float32
BF16 = jnp.bfloat16
HBM = pl.BlockSpec(memory_space=pltpu.HBM)
VMEM = pl.BlockSpec(memory_space=pltpu.VMEM)
ANY = pl.BlockSpec(memory_space=pl.ANY)
NT = (((1,), (1,)), ((), ()))


def struct(shape, dtype):
    return jax.ShapeDtypeStruct(shape, dtype)


def call(kernel, name, outs, ins, scratch=(), megabytes=12, pinned=True):
    args = [pltpu.with_memory_space_constraint(arg, pltpu.HBM) if spec is HBM else arg for spec, arg in ins]
    return pl.pallas_call(
        kernel,
        out_shape=jax.tree.map(lambda out: pltpu.VMEM(out.shape, out.dtype), outs) if pinned else outs,
        in_specs=[spec for spec, _ in ins],
        out_specs=jax.tree.map(lambda _: VMEM, outs),
        scratch_shapes=list(scratch),
        name=name,
        compiler_params=pltpu.CompilerParams(vmem_limit_bytes=megabytes << 20),
    )(*args)


def offsets(count):
    down = list(range(count - 1, 0, -1))
    return [[3, 1, 2], [2, 3, 1]] if count == 4 else [down, down]


def targets(count):
    return [[1, 1, 2], [2, 3, 1]] if count == 4 else offsets(count)


def head_offset(slot, count):
    first, second = (order[slot] for order in offsets(count))
    return jnp.where(core_index() == 0, first, second)


def core_index():
    return lax.axis_index("exp") % 2


def chip_index():
    return lax.axis_index("exp") // 2


def copies(sems, sources, targets):
    made = [pltpu.make_async_copy(s, t, sems.at[i]) for i, (s, t) in enumerate(zip(sources, targets))]
    for copy in made:
        copy.start()
    return made


def decays(dt_rows, a_log):
    heads, length = dt_rows.shape
    step = jnp.maximum(dt_rows, 0.0) + jnp.log1p(jnp.exp(-jnp.abs(dt_rows)))
    same = lax.broadcasted_iota(jnp.int32, (heads, heads), 0) == lax.broadcasted_iota(jnp.int32, (heads, heads), 1)
    a_column = jnp.sum(jnp.where(same, jnp.broadcast_to(a_log, (heads, heads)), 0.0), axis=1, keepdims=True)
    rate = -step * jnp.exp(a_column)
    row = lax.broadcasted_iota(jnp.int32, (length, length), 0)
    col = lax.broadcasted_iota(jnp.int32, (length, length), 1)
    upper = (row <= col).astype(F32)
    cum = jnp.dot(rate, upper, precision=lax.Precision.HIGHEST, preferred_element_type=F32)
    return step, cum


def pair_lanes(values, pair):
    rows = values.shape[0]
    lane = lax.broadcasted_iota(jnp.int32, (rows, LANES), 1)
    left = jnp.broadcast_to(values[:, 2 * pair : 2 * pair + 1], (rows, LANES))
    right = jnp.broadcast_to(values[:, 2 * pair + 1 : 2 * pair + 2], (rows, LANES))
    return jnp.where(lane < HEAD_DIM, left, right)


def unpacked(block):
    pairs = block.shape[0] // STATE
    tail = block[pairs * STATE :].astype(F32)
    totals = [tail[pair : pair + 1] + tail[pairs + pair : pairs + pair + 1] for pair in range(pairs)]
    return jnp.stack(totals), block[: pairs * STATE].astype(F32).reshape(pairs, STATE, LANES)


def pack(ref, total, state):
    pairs = state.shape[0]
    ref[0 : pairs * STATE, :] = state.reshape(pairs * STATE, LANES).astype(BF16)
    row = lax.broadcasted_iota(jnp.int32, (TILE, LANES), 0)
    tail = jnp.zeros((TILE, LANES), F32)
    for pair in range(pairs):
        wide = jnp.broadcast_to(total[pair], (TILE, LANES))
        high = wide.astype(BF16).astype(F32)
        tail = jnp.where(row == pair, high, jnp.where(row == pairs + pair, wide - high, tail))
    ref[pairs * STATE :, :] = tail.astype(BF16)


def state_kernel(x_hbm, b_hbm, dt_hbm, a_hbm, keep_ref, send_ref, *scratch):
    x_ref, b_ref, dt_ref, a_ref, packed_ref, sems = scratch
    loads = copies(sems, (dt_hbm, a_hbm, x_hbm, b_hbm), (dt_ref, a_ref, x_ref, b_ref))
    loads[0].wait()
    loads[1].wait()
    step, cum = decays(dt_ref[...], a_ref[...])
    length = cum.shape[1]
    total = cum[:, length - 1 :]
    tail = (jnp.exp(total - cum) * step).T
    total = jnp.broadcast_to(total, cum.shape).T[0:1]
    loads[2].wait()
    loads[3].wait()
    pairs = x_ref.shape[1] // LANES
    half = pairs // 2
    groups = b_ref.shape[1] // STATE
    totals, states = [], []
    for group in range(groups):
        turned = b_ref[:, group * STATE : (group + 1) * STATE].T
        for pair in range(group * pairs // groups, (group + 1) * pairs // groups):
            x_pair = x_ref[:, pair * LANES : (pair + 1) * LANES].astype(F32)
            weighted = (pair_lanes(tail, pair) * x_pair).astype(BF16)
            state = jnp.dot(turned, weighted, preferred_element_type=F32)
            totals.append(pair_lanes(total, pair))
            states.append(state)
    for at in range(2):
        span = slice(at * half, (at + 1) * half)
        pack(packed_ref.at[at], totals[span], jnp.stack(states[span]))
    keep_ref[...] = packed_ref[core_index()]
    send_ref[...] = packed_ref[1 - core_index()]


def chip_state_kernel(keep_ref, got_ref, out_ref):
    first = core_index() == 0
    keep, got = unpacked(keep_ref[...]), unpacked(got_ref[...])
    early = [jnp.where(first, mine, other) for mine, other in zip(keep, got)]
    late = [jnp.where(first, other, mine) for mine, other in zip(keep, got)]
    pack(out_ref, early[0] + late[0], jnp.exp(late[0]) * early[1] + late[1])


def weights_kernel(after_ref, up_hbm, down_hbm, up_ref, down_ref, sems):
    for load in copies(sems, (up_hbm, down_hbm), (up_ref, down_ref)):
        load.wait()


def span_kernel(after_ref, *rest):
    ins, out_ref, block_ref = rest[:-2], rest[-2], rest[-1]
    for mask, part in enumerate(ins):
        block_ref[chip_index() ^ mask] = part[...]
    total, state = unpacked(block_ref[0])
    for chip in range(1, len(ins)):
        here, own = unpacked(block_ref[chip])
        total, state = total + here, jnp.exp(here) * state + own
    pack(out_ref, total, state)


def before_kernel(chips, after_ref, keep_ref, got_ref, *rest):
    ins, (mine_ref, send_ref, chip_ref, part_ref) = rest[:-4], rest[-4:]
    for mask in range(chips):
        chip_ref[chip_index() ^ mask] = ins[mask][...]
    parts = len(ins) - chips
    for mask in range(parts):
        part_ref[lax.axis_index("seq") ^ mask] = ins[chips + mask][...]
    carry = jnp.zeros(mine_ref.shape, F32)
    for ref, count, own in ((part_ref, parts, lax.axis_index("seq")), (chip_ref, chips, chip_index())):
        for index in range(count - 1):
            total, state = unpacked(ref[index])
            carry = jnp.where(index < own, jnp.exp(total) * carry + state, carry)
    first = core_index() == 0
    total, state = (jnp.where(first, k, g) for k, g in zip(unpacked(keep_ref[...]), unpacked(got_ref[...])))
    later = jnp.exp(total) * carry + state
    mine_ref[...] = jnp.where(first, carry, later).astype(BF16)
    send_ref[...] = jnp.where(first, later, carry).astype(BF16)


def inside_kernel(x_hbm, z_hbm, b_hbm, c_hbm, dt_hbm, a_hbm, d_hbm, local_ref, grown_ref, c_ref, *scratch):
    x_ref, z_ref, b_ref, dt_ref, a_ref, d_ref, sems = scratch
    loads = copies(
        sems,
        (dt_hbm, a_hbm, d_hbm, b_hbm, c_hbm, x_hbm, z_hbm),
        (dt_ref, a_ref, d_ref, b_ref, c_ref, x_ref, z_ref),
    )
    for load in loads:
        load.wait()
    step_rows, cum_rows = decays(dt_ref[...], a_ref[...])
    cum = cum_rows.T
    grown = jnp.exp(cum)
    length = cum.shape[0]
    pairs = x_ref.shape[1] // LANES
    groups = b_ref.shape[1] // STATE
    row = lax.broadcasted_iota(jnp.int32, (length, length), 0)
    col = lax.broadcasted_iota(jnp.int32, (length, length), 1)
    lane = lax.broadcasted_iota(jnp.int32, (length, LANES), 1)
    for group in range(groups):
        span = slice(group * STATE, (group + 1) * STATE)
        scores = lax.dot_general(c_ref[:, span], b_ref[:, span], NT, preferred_element_type=F32)
        scores = jnp.where(row >= col, scores, 0.0)
        for pair in range(group * pairs // groups, (group + 1) * pairs // groups):
            at = slice(pair * LANES, (pair + 1) * LANES)
            x_pair = x_ref[:, at]
            halves = []
            for head in (2 * pair, 2 * pair + 1):
                distance = cum[:, head : head + 1] - cum_rows[head : head + 1, :]
                decay = jnp.exp(jnp.where(row >= col, distance, FAR))
                mixing = (scores * (decay * step_rows[head : head + 1, :])).astype(BF16)
                halves.append(jnp.dot(mixing, x_pair, preferred_element_type=F32))
            inside = jnp.where(lane < HEAD_DIM, halves[0], halves[1])
            skip = pair_lanes(d_ref[...], pair) * x_pair.astype(F32)
            z = z_ref[:, at].astype(F32)
            gate = z / (1.0 + jnp.exp(-z))
            local_ref[:, at] = (inside + skip) * gate
            grown_ref[:, at] = pair_lanes(grown, pair) * gate


def prep_kernel(experts, width, resid_hbm, routes_hbm, gates_hbm, gain_hbm, norm_hbm, w_hbm, *rest):
    gate_ref, resid_ref, gain_ref, norm_ref, w_ref, routes_ref, gates_ref, sems = rest
    loads = copies(
        sems,
        (routes_hbm, gates_hbm, resid_hbm, gain_hbm, norm_hbm, w_hbm),
        (routes_ref, gates_ref, resid_ref, gain_ref, norm_ref, w_ref),
    )
    loads[0].wait()
    loads[1].wait()
    count, extent = gate_ref.shape
    start = width // LANES * LANES
    lane = lax.broadcasted_iota(jnp.int32, (extent, count), 0) + start - width
    expert = jnp.where(lane >= experts, lane - experts, lane)
    gate = jnp.zeros((extent, count), F32)
    for pick in range(routes_ref.shape[0]):
        gate = gate + jnp.where(routes_ref[pick] == expert, gates_ref[pick], 0.0)
    high = gate.astype(BF16).astype(F32)
    gate = jnp.where(lane < experts, high, jnp.where(lane < 2 * experts, gate - high, 0.0))
    gate_ref[...] = gate.T.astype(BF16)
    for load in loads[2:]:
        load.wait()


def half_product(half, local_ref, grown_ref, c_ref, norm_ref, w_ref, state_ref, normed_ref, count):
    pairs = state_ref.shape[0]
    width = pairs * LANES
    base = pl.multiple_of(half * width, width)
    groups = c_ref.shape[1] // STATE // 2
    per_group = pairs // groups
    for group in range(groups):
        c_group = c_ref[:, pl.ds(pl.multiple_of((half * groups + group) * STATE, STATE), STATE)]
        gated, squares = [], 0.0
        for pair in range(group * per_group, (group + 1) * per_group):
            span = pl.ds(pl.multiple_of(base + pair * LANES, LANES), LANES)
            carried = jnp.dot(c_group, state_ref[pair], preferred_element_type=F32)
            value = local_ref[:, span] + grown_ref[:, span] * carried
            gated.append(value)
            squares = squares + value * value
        mean = jnp.sum(squares, axis=1, keepdims=True) / (per_group * LANES)
        inverse = lax.rsqrt(mean + 1e-05)
        for offset, value in enumerate(gated):
            pair = group * per_group + offset
            gain = norm_ref[:, pl.ds(pl.multiple_of(base + pair * LANES, LANES), LANES)]
            normed_ref[:, pair * LANES : (pair + 1) * LANES] = (value * inverse * gain).astype(BF16)
    rows = normed_ref.shape[0] // count
    blocks = []
    for shift in range(count):
        owner = lax.axis_index("head") ^ (head_offset(shift - 1, count) if shift else 0)
        blocks.append(normed_ref[pl.ds(pl.multiple_of(owner * rows, rows), rows), :])
    weight = w_ref[:, pl.ds(base, width)]
    return lax.dot_general(jnp.concatenate(blocks, axis=0), weight, NT, preferred_element_type=F32)


def first_half_kernel(count, local_ref, grown_ref, c_ref, norm_ref, w_ref, mine_ref, out_ref, normed_ref):
    out_ref[...] = half_product(
        core_index(), local_ref, grown_ref, c_ref, norm_ref, w_ref, mine_ref, normed_ref, count
    )


def mixed_kernel(after_up, after_down, local_ref, grown_ref, c_ref, norm_ref, w_ref, got_ref, first_ref, *rest):
    outs, normed_ref = rest[:-1], rest[-1]
    product = first_ref[...] + half_product(
        1 - core_index(), local_ref, grown_ref, c_ref, norm_ref, w_ref, got_ref, normed_ref, len(outs)
    )
    rows = outs[0].shape[0]
    for shift, out in enumerate(outs):
        out[...] = product[shift * rows : (shift + 1) * rows].astype(BF16)


def relay_kernel(own_ref, got_ref, out_ref):
    got = jnp.where(core_index() == 0, got_ref[...].astype(F32), 0.0)
    out_ref[...] = (own_ref[...].astype(F32) + got).astype(BF16)


def rows_kernel(after_ref, resid_ref, gate_ref, gain_ref, *rest):
    parts, hidden_ref, rows_ref = rest[:-2], rest[-2], rest[-1]
    mixed = parts[0][...].astype(F32)
    for at, part in enumerate(parts[1:]):
        value = part[...].astype(F32)
        if at == 0 and len(parts) == 4:
            value = jnp.where(core_index() == 1, value, 0.0)
        mixed = mixed + value
    hidden = (resid_ref[0].astype(F32) + mixed).astype(BF16)
    hidden_ref[...] = hidden
    value = hidden.astype(F32)
    scale = lax.rsqrt(jnp.mean(value * value, axis=1, keepdims=True) + 1e-05)
    width = value.shape[1]
    rows_ref[:, width // LANES * LANES :] = gate_ref[...]
    rows_ref[:, :width] = (value * scale * gain_ref[...]).astype(BF16)


def expert_kernel(experts, count, carried, up_ref, down_ref, other_up_ref, other_down_ref, *rest):
    ins, done, outs = rest[:count], rest[count : count + len(carried)], rest[count + len(carried) :]
    width = up_ref.shape[2]
    start = width // LANES * LANES
    rows = jnp.concatenate([ref[:, :width] for ref in ins], axis=0)
    tail = jnp.concatenate([ref[:, start:] for ref in ins], axis=0).astype(F32)
    lane = lax.broadcasted_iota(jnp.int32, tail.shape, 1) + start - width
    own = lax.axis_index("head") * lax.axis_size("exp") + lax.axis_index("exp")
    other = own + 1 - 2 * core_index()
    total = 0.0
    for expert, up_of, down_of in ((own, up_ref, down_ref), (other, other_up_ref, other_down_ref)):
        up = lax.dot_general(rows, up_of[0], NT, preferred_element_type=F32)
        up = jnp.maximum(up, 0.0)
        activated = (up * up).astype(BF16)
        chosen = (lane == expert) | (lane == expert + experts)
        gate = jnp.sum(jnp.where(chosen, tail, 0.0), axis=1, keepdims=True)
        total = total + jnp.dot(activated, down_of[0], preferred_element_type=F32) * gate
    size = ins[0].shape[0]
    for at, out in enumerate(outs):
        out[0:size] = total[at * size : (at + 1) * size].astype(BF16)
    for at, ref in zip(carried, done):
        outs[at][size:] = ref[...]


def sum_kernel(*refs):
    rows = refs[-1].shape[0]
    total = refs[0][...].astype(F32)
    for ref in refs[1:-1]:
        total = total + ref[0:rows].astype(F32)
    refs[-1][...] = total.astype(BF16)


def last_kernel(hidden_ref, *rest):
    parts, out_ref = rest[:-1], rest[-1]
    rows = out_ref.shape[1]
    total = parts[0][...].astype(F32)
    for part in parts[1:]:
        total = total + part[part.shape[0] - rows :].astype(F32)
    out_ref[0] = (hidden_ref[...].astype(F32) + total).astype(BF16)


def swap(value, axis, mask):
    size = lax.axis_size(axis)
    return lax.ppermute(value, axis, [(i, i ^ mask) for i in range(size)])


def swap_slot(value, slot):
    heads, size = lax.axis_size("head"), lax.axis_size("exp")
    order = targets(heads)
    pairs = []
    for i in range(heads * size):
        head, exp = i // size, i % size
        pairs.append((i, (head ^ order[exp % 2][slot]) * size + exp))
    return lax.ppermute(value, ("head", "exp"), pairs)


def per_device(
    x_in, z_in, b_in, c_in, dt_in, a_log, d_skip, norm_w, w_out, resid, routes, gates, moe_gain, w_up, w_down
):
    length, heads = dt_in.shape
    channels = x_in.shape[1]
    model = w_out.shape[1]
    hidden_units = w_up.shape[2]
    seq_size, head_size, exp_size = lax.axis_size("seq"), lax.axis_size("head"), lax.axis_size("exp")
    chips = exp_size // 2
    rows = resid.shape[1]
    experts = head_size * exp_size
    pairs = channels // LANES
    half = pairs // 2
    dt_rows, a_row, d_row = dt_in.T, a_log[None], d_skip[None]
    dma = pltpu.SemaphoreType.DMA
    packed = struct((half * STATE + TILE, LANES), BF16)

    keep, send = call(
        state_kernel,
        "state",
        [packed, packed],
        [(HBM, x_in), (HBM, b_in), (HBM, dt_rows), (HBM, a_row)],
        [pltpu.VMEM(x_in.shape, BF16), pltpu.VMEM(b_in.shape, BF16), pltpu.VMEM(dt_rows.shape, F32),
         pltpu.VMEM(a_row.shape, F32), pltpu.VMEM((2, half * STATE + TILE, LANES), BF16), dma((4,))],
        megabytes=16,
    )
    local, grown, c_held = call(
        inside_kernel,
        "inside",
        [struct((length, channels), F32), struct((length, channels), F32), struct(c_in.shape, BF16)],
        [(HBM, value) for value in (x_in, z_in, b_in, c_in, dt_rows, a_row, d_row)],
        [pltpu.VMEM(x_in.shape, BF16), pltpu.VMEM(z_in.shape, BF16), pltpu.VMEM(b_in.shape, BF16),
         pltpu.VMEM(dt_rows.shape, F32), pltpu.VMEM(a_row.shape, F32), pltpu.VMEM(d_row.shape, F32), dma((7,))],
        megabytes=16,
    )
    wide = -(-(model + 2 * experts) // LANES) * LANES
    turned = [jnp.transpose(value, (2, 0, 1)) for value in (routes, gates)]
    gate_lanes, resid_held, gain_held, norm_held, w_held = call(
        functools.partial(prep_kernel, experts, model),
        "prep",
        [struct((rows, wide - model // LANES * LANES), BF16), struct(resid.shape, BF16), struct((1, model), F32),
         struct((1, channels), F32), struct((model, channels), BF16)],
        [(HBM, value) for value in (resid, *turned, moe_gain[None], norm_w[None], w_out.T)],
        [pltpu.VMEM(turned[0].shape, jnp.int32), pltpu.VMEM(turned[1].shape, F32), dma((6,))],
        megabytes=16,
    )
    up_turned = jnp.swapaxes(w_up, 1, 2)
    got = swap(send, "exp", 1)
    chip = call(chip_state_kernel, "chip_state", packed, [(VMEM, keep), (VMEM, got)])
    chip, up_after, down_after = lax.optimization_barrier((chip, up_turned, w_down))
    other_up, other_down = swap(up_after, "exp", 1), swap(down_after, "exp", 1)
    along_y = [chip] + [swap(chip, "exp", 2 * d) for d in range(1, chips)]
    span = call(
        span_kernel,
        "span",
        packed,
        [(ANY, c_held)] + [(VMEM, value) for value in along_y],
        [pltpu.VMEM((chips, *packed.shape), BF16)],
    )
    along_x = [span] + [swap(span, "seq", d) for d in range(1, seq_size)]
    before, before_send = call(
        functools.partial(before_kernel, chips),
        "before",
        [struct((half, STATE, LANES), BF16)] * 2,
        [(ANY, gate_lanes)] + [(VMEM, value) for value in (keep, got, *along_y, *along_x)],
        [pltpu.VMEM((chips, *packed.shape), BF16), pltpu.VMEM((seq_size, *packed.shape), BF16)],
        megabytes=24,
    )
    before_got = swap(before_send, "exp", 1)
    shared = [(VMEM, value) for value in (local, grown, c_held, norm_held, w_held)]
    normed_half = pltpu.VMEM((length, channels // 2), BF16)
    first = call(
        functools.partial(first_half_kernel, head_size),
        "first_half",
        struct((length, model), F32),
        shared + [(VMEM, before)],
        [normed_half],
    )
    mixed = call(
        mixed_kernel,
        "mixed",
        [struct((rows, model), BF16)] * head_size,
        [(ANY, other_up), (ANY, other_down)] + shared + [(VMEM, before_got), (VMEM, first)],
        [normed_half],
    )
    up_held, down_held = call(
        weights_kernel,
        "weights",
        [struct(up_turned.shape, BF16), struct(w_down.shape, BF16)],
        [(ANY, mixed[0]), (HBM, up_turned), (HBM, w_down)],
        [dma((2,))],
    )
    slots = list(range(head_size - 1))
    parts, last = [swap_slot(mixed[k + 1], k) for k in slots[:-1]], mixed[-1]
    if head_size == 4:
        last = call(relay_kernel, "relay", struct((rows, model), BF16), [(VMEM, last), (VMEM, parts[0])])
    parts = [mixed[0]] + parts + [swap_slot(last, slots[-1])]
    hidden, own_rows = call(
        rows_kernel,
        "rows",
        [struct((rows, model), BF16), struct((rows, wide), BF16)],
        [(ANY, up_held)] + [(VMEM, value) for value in (resid_held, gate_lanes, gain_held, *parts)],
    )

    def through_experts(members, carried=()):
        places = [at for at, _ in carried]
        return call(
            functools.partial(expert_kernel, experts, len(members), places),
            "experts",
            [struct((rows * (2 if at in places else 1), model), BF16) for at in range(len(members))],
            [(VMEM, value) for value in (up_held, down_held, other_up, other_down, *members)]
            + [(VMEM, value) for _, value in carried],
            megabytes=16,
        )

    both = ("head", "exp")
    group = [z * exp_size + 2 * d for z in (0, 1) for d in range(chips)][1:]

    def spread(block):
        return [block] + [swap(block, both, mask) for mask in group]

    sets = [spread(swap(own_rows, "head", high)) for high in range(2, head_size, 2)]
    near = through_experts(spread(own_rows))
    near, sets = lax.optimization_barrier((near, sets))
    joined = [at for at, mask in enumerate(group, 1) if mask >= exp_size]
    arrived, later = [], [at for at in range(1, len(near)) if at not in joined]
    apart = [near[at] for at in later]
    for high, members in zip(range(2, head_size, 2), sets):
        pieces = through_experts(members, [(at, near[at]) for at in joined] if high == 2 else ())
        got = [swap(piece, both, mask) for piece, mask in zip(pieces[:0:-1], group[::-1])]
        total = call(sum_kernel, "sum", struct((rows, model), BF16), [(VMEM, v) for v in (pieces[0], *got)])
        if high == 2:
            total, apart = lax.optimization_barrier((total, apart))
            arrived += [part for part, mask in zip(got, group[::-1]) if mask >= exp_size]
        arrived.append(swap(total, "head", high))
    arrived += [swap(piece, both, group[at - 1]) for piece, at in zip(apart, later)]
    return call(
        last_kernel,
        "last",
        struct(resid.shape, BF16),
        [(VMEM, value) for value in (hidden, near[0], *arrived)],
        pinned=False,
    )


def solution(mesh):
    placed = (
        P(("seq", "exp"), "head"),
        P(("seq", "exp"), "head"),
        P(("seq", "exp"), "head"),
        P(("seq", "exp"), "head"),
        P(("seq", "exp"), "head"),
        P("head"),
        P("head"),
        P("head"),
        P("head", None),
        P(("seq", "exp"), "head", None),
        P(("seq", "exp"), "head", None),
        P(("seq", "exp"), "head", None),
        P(),
        P(("head", "exp"), None, None),
        P(("head", "exp"), None, None),
    )
    return jax.shard_map(
        per_device,
        mesh=mesh,
        in_specs=placed,
        out_specs=P(("seq", "exp"), "head", None),
        check_vma=False,
    )
```

```python
import functools

import jax
import jax.numpy as jnp
from jax import lax
from jax.experimental import pallas as pl
from jax.experimental.pallas import tpu as pltpu
from jax.sharding import PartitionSpec as P

HEAD_DIM = 64
STATE = 128
LANES = 128
TILE = 16
FAR = -1e30
F32 = jnp.float32
BF16 = jnp.bfloat16
HBM = pl.BlockSpec(memory_space=pltpu.HBM)
VMEM = pl.BlockSpec(memory_space=pltpu.VMEM)
ANY = pl.BlockSpec(memory_space=pl.ANY)
NT = (((1,), (1,)), ((), ()))


def struct(shape, dtype):
    return jax.ShapeDtypeStruct(shape, dtype)


def call(kernel, name, outs, ins, scratch=(), megabytes=12, pinned=True):
    args = [pltpu.with_memory_space_constraint(arg, pltpu.HBM) if spec is HBM else arg for spec, arg in ins]
    return pl.pallas_call(
        kernel,
        out_shape=jax.tree.map(lambda out: pltpu.VMEM(out.shape, out.dtype), outs) if pinned else outs,
        in_specs=[spec for spec, _ in ins],
        out_specs=jax.tree.map(lambda _: VMEM, outs),
        scratch_shapes=list(scratch),
        name=name,
        compiler_params=pltpu.CompilerParams(vmem_limit_bytes=megabytes << 20),
    )(*args)


def offsets(count):
    down = list(range(count - 1, 0, -1))
    return [[3, 1, 2], [2, 3, 1]] if count == 4 else [down, down]


def targets(count):
    return [[1, 1, 2], [2, 3, 1]] if count == 4 else offsets(count)


def head_offset(slot, count):
    first, second = (order[slot] for order in offsets(count))
    return jnp.where(core_index() == 0, first, second)


def core_index():
    return lax.axis_index("exp") % 2


def chip_index():
    return lax.axis_index("exp") // 2


def copies(sems, sources, targets):
    made = [pltpu.make_async_copy(s, t, sems.at[i]) for i, (s, t) in enumerate(zip(sources, targets))]
    for copy in made:
        copy.start()
    return made


def decays(dt_rows, a_log):
    heads, length = dt_rows.shape
    step = jnp.maximum(dt_rows, 0.0) + jnp.log1p(jnp.exp(-jnp.abs(dt_rows)))
    same = lax.broadcasted_iota(jnp.int32, (heads, heads), 0) == lax.broadcasted_iota(jnp.int32, (heads, heads), 1)
    a_column = jnp.sum(jnp.where(same, jnp.broadcast_to(a_log, (heads, heads)), 0.0), axis=1, keepdims=True)
    rate = -step * jnp.exp(a_column)
    row = lax.broadcasted_iota(jnp.int32, (length, length), 0)
    col = lax.broadcasted_iota(jnp.int32, (length, length), 1)
    upper = (row <= col).astype(F32)
    cum = jnp.dot(rate, upper, precision=lax.Precision.HIGHEST, preferred_element_type=F32)
    return step, cum


def pair_lanes(values, pair):
    rows = values.shape[0]
    lane = lax.broadcasted_iota(jnp.int32, (rows, LANES), 1)
    left = jnp.broadcast_to(values[:, 2 * pair : 2 * pair + 1], (rows, LANES))
    right = jnp.broadcast_to(values[:, 2 * pair + 1 : 2 * pair + 2], (rows, LANES))
    return jnp.where(lane < HEAD_DIM, left, right)


def unpacked(block):
    pairs = block.shape[0] // STATE
    tail = block[pairs * STATE :].astype(F32)
    totals = [tail[pair : pair + 1] + tail[pairs + pair : pairs + pair + 1] for pair in range(pairs)]
    return jnp.stack(totals), block[: pairs * STATE].astype(F32).reshape(pairs, STATE, LANES)


def pack(ref, total, state):
    pairs = state.shape[0]
    ref[0 : pairs * STATE, :] = state.reshape(pairs * STATE, LANES).astype(BF16)
    row = lax.broadcasted_iota(jnp.int32, (TILE, LANES), 0)
    tail = jnp.zeros((TILE, LANES), F32)
    for pair in range(pairs):
        wide = jnp.broadcast_to(total[pair], (TILE, LANES))
        high = wide.astype(BF16).astype(F32)
        tail = jnp.where(row == pair, high, jnp.where(row == pairs + pair, wide - high, tail))
    ref[pairs * STATE :, :] = tail.astype(BF16)


def state_kernel(x_hbm, b_hbm, dt_hbm, a_hbm, keep_ref, send_ref, *scratch):
    x_ref, b_ref, dt_ref, a_ref, packed_ref, sems = scratch
    loads = copies(sems, (dt_hbm, a_hbm, x_hbm, b_hbm), (dt_ref, a_ref, x_ref, b_ref))
    loads[0].wait()
    loads[1].wait()
    step, cum = decays(dt_ref[...], a_ref[...])
    length = cum.shape[1]
    total = cum[:, length - 1 :]
    tail = (jnp.exp(total - cum) * step).T
    total = jnp.broadcast_to(total, cum.shape).T[0:1]
    loads[2].wait()
    loads[3].wait()
    pairs = x_ref.shape[1] // LANES
    half = pairs // 2
    groups = b_ref.shape[1] // STATE
    totals, states = [], []
    for group in range(groups):
        turned = b_ref[:, group * STATE : (group + 1) * STATE].T
        for pair in range(group * pairs // groups, (group + 1) * pairs // groups):
            x_pair = x_ref[:, pair * LANES : (pair + 1) * LANES].astype(F32)
            weighted = (pair_lanes(tail, pair) * x_pair).astype(BF16)
            state = jnp.dot(turned, weighted, preferred_element_type=F32)
            totals.append(pair_lanes(total, pair))
            states.append(state)
    for at in range(2):
        span = slice(at * half, (at + 1) * half)
        pack(packed_ref.at[at], totals[span], jnp.stack(states[span]))
    keep_ref[...] = packed_ref[core_index()]
    send_ref[...] = packed_ref[1 - core_index()]


def chip_state_kernel(after_ref, keep_ref, got_ref, *outs):
    first = core_index() == 0
    keep, got = unpacked(keep_ref[...]), unpacked(got_ref[...])
    early = [jnp.where(first, mine, other) for mine, other in zip(keep, got)]
    late = [jnp.where(first, other, mine) for mine, other in zip(keep, got)]
    total, state = early[0] + late[0], jnp.exp(late[0]) * early[1] + late[1]
    size = total.shape[0] // len(outs)
    for at, out in enumerate(outs):
        pack(out, total[at * size : (at + 1) * size], state[at * size : (at + 1) * size])


def weights_kernel(after_ref, up_hbm, down_hbm, up_ref, down_ref, sems):
    for load in copies(sems, (up_hbm, down_hbm), (up_ref, down_ref)):
        load.wait()


def span_kernel(after_ref, *rest):
    ins, out_ref, block_ref = rest[:-2], rest[-2], rest[-1]
    for mask, part in enumerate(ins):
        block_ref[chip_index() ^ mask] = part[...]
    total, state = unpacked(block_ref[0])
    for chip in range(1, len(ins)):
        here, own = unpacked(block_ref[chip])
        total, state = total + here, jnp.exp(here) * state + own
    pack(out_ref, total, state)


def before_kernel(chips, parts, after_ref, keep_ref, got_ref, *rest):
    ins, (mine_ref, send_ref, chip_ref, part_ref) = rest[:-4], rest[-4:]
    first = core_index() == 0
    totals, states = (jnp.where(first, k, g) for k, g in zip(unpacked(keep_ref[...]), unpacked(got_ref[...])))
    each = chips + parts
    chunks = len(ins) // each
    size = totals.shape[0] // chunks
    for chunk in range(chunks):
        span = slice(chunk * size, (chunk + 1) * size)
        for mask in range(chips):
            chip_ref[chip_index() ^ mask] = ins[chunk * each + mask][...]
        for mask in range(parts):
            part_ref[lax.axis_index("seq") ^ mask] = ins[chunk * each + chips + mask][...]
        carry = jnp.zeros(states[span].shape, F32)
        for ref, count, own in ((part_ref, parts, lax.axis_index("seq")), (chip_ref, chips, chip_index())):
            for index in range(count - 1):
                total, state = unpacked(ref[index])
                carry = jnp.where(index < own, jnp.exp(total) * carry + state, carry)
        later = jnp.exp(totals[span]) * carry + states[span]
        mine_ref[span] = jnp.where(first, carry, later).astype(BF16)
        send_ref[span] = jnp.where(first, later, carry).astype(BF16)


def inside_kernel(x_hbm, z_hbm, b_hbm, c_hbm, dt_hbm, a_hbm, d_hbm, local_ref, grown_ref, c_ref, *scratch):
    x_ref, z_ref, b_ref, dt_ref, a_ref, d_ref, sems = scratch
    loads = copies(
        sems,
        (dt_hbm, a_hbm, d_hbm, b_hbm, c_hbm, x_hbm, z_hbm),
        (dt_ref, a_ref, d_ref, b_ref, c_ref, x_ref, z_ref),
    )
    for load in loads:
        load.wait()
    step_rows, cum_rows = decays(dt_ref[...], a_ref[...])
    cum = cum_rows.T
    grown = jnp.exp(cum)
    length = cum.shape[0]
    pairs = x_ref.shape[1] // LANES
    groups = b_ref.shape[1] // STATE
    row = lax.broadcasted_iota(jnp.int32, (length, length), 0)
    col = lax.broadcasted_iota(jnp.int32, (length, length), 1)
    lane = lax.broadcasted_iota(jnp.int32, (length, LANES), 1)
    for group in range(groups):
        span = slice(group * STATE, (group + 1) * STATE)
        scores = lax.dot_general(c_ref[:, span], b_ref[:, span], NT, preferred_element_type=F32)
        scores = jnp.where(row >= col, scores, 0.0)
        for pair in range(group * pairs // groups, (group + 1) * pairs // groups):
            at = slice(pair * LANES, (pair + 1) * LANES)
            x_pair = x_ref[:, at]
            halves = []
            for head in (2 * pair, 2 * pair + 1):
                distance = cum[:, head : head + 1] - cum_rows[head : head + 1, :]
                decay = jnp.exp(jnp.where(row >= col, distance, FAR))
                mixing = (scores * (decay * step_rows[head : head + 1, :])).astype(BF16)
                halves.append(jnp.dot(mixing, x_pair, preferred_element_type=F32))
            inside = jnp.where(lane < HEAD_DIM, halves[0], halves[1])
            skip = pair_lanes(d_ref[...], pair) * x_pair.astype(F32)
            z = z_ref[:, at].astype(F32)
            gate = z / (1.0 + jnp.exp(-z))
            local_ref[:, at] = (inside + skip) * gate
            grown_ref[:, at] = pair_lanes(grown, pair) * gate


def projection_kernel(norm_hbm, w_hbm, norm_ref, w_ref, sems):
    for load in copies(sems, (norm_hbm, w_hbm), (norm_ref, w_ref)):
        load.wait()


def prep_kernel(experts, width, after_ref, resid_hbm, routes_hbm, gates_hbm, gain_hbm, *rest):
    gate_ref, resid_ref, gain_ref, routes_ref, gates_ref, sems = rest
    loads = copies(
        sems,
        (routes_hbm, gates_hbm, resid_hbm, gain_hbm),
        (routes_ref, gates_ref, resid_ref, gain_ref.at[0]),
    )
    loads[0].wait()
    loads[1].wait()
    count, extent = gate_ref.shape
    start = width // LANES * LANES
    lane = lax.broadcasted_iota(jnp.int32, (extent, count), 0) + start - width
    expert = jnp.where(lane >= experts, lane - experts, lane)
    gate = jnp.zeros((extent, count), F32)
    for pick in range(routes_ref.shape[0]):
        gate = gate + jnp.where(routes_ref[pick] == expert, gates_ref[pick], 0.0)
    high = gate.astype(BF16).astype(F32)
    gate = jnp.where(lane < experts, high, jnp.where(lane < 2 * experts, gate - high, 0.0))
    gate_ref[...] = gate.T.astype(BF16)
    for load in loads[2:]:
        load.wait()


def half_product(half, local_ref, grown_ref, c_ref, norm_ref, w_ref, state_ref, normed_ref, count):
    pairs = state_ref.shape[0]
    width = pairs * LANES
    base = pl.multiple_of(half * width, width)
    groups = c_ref.shape[1] // STATE // 2
    per_group = pairs // groups
    for group in range(groups):
        c_group = c_ref[:, pl.ds(pl.multiple_of((half * groups + group) * STATE, STATE), STATE)]
        gated, squares = [], 0.0
        for pair in range(group * per_group, (group + 1) * per_group):
            span = pl.ds(pl.multiple_of(base + pair * LANES, LANES), LANES)
            carried = jnp.dot(c_group, state_ref[pair], preferred_element_type=F32)
            value = local_ref[:, span] + grown_ref[:, span] * carried
            gated.append(value)
            squares = squares + value * value
        mean = jnp.sum(squares, axis=1, keepdims=True) / (per_group * LANES)
        inverse = lax.rsqrt(mean + 1e-05)
        for offset, value in enumerate(gated):
            pair = group * per_group + offset
            gain = norm_ref[:, pl.ds(pl.multiple_of(base + pair * LANES, LANES), LANES)]
            normed_ref[:, pair * LANES : (pair + 1) * LANES] = (value * inverse * gain).astype(BF16)
    rows = normed_ref.shape[0] // count
    blocks = []
    for shift in range(count):
        owner = lax.axis_index("head") ^ (head_offset(shift - 1, count) if shift else 0)
        blocks.append(normed_ref[pl.ds(pl.multiple_of(owner * rows, rows), rows), :])
    weight = w_ref[:, pl.ds(base, width)]
    return lax.dot_general(jnp.concatenate(blocks, axis=0), weight, NT, preferred_element_type=F32)


def first_half_kernel(count, local_ref, grown_ref, c_ref, norm_ref, w_ref, mine_ref, out_ref, normed_ref):
    out_ref[...] = half_product(
        core_index(), local_ref, grown_ref, c_ref, norm_ref, w_ref, mine_ref, normed_ref, count
    )


def mixed_kernel(after_up, after_down, local_ref, grown_ref, c_ref, norm_ref, w_ref, got_ref, first_ref, *rest):
    outs, normed_ref = rest[:-1], rest[-1]
    product = first_ref[...] + half_product(
        1 - core_index(), local_ref, grown_ref, c_ref, norm_ref, w_ref, got_ref, normed_ref, len(outs)
    )
    rows = outs[0].shape[0]
    for shift, out in enumerate(outs):
        out[...] = product[shift * rows : (shift + 1) * rows].astype(BF16)


def relay_kernel(own_ref, got_ref, out_ref):
    got = jnp.where(core_index() == 0, got_ref[...].astype(F32), 0.0)
    out_ref[...] = (own_ref[...].astype(F32) + got).astype(BF16)


def rows_kernel(after_ref, resid_ref, gate_ref, gain_ref, *rest):
    parts, hidden_ref, rows_ref = rest[:-2], rest[-2], rest[-1]
    mixed = parts[0][...].astype(F32)
    for at, part in enumerate(parts[1:]):
        value = part[...].astype(F32)
        if at == 0 and len(parts) == 4:
            value = jnp.where(core_index() == 1, value, 0.0)
        mixed = mixed + value
    hidden = (resid_ref[0].astype(F32) + mixed).astype(BF16)
    hidden_ref[...] = hidden
    value = hidden.astype(F32)
    scale = lax.rsqrt(jnp.mean(value * value, axis=1, keepdims=True) + 1e-05)
    width = value.shape[1]
    rows_ref[:, width // LANES * LANES :] = gate_ref[...]
    rows_ref[:, :width] = (value * scale * gain_ref[...]).astype(BF16)


def expert_kernel(experts, count, carried, up_ref, down_ref, other_up_ref, other_down_ref, *rest):
    ins, done, outs = rest[:count], rest[count : count + len(carried)], rest[count + len(carried) :]
    width = up_ref.shape[2]
    start = width // LANES * LANES
    rows = jnp.concatenate([ref[:, :width] for ref in ins], axis=0)
    tail = jnp.concatenate([ref[:, start:] for ref in ins], axis=0).astype(F32)
    lane = lax.broadcasted_iota(jnp.int32, tail.shape, 1) + start - width
    own = lax.axis_index("head") * lax.axis_size("exp") + lax.axis_index("exp")
    other = own + 1 - 2 * core_index()
    total = 0.0
    for expert, up_of, down_of in ((own, up_ref, down_ref), (other, other_up_ref, other_down_ref)):
        up = lax.dot_general(rows, up_of[0], NT, preferred_element_type=F32)
        up = jnp.maximum(up, 0.0)
        activated = (up * up).astype(BF16)
        chosen = (lane == expert) | (lane == expert + experts)
        gate = jnp.sum(jnp.where(chosen, tail, 0.0), axis=1, keepdims=True)
        total = total + jnp.dot(activated, down_of[0], preferred_element_type=F32) * gate
    size = ins[0].shape[0]
    for at, out in enumerate(outs):
        out[0:size] = total[at * size : (at + 1) * size].astype(BF16)
    for at, ref in zip(carried, done):
        outs[at][size:] = ref[...]


def sum_kernel(*refs):
    rows = refs[-1].shape[0]
    total = refs[0][...].astype(F32)
    for ref in refs[1:-1]:
        total = total + ref[0:rows].astype(F32)
    refs[-1][...] = total.astype(BF16)


def last_kernel(hidden_ref, *rest):
    parts, out_ref = rest[:-1], rest[-1]
    rows = out_ref.shape[1]
    total = parts[0][...].astype(F32)
    for part in parts[1:]:
        total = total + part[part.shape[0] - rows :].astype(F32)
    out_ref[0] = (hidden_ref[...].astype(F32) + total).astype(BF16)


def swap(value, axis, mask):
    size = lax.axis_size(axis)
    return lax.ppermute(value, axis, [(i, i ^ mask) for i in range(size)])


def swap_slot(value, slot):
    heads, size = lax.axis_size("head"), lax.axis_size("exp")
    order = targets(heads)
    pairs = []
    for i in range(heads * size):
        head, exp = i // size, i % size
        pairs.append((i, (head ^ order[exp % 2][slot]) * size + exp))
    return lax.ppermute(value, ("head", "exp"), pairs)


def per_device(
    x_in, z_in, b_in, c_in, dt_in, a_log, d_skip, norm_w, w_out, resid, routes, gates, moe_gain, w_up, w_down
):
    length, heads = dt_in.shape
    channels = x_in.shape[1]
    model = w_out.shape[1]
    hidden_units = w_up.shape[2]
    seq_size, head_size, exp_size = lax.axis_size("seq"), lax.axis_size("head"), lax.axis_size("exp")
    chips = exp_size // 2
    rows = resid.shape[1]
    experts = head_size * exp_size
    pairs = channels // LANES
    half = pairs // 2
    dt_rows, a_row, d_row = dt_in.T, a_log[None], d_skip[None]
    dma = pltpu.SemaphoreType.DMA
    packed = struct((half * STATE + TILE, LANES), BF16)

    keep, send = call(
        state_kernel,
        "state",
        [packed, packed],
        [(HBM, x_in), (HBM, b_in), (HBM, dt_rows), (HBM, a_row)],
        [pltpu.VMEM(x_in.shape, BF16), pltpu.VMEM(b_in.shape, BF16), pltpu.VMEM(dt_rows.shape, F32),
         pltpu.VMEM(a_row.shape, F32), pltpu.VMEM((2, half * STATE + TILE, LANES), BF16), dma((4,))],
        megabytes=16,
    )
    local, grown, c_held = call(
        inside_kernel,
        "inside",
        [struct((length, channels), F32), struct((length, channels), F32), struct(c_in.shape, BF16)],
        [(HBM, value) for value in (x_in, z_in, b_in, c_in, dt_rows, a_row, d_row)],
        [pltpu.VMEM(x_in.shape, BF16), pltpu.VMEM(z_in.shape, BF16), pltpu.VMEM(b_in.shape, BF16),
         pltpu.VMEM(dt_rows.shape, F32), pltpu.VMEM(a_row.shape, F32), pltpu.VMEM(d_row.shape, F32), dma((7,))],
        megabytes=16,
    )
    wide = -(-(model + 2 * experts) // LANES) * LANES
    turned = [jnp.transpose(value, (2, 0, 1)) for value in (routes, gates)]
    norm_held, w_held = call(
        projection_kernel,
        "projection",
        [struct((1, channels), F32), struct((model, channels), BF16)],
        [(HBM, norm_w[None]), (HBM, w_out.T)],
        [dma((2,))],
    )
    gate_lanes, resid_held, gain_held = call(
        functools.partial(prep_kernel, experts, model),
        "prep",
        [struct((rows, wide - model // LANES * LANES), BF16), struct(resid.shape, BF16), struct((1, model), F32)],
        [(ANY, keep)] + [(HBM, value) for value in (resid, *turned, moe_gain)],
        [pltpu.VMEM(turned[0].shape, jnp.int32), pltpu.VMEM(turned[1].shape, F32), dma((4,))],
        megabytes=16,
    )
    up_turned = jnp.swapaxes(w_up, 1, 2)
    got = swap(send, "exp", 1)
    chunks = 2 if half % 2 == 0 else 1
    packed = struct((half // chunks * STATE + TILE, LANES), BF16)
    chip = call(chip_state_kernel, "chip_state", [packed] * chunks, [(ANY, gate_lanes), (VMEM, keep), (VMEM, got)])
    chip, up_after, down_after = lax.optimization_barrier((chip, up_turned, w_down))
    other_up, other_down = swap(up_after, "exp", 1), swap(down_after, "exp", 1)
    exchanged = []
    for own in chip:
        along_y = [own] + [swap(own, "exp", 2 * d) for d in range(1, chips)]
        span = call(
            span_kernel,
            "span",
            packed,
            [(ANY, c_held)] + [(VMEM, value) for value in along_y],
            [pltpu.VMEM((chips, *packed.shape), BF16)],
        )
        exchanged += along_y + [span] + [swap(span, "seq", d) for d in range(1, seq_size)]
    before, before_send = call(
        functools.partial(before_kernel, chips, seq_size),
        "before",
        [struct((half, STATE, LANES), BF16)] * 2,
        [(ANY, norm_held)] + [(VMEM, value) for value in (keep, got, *exchanged)],
        [pltpu.VMEM((chips, *packed.shape), BF16), pltpu.VMEM((seq_size, *packed.shape), BF16)],
        megabytes=24,
    )
    before_got = swap(before_send, "exp", 1)
    shared = [(VMEM, value) for value in (local, grown, c_held, norm_held, w_held)]
    normed_half = pltpu.VMEM((length, channels // 2), BF16)
    first = call(
        functools.partial(first_half_kernel, head_size),
        "first_half",
        struct((length, model), F32),
        shared + [(VMEM, before)],
        [normed_half],
    )
    mixed = call(
        mixed_kernel,
        "mixed",
        [struct((rows, model), BF16)] * head_size,
        [(ANY, other_up), (ANY, other_down)] + shared + [(VMEM, before_got), (VMEM, first)],
        [normed_half],
    )
    up_held, down_held = call(
        weights_kernel,
        "weights",
        [struct(up_turned.shape, BF16), struct(w_down.shape, BF16)],
        [(ANY, mixed[0]), (HBM, up_turned), (HBM, w_down)],
        [dma((2,))],
    )
    slots = list(range(head_size - 1))
    parts, last = [swap_slot(mixed[k + 1], k) for k in slots[:-1]], mixed[-1]
    if head_size == 4:
        last = call(relay_kernel, "relay", struct((rows, model), BF16), [(VMEM, last), (VMEM, parts[0])])
    parts = [mixed[0]] + parts + [swap_slot(last, slots[-1])]
    hidden, own_rows = call(
        rows_kernel,
        "rows",
        [struct((rows, model), BF16), struct((rows, wide), BF16)],
        [(ANY, up_held)] + [(VMEM, value) for value in (resid_held, gate_lanes, gain_held, *parts)],
    )

    def through_experts(members, carried=()):
        places = [at for at, _ in carried]
        return call(
            functools.partial(expert_kernel, experts, len(members), places),
            "experts",
            [struct((rows * (2 if at in places else 1), model), BF16) for at in range(len(members))],
            [(VMEM, value) for value in (up_held, down_held, other_up, other_down, *members)]
            + [(VMEM, value) for _, value in carried],
            megabytes=16,
        )

    both = ("head", "exp")
    group = [z * exp_size + 2 * d for z in (0, 1) for d in range(chips)][1:]

    def spread(block):
        return [block] + [swap(block, both, mask) for mask in group]

    sets = [spread(swap(own_rows, "head", high)) for high in range(2, head_size, 2)]
    near = through_experts(spread(own_rows))
    near, sets = lax.optimization_barrier((near, sets))
    joined = [at for at, mask in enumerate(group, 1) if mask >= exp_size]
    arrived, later = [], [at for at in range(1, len(near)) if at not in joined]
    apart = [near[at] for at in later]
    for high, members in zip(range(2, head_size, 2), sets):
        pieces = through_experts(members, [(at, near[at]) for at in joined] if high == 2 else ())
        got = [swap(piece, both, mask) for piece, mask in zip(pieces[:0:-1], group[::-1])]
        total = call(sum_kernel, "sum", struct((rows, model), BF16), [(VMEM, v) for v in (pieces[0], *got)])
        if high == 2:
            total, apart = lax.optimization_barrier((total, apart))
            arrived += [part for part, mask in zip(got, group[::-1]) if mask >= exp_size]
        arrived.append(swap(total, "head", high))
    arrived += [swap(piece, both, group[at - 1]) for piece, at in zip(apart, later)]
    return call(
        last_kernel,
        "last",
        struct(resid.shape, BF16),
        [(VMEM, value) for value in (hidden, near[0], *arrived)],
        pinned=False,
    )


def solution(mesh):
    placed = (
        P(("seq", "exp"), "head"),
        P(("seq", "exp"), "head"),
        P(("seq", "exp"), "head"),
        P(("seq", "exp"), "head"),
        P(("seq", "exp"), "head"),
        P("head"),
        P("head"),
        P("head"),
        P("head", None),
        P(("seq", "exp"), "head", None),
        P(("seq", "exp"), "head", None),
        P(("seq", "exp"), "head", None),
        P(),
        P(("head", "exp"), None, None),
        P(("head", "exp"), None, None),
    )
    return jax.shard_map(
        per_device,
        mesh=mesh,
        in_specs=placed,
        out_specs=P(("seq", "exp"), "head", None),
        check_vma=False,
    )
```

```python
import functools

import jax
import jax.numpy as jnp
from jax import lax
from jax.experimental import pallas as pl
from jax.experimental.pallas import tpu as pltpu
from jax.sharding import PartitionSpec as P

HEAD_DIM = 64
STATE = 128
LANES = 128
TILE = 16
FAR = -1e30
F32 = jnp.float32
BF16 = jnp.bfloat16
HBM = pl.BlockSpec(memory_space=pltpu.HBM)
VMEM = pl.BlockSpec(memory_space=pltpu.VMEM)
ANY = pl.BlockSpec(memory_space=pl.ANY)
NT = (((1,), (1,)), ((), ()))


def struct(shape, dtype):
    return jax.ShapeDtypeStruct(shape, dtype)


def call(kernel, name, outs, ins, scratch=(), megabytes=12, pinned=True):
    args = [pltpu.with_memory_space_constraint(arg, pltpu.HBM) if spec is HBM else arg for spec, arg in ins]
    return pl.pallas_call(
        kernel,
        out_shape=jax.tree.map(lambda out: pltpu.VMEM(out.shape, out.dtype), outs) if pinned else outs,
        in_specs=[spec for spec, _ in ins],
        out_specs=jax.tree.map(lambda _: VMEM, outs),
        scratch_shapes=list(scratch),
        name=name,
        compiler_params=pltpu.CompilerParams(vmem_limit_bytes=megabytes << 20),
    )(*args)


def offsets(count):
    down = list(range(count - 1, 0, -1))
    return [[3, 1, 2], [2, 3, 1]] if count == 4 else [down, down]


def targets(count):
    return [[1, 1, 2], [2, 3, 1]] if count == 4 else offsets(count)


def head_offset(slot, count):
    first, second = (order[slot] for order in offsets(count))
    return jnp.where(core_index() == 0, first, second)


def core_index():
    return lax.axis_index("exp") % 2


def chip_index():
    return lax.axis_index("exp") // 2


def copies(sems, sources, targets):
    made = [pltpu.make_async_copy(s, t, sems.at[i]) for i, (s, t) in enumerate(zip(sources, targets))]
    for copy in made:
        copy.start()
    return made


def decays(dt_rows, a_log):
    heads, length = dt_rows.shape
    step = jnp.maximum(dt_rows, 0.0) + jnp.log1p(jnp.exp(-jnp.abs(dt_rows)))
    same = lax.broadcasted_iota(jnp.int32, (heads, heads), 0) == lax.broadcasted_iota(jnp.int32, (heads, heads), 1)
    a_column = jnp.sum(jnp.where(same, jnp.broadcast_to(a_log, (heads, heads)), 0.0), axis=1, keepdims=True)
    rate = -step * jnp.exp(a_column)
    row = lax.broadcasted_iota(jnp.int32, (length, length), 0)
    col = lax.broadcasted_iota(jnp.int32, (length, length), 1)
    upper = (row <= col).astype(F32)
    cum = jnp.dot(rate, upper, precision=lax.Precision.HIGHEST, preferred_element_type=F32)
    return step, cum


def pair_lanes(values, pair):
    rows = values.shape[0]
    lane = lax.broadcasted_iota(jnp.int32, (rows, LANES), 1)
    left = jnp.broadcast_to(values[:, 2 * pair : 2 * pair + 1], (rows, LANES))
    right = jnp.broadcast_to(values[:, 2 * pair + 1 : 2 * pair + 2], (rows, LANES))
    return jnp.where(lane < HEAD_DIM, left, right)


def unpacked(block):
    pairs = block.shape[0] // STATE
    tail = block[pairs * STATE :].astype(F32)
    totals = [tail[pair : pair + 1] + tail[pairs + pair : pairs + pair + 1] for pair in range(pairs)]
    return jnp.stack(totals), block[: pairs * STATE].astype(F32).reshape(pairs, STATE, LANES)


def pack(ref, total, state):
    pairs = state.shape[0]
    ref[0 : pairs * STATE, :] = state.reshape(pairs * STATE, LANES).astype(BF16)
    row = lax.broadcasted_iota(jnp.int32, (TILE, LANES), 0)
    tail = jnp.zeros((TILE, LANES), F32)
    for pair in range(pairs):
        wide = jnp.broadcast_to(total[pair], (TILE, LANES))
        high = wide.astype(BF16).astype(F32)
        tail = jnp.where(row == pair, high, jnp.where(row == pairs + pair, wide - high, tail))
    ref[pairs * STATE :, :] = tail.astype(BF16)


def state_kernel(x_hbm, b_hbm, dt_hbm, a_hbm, keep_ref, send_ref, *scratch):
    x_ref, b_ref, dt_ref, a_ref, packed_ref, sems = scratch
    loads = copies(sems, (dt_hbm, a_hbm, x_hbm, b_hbm), (dt_ref, a_ref, x_ref, b_ref))
    loads[0].wait()
    loads[1].wait()
    step, cum = decays(dt_ref[...], a_ref[...])
    length = cum.shape[1]
    total = cum[:, length - 1 :]
    tail = (jnp.exp(total - cum) * step).T
    total = jnp.broadcast_to(total, cum.shape).T[0:1]
    loads[2].wait()
    loads[3].wait()
    pairs = x_ref.shape[1] // LANES
    half = pairs // 2
    groups = b_ref.shape[1] // STATE
    totals, states = [], []
    for group in range(groups):
        turned = b_ref[:, group * STATE : (group + 1) * STATE].T
        for pair in range(group * pairs // groups, (group + 1) * pairs // groups):
            x_pair = x_ref[:, pair * LANES : (pair + 1) * LANES].astype(F32)
            weighted = (pair_lanes(tail, pair) * x_pair).astype(BF16)
            state = jnp.dot(turned, weighted, preferred_element_type=F32)
            totals.append(pair_lanes(total, pair))
            states.append(state)
    for at in range(2):
        span = slice(at * half, (at + 1) * half)
        pack(packed_ref.at[at], totals[span], jnp.stack(states[span]))
    keep_ref[...] = packed_ref[core_index()]
    send_ref[...] = packed_ref[1 - core_index()]


def chip_state_kernel(after_ref, keep_ref, got_ref, *outs):
    first = core_index() == 0
    keep, got = unpacked(keep_ref[...]), unpacked(got_ref[...])
    early = [jnp.where(first, mine, other) for mine, other in zip(keep, got)]
    late = [jnp.where(first, other, mine) for mine, other in zip(keep, got)]
    total, state = early[0] + late[0], jnp.exp(late[0]) * early[1] + late[1]
    size = total.shape[0] // len(outs)
    for at, out in enumerate(outs):
        pack(out, total[at * size : (at + 1) * size], state[at * size : (at + 1) * size])


def weights_kernel(after_ref, up_hbm, down_hbm, up_ref, down_ref, sems):
    for load in copies(sems, (up_hbm, down_hbm), (up_ref, down_ref)):
        load.wait()


def span_kernel(after_ref, *rest):
    ins, out_ref, block_ref = rest[:-2], rest[-2], rest[-1]
    for mask, part in enumerate(ins):
        block_ref[chip_index() ^ mask] = part[...]
    total, state = unpacked(block_ref[0])
    for chip in range(1, len(ins)):
        here, own = unpacked(block_ref[chip])
        total, state = total + here, jnp.exp(here) * state + own
    pack(out_ref, total, state)


def before_kernel(chips, parts, after_ref, keep_ref, got_ref, *rest):
    ins, (mine_ref, send_ref, chip_ref, part_ref) = rest[:-4], rest[-4:]
    first = core_index() == 0
    totals, states = (jnp.where(first, k, g) for k, g in zip(unpacked(keep_ref[...]), unpacked(got_ref[...])))
    each = chips + parts
    chunks = len(ins) // each
    size = totals.shape[0] // chunks
    for chunk in range(chunks):
        span = slice(chunk * size, (chunk + 1) * size)
        for mask in range(chips):
            chip_ref[chip_index() ^ mask] = ins[chunk * each + mask][...]
        for mask in range(parts):
            part_ref[lax.axis_index("seq") ^ mask] = ins[chunk * each + chips + mask][...]
        carry = jnp.zeros(states[span].shape, F32)
        for ref, count, own in ((part_ref, parts, lax.axis_index("seq")), (chip_ref, chips, chip_index())):
            for index in range(count - 1):
                total, state = unpacked(ref[index])
                carry = jnp.where(index < own, jnp.exp(total) * carry + state, carry)
        later = jnp.exp(totals[span]) * carry + states[span]
        mine_ref[span] = jnp.where(first, carry, later).astype(BF16)
        send_ref[span] = jnp.where(first, later, carry).astype(BF16)


def inside_kernel(x_hbm, z_hbm, b_hbm, c_hbm, dt_hbm, a_hbm, d_hbm, local_ref, grown_ref, c_ref, *scratch):
    x_ref, z_ref, b_ref, dt_ref, a_ref, d_ref, sems = scratch
    loads = copies(
        sems,
        (dt_hbm, a_hbm, d_hbm, b_hbm, c_hbm, x_hbm, z_hbm),
        (dt_ref, a_ref, d_ref, b_ref, c_ref, x_ref, z_ref),
    )
    for load in loads:
        load.wait()
    step_rows, cum_rows = decays(dt_ref[...], a_ref[...])
    cum = cum_rows.T
    grown = jnp.exp(cum)
    length = cum.shape[0]
    pairs = x_ref.shape[1] // LANES
    groups = b_ref.shape[1] // STATE
    row = lax.broadcasted_iota(jnp.int32, (length, length), 0)
    col = lax.broadcasted_iota(jnp.int32, (length, length), 1)
    lane = lax.broadcasted_iota(jnp.int32, (length, LANES), 1)
    for group in range(groups):
        span = slice(group * STATE, (group + 1) * STATE)
        scores = lax.dot_general(c_ref[:, span], b_ref[:, span], NT, preferred_element_type=F32)
        scores = jnp.where(row >= col, scores, 0.0)
        for pair in range(group * pairs // groups, (group + 1) * pairs // groups):
            at = slice(pair * LANES, (pair + 1) * LANES)
            x_pair = x_ref[:, at]
            halves = []
            for head in (2 * pair, 2 * pair + 1):
                distance = cum[:, head : head + 1] - cum_rows[head : head + 1, :]
                decay = jnp.exp(jnp.where(row >= col, distance, FAR))
                mixing = (scores * (decay * step_rows[head : head + 1, :])).astype(BF16)
                halves.append(jnp.dot(mixing, x_pair, preferred_element_type=F32))
            inside = jnp.where(lane < HEAD_DIM, halves[0], halves[1])
            skip = pair_lanes(d_ref[...], pair) * x_pair.astype(F32)
            z = z_ref[:, at].astype(F32)
            gate = z / (1.0 + jnp.exp(-z))
            local_ref[:, at] = (inside + skip) * gate
            grown_ref[:, at] = pair_lanes(grown, pair) * gate


def projection_kernel(norm_hbm, w_hbm, norm_ref, w_ref, sems):
    for load in copies(sems, (norm_hbm, w_hbm), (norm_ref, w_ref)):
        load.wait()


def prep_kernel(experts, width, after_ref, resid_hbm, routes_hbm, gates_hbm, gain_hbm, *rest):
    gate_ref, resid_ref, gain_ref, routes_ref, gates_ref, sems = rest
    loads = copies(
        sems,
        (routes_hbm, gates_hbm, resid_hbm, gain_hbm),
        (routes_ref, gates_ref, resid_ref, gain_ref.at[0]),
    )
    loads[0].wait()
    loads[1].wait()
    count, extent = gate_ref.shape
    start = width // LANES * LANES
    lane = lax.broadcasted_iota(jnp.int32, (extent, count), 0) + start - width
    expert = jnp.where(lane >= experts, lane - experts, lane)
    gate = jnp.zeros((extent, count), F32)
    for pick in range(routes_ref.shape[0]):
        gate = gate + jnp.where(routes_ref[pick] == expert, gates_ref[pick], 0.0)
    high = gate.astype(BF16).astype(F32)
    gate = jnp.where(lane < experts, high, jnp.where(lane < 2 * experts, gate - high, 0.0))
    gate_ref[...] = gate.T.astype(BF16)
    for load in loads[2:]:
        load.wait()


def half_product(half, local_ref, grown_ref, c_ref, norm_ref, w_ref, state_ref, normed_ref, count):
    pairs = state_ref.shape[0]
    width = pairs * LANES
    base = pl.multiple_of(half * width, width)
    groups = c_ref.shape[1] // STATE // 2
    per_group = pairs // groups
    for group in range(groups):
        c_group = c_ref[:, pl.ds(pl.multiple_of((half * groups + group) * STATE, STATE), STATE)]
        gated, squares = [], 0.0
        for pair in range(group * per_group, (group + 1) * per_group):
            span = pl.ds(pl.multiple_of(base + pair * LANES, LANES), LANES)
            carried = jnp.dot(c_group, state_ref[pair], preferred_element_type=F32)
            value = local_ref[:, span] + grown_ref[:, span] * carried
            gated.append(value)
            squares = squares + value * value
        mean = jnp.sum(squares, axis=1, keepdims=True) / (per_group * LANES)
        inverse = lax.rsqrt(mean + 1e-05)
        for offset, value in enumerate(gated):
            pair = group * per_group + offset
            gain = norm_ref[:, pl.ds(pl.multiple_of(base + pair * LANES, LANES), LANES)]
            normed_ref[:, pair * LANES : (pair + 1) * LANES] = (value * inverse * gain).astype(BF16)
    rows = normed_ref.shape[0] // count
    blocks = []
    for shift in range(count):
        owner = lax.axis_index("head") ^ (head_offset(shift - 1, count) if shift else 0)
        blocks.append(normed_ref[pl.ds(pl.multiple_of(owner * rows, rows), rows), :])
    weight = w_ref[:, pl.ds(base, width)]
    return lax.dot_general(jnp.concatenate(blocks, axis=0), weight, NT, preferred_element_type=F32)


def first_half_kernel(count, local_ref, grown_ref, c_ref, norm_ref, w_ref, mine_ref, out_ref, normed_ref):
    out_ref[...] = half_product(
        core_index(), local_ref, grown_ref, c_ref, norm_ref, w_ref, mine_ref, normed_ref, count
    )


def mixed_kernel(after_up, after_down, local_ref, grown_ref, c_ref, norm_ref, w_ref, got_ref, first_ref, *rest):
    outs, normed_ref = rest[:-1], rest[-1]
    product = first_ref[...] + half_product(
        1 - core_index(), local_ref, grown_ref, c_ref, norm_ref, w_ref, got_ref, normed_ref, len(outs)
    )
    rows = outs[0].shape[0]
    for shift, out in enumerate(outs):
        out[...] = product[shift * rows : (shift + 1) * rows].astype(BF16)


def relay_kernel(own_ref, got_ref, out_ref):
    got = jnp.where(core_index() == 0, got_ref[...].astype(F32), 0.0)
    out_ref[...] = (own_ref[...].astype(F32) + got).astype(BF16)


def rows_kernel(after_ref, resid_ref, gate_ref, gain_ref, *rest):
    parts, hidden_ref, rows_ref = rest[:-2], rest[-2], rest[-1]
    mixed = parts[0][...].astype(F32)
    for at, part in enumerate(parts[1:]):
        value = part[...].astype(F32)
        if at == 0 and len(parts) == 4:
            value = jnp.where(core_index() == 1, value, 0.0)
        mixed = mixed + value
    hidden = (resid_ref[0].astype(F32) + mixed).astype(BF16)
    hidden_ref[...] = hidden
    value = hidden.astype(F32)
    scale = lax.rsqrt(jnp.mean(value * value, axis=1, keepdims=True) + 1e-05)
    width = value.shape[1]
    rows_ref[:, width // LANES * LANES :] = gate_ref[...]
    rows_ref[:, :width] = (value * scale * gain_ref[...]).astype(BF16)


def expert_kernel(experts, count, up_ref, down_ref, other_up_ref, other_down_ref, *rest):
    ins, outs = rest[:count], rest[count:]
    width = up_ref.shape[2]
    start = width // LANES * LANES
    rows = jnp.concatenate([ref[:, :width] for ref in ins], axis=0)
    tail = jnp.concatenate([ref[:, start:] for ref in ins], axis=0).astype(F32)
    lane = lax.broadcasted_iota(jnp.int32, tail.shape, 1) + start - width
    own = lax.axis_index("head") * lax.axis_size("exp") + lax.axis_index("exp")
    other = own + 1 - 2 * core_index()
    total = 0.0
    for expert, up_of, down_of in ((own, up_ref, down_ref), (other, other_up_ref, other_down_ref)):
        up = lax.dot_general(rows, up_of[0], NT, preferred_element_type=F32)
        up = jnp.maximum(up, 0.0)
        activated = (up * up).astype(BF16)
        chosen = (lane == expert) | (lane == expert + experts)
        gate = jnp.sum(jnp.where(chosen, tail, 0.0), axis=1, keepdims=True)
        total = total + jnp.dot(activated, down_of[0], preferred_element_type=F32) * gate
    size = ins[0].shape[0]
    for at, out in enumerate(outs):
        out[...] = total[at * size : (at + 1) * size].astype(BF16)


def sum_kernel(*refs):
    total = refs[0][...].astype(F32)
    for ref in refs[1:-1]:
        total = total + ref[...].astype(F32)
    refs[-1][...] = total.astype(BF16)


def last_kernel(hidden_ref, *rest):
    parts, out_ref = rest[:-1], rest[-1]
    total = parts[0][...].astype(F32)
    for part in parts[1:]:
        total = total + part[...].astype(F32)
    out_ref[0] = (hidden_ref[...].astype(F32) + total).astype(BF16)


def swap(value, axis, mask):
    size = lax.axis_size(axis)
    return lax.ppermute(value, axis, [(i, i ^ mask) for i in range(size)])


def swap_slot(value, slot):
    heads, size = lax.axis_size("head"), lax.axis_size("exp")
    order = targets(heads)
    pairs = []
    for i in range(heads * size):
        head, exp = i // size, i % size
        pairs.append((i, (head ^ order[exp % 2][slot]) * size + exp))
    return lax.ppermute(value, ("head", "exp"), pairs)


def per_device(
    x_in, z_in, b_in, c_in, dt_in, a_log, d_skip, norm_w, w_out, resid, routes, gates, moe_gain, w_up, w_down
):
    length, heads = dt_in.shape
    channels = x_in.shape[1]
    model = w_out.shape[1]
    hidden_units = w_up.shape[2]
    seq_size, head_size, exp_size = lax.axis_size("seq"), lax.axis_size("head"), lax.axis_size("exp")
    chips = exp_size // 2
    rows = resid.shape[1]
    experts = head_size * exp_size
    pairs = channels // LANES
    half = pairs // 2
    dt_rows, a_row, d_row = dt_in.T, a_log[None], d_skip[None]
    dma = pltpu.SemaphoreType.DMA
    packed = struct((half * STATE + TILE, LANES), BF16)

    keep, send = call(
        state_kernel,
        "state",
        [packed, packed],
        [(HBM, x_in), (HBM, b_in), (HBM, dt_rows), (HBM, a_row)],
        [pltpu.VMEM(x_in.shape, BF16), pltpu.VMEM(b_in.shape, BF16), pltpu.VMEM(dt_rows.shape, F32),
         pltpu.VMEM(a_row.shape, F32), pltpu.VMEM((2, half * STATE + TILE, LANES), BF16), dma((4,))],
        megabytes=16,
    )
    local, grown, c_held = call(
        inside_kernel,
        "inside",
        [struct((length, channels), F32), struct((length, channels), F32), struct(c_in.shape, BF16)],
        [(HBM, value) for value in (x_in, z_in, b_in, c_in, dt_rows, a_row, d_row)],
        [pltpu.VMEM(x_in.shape, BF16), pltpu.VMEM(z_in.shape, BF16), pltpu.VMEM(b_in.shape, BF16),
         pltpu.VMEM(dt_rows.shape, F32), pltpu.VMEM(a_row.shape, F32), pltpu.VMEM(d_row.shape, F32), dma((7,))],
        megabytes=16,
    )
    wide = -(-(model + 2 * experts) // LANES) * LANES
    turned = [jnp.transpose(value, (2, 0, 1)) for value in (routes, gates)]
    norm_held, w_held = call(
        projection_kernel,
        "projection",
        [struct((1, channels), F32), struct((model, channels), BF16)],
        [(HBM, norm_w[None]), (HBM, w_out.T)],
        [dma((2,))],
    )
    gate_lanes, resid_held, gain_held = call(
        functools.partial(prep_kernel, experts, model),
        "prep",
        [struct((rows, wide - model // LANES * LANES), BF16), struct(resid.shape, BF16), struct((1, model), F32)],
        [(ANY, keep)] + [(HBM, value) for value in (resid, *turned, moe_gain)],
        [pltpu.VMEM(turned[0].shape, jnp.int32), pltpu.VMEM(turned[1].shape, F32), dma((4,))],
        megabytes=16,
    )
    up_turned = jnp.swapaxes(w_up, 1, 2)
    got = swap(send, "exp", 1)
    chunks = 2 if half % 2 == 0 else 1
    packed = struct((half // chunks * STATE + TILE, LANES), BF16)
    chip = call(chip_state_kernel, "chip_state", [packed] * chunks, [(ANY, gate_lanes), (VMEM, keep), (VMEM, got)])
    chip, up_after, down_after = lax.optimization_barrier((chip, up_turned, w_down))
    other_up, other_down = swap(up_after, "exp", 1), swap(down_after, "exp", 1)
    exchanged = []
    for own in chip:
        along_y = [own] + [swap(own, "exp", 2 * d) for d in range(1, chips)]
        span = call(
            span_kernel,
            "span",
            packed,
            [(ANY, c_held)] + [(VMEM, value) for value in along_y],
            [pltpu.VMEM((chips, *packed.shape), BF16)],
        )
        exchanged += along_y + [span] + [swap(span, "seq", d) for d in range(1, seq_size)]
    before, before_send = call(
        functools.partial(before_kernel, chips, seq_size),
        "before",
        [struct((half, STATE, LANES), BF16)] * 2,
        [(ANY, norm_held)] + [(VMEM, value) for value in (keep, got, *exchanged)],
        [pltpu.VMEM((chips, *packed.shape), BF16), pltpu.VMEM((seq_size, *packed.shape), BF16)],
        megabytes=24,
    )
    before_got = swap(before_send, "exp", 1)
    shared = [(VMEM, value) for value in (local, grown, c_held, norm_held, w_held)]
    normed_half = pltpu.VMEM((length, channels // 2), BF16)
    first = call(
        functools.partial(first_half_kernel, head_size),
        "first_half",
        struct((length, model), F32),
        shared + [(VMEM, before)],
        [normed_half],
    )
    mixed = call(
        mixed_kernel,
        "mixed",
        [struct((rows, model), BF16)] * head_size,
        [(ANY, other_up), (ANY, other_down)] + shared + [(VMEM, before_got), (VMEM, first)],
        [normed_half],
    )
    up_held, down_held = call(
        weights_kernel,
        "weights",
        [struct(up_turned.shape, BF16), struct(w_down.shape, BF16)],
        [(ANY, mixed[0]), (HBM, up_turned), (HBM, w_down)],
        [dma((2,))],
    )
    slots = list(range(head_size - 1))
    parts, last = [swap_slot(mixed[k + 1], k) for k in slots[:-1]], mixed[-1]
    if head_size == 4:
        last = call(relay_kernel, "relay", struct((rows, model), BF16), [(VMEM, last), (VMEM, parts[0])])
    parts = [mixed[0]] + parts + [swap_slot(last, slots[-1])]
    hidden, own_rows = call(
        rows_kernel,
        "rows",
        [struct((rows, model), BF16), struct((rows, wide), BF16)],
        [(ANY, up_held)] + [(VMEM, value) for value in (resid_held, gate_lanes, gain_held, *parts)],
    )

    def through_experts(members):
        return call(
            functools.partial(expert_kernel, experts, len(members)),
            "experts",
            [struct((rows, model), BF16)] * len(members),
            [(VMEM, value) for value in (up_held, down_held, other_up, other_down, *members)],
            megabytes=16,
        )

    both = ("head", "exp")
    group = [z * exp_size + 2 * d for z in (0, 1) for d in range(chips)][1:]

    def spread(block):
        return [block] + [swap(block, both, mask) for mask in group]

    sets = [spread(swap(own_rows, "head", high)) for high in range(2, head_size, 2)]
    near = through_experts(spread(own_rows))
    near, sets = lax.optimization_barrier((near, sets))
    arrived = []
    for high, members in zip(range(2, head_size, 2), sets):
        pieces = through_experts(members)
        got = [swap(piece, both, mask) for piece, mask in zip(pieces[:0:-1], group[::-1])]
        total = call(sum_kernel, "sum", struct((rows, model), BF16), [(VMEM, v) for v in (pieces[0], *got)])
        arrived.append(swap(total, "head", high))
    arrived += [swap(piece, both, mask) for piece, mask in zip(near[:0:-1], group[::-1])]
    return call(
        last_kernel,
        "last",
        struct(resid.shape, BF16),
        [(VMEM, value) for value in (hidden, near[0], *arrived)],
        pinned=False,
    )


def solution(mesh):
    placed = (
        P(("seq", "exp"), "head"),
        P(("seq", "exp"), "head"),
        P(("seq", "exp"), "head"),
        P(("seq", "exp"), "head"),
        P(("seq", "exp"), "head"),
        P("head"),
        P("head"),
        P("head"),
        P("head", None),
        P(("seq", "exp"), "head", None),
        P(("seq", "exp"), "head", None),
        P(("seq", "exp"), "head", None),
        P(),
        P(("head", "exp"), None, None),
        P(("head", "exp"), None, None),
    )
    return jax.shard_map(
        per_device,
        mesh=mesh,
        in_specs=placed,
        out_specs=P(("seq", "exp"), "head", None),
        check_vma=False,
    )
```

```python
import functools

import jax
import jax.numpy as jnp
from jax import lax
from jax.experimental import pallas as pl
from jax.experimental.pallas import tpu as pltpu
from jax.sharding import PartitionSpec as P

HEAD_DIM = 64
STATE = 128
LANES = 128
TILE = 16
FAR = -1e30
F32 = jnp.float32
BF16 = jnp.bfloat16
HBM = pl.BlockSpec(memory_space=pltpu.HBM)
VMEM = pl.BlockSpec(memory_space=pltpu.VMEM)
ANY = pl.BlockSpec(memory_space=pl.ANY)
NT = (((1,), (1,)), ((), ()))


def struct(shape, dtype):
    return jax.ShapeDtypeStruct(shape, dtype)


def call(kernel, name, outs, ins, scratch=(), megabytes=12, pinned=True):
    args = [pltpu.with_memory_space_constraint(arg, pltpu.HBM) if spec is HBM else arg for spec, arg in ins]
    return pl.pallas_call(
        kernel,
        out_shape=jax.tree.map(lambda out: pltpu.VMEM(out.shape, out.dtype), outs) if pinned else outs,
        in_specs=[spec for spec, _ in ins],
        out_specs=jax.tree.map(lambda _: VMEM, outs),
        scratch_shapes=list(scratch),
        name=name,
        compiler_params=pltpu.CompilerParams(vmem_limit_bytes=megabytes << 20),
    )(*args)


def offsets(count):
    down = list(range(count - 1, 0, -1))
    return [[3, 1, 2], [2, 3, 1]] if count == 4 else [down, down]


def targets(count):
    return [[1, 1, 2], [2, 3, 1]] if count == 4 else offsets(count)


def head_offset(slot, count):
    first, second = (order[slot] for order in offsets(count))
    return jnp.where(core_index() == 0, first, second)


def core_index():
    return lax.axis_index("exp") % 2


def chip_index():
    return lax.axis_index("exp") // 2


def copies(sems, sources, targets):
    made = [pltpu.make_async_copy(s, t, sems.at[i]) for i, (s, t) in enumerate(zip(sources, targets))]
    for copy in made:
        copy.start()
    return made


def decays(dt_rows, a_log):
    heads, length = dt_rows.shape
    step = jnp.maximum(dt_rows, 0.0) + jnp.log1p(jnp.exp(-jnp.abs(dt_rows)))
    same = lax.broadcasted_iota(jnp.int32, (heads, heads), 0) == lax.broadcasted_iota(jnp.int32, (heads, heads), 1)
    a_column = jnp.sum(jnp.where(same, jnp.broadcast_to(a_log, (heads, heads)), 0.0), axis=1, keepdims=True)
    rate = -step * jnp.exp(a_column)
    row = lax.broadcasted_iota(jnp.int32, (length, length), 0)
    col = lax.broadcasted_iota(jnp.int32, (length, length), 1)
    upper = (row <= col).astype(F32)
    cum = jnp.dot(rate, upper, precision=lax.Precision.HIGHEST, preferred_element_type=F32)
    return step, cum


def pair_lanes(values, pair):
    rows = values.shape[0]
    lane = lax.broadcasted_iota(jnp.int32, (rows, LANES), 1)
    left = jnp.broadcast_to(values[:, 2 * pair : 2 * pair + 1], (rows, LANES))
    right = jnp.broadcast_to(values[:, 2 * pair + 1 : 2 * pair + 2], (rows, LANES))
    return jnp.where(lane < HEAD_DIM, left, right)


def unpacked(block):
    pairs = block.shape[0] // STATE
    tail = block[pairs * STATE :].astype(F32)
    totals = [tail[pair : pair + 1] + tail[pairs + pair : pairs + pair + 1] for pair in range(pairs)]
    return jnp.stack(totals), block[: pairs * STATE].astype(F32).reshape(pairs, STATE, LANES)


def pack(ref, total, state):
    pairs = state.shape[0]
    ref[0 : pairs * STATE, :] = state.reshape(pairs * STATE, LANES).astype(BF16)
    row = lax.broadcasted_iota(jnp.int32, (TILE, LANES), 0)
    tail = jnp.zeros((TILE, LANES), F32)
    for pair in range(pairs):
        wide = jnp.broadcast_to(total[pair], (TILE, LANES))
        high = wide.astype(BF16).astype(F32)
        tail = jnp.where(row == pair, high, jnp.where(row == pairs + pair, wide - high, tail))
    ref[pairs * STATE :, :] = tail.astype(BF16)


def state_kernel(x_hbm, b_hbm, dt_hbm, a_hbm, keep_ref, send_ref, *scratch):
    x_ref, b_ref, dt_ref, a_ref, packed_ref, sems = scratch
    loads = copies(sems, (dt_hbm, a_hbm, x_hbm, b_hbm), (dt_ref, a_ref, x_ref, b_ref))
    loads[0].wait()
    loads[1].wait()
    step, cum = decays(dt_ref[...], a_ref[...])
    length = cum.shape[1]
    total = cum[:, length - 1 :]
    tail = (jnp.exp(total - cum) * step).T
    total = jnp.broadcast_to(total, cum.shape).T[0:1]
    loads[2].wait()
    loads[3].wait()
    pairs = x_ref.shape[1] // LANES
    half = pairs // 2
    groups = b_ref.shape[1] // STATE
    totals, states = [], []
    for group in range(groups):
        turned = b_ref[:, group * STATE : (group + 1) * STATE].T
        for pair in range(group * pairs // groups, (group + 1) * pairs // groups):
            x_pair = x_ref[:, pair * LANES : (pair + 1) * LANES].astype(F32)
            weighted = (pair_lanes(tail, pair) * x_pair).astype(BF16)
            state = jnp.dot(turned, weighted, preferred_element_type=F32)
            totals.append(pair_lanes(total, pair))
            states.append(state)
    for at in range(2):
        span = slice(at * half, (at + 1) * half)
        pack(packed_ref.at[at], totals[span], jnp.stack(states[span]))
    keep_ref[...] = packed_ref[core_index()]
    send_ref[...] = packed_ref[1 - core_index()]


def chip_state_kernel(after_ref, keep_ref, got_ref, *outs):
    first = core_index() == 0
    keep, got = unpacked(keep_ref[...]), unpacked(got_ref[...])
    early = [jnp.where(first, mine, other) for mine, other in zip(keep, got)]
    late = [jnp.where(first, other, mine) for mine, other in zip(keep, got)]
    total, state = early[0] + late[0], jnp.exp(late[0]) * early[1] + late[1]
    size = total.shape[0] // len(outs)
    for at, out in enumerate(outs):
        pack(out, total[at * size : (at + 1) * size], state[at * size : (at + 1) * size])


def weights_kernel(after_ref, up_hbm, down_hbm, up_ref, down_ref, sems):
    for load in copies(sems, (up_hbm, down_hbm), (up_ref, down_ref)):
        load.wait()


def span_kernel(after_ref, *rest):
    ins, out_ref, block_ref = rest[:-2], rest[-2], rest[-1]
    for mask, part in enumerate(ins):
        block_ref[chip_index() ^ mask] = part[...]
    total, state = unpacked(block_ref[0])
    for chip in range(1, len(ins)):
        here, own = unpacked(block_ref[chip])
        total, state = total + here, jnp.exp(here) * state + own
    pack(out_ref, total, state)


def before_kernel(chips, parts, after_ref, keep_ref, got_ref, *rest):
    ins, (mine_ref, send_ref, chip_ref, part_ref) = rest[:-4], rest[-4:]
    first = core_index() == 0
    totals, states = (jnp.where(first, k, g) for k, g in zip(unpacked(keep_ref[...]), unpacked(got_ref[...])))
    each = chips + parts
    chunks = len(ins) // each
    size = totals.shape[0] // chunks
    for chunk in range(chunks):
        span = slice(chunk * size, (chunk + 1) * size)
        for mask in range(chips):
            chip_ref[chip_index() ^ mask] = ins[chunk * each + mask][...]
        for mask in range(parts):
            part_ref[lax.axis_index("seq") ^ mask] = ins[chunk * each + chips + mask][...]
        carry = jnp.zeros(states[span].shape, F32)
        for ref, count, own in ((part_ref, parts, lax.axis_index("seq")), (chip_ref, chips, chip_index())):
            for index in range(count - 1):
                total, state = unpacked(ref[index])
                carry = jnp.where(index < own, jnp.exp(total) * carry + state, carry)
        later = jnp.exp(totals[span]) * carry + states[span]
        mine_ref[span] = jnp.where(first, carry, later).astype(BF16)
        send_ref[span] = jnp.where(first, later, carry).astype(BF16)


def inside_kernel(x_hbm, z_hbm, b_hbm, c_hbm, dt_hbm, a_hbm, d_hbm, local_ref, grown_ref, c_ref, *scratch):
    x_ref, z_ref, b_ref, dt_ref, a_ref, d_ref, sems = scratch
    loads = copies(
        sems,
        (dt_hbm, a_hbm, d_hbm, b_hbm, c_hbm, x_hbm, z_hbm),
        (dt_ref, a_ref, d_ref, b_ref, c_ref, x_ref, z_ref),
    )
    for load in loads:
        load.wait()
    step_rows, cum_rows = decays(dt_ref[...], a_ref[...])
    cum = cum_rows.T
    grown = jnp.exp(cum)
    length = cum.shape[0]
    pairs = x_ref.shape[1] // LANES
    groups = b_ref.shape[1] // STATE
    row = lax.broadcasted_iota(jnp.int32, (length, length), 0)
    col = lax.broadcasted_iota(jnp.int32, (length, length), 1)
    lane = lax.broadcasted_iota(jnp.int32, (length, LANES), 1)
    for group in range(groups):
        span = slice(group * STATE, (group + 1) * STATE)
        scores = lax.dot_general(c_ref[:, span], b_ref[:, span], NT, preferred_element_type=F32)
        scores = jnp.where(row >= col, scores, 0.0)
        for pair in range(group * pairs // groups, (group + 1) * pairs // groups):
            at = slice(pair * LANES, (pair + 1) * LANES)
            x_pair = x_ref[:, at]
            halves = []
            for head in (2 * pair, 2 * pair + 1):
                distance = cum[:, head : head + 1] - cum_rows[head : head + 1, :]
                decay = jnp.exp(jnp.where(row >= col, distance, FAR))
                mixing = (scores * (decay * step_rows[head : head + 1, :])).astype(BF16)
                halves.append(jnp.dot(mixing, x_pair, preferred_element_type=F32))
            inside = jnp.where(lane < HEAD_DIM, halves[0], halves[1])
            skip = pair_lanes(d_ref[...], pair) * x_pair.astype(F32)
            z = z_ref[:, at].astype(F32)
            gate = z / (1.0 + jnp.exp(-z))
            local_ref[:, at] = (inside + skip) * gate
            grown_ref[:, at] = pair_lanes(grown, pair) * gate


def projection_kernel(norm_hbm, w_hbm, norm_ref, w_ref, sems):
    for load in copies(sems, (norm_hbm, w_hbm), (norm_ref, w_ref)):
        load.wait()


def prep_kernel(experts, width, after_ref, resid_hbm, routes_hbm, gates_hbm, gain_hbm, *rest):
    gate_ref, resid_ref, gain_ref, routes_ref, gates_ref, sems = rest
    loads = copies(
        sems,
        (routes_hbm, gates_hbm, resid_hbm, gain_hbm),
        (routes_ref, gates_ref, resid_ref, gain_ref.at[0]),
    )
    loads[0].wait()
    loads[1].wait()
    count, extent = gate_ref.shape
    start = width // LANES * LANES
    lane = lax.broadcasted_iota(jnp.int32, (extent, count), 0) + start - width
    expert = jnp.where(lane >= experts, lane - experts, lane)
    gate = jnp.zeros((extent, count), F32)
    for pick in range(routes_ref.shape[0]):
        gate = gate + jnp.where(routes_ref[pick] == expert, gates_ref[pick], 0.0)
    high = gate.astype(BF16).astype(F32)
    gate = jnp.where(lane < experts, high, jnp.where(lane < 2 * experts, gate - high, 0.0))
    gate_ref[...] = gate.T.astype(BF16)
    for load in loads[2:]:
        load.wait()


def half_product(half, local_ref, grown_ref, c_ref, norm_ref, w_ref, state_ref, normed_ref, count):
    pairs = state_ref.shape[0]
    width = pairs * LANES
    base = pl.multiple_of(half * width, width)
    groups = c_ref.shape[1] // STATE // 2
    per_group = pairs // groups
    for group in range(groups):
        c_group = c_ref[:, pl.ds(pl.multiple_of((half * groups + group) * STATE, STATE), STATE)]
        gated, squares = [], 0.0
        for pair in range(group * per_group, (group + 1) * per_group):
            span = pl.ds(pl.multiple_of(base + pair * LANES, LANES), LANES)
            carried = jnp.dot(c_group, state_ref[pair], preferred_element_type=F32)
            value = local_ref[:, span] + grown_ref[:, span] * carried
            gated.append(value)
            squares = squares + value * value
        mean = jnp.sum(squares, axis=1, keepdims=True) / (per_group * LANES)
        inverse = lax.rsqrt(mean + 1e-05)
        for offset, value in enumerate(gated):
            pair = group * per_group + offset
            gain = norm_ref[:, pl.ds(pl.multiple_of(base + pair * LANES, LANES), LANES)]
            normed_ref[:, pair * LANES : (pair + 1) * LANES] = (value * inverse * gain).astype(BF16)
    rows = normed_ref.shape[0] // count
    blocks = []
    for shift in range(count):
        owner = lax.axis_index("head") ^ (head_offset(shift - 1, count) if shift else 0)
        blocks.append(normed_ref[pl.ds(pl.multiple_of(owner * rows, rows), rows), :])
    weight = w_ref[:, pl.ds(base, width)]
    return lax.dot_general(jnp.concatenate(blocks, axis=0), weight, NT, preferred_element_type=F32)


def first_half_kernel(count, local_ref, grown_ref, c_ref, norm_ref, w_ref, mine_ref, out_ref, normed_ref):
    out_ref[...] = half_product(
        core_index(), local_ref, grown_ref, c_ref, norm_ref, w_ref, mine_ref, normed_ref, count
    )


def mixed_kernel(after_up, after_down, local_ref, grown_ref, c_ref, norm_ref, w_ref, got_ref, first_ref, *rest):
    outs, normed_ref = rest[:-1], rest[-1]
    product = first_ref[...] + half_product(
        1 - core_index(), local_ref, grown_ref, c_ref, norm_ref, w_ref, got_ref, normed_ref, len(outs)
    )
    rows = outs[0].shape[0]
    for shift, out in enumerate(outs):
        out[...] = product[shift * rows : (shift + 1) * rows].astype(BF16)


def relay_kernel(own_ref, got_ref, out_ref):
    got = jnp.where(core_index() == 0, got_ref[...].astype(F32), 0.0)
    out_ref[...] = (own_ref[...].astype(F32) + got).astype(BF16)


def rows_kernel(after_ref, resid_ref, gate_ref, gain_ref, *rest):
    parts, hidden_ref, rows_ref = rest[:-2], rest[-2], rest[-1]
    mixed = parts[0][...].astype(F32)
    for at, part in enumerate(parts[1:]):
        value = part[...].astype(F32)
        if at == 0 and len(parts) == 4:
            value = jnp.where(core_index() == 1, value, 0.0)
        mixed = mixed + value
    hidden = (resid_ref[0].astype(F32) + mixed).astype(BF16)
    hidden_ref[...] = hidden
    value = hidden.astype(F32)
    scale = lax.rsqrt(jnp.mean(value * value, axis=1, keepdims=True) + 1e-05)
    width = value.shape[1]
    rows_ref[:, width // LANES * LANES :] = gate_ref[...]
    rows_ref[:, :width] = (value * scale * gain_ref[...]).astype(BF16)


def expert_kernel(experts, count, up_ref, down_ref, other_up_ref, other_down_ref, *rest):
    ins, outs = rest[:count], rest[count:]
    width = up_ref.shape[2]
    start = width // LANES * LANES
    rows = jnp.concatenate([ref[:, :width] for ref in ins], axis=0)
    tail = jnp.concatenate([ref[:, start:] for ref in ins], axis=0).astype(F32)
    lane = lax.broadcasted_iota(jnp.int32, tail.shape, 1) + start - width
    own = lax.axis_index("head") * lax.axis_size("exp") + lax.axis_index("exp")
    other = own + 1 - 2 * core_index()
    total = 0.0
    for expert, up_of, down_of in ((own, up_ref, down_ref), (other, other_up_ref, other_down_ref)):
        up = lax.dot_general(rows, up_of[0], NT, preferred_element_type=F32)
        up = jnp.maximum(up, 0.0)
        activated = (up * up).astype(BF16)
        chosen = (lane == expert) | (lane == expert + experts)
        gate = jnp.sum(jnp.where(chosen, tail, 0.0), axis=1, keepdims=True)
        total = total + jnp.dot(activated, down_of[0], preferred_element_type=F32) * gate
    at = 0
    for out in outs:
        out[...] = total[at : at + out.shape[0]].astype(BF16)
        at += out.shape[0]


def sum_kernel(block, own_ref, *rest):
    parts, out_ref = rest[:-1], rest[-1]
    rows = out_ref.shape[0]
    total = own_ref[...].astype(F32)
    for part in parts:
        total = total + part[block * rows : (block + 1) * rows].astype(F32)
    out_ref[...] = total.astype(BF16)


def last_kernel(hidden_ref, *rest):
    parts, out_ref = rest[:-1], rest[-1]
    total = parts[0][...].astype(F32)
    for part in parts[1:]:
        total = total + part[...].astype(F32)
    out_ref[0] = (hidden_ref[...].astype(F32) + total).astype(BF16)


def swap(value, axis, mask):
    size = lax.axis_size(axis)
    return lax.ppermute(value, axis, [(i, i ^ mask) for i in range(size)])


def swap_slot(value, slot):
    heads, size = lax.axis_size("head"), lax.axis_size("exp")
    order = targets(heads)
    pairs = []
    for i in range(heads * size):
        head, exp = i // size, i % size
        pairs.append((i, (head ^ order[exp % 2][slot]) * size + exp))
    return lax.ppermute(value, ("head", "exp"), pairs)


def per_device(
    x_in, z_in, b_in, c_in, dt_in, a_log, d_skip, norm_w, w_out, resid, routes, gates, moe_gain, w_up, w_down
):
    length, heads = dt_in.shape
    channels = x_in.shape[1]
    model = w_out.shape[1]
    hidden_units = w_up.shape[2]
    seq_size, head_size, exp_size = lax.axis_size("seq"), lax.axis_size("head"), lax.axis_size("exp")
    chips = exp_size // 2
    rows = resid.shape[1]
    experts = head_size * exp_size
    pairs = channels // LANES
    half = pairs // 2
    dt_rows, a_row, d_row = dt_in.T, a_log[None], d_skip[None]
    dma = pltpu.SemaphoreType.DMA
    packed = struct((half * STATE + TILE, LANES), BF16)

    keep, send = call(
        state_kernel,
        "state",
        [packed, packed],
        [(HBM, x_in), (HBM, b_in), (HBM, dt_rows), (HBM, a_row)],
        [pltpu.VMEM(x_in.shape, BF16), pltpu.VMEM(b_in.shape, BF16), pltpu.VMEM(dt_rows.shape, F32),
         pltpu.VMEM(a_row.shape, F32), pltpu.VMEM((2, half * STATE + TILE, LANES), BF16), dma((4,))],
        megabytes=16,
    )
    local, grown, c_held = call(
        inside_kernel,
        "inside",
        [struct((length, channels), F32), struct((length, channels), F32), struct(c_in.shape, BF16)],
        [(HBM, value) for value in (x_in, z_in, b_in, c_in, dt_rows, a_row, d_row)],
        [pltpu.VMEM(x_in.shape, BF16), pltpu.VMEM(z_in.shape, BF16), pltpu.VMEM(b_in.shape, BF16),
         pltpu.VMEM(dt_rows.shape, F32), pltpu.VMEM(a_row.shape, F32), pltpu.VMEM(d_row.shape, F32), dma((7,))],
        megabytes=16,
    )
    wide = -(-(model + 2 * experts) // LANES) * LANES
    turned = [jnp.transpose(value, (2, 0, 1)) for value in (routes, gates)]
    norm_held, w_held = call(
        projection_kernel,
        "projection",
        [struct((1, channels), F32), struct((model, channels), BF16)],
        [(HBM, norm_w[None]), (HBM, w_out.T)],
        [dma((2,))],
    )
    gate_lanes, resid_held, gain_held = call(
        functools.partial(prep_kernel, experts, model),
        "prep",
        [struct((rows, wide - model // LANES * LANES), BF16), struct(resid.shape, BF16), struct((1, model), F32)],
        [(ANY, keep)] + [(HBM, value) for value in (resid, *turned, moe_gain)],
        [pltpu.VMEM(turned[0].shape, jnp.int32), pltpu.VMEM(turned[1].shape, F32), dma((4,))],
        megabytes=16,
    )
    up_turned = jnp.swapaxes(w_up, 1, 2)
    got = swap(send, "exp", 1)
    chunks = 2 if half % 2 == 0 else 1
    packed = struct((half // chunks * STATE + TILE, LANES), BF16)
    chip = call(chip_state_kernel, "chip_state", [packed] * chunks, [(ANY, gate_lanes), (VMEM, keep), (VMEM, got)])
    chip, up_after, down_after = lax.optimization_barrier((chip, up_turned, w_down))
    other_up, other_down = swap(up_after, "exp", 1), swap(down_after, "exp", 1)
    exchanged = []
    for own in chip:
        along_y = [own] + [swap(own, "exp", 2 * d) for d in range(1, chips)]
        span = call(
            span_kernel,
            "span",
            packed,
            [(ANY, c_held)] + [(VMEM, value) for value in along_y],
            [pltpu.VMEM((chips, *packed.shape), BF16)],
        )
        exchanged += along_y + [span] + [swap(span, "seq", d) for d in range(1, seq_size)]
    before, before_send = call(
        functools.partial(before_kernel, chips, seq_size),
        "before",
        [struct((half, STATE, LANES), BF16)] * 2,
        [(ANY, norm_held)] + [(VMEM, value) for value in (keep, got, *exchanged)],
        [pltpu.VMEM((chips, *packed.shape), BF16), pltpu.VMEM((seq_size, *packed.shape), BF16)],
        megabytes=24,
    )
    before_got = swap(before_send, "exp", 1)
    shared = [(VMEM, value) for value in (local, grown, c_held, norm_held, w_held)]
    normed_half = pltpu.VMEM((length, channels // 2), BF16)
    first = call(
        functools.partial(first_half_kernel, head_size),
        "first_half",
        struct((length, model), F32),
        shared + [(VMEM, before)],
        [normed_half],
    )
    mixed = call(
        mixed_kernel,
        "mixed",
        [struct((rows, model), BF16)] * head_size,
        [(ANY, other_up), (ANY, other_down)] + shared + [(VMEM, before_got), (VMEM, first)],
        [normed_half],
    )
    up_held, down_held = call(
        weights_kernel,
        "weights",
        [struct(up_turned.shape, BF16), struct(w_down.shape, BF16)],
        [(ANY, mixed[0]), (HBM, up_turned), (HBM, w_down)],
        [dma((2,))],
    )
    slots = list(range(head_size - 1))
    parts, last = [swap_slot(mixed[k + 1], k) for k in slots[:-1]], mixed[-1]
    if head_size == 4:
        last = call(relay_kernel, "relay", struct((rows, model), BF16), [(VMEM, last), (VMEM, parts[0])])
    parts = [mixed[0]] + parts + [swap_slot(last, slots[-1])]
    hidden, own_rows = call(
        rows_kernel,
        "rows",
        [struct((rows, model), BF16), struct((rows, wide), BF16)],
        [(ANY, up_held)] + [(VMEM, value) for value in (resid_held, gate_lanes, gain_held, *parts)],
    )

    def through_experts(members, sizes):
        return call(
            functools.partial(expert_kernel, experts, len(members)),
            "experts",
            [struct((size * rows, model), BF16) for size in sizes],
            [(VMEM, value) for value in (up_held, down_held, other_up, other_down, *members)],
            megabytes=16,
        )

    both = ("head", "exp")
    group = [z * exp_size + 2 * d for z in (0, 1) for d in range(chips)][1:]
    paired = [z * exp_size + 2 * d for d in range(chips) for z in (0, 1)][1:]

    def spread(block, masks):
        return [block] + [swap(block, both, mask) for mask in masks]

    sets = [spread(swap(own_rows, "head", high), paired) for high in range(2, head_size, 2)]
    near = through_experts(spread(own_rows, group), [1] * (1 + len(group)))
    near, sets = lax.optimization_barrier((near, sets))
    arrived = []
    for high, members in zip(range(2, head_size, 2), sets):
        pieces = through_experts(members, [1, 1] + [2] * (chips - 1))
        got = [swap(piece, "exp", 2 * d) for d, piece in enumerate(pieces[2:], 1)]
        for z in (1, 0):
            total = call(
                functools.partial(sum_kernel, z),
                "sum",
                struct((rows, model), BF16),
                [(VMEM, value) for value in (pieces[z], *got)],
            )
            arrived.append(swap(total, "head", high + z))
    arrived += [swap(piece, both, mask) for piece, mask in zip(near[:0:-1], group[::-1])]
    return call(
        last_kernel,
        "last",
        struct(resid.shape, BF16),
        [(VMEM, value) for value in (hidden, near[0], *arrived)],
        pinned=False,
    )


def solution(mesh):
    placed = (
        P(("seq", "exp"), "head"),
        P(("seq", "exp"), "head"),
        P(("seq", "exp"), "head"),
        P(("seq", "exp"), "head"),
        P(("seq", "exp"), "head"),
        P("head"),
        P("head"),
        P("head"),
        P("head", None),
        P(("seq", "exp"), "head", None),
        P(("seq", "exp"), "head", None),
        P(("seq", "exp"), "head", None),
        P(),
        P(("head", "exp"), None, None),
        P(("head", "exp"), None, None),
    )
    return jax.shard_map(
        per_device,
        mesh=mesh,
        in_specs=placed,
        out_specs=P(("seq", "exp"), "head", None),
        check_vma=False,
    )
```

```python
import functools

import jax
import jax.numpy as jnp
from jax import lax
from jax.experimental import pallas as pl
from jax.experimental.pallas import tpu as pltpu
from jax.sharding import PartitionSpec as P

HEAD_DIM = 64
STATE = 128
LANES = 128
TILE = 16
FAR = -1e30
F32 = jnp.float32
BF16 = jnp.bfloat16
HBM = pl.BlockSpec(memory_space=pltpu.HBM)
VMEM = pl.BlockSpec(memory_space=pltpu.VMEM)
ANY = pl.BlockSpec(memory_space=pl.ANY)
NT = (((1,), (1,)), ((), ()))


def struct(shape, dtype):
    return jax.ShapeDtypeStruct(shape, dtype)


def call(kernel, name, outs, ins, scratch=(), megabytes=12, pinned=True):
    args = [pltpu.with_memory_space_constraint(arg, pltpu.HBM) if spec is HBM else arg for spec, arg in ins]
    return pl.pallas_call(
        kernel,
        out_shape=jax.tree.map(lambda out: pltpu.VMEM(out.shape, out.dtype), outs) if pinned else outs,
        in_specs=[spec for spec, _ in ins],
        out_specs=jax.tree.map(lambda _: VMEM, outs),
        scratch_shapes=list(scratch),
        name=name,
        compiler_params=pltpu.CompilerParams(vmem_limit_bytes=megabytes << 20),
    )(*args)


def offsets(count):
    down = list(range(count - 1, 0, -1))
    return [[3, 1, 2], [2, 3, 1]] if count == 4 else [down, down]


def targets(count):
    return [[1, 1, 2], [2, 3, 1]] if count == 4 else offsets(count)


def head_offset(slot, count):
    first, second = (order[slot] for order in offsets(count))
    return jnp.where(core_index() == 0, first, second)


def core_index():
    return lax.axis_index("exp") % 2


def chip_index():
    return lax.axis_index("exp") // 2


def copies(sems, sources, targets):
    made = [pltpu.make_async_copy(s, t, sems.at[i]) for i, (s, t) in enumerate(zip(sources, targets))]
    for copy in made:
        copy.start()
    return made


def decays(dt_rows, a_log):
    heads, length = dt_rows.shape
    step = jnp.maximum(dt_rows, 0.0) + jnp.log1p(jnp.exp(-jnp.abs(dt_rows)))
    same = lax.broadcasted_iota(jnp.int32, (heads, heads), 0) == lax.broadcasted_iota(jnp.int32, (heads, heads), 1)
    a_column = jnp.sum(jnp.where(same, jnp.broadcast_to(a_log, (heads, heads)), 0.0), axis=1, keepdims=True)
    rate = -step * jnp.exp(a_column)
    row = lax.broadcasted_iota(jnp.int32, (length, length), 0)
    col = lax.broadcasted_iota(jnp.int32, (length, length), 1)
    upper = (row <= col).astype(F32)
    cum = jnp.dot(rate, upper, precision=lax.Precision.HIGHEST, preferred_element_type=F32)
    return step, cum


def pair_lanes(values, pair):
    rows = values.shape[0]
    lane = lax.broadcasted_iota(jnp.int32, (rows, LANES), 1)
    left = jnp.broadcast_to(values[:, 2 * pair : 2 * pair + 1], (rows, LANES))
    right = jnp.broadcast_to(values[:, 2 * pair + 1 : 2 * pair + 2], (rows, LANES))
    return jnp.where(lane < HEAD_DIM, left, right)


def unpacked(block):
    pairs = block.shape[0] // STATE
    tail = block[pairs * STATE :].astype(F32)
    totals = [tail[pair : pair + 1] + tail[pairs + pair : pairs + pair + 1] for pair in range(pairs)]
    return jnp.stack(totals), block[: pairs * STATE].astype(F32).reshape(pairs, STATE, LANES)


def pack(ref, total, state):
    pairs = state.shape[0]
    ref[0 : pairs * STATE, :] = state.reshape(pairs * STATE, LANES).astype(BF16)
    row = lax.broadcasted_iota(jnp.int32, (TILE, LANES), 0)
    tail = jnp.zeros((TILE, LANES), F32)
    for pair in range(pairs):
        wide = jnp.broadcast_to(total[pair], (TILE, LANES))
        high = wide.astype(BF16).astype(F32)
        tail = jnp.where(row == pair, high, jnp.where(row == pairs + pair, wide - high, tail))
    ref[pairs * STATE :, :] = tail.astype(BF16)


def state_kernel(x_hbm, b_hbm, dt_hbm, a_hbm, keep_ref, send_ref, *scratch):
    x_ref, b_ref, dt_ref, a_ref, packed_ref, sems = scratch
    loads = copies(sems, (dt_hbm, a_hbm, x_hbm, b_hbm), (dt_ref, a_ref, x_ref, b_ref))
    loads[0].wait()
    loads[1].wait()
    step, cum = decays(dt_ref[...], a_ref[...])
    length = cum.shape[1]
    total = cum[:, length - 1 :]
    tail = (jnp.exp(total - cum) * step).T
    total = jnp.broadcast_to(total, cum.shape).T[0:1]
    loads[2].wait()
    loads[3].wait()
    pairs = x_ref.shape[1] // LANES
    half = pairs // 2
    groups = b_ref.shape[1] // STATE
    totals, states = [], []
    for group in range(groups):
        turned = b_ref[:, group * STATE : (group + 1) * STATE].T
        for pair in range(group * pairs // groups, (group + 1) * pairs // groups):
            x_pair = x_ref[:, pair * LANES : (pair + 1) * LANES].astype(F32)
            weighted = (pair_lanes(tail, pair) * x_pair).astype(BF16)
            state = jnp.dot(turned, weighted, preferred_element_type=F32)
            totals.append(pair_lanes(total, pair))
            states.append(state)
    for at in range(2):
        span = slice(at * half, (at + 1) * half)
        pack(packed_ref.at[at], totals[span], jnp.stack(states[span]))
    keep_ref[...] = packed_ref[core_index()]
    send_ref[...] = packed_ref[1 - core_index()]


def chip_state_kernel(after_ref, keep_ref, got_ref, out_ref):
    first = core_index() == 0
    keep, got = unpacked(keep_ref[...]), unpacked(got_ref[...])
    early = [jnp.where(first, mine, other) for mine, other in zip(keep, got)]
    late = [jnp.where(first, other, mine) for mine, other in zip(keep, got)]
    pack(out_ref, early[0] + late[0], jnp.exp(late[0]) * early[1] + late[1])


def weights_kernel(after_ref, up_hbm, down_hbm, up_ref, down_ref, sems):
    for load in copies(sems, (up_hbm, down_hbm), (up_ref, down_ref)):
        load.wait()


def span_kernel(*rest):
    ins, out_ref, block_ref = rest[:-2], rest[-2], rest[-1]
    for mask, part in enumerate(ins):
        block_ref[chip_index() ^ mask] = part[...]
    total, state = unpacked(block_ref[0])
    for chip in range(1, len(ins)):
        here, own = unpacked(block_ref[chip])
        total, state = total + here, jnp.exp(here) * state + own
    pack(out_ref, total, state)


def before_kernel(chips, parts, flat, after_a, after_b, keep_ref, got_ref, *rest):
    ins, (mine_ref, send_ref, chip_ref, part_ref) = rest[:-4], rest[-4:]
    first = core_index() == 0
    totals, states = (jnp.where(first, k, g) for k, g in zip(unpacked(keep_ref[...]), unpacked(got_ref[...])))
    place = chip_index()
    if flat:
        place = lax.axis_index("seq") * (lax.axis_size("exp") // 2) + place
    for mask in range(chips):
        chip_ref[place ^ mask] = ins[mask][...]
    for mask in range(parts):
        part_ref[lax.axis_index("seq") ^ mask] = ins[chips + mask][...]
    carry = jnp.zeros(states.shape, F32)
    for ref, count, own in ((part_ref, parts, lax.axis_index("seq")), (chip_ref, chips, place)):
        for index in range(count - 1):
            total, state = unpacked(ref[index])
            carry = jnp.where(index < own, jnp.exp(total) * carry + state, carry)
    later = jnp.exp(totals) * carry + states
    mine_ref[...] = jnp.where(first, carry, later).astype(BF16)
    send_ref[...] = jnp.where(first, later, carry).astype(BF16)


def inside_kernel(x_hbm, z_hbm, b_hbm, c_hbm, dt_hbm, a_hbm, d_hbm, local_ref, grown_ref, c_ref, *scratch):
    x_ref, z_ref, b_ref, dt_ref, a_ref, d_ref, sems = scratch
    loads = copies(
        sems,
        (dt_hbm, a_hbm, d_hbm, b_hbm, c_hbm, x_hbm, z_hbm),
        (dt_ref, a_ref, d_ref, b_ref, c_ref, x_ref, z_ref),
    )
    for load in loads:
        load.wait()
    step_rows, cum_rows = decays(dt_ref[...], a_ref[...])
    cum = cum_rows.T
    grown = jnp.exp(cum)
    length = cum.shape[0]
    pairs = x_ref.shape[1] // LANES
    groups = b_ref.shape[1] // STATE
    row = lax.broadcasted_iota(jnp.int32, (length, length), 0)
    col = lax.broadcasted_iota(jnp.int32, (length, length), 1)
    lane = lax.broadcasted_iota(jnp.int32, (length, LANES), 1)
    for group in range(groups):
        span = slice(group * STATE, (group + 1) * STATE)
        scores = lax.dot_general(c_ref[:, span], b_ref[:, span], NT, preferred_element_type=F32)
        scores = jnp.where(row >= col, scores, 0.0)
        for pair in range(group * pairs // groups, (group + 1) * pairs // groups):
            at = slice(pair * LANES, (pair + 1) * LANES)
            x_pair = x_ref[:, at]
            halves = []
            for head in (2 * pair, 2 * pair + 1):
                distance = cum[:, head : head + 1] - cum_rows[head : head + 1, :]
                decay = jnp.exp(jnp.where(row >= col, distance, FAR))
                mixing = (scores * (decay * step_rows[head : head + 1, :])).astype(BF16)
                halves.append(jnp.dot(mixing, x_pair, preferred_element_type=F32))
            inside = jnp.where(lane < HEAD_DIM, halves[0], halves[1])
            skip = pair_lanes(d_ref[...], pair) * x_pair.astype(F32)
            z = z_ref[:, at].astype(F32)
            gate = z / (1.0 + jnp.exp(-z))
            local_ref[:, at] = (inside + skip) * gate
            grown_ref[:, at] = pair_lanes(grown, pair) * gate


def projection_kernel(norm_hbm, w_hbm, norm_ref, w_ref, sems):
    for load in copies(sems, (norm_hbm, w_hbm), (norm_ref, w_ref)):
        load.wait()


def prep_kernel(experts, width, after_ref, resid_hbm, routes_hbm, gates_hbm, gain_hbm, *rest):
    gate_ref, resid_ref, gain_ref, routes_ref, gates_ref, sems = rest
    loads = copies(
        sems,
        (routes_hbm, gates_hbm, resid_hbm, gain_hbm),
        (routes_ref, gates_ref, resid_ref, gain_ref.at[0]),
    )
    loads[0].wait()
    loads[1].wait()
    count, extent = gate_ref.shape
    start = width // LANES * LANES
    lane = lax.broadcasted_iota(jnp.int32, (extent, count), 0) + start - width
    expert = jnp.where(lane >= experts, lane - experts, lane)
    gate = jnp.zeros((extent, count), F32)
    for pick in range(routes_ref.shape[0]):
        gate = gate + jnp.where(routes_ref[pick] == expert, gates_ref[pick], 0.0)
    high = gate.astype(BF16).astype(F32)
    gate = jnp.where(lane < experts, high, jnp.where(lane < 2 * experts, gate - high, 0.0))
    gate_ref[...] = gate.T.astype(BF16)
    for load in loads[2:]:
        load.wait()


def half_product(half, local_ref, grown_ref, c_ref, norm_ref, w_ref, state_ref, normed_ref, count):
    pairs = state_ref.shape[0]
    width = pairs * LANES
    base = pl.multiple_of(half * width, width)
    groups = c_ref.shape[1] // STATE // 2
    per_group = pairs // groups
    for group in range(groups):
        c_group = c_ref[:, pl.ds(pl.multiple_of((half * groups + group) * STATE, STATE), STATE)]
        gated, squares = [], 0.0
        for pair in range(group * per_group, (group + 1) * per_group):
            span = pl.ds(pl.multiple_of(base + pair * LANES, LANES), LANES)
            carried = jnp.dot(c_group, state_ref[pair], preferred_element_type=F32)
            value = local_ref[:, span] + grown_ref[:, span] * carried
            gated.append(value)
            squares = squares + value * value
        mean = jnp.sum(squares, axis=1, keepdims=True) / (per_group * LANES)
        inverse = lax.rsqrt(mean + 1e-05)
        for offset, value in enumerate(gated):
            pair = group * per_group + offset
            gain = norm_ref[:, pl.ds(pl.multiple_of(base + pair * LANES, LANES), LANES)]
            normed_ref[:, pair * LANES : (pair + 1) * LANES] = (value * inverse * gain).astype(BF16)
    rows = normed_ref.shape[0] // count
    blocks = []
    for shift in range(count):
        owner = lax.axis_index("head") ^ (head_offset(shift - 1, count) if shift else 0)
        blocks.append(normed_ref[pl.ds(pl.multiple_of(owner * rows, rows), rows), :])
    weight = w_ref[:, pl.ds(base, width)]
    return lax.dot_general(jnp.concatenate(blocks, axis=0), weight, NT, preferred_element_type=F32)


def first_half_kernel(count, local_ref, grown_ref, c_ref, norm_ref, w_ref, mine_ref, out_ref, normed_ref):
    out_ref[...] = half_product(
        core_index(), local_ref, grown_ref, c_ref, norm_ref, w_ref, mine_ref, normed_ref, count
    )


def mixed_kernel(after_up, after_down, local_ref, grown_ref, c_ref, norm_ref, w_ref, got_ref, first_ref, *rest):
    outs, normed_ref = rest[:-1], rest[-1]
    product = first_ref[...] + half_product(
        1 - core_index(), local_ref, grown_ref, c_ref, norm_ref, w_ref, got_ref, normed_ref, len(outs)
    )
    rows = outs[0].shape[0]
    for shift, out in enumerate(outs):
        out[...] = product[shift * rows : (shift + 1) * rows].astype(BF16)


def relay_kernel(own_ref, got_ref, out_ref):
    got = jnp.where(core_index() == 0, got_ref[...].astype(F32), 0.0)
    out_ref[...] = (own_ref[...].astype(F32) + got).astype(BF16)


def rows_kernel(after_ref, resid_ref, gate_ref, gain_ref, *rest):
    parts, hidden_ref, rows_ref = rest[:-2], rest[-2], rest[-1]
    mixed = parts[0][...].astype(F32)
    for at, part in enumerate(parts[1:]):
        value = part[...].astype(F32)
        if at == 0 and len(parts) == 4:
            value = jnp.where(core_index() == 1, value, 0.0)
        mixed = mixed + value
    hidden = (resid_ref[0].astype(F32) + mixed).astype(BF16)
    hidden_ref[...] = hidden
    value = hidden.astype(F32)
    scale = lax.rsqrt(jnp.mean(value * value, axis=1, keepdims=True) + 1e-05)
    width = value.shape[1]
    rows_ref[:, width // LANES * LANES :] = gate_ref[...]
    rows_ref[:, :width] = (value * scale * gain_ref[...]).astype(BF16)


def expert_kernel(experts, count, carried, up_ref, down_ref, other_up_ref, other_down_ref, *rest):
    ins, done, outs = rest[:count], rest[count : count + len(carried)], rest[count + len(carried) :]
    width = up_ref.shape[2]
    start = width // LANES * LANES
    rows = jnp.concatenate([ref[:, :width] for ref in ins], axis=0)
    tail = jnp.concatenate([ref[:, start:] for ref in ins], axis=0).astype(F32)
    lane = lax.broadcasted_iota(jnp.int32, tail.shape, 1) + start - width
    own = lax.axis_index("head") * lax.axis_size("exp") + lax.axis_index("exp")
    other = own + 1 - 2 * core_index()
    total = 0.0
    for expert, up_of, down_of in ((own, up_ref, down_ref), (other, other_up_ref, other_down_ref)):
        up = lax.dot_general(rows, up_of[0], NT, preferred_element_type=F32)
        up = jnp.maximum(up, 0.0)
        activated = (up * up).astype(BF16)
        chosen = (lane == expert) | (lane == expert + experts)
        gate = jnp.sum(jnp.where(chosen, tail, 0.0), axis=1, keepdims=True)
        total = total + jnp.dot(activated, down_of[0], preferred_element_type=F32) * gate
    size = ins[0].shape[0]
    for at, out in enumerate(outs):
        out[0:size] = total[at * size : (at + 1) * size].astype(BF16)
    for at, ref in zip(carried, done):
        outs[at][size:] = ref[...]


def sum_kernel(*refs):
    rows = refs[-1].shape[0]
    total = refs[0][...].astype(F32)
    for ref in refs[1:-1]:
        total = total + ref[0:rows].astype(F32)
    refs[-1][...] = total.astype(BF16)


def last_kernel(hidden_ref, *rest):
    parts, out_ref = rest[:-1], rest[-1]
    rows = out_ref.shape[1]
    total = parts[0][...].astype(F32)
    for part in parts[1:]:
        total = total + part[part.shape[0] - rows :].astype(F32)
    out_ref[0] = (hidden_ref[...].astype(F32) + total).astype(BF16)


def swap(value, axis, mask):
    size = lax.axis_size(axis)
    return lax.ppermute(value, axis, [(i, i ^ mask) for i in range(size)])


def swap_slot(value, slot):
    heads, size = lax.axis_size("head"), lax.axis_size("exp")
    order = targets(heads)
    pairs = []
    for i in range(heads * size):
        head, exp = i // size, i % size
        pairs.append((i, (head ^ order[exp % 2][slot]) * size + exp))
    return lax.ppermute(value, ("head", "exp"), pairs)


def per_device(
    x_in, z_in, b_in, c_in, dt_in, a_log, d_skip, norm_w, w_out, resid, routes, gates, moe_gain, w_up, w_down
):
    length, heads = dt_in.shape
    channels = x_in.shape[1]
    model = w_out.shape[1]
    hidden_units = w_up.shape[2]
    seq_size, head_size, exp_size = lax.axis_size("seq"), lax.axis_size("head"), lax.axis_size("exp")
    chips = exp_size // 2
    rows = resid.shape[1]
    experts = head_size * exp_size
    pairs = channels // LANES
    half = pairs // 2
    dt_rows, a_row, d_row = dt_in.T, a_log[None], d_skip[None]
    dma = pltpu.SemaphoreType.DMA
    packed = struct((half * STATE + TILE, LANES), BF16)

    keep, send = call(
        state_kernel,
        "state",
        [packed, packed],
        [(HBM, x_in), (HBM, b_in), (HBM, dt_rows), (HBM, a_row)],
        [pltpu.VMEM(x_in.shape, BF16), pltpu.VMEM(b_in.shape, BF16), pltpu.VMEM(dt_rows.shape, F32),
         pltpu.VMEM(a_row.shape, F32), pltpu.VMEM((2, half * STATE + TILE, LANES), BF16), dma((4,))],
        megabytes=16,
    )
    local, grown, c_held = call(
        inside_kernel,
        "inside",
        [struct((length, channels), F32), struct((length, channels), F32), struct(c_in.shape, BF16)],
        [(HBM, value) for value in (x_in, z_in, b_in, c_in, dt_rows, a_row, d_row)],
        [pltpu.VMEM(x_in.shape, BF16), pltpu.VMEM(z_in.shape, BF16), pltpu.VMEM(b_in.shape, BF16),
         pltpu.VMEM(dt_rows.shape, F32), pltpu.VMEM(a_row.shape, F32), pltpu.VMEM(d_row.shape, F32), dma((7,))],
        megabytes=16,
    )
    wide = -(-(model + 2 * experts) // LANES) * LANES
    turned = [jnp.transpose(value, (2, 0, 1)) for value in (routes, gates)]
    norm_held, w_held = call(
        projection_kernel,
        "projection",
        [struct((1, channels), F32), struct((model, channels), BF16)],
        [(HBM, norm_w[None]), (HBM, w_out.T)],
        [dma((2,))],
    )
    gate_lanes, resid_held, gain_held = call(
        functools.partial(prep_kernel, experts, model),
        "prep",
        [struct((rows, wide - model // LANES * LANES), BF16), struct(resid.shape, BF16), struct((1, model), F32)],
        [(ANY, keep)] + [(HBM, value) for value in (resid, *turned, moe_gain)],
        [pltpu.VMEM(turned[0].shape, jnp.int32), pltpu.VMEM(turned[1].shape, F32), dma((4,))],
        megabytes=16,
    )
    up_turned = jnp.swapaxes(w_up, 1, 2)
    got = swap(send, "exp", 1)
    chip = call(chip_state_kernel, "chip_state", packed, [(ANY, gate_lanes), (VMEM, keep), (VMEM, got)])
    chip, up_after, down_after = lax.optimization_barrier((chip, up_turned, w_down))
    other_up, other_down = swap(up_after, "exp", 1), swap(down_after, "exp", 1)
    flat = seq_size * chips <= 8
    if flat:
        masks = [x * exp_size + 2 * y for x in range(seq_size) for y in range(chips)]
        exchanged = [chip] + [swap(chip, ("seq", "exp"), mask) for mask in masks[1:]]
        counts = (seq_size * chips, 0)
    else:
        along_y = [chip] + [swap(chip, "exp", 2 * d) for d in range(1, chips)]
        span = call(
            span_kernel,
            "span",
            packed,
            [(VMEM, value) for value in along_y],
            [pltpu.VMEM((chips, *packed.shape), BF16)],
        )
        exchanged = along_y + [span] + [swap(span, "seq", d) for d in range(1, seq_size)]
        counts = (chips, seq_size)
    before, before_send = call(
        functools.partial(before_kernel, *counts, flat),
        "before",
        [struct((half, STATE, LANES), BF16)] * 2,
        [(ANY, norm_held), (ANY, c_held)] + [(VMEM, value) for value in (keep, got, *exchanged)],
        [pltpu.VMEM((counts[0], *packed.shape), BF16), pltpu.VMEM((max(1, counts[1]), *packed.shape), BF16)],
        megabytes=24,
    )
    before_got = swap(before_send, "exp", 1)
    shared = [(VMEM, value) for value in (local, grown, c_held, norm_held, w_held)]
    normed_half = pltpu.VMEM((length, channels // 2), BF16)
    first = call(
        functools.partial(first_half_kernel, head_size),
        "first_half",
        struct((length, model), F32),
        shared + [(VMEM, before)],
        [normed_half],
    )
    mixed = call(
        mixed_kernel,
        "mixed",
        [struct((rows, model), BF16)] * head_size,
        [(ANY, other_up), (ANY, other_down)] + shared + [(VMEM, before_got), (VMEM, first)],
        [normed_half],
    )
    up_held, down_held = call(
        weights_kernel,
        "weights",
        [struct(up_turned.shape, BF16), struct(w_down.shape, BF16)],
        [(ANY, mixed[0]), (HBM, up_turned), (HBM, w_down)],
        [dma((2,))],
    )
    slots = list(range(head_size - 1))
    parts, last = [swap_slot(mixed[k + 1], k) for k in slots[:-1]], mixed[-1]
    if head_size == 4:
        last = call(relay_kernel, "relay", struct((rows, model), BF16), [(VMEM, last), (VMEM, parts[0])])
    parts = [mixed[0]] + parts + [swap_slot(last, slots[-1])]
    hidden, own_rows = call(
        rows_kernel,
        "rows",
        [struct((rows, model), BF16), struct((rows, wide), BF16)],
        [(ANY, up_held)] + [(VMEM, value) for value in (resid_held, gate_lanes, gain_held, *parts)],
    )

    def through_experts(members, carried=()):
        places = [at for at, _ in carried]
        return call(
            functools.partial(expert_kernel, experts, len(members), places),
            "experts",
            [struct((rows * (2 if at in places else 1), model), BF16) for at in range(len(members))],
            [(VMEM, value) for value in (up_held, down_held, other_up, other_down, *members)]
            + [(VMEM, value) for _, value in carried],
            megabytes=16,
        )

    both = ("head", "exp")
    group = [z * exp_size + 2 * d for z in (0, 1) for d in range(chips)][1:]

    def spread(block):
        return [block] + [swap(block, both, mask) for mask in group]

    sets = [spread(swap(own_rows, "head", high)) for high in range(2, head_size, 2)]
    near = through_experts(spread(own_rows))
    near, sets = lax.optimization_barrier((near, sets))
    joined = [at for at, mask in enumerate(group, 1) if mask >= exp_size]
    arrived, later = [], [at for at in range(1, len(near)) if at not in joined]
    apart = [near[at] for at in later]
    for high, members in zip(range(2, head_size, 2), sets):
        pieces = through_experts(members, [(at, near[at]) for at in joined] if high == 2 else ())
        got = [swap(piece, both, mask) for piece, mask in zip(pieces[:0:-1], group[::-1])]
        total = call(sum_kernel, "sum", struct((rows, model), BF16), [(VMEM, v) for v in (pieces[0], *got)])
        if high == 2:
            total, apart = lax.optimization_barrier((total, apart))
            arrived += [part for part, mask in zip(got, group[::-1]) if mask >= exp_size]
        arrived.append(swap(total, "head", high))
    arrived += [swap(piece, both, group[at - 1]) for piece, at in zip(apart, later)]
    return call(
        last_kernel,
        "last",
        struct(resid.shape, BF16),
        [(VMEM, value) for value in (hidden, near[0], *arrived)],
        pinned=False,
    )


def solution(mesh):
    placed = (
        P(("seq", "exp"), "head"),
        P(("seq", "exp"), "head"),
        P(("seq", "exp"), "head"),
        P(("seq", "exp"), "head"),
        P(("seq", "exp"), "head"),
        P("head"),
        P("head"),
        P("head"),
        P("head", None),
        P(("seq", "exp"), "head", None),
        P(("seq", "exp"), "head", None),
        P(("seq", "exp"), "head", None),
        P(),
        P(("head", "exp"), None, None),
        P(("head", "exp"), None, None),
    )
    return jax.shard_map(
        per_device,
        mesh=mesh,
        in_specs=placed,
        out_specs=P(("seq", "exp"), "head", None),
        check_vma=False,
    )
```

```python
import functools

import jax
import jax.numpy as jnp
from jax import lax
from jax.experimental import pallas as pl
from jax.experimental.pallas import tpu as pltpu
from jax.sharding import PartitionSpec as P

HEAD_DIM = 64
STATE = 128
LANES = 128
TILE = 16
FAR = -1e30
F32 = jnp.float32
BF16 = jnp.bfloat16
HBM = pl.BlockSpec(memory_space=pltpu.HBM)
VMEM = pl.BlockSpec(memory_space=pltpu.VMEM)
ANY = pl.BlockSpec(memory_space=pl.ANY)
NT = (((1,), (1,)), ((), ()))


def struct(shape, dtype):
    return jax.ShapeDtypeStruct(shape, dtype)


def call(kernel, name, outs, ins, scratch=(), megabytes=12, pinned=True):
    args = [pltpu.with_memory_space_constraint(arg, pltpu.HBM) if spec is HBM else arg for spec, arg in ins]
    return pl.pallas_call(
        kernel,
        out_shape=jax.tree.map(lambda out: pltpu.VMEM(out.shape, out.dtype), outs) if pinned else outs,
        in_specs=[spec for spec, _ in ins],
        out_specs=jax.tree.map(lambda _: VMEM, outs),
        scratch_shapes=list(scratch),
        name=name,
        compiler_params=pltpu.CompilerParams(vmem_limit_bytes=megabytes << 20),
    )(*args)


def offsets(count):
    down = list(range(count - 1, 0, -1))
    return [[3, 1, 2], [2, 3, 1]] if count == 4 else [down, down]


def targets(count):
    return [[1, 1, 2], [2, 3, 1]] if count == 4 else offsets(count)


def head_offset(slot, count):
    first, second = (order[slot] for order in offsets(count))
    return jnp.where(core_index() == 0, first, second)


def core_index():
    return lax.axis_index("exp") % 2


def chip_index():
    return lax.axis_index("exp") // 2


def copies(sems, sources, targets):
    made = [pltpu.make_async_copy(s, t, sems.at[i]) for i, (s, t) in enumerate(zip(sources, targets))]
    for copy in made:
        copy.start()
    return made


def decays(dt_rows, a_log):
    heads, length = dt_rows.shape
    step = jnp.maximum(dt_rows, 0.0) + jnp.log1p(jnp.exp(-jnp.abs(dt_rows)))
    same = lax.broadcasted_iota(jnp.int32, (heads, heads), 0) == lax.broadcasted_iota(jnp.int32, (heads, heads), 1)
    a_column = jnp.sum(jnp.where(same, jnp.broadcast_to(a_log, (heads, heads)), 0.0), axis=1, keepdims=True)
    rate = -step * jnp.exp(a_column)
    row = lax.broadcasted_iota(jnp.int32, (length, length), 0)
    col = lax.broadcasted_iota(jnp.int32, (length, length), 1)
    upper = (row <= col).astype(F32)
    cum = jnp.dot(rate, upper, precision=lax.Precision.HIGHEST, preferred_element_type=F32)
    return step, cum


def pair_lanes(values, pair):
    rows = values.shape[0]
    lane = lax.broadcasted_iota(jnp.int32, (rows, LANES), 1)
    left = jnp.broadcast_to(values[:, 2 * pair : 2 * pair + 1], (rows, LANES))
    right = jnp.broadcast_to(values[:, 2 * pair + 1 : 2 * pair + 2], (rows, LANES))
    return jnp.where(lane < HEAD_DIM, left, right)


def unpacked(block):
    pairs = block.shape[0] // STATE
    tail = block[pairs * STATE :].astype(F32)
    totals = [tail[pair : pair + 1] + tail[pairs + pair : pairs + pair + 1] for pair in range(pairs)]
    return jnp.stack(totals), block[: pairs * STATE].astype(F32).reshape(pairs, STATE, LANES)


def pack(ref, total, state):
    pairs = state.shape[0]
    ref[0 : pairs * STATE, :] = state.reshape(pairs * STATE, LANES).astype(BF16)
    row = lax.broadcasted_iota(jnp.int32, (TILE, LANES), 0)
    tail = jnp.zeros((TILE, LANES), F32)
    for pair in range(pairs):
        wide = jnp.broadcast_to(total[pair], (TILE, LANES))
        high = wide.astype(BF16).astype(F32)
        tail = jnp.where(row == pair, high, jnp.where(row == pairs + pair, wide - high, tail))
    ref[pairs * STATE :, :] = tail.astype(BF16)


def state_kernel(x_hbm, b_hbm, dt_hbm, a_hbm, keep_ref, send_ref, *scratch):
    x_ref, b_ref, dt_ref, a_ref, packed_ref, sems = scratch
    loads = copies(sems, (dt_hbm, a_hbm, x_hbm, b_hbm), (dt_ref, a_ref, x_ref, b_ref))
    loads[0].wait()
    loads[1].wait()
    step, cum = decays(dt_ref[...], a_ref[...])
    length = cum.shape[1]
    total = cum[:, length - 1 :]
    tail = (jnp.exp(total - cum) * step).T
    total = jnp.broadcast_to(total, cum.shape).T[0:1]
    loads[2].wait()
    loads[3].wait()
    pairs = x_ref.shape[1] // LANES
    half = pairs // 2
    groups = b_ref.shape[1] // STATE
    totals, states = [], []
    for group in range(groups):
        turned = b_ref[:, group * STATE : (group + 1) * STATE].T
        for pair in range(group * pairs // groups, (group + 1) * pairs // groups):
            x_pair = x_ref[:, pair * LANES : (pair + 1) * LANES].astype(F32)
            weighted = (pair_lanes(tail, pair) * x_pair).astype(BF16)
            state = jnp.dot(turned, weighted, preferred_element_type=F32)
            totals.append(pair_lanes(total, pair))
            states.append(state)
    for at in range(2):
        span = slice(at * half, (at + 1) * half)
        pack(packed_ref.at[at], totals[span], jnp.stack(states[span]))
    keep_ref[...] = packed_ref[core_index()]
    send_ref[...] = packed_ref[1 - core_index()]


def chip_state_kernel(after_ref, keep_ref, got_ref, out_ref):
    first = core_index() == 0
    keep, got = unpacked(keep_ref[...]), unpacked(got_ref[...])
    early = [jnp.where(first, mine, other) for mine, other in zip(keep, got)]
    late = [jnp.where(first, other, mine) for mine, other in zip(keep, got)]
    pack(out_ref, early[0] + late[0], jnp.exp(late[0]) * early[1] + late[1])


def weights_kernel(after_ref, up_hbm, down_hbm, up_ref, down_ref, sems):
    for load in copies(sems, (up_hbm, down_hbm), (up_ref, down_ref)):
        load.wait()


def span_kernel(*rest):
    ins, out_ref, block_ref = rest[:-2], rest[-2], rest[-1]
    for mask, part in enumerate(ins):
        block_ref[chip_index() ^ mask] = part[...]
    total, state = unpacked(block_ref[0])
    for chip in range(1, len(ins)):
        here, own = unpacked(block_ref[chip])
        total, state = total + here, jnp.exp(here) * state + own
    pack(out_ref, total, state)


def before_kernel(chips, parts, flat, after_a, after_b, keep_ref, got_ref, *rest):
    ins, (mine_ref, send_ref, chip_ref, part_ref) = rest[:-4], rest[-4:]
    first = core_index() == 0
    totals, states = (jnp.where(first, k, g) for k, g in zip(unpacked(keep_ref[...]), unpacked(got_ref[...])))
    place = chip_index()
    if flat:
        place = lax.axis_index("seq") * (lax.axis_size("exp") // 2) + place
    for mask in range(chips):
        chip_ref[place ^ mask] = ins[mask][...]
    for mask in range(parts):
        part_ref[lax.axis_index("seq") ^ mask] = ins[chips + mask][...]
    carry = jnp.zeros(states.shape, F32)
    for ref, count, own in ((part_ref, parts, lax.axis_index("seq")), (chip_ref, chips, place)):
        for index in range(count - 1):
            total, state = unpacked(ref[index])
            carry = jnp.where(index < own, jnp.exp(total) * carry + state, carry)
    later = jnp.exp(totals) * carry + states
    mine_ref[...] = jnp.where(first, carry, later).astype(BF16)
    send_ref[...] = jnp.where(first, later, carry).astype(BF16)


def inside_kernel(x_hbm, z_hbm, b_hbm, c_hbm, dt_hbm, a_hbm, d_hbm, local_ref, grown_ref, c_ref, *scratch):
    x_ref, z_ref, b_ref, dt_ref, a_ref, d_ref, sems = scratch
    loads = copies(
        sems,
        (dt_hbm, a_hbm, d_hbm, b_hbm, c_hbm, x_hbm, z_hbm),
        (dt_ref, a_ref, d_ref, b_ref, c_ref, x_ref, z_ref),
    )
    for load in loads:
        load.wait()
    step_rows, cum_rows = decays(dt_ref[...], a_ref[...])
    cum = cum_rows.T
    grown = jnp.exp(cum)
    length = cum.shape[0]
    pairs = x_ref.shape[1] // LANES
    groups = b_ref.shape[1] // STATE
    row = lax.broadcasted_iota(jnp.int32, (length, length), 0)
    col = lax.broadcasted_iota(jnp.int32, (length, length), 1)
    lane = lax.broadcasted_iota(jnp.int32, (length, LANES), 1)
    for group in range(groups):
        span = slice(group * STATE, (group + 1) * STATE)
        scores = lax.dot_general(c_ref[:, span], b_ref[:, span], NT, preferred_element_type=F32)
        scores = jnp.where(row >= col, scores, 0.0)
        for pair in range(group * pairs // groups, (group + 1) * pairs // groups):
            at = slice(pair * LANES, (pair + 1) * LANES)
            x_pair = x_ref[:, at]
            halves = []
            for head in (2 * pair, 2 * pair + 1):
                distance = cum[:, head : head + 1] - cum_rows[head : head + 1, :]
                decay = jnp.exp(jnp.where(row >= col, distance, FAR))
                mixing = (scores * (decay * step_rows[head : head + 1, :])).astype(BF16)
                halves.append(jnp.dot(mixing, x_pair, preferred_element_type=F32))
            inside = jnp.where(lane < HEAD_DIM, halves[0], halves[1])
            skip = pair_lanes(d_ref[...], pair) * x_pair.astype(F32)
            z = z_ref[:, at].astype(F32)
            gate = z / (1.0 + jnp.exp(-z))
            local_ref[:, at] = (inside + skip) * gate
            grown_ref[:, at] = pair_lanes(grown, pair) * gate


def projection_kernel(norm_hbm, w_hbm, norm_ref, w_ref, sems):
    for load in copies(sems, (norm_hbm, w_hbm), (norm_ref, w_ref)):
        load.wait()


def prep_kernel(experts, width, after_ref, resid_hbm, routes_hbm, gates_hbm, gain_hbm, *rest):
    gate_ref, resid_ref, gain_ref, routes_ref, gates_ref, sems = rest
    loads = copies(
        sems,
        (routes_hbm, gates_hbm, resid_hbm, gain_hbm),
        (routes_ref, gates_ref, resid_ref, gain_ref.at[0]),
    )
    loads[0].wait()
    loads[1].wait()
    count, extent = gate_ref.shape
    start = width // LANES * LANES
    lane = lax.broadcasted_iota(jnp.int32, (extent, count), 0) + start - width
    expert = jnp.where(lane >= experts, lane - experts, lane)
    gate = jnp.zeros((extent, count), F32)
    for pick in range(routes_ref.shape[0]):
        gate = gate + jnp.where(routes_ref[pick] == expert, gates_ref[pick], 0.0)
    high = gate.astype(BF16).astype(F32)
    gate = jnp.where(lane < experts, high, jnp.where(lane < 2 * experts, gate - high, 0.0))
    gate_ref[...] = gate.T.astype(BF16)
    for load in loads[2:]:
        load.wait()


def half_product(half, local_ref, grown_ref, c_ref, norm_ref, w_ref, state_ref, normed_ref, count):
    pairs = state_ref.shape[0]
    width = pairs * LANES
    base = pl.multiple_of(half * width, width)
    groups = c_ref.shape[1] // STATE // 2
    per_group = pairs // groups
    for group in range(groups):
        c_group = c_ref[:, pl.ds(pl.multiple_of((half * groups + group) * STATE, STATE), STATE)]
        gated, squares = [], 0.0
        for pair in range(group * per_group, (group + 1) * per_group):
            span = pl.ds(pl.multiple_of(base + pair * LANES, LANES), LANES)
            carried = jnp.dot(c_group, state_ref[pair], preferred_element_type=F32)
            value = local_ref[:, span] + grown_ref[:, span] * carried
            gated.append(value)
            squares = squares + value * value
        mean = jnp.sum(squares, axis=1, keepdims=True) / (per_group * LANES)
        inverse = lax.rsqrt(mean + 1e-05)
        for offset, value in enumerate(gated):
            pair = group * per_group + offset
            gain = norm_ref[:, pl.ds(pl.multiple_of(base + pair * LANES, LANES), LANES)]
            normed_ref[:, pair * LANES : (pair + 1) * LANES] = (value * inverse * gain).astype(BF16)
    rows = normed_ref.shape[0] // count
    blocks = []
    for shift in range(count):
        owner = lax.axis_index("head") ^ (head_offset(shift - 1, count) if shift else 0)
        blocks.append(normed_ref[pl.ds(pl.multiple_of(owner * rows, rows), rows), :])
    weight = w_ref[:, pl.ds(base, width)]
    return lax.dot_general(jnp.concatenate(blocks, axis=0), weight, NT, preferred_element_type=F32)


def first_half_kernel(count, local_ref, grown_ref, c_ref, norm_ref, w_ref, mine_ref, out_ref, normed_ref):
    out_ref[...] = half_product(
        core_index(), local_ref, grown_ref, c_ref, norm_ref, w_ref, mine_ref, normed_ref, count
    )


def mixed_kernel(after_up, after_down, local_ref, grown_ref, c_ref, norm_ref, w_ref, got_ref, first_ref, *rest):
    outs, normed_ref = rest[:-1], rest[-1]
    product = first_ref[...] + half_product(
        1 - core_index(), local_ref, grown_ref, c_ref, norm_ref, w_ref, got_ref, normed_ref, len(outs)
    )
    rows = outs[0].shape[0]
    for shift, out in enumerate(outs):
        out[...] = product[shift * rows : (shift + 1) * rows].astype(BF16)


def relay_kernel(own_ref, got_ref, out_ref):
    got = jnp.where(core_index() == 0, got_ref[...].astype(F32), 0.0)
    out_ref[...] = (own_ref[...].astype(F32) + got).astype(BF16)


def rows_kernel(after_ref, resid_ref, gate_ref, gain_ref, *rest):
    parts, hidden_ref, rows_ref = rest[:-2], rest[-2], rest[-1]
    mixed = parts[0][...].astype(F32)
    for at, part in enumerate(parts[1:]):
        value = part[...].astype(F32)
        if at == 0 and len(parts) == 4:
            value = jnp.where(core_index() == 1, value, 0.0)
        mixed = mixed + value
    hidden = (resid_ref[0].astype(F32) + mixed).astype(BF16)
    hidden_ref[...] = hidden
    value = hidden.astype(F32)
    scale = lax.rsqrt(jnp.mean(value * value, axis=1, keepdims=True) + 1e-05)
    width = value.shape[1]
    rows_ref[:, width // LANES * LANES :] = gate_ref[...]
    rows_ref[:, :width] = (value * scale * gain_ref[...]).astype(BF16)


def expert_kernel(experts, count, carried, up_ref, down_ref, other_up_ref, other_down_ref, *rest):
    ins, done, outs = rest[:count], rest[count : count + len(carried)], rest[count + len(carried) :]
    width = up_ref.shape[2]
    start = width // LANES * LANES
    rows = jnp.concatenate([ref[:, :width] for ref in ins], axis=0)
    tail = jnp.concatenate([ref[:, start:] for ref in ins], axis=0).astype(F32)
    lane = lax.broadcasted_iota(jnp.int32, tail.shape, 1) + start - width
    own = lax.axis_index("head") * lax.axis_size("exp") + lax.axis_index("exp")
    other = own + 1 - 2 * core_index()
    total = 0.0
    for expert, up_of, down_of in ((own, up_ref, down_ref), (other, other_up_ref, other_down_ref)):
        up = lax.dot_general(rows, up_of[0], NT, preferred_element_type=F32)
        up = jnp.maximum(up, 0.0)
        activated = (up * up).astype(BF16)
        chosen = (lane == expert) | (lane == expert + experts)
        gate = jnp.sum(jnp.where(chosen, tail, 0.0), axis=1, keepdims=True)
        total = total + jnp.dot(activated, down_of[0], preferred_element_type=F32) * gate
    size = ins[0].shape[0]
    for at, out in enumerate(outs):
        out[0:size] = total[at * size : (at + 1) * size].astype(BF16)
    for at, ref in zip(carried, done):
        outs[at][size:] = ref[...]


def sum_kernel(*refs):
    rows = refs[-1].shape[0]
    total = refs[0][...].astype(F32)
    for ref in refs[1:-1]:
        total = total + ref[0:rows].astype(F32)
    refs[-1][...] = total.astype(BF16)


def last_kernel(hidden_ref, *rest):
    parts, out_ref = rest[:-1], rest[-1]
    rows = out_ref.shape[1]
    total = parts[0][...].astype(F32)
    for part in parts[1:]:
        total = total + part[part.shape[0] - rows :].astype(F32)
    out_ref[0] = (hidden_ref[...].astype(F32) + total).astype(BF16)


def swap(value, axis, mask):
    size = lax.axis_size(axis)
    return lax.ppermute(value, axis, [(i, i ^ mask) for i in range(size)])


def swap_slot(value, slot):
    heads, size = lax.axis_size("head"), lax.axis_size("exp")
    order = targets(heads)
    pairs = []
    for i in range(heads * size):
        head, exp = i // size, i % size
        pairs.append((i, (head ^ order[exp % 2][slot]) * size + exp))
    return lax.ppermute(value, ("head", "exp"), pairs)


def per_device(
    x_in, z_in, b_in, c_in, dt_in, a_log, d_skip, norm_w, w_out, resid, routes, gates, moe_gain, w_up, w_down
):
    length, heads = dt_in.shape
    channels = x_in.shape[1]
    model = w_out.shape[1]
    hidden_units = w_up.shape[2]
    seq_size, head_size, exp_size = lax.axis_size("seq"), lax.axis_size("head"), lax.axis_size("exp")
    chips = exp_size // 2
    rows = resid.shape[1]
    experts = head_size * exp_size
    pairs = channels // LANES
    half = pairs // 2
    dt_rows, a_row, d_row = dt_in.T, a_log[None], d_skip[None]
    dma = pltpu.SemaphoreType.DMA
    packed = struct((half * STATE + TILE, LANES), BF16)

    keep, send = call(
        state_kernel,
        "state",
        [packed, packed],
        [(HBM, x_in), (HBM, b_in), (HBM, dt_rows), (HBM, a_row)],
        [pltpu.VMEM(x_in.shape, BF16), pltpu.VMEM(b_in.shape, BF16), pltpu.VMEM(dt_rows.shape, F32),
         pltpu.VMEM(a_row.shape, F32), pltpu.VMEM((2, half * STATE + TILE, LANES), BF16), dma((4,))],
        megabytes=16,
    )
    local, grown, c_held = call(
        inside_kernel,
        "inside",
        [struct((length, channels), F32), struct((length, channels), F32), struct(c_in.shape, BF16)],
        [(HBM, value) for value in (x_in, z_in, b_in, c_in, dt_rows, a_row, d_row)],
        [pltpu.VMEM(x_in.shape, BF16), pltpu.VMEM(z_in.shape, BF16), pltpu.VMEM(b_in.shape, BF16),
         pltpu.VMEM(dt_rows.shape, F32), pltpu.VMEM(a_row.shape, F32), pltpu.VMEM(d_row.shape, F32), dma((7,))],
        megabytes=16,
    )
    wide = -(-(model + 2 * experts) // LANES) * LANES
    turned = [jnp.transpose(value, (2, 0, 1)) for value in (routes, gates)]
    norm_held, w_held = call(
        projection_kernel,
        "projection",
        [struct((1, channels), F32), struct((model, channels), BF16)],
        [(HBM, norm_w[None]), (HBM, w_out.T)],
        [dma((2,))],
    )
    gate_lanes, resid_held, gain_held = call(
        functools.partial(prep_kernel, experts, model),
        "prep",
        [struct((rows, wide - model // LANES * LANES), BF16), struct(resid.shape, BF16), struct((1, model), F32)],
        [(ANY, keep)] + [(HBM, value) for value in (resid, *turned, moe_gain)],
        [pltpu.VMEM(turned[0].shape, jnp.int32), pltpu.VMEM(turned[1].shape, F32), dma((4,))],
        megabytes=16,
    )
    up_turned = jnp.swapaxes(w_up, 1, 2)
    got = swap(send, "exp", 1)
    chip = call(chip_state_kernel, "chip_state", packed, [(ANY, gate_lanes), (VMEM, keep), (VMEM, got)])
    chip, up_after, down_after = lax.optimization_barrier((chip, up_turned, w_down))
    other_up, other_down = swap(up_after, "exp", 1), swap(down_after, "exp", 1)
    flat = seq_size * chips <= 8
    if flat:
        masks = [x * exp_size + 2 * y for x in range(seq_size) for y in range(chips)]
        exchanged = [chip] + [swap(chip, ("seq", "exp"), mask) for mask in masks[1:]]
        counts = (seq_size * chips, 0)
    else:
        along_y = [chip] + [swap(chip, "exp", 2 * d) for d in range(1, chips)]
        span = call(
            span_kernel,
            "span",
            packed,
            [(VMEM, value) for value in along_y],
            [pltpu.VMEM((chips, *packed.shape), BF16)],
        )
        exchanged = along_y + [span] + [swap(span, "seq", d) for d in range(1, seq_size)]
        counts = (chips, seq_size)
    before, before_send = call(
        functools.partial(before_kernel, *counts, flat),
        "before",
        [struct((half, STATE, LANES), BF16)] * 2,
        [(ANY, norm_held), (ANY, c_held)] + [(VMEM, value) for value in (keep, got, *exchanged)],
        [pltpu.VMEM((counts[0], *packed.shape), BF16), pltpu.VMEM((max(1, counts[1]), *packed.shape), BF16)],
        megabytes=24,
    )
    before_got = swap(before_send, "exp", 1)
    shared = [(VMEM, value) for value in (local, grown, c_held, norm_held, w_held)]
    normed_half = pltpu.VMEM((length, channels // 2), BF16)
    first = call(
        functools.partial(first_half_kernel, head_size),
        "first_half",
        struct((length, model), F32),
        shared + [(VMEM, before)],
        [normed_half],
    )
    mixed = call(
        mixed_kernel,
        "mixed",
        [struct((rows, model), BF16)] * head_size,
        [(ANY, other_up), (ANY, other_down)] + shared + [(VMEM, before_got), (VMEM, first)],
        [normed_half],
    )
    up_held, down_held = call(
        weights_kernel,
        "weights",
        [struct(up_turned.shape, BF16), struct(w_down.shape, BF16)],
        [(ANY, mixed[0]), (HBM, up_turned), (HBM, w_down)],
        [dma((2,))],
    )
    slots = list(range(head_size - 1))
    parts, last = [swap_slot(mixed[k + 1], k) for k in slots[:-1]], mixed[-1]
    if head_size == 4:
        last = call(relay_kernel, "relay", struct((rows, model), BF16), [(VMEM, last), (VMEM, parts[0])])
    parts = [mixed[0]] + parts + [swap_slot(last, slots[-1])]
    hidden, own_rows = call(
        rows_kernel,
        "rows",
        [struct((rows, model), BF16), struct((rows, wide), BF16)],
        [(ANY, up_held)] + [(VMEM, value) for value in (resid_held, gate_lanes, gain_held, *parts)],
    )

    def through_experts(members, carried=()):
        places = [at for at, _ in carried]
        return call(
            functools.partial(expert_kernel, experts, len(members), places),
            "experts",
            [struct((rows * (2 if at in places else 1), model), BF16) for at in range(len(members))],
            [(VMEM, value) for value in (up_held, down_held, other_up, other_down, *members)]
            + [(VMEM, value) for _, value in carried],
            megabytes=16,
        )

    both = ("head", "exp")
    group = [z * exp_size + 2 * d for z in (0, 1) for d in range(chips)][1:]

    def spread(block):
        return [block] + [swap(block, both, mask) for mask in group]

    sets = [spread(swap(own_rows, "head", high)) for high in range(2, head_size, 2)]
    near = through_experts(spread(own_rows))
    near, sets = lax.optimization_barrier((near, sets))
    joined = list(range(1, len(near)))
    arrived = []
    for high, members in zip(range(2, head_size, 2), sets):
        pieces = through_experts(members, [(at, near[at]) for at in joined] if high == 2 else ())
        got = [swap(piece, both, mask) for piece, mask in zip(pieces[:0:-1], group[::-1])]
        total = call(sum_kernel, "sum", struct((rows, model), BF16), [(VMEM, v) for v in (pieces[0], *got)])
        if high == 2:
            arrived += got
        arrived.append(swap(total, "head", high))
    return call(
        last_kernel,
        "last",
        struct(resid.shape, BF16),
        [(VMEM, value) for value in (hidden, near[0], *arrived)],
        pinned=False,
    )


def solution(mesh):
    placed = (
        P(("seq", "exp"), "head"),
        P(("seq", "exp"), "head"),
        P(("seq", "exp"), "head"),
        P(("seq", "exp"), "head"),
        P(("seq", "exp"), "head"),
        P("head"),
        P("head"),
        P("head"),
        P("head", None),
        P(("seq", "exp"), "head", None),
        P(("seq", "exp"), "head", None),
        P(("seq", "exp"), "head", None),
        P(),
        P(("head", "exp"), None, None),
        P(("head", "exp"), None, None),
    )
    return jax.shard_map(
        per_device,
        mesh=mesh,
        in_specs=placed,
        out_specs=P(("seq", "exp"), "head", None),
        check_vma=False,
    )
```

```python
import functools

import jax
import jax.numpy as jnp
from jax import lax
from jax.experimental import pallas as pl
from jax.experimental.pallas import tpu as pltpu
from jax.sharding import PartitionSpec as P

HEAD_DIM = 64
STATE = 128
LANES = 128
TILE = 16
FAR = -1e30
F32 = jnp.float32
BF16 = jnp.bfloat16
HBM = pl.BlockSpec(memory_space=pltpu.HBM)
VMEM = pl.BlockSpec(memory_space=pltpu.VMEM)
ANY = pl.BlockSpec(memory_space=pl.ANY)
NT = (((1,), (1,)), ((), ()))


def struct(shape, dtype):
    return jax.ShapeDtypeStruct(shape, dtype)


def call(kernel, name, outs, ins, scratch=(), megabytes=12, pinned=True):
    args = [pltpu.with_memory_space_constraint(arg, pltpu.HBM) if spec is HBM else arg for spec, arg in ins]
    return pl.pallas_call(
        kernel,
        out_shape=jax.tree.map(lambda out: pltpu.VMEM(out.shape, out.dtype), outs) if pinned else outs,
        in_specs=[spec for spec, _ in ins],
        out_specs=jax.tree.map(lambda _: VMEM, outs),
        scratch_shapes=list(scratch),
        name=name,
        compiler_params=pltpu.CompilerParams(vmem_limit_bytes=megabytes << 20),
    )(*args)


def offsets(count):
    down = list(range(count - 1, 0, -1))
    return [[3, 1, 2], [2, 3, 1]] if count == 4 else [down, down]


def targets(count):
    return [[1, 1, 2], [2, 3, 1]] if count == 4 else offsets(count)


def head_offset(slot, count):
    first, second = (order[slot] for order in offsets(count))
    return jnp.where(core_index() == 0, first, second)


def core_index():
    return lax.axis_index("exp") % 2


def chip_index():
    return lax.axis_index("exp") // 2


def copies(sems, sources, targets):
    made = [pltpu.make_async_copy(s, t, sems.at[i]) for i, (s, t) in enumerate(zip(sources, targets))]
    for copy in made:
        copy.start()
    return made


def decays(dt_rows, a_log):
    heads, length = dt_rows.shape
    step = jnp.maximum(dt_rows, 0.0) + jnp.log1p(jnp.exp(-jnp.abs(dt_rows)))
    same = lax.broadcasted_iota(jnp.int32, (heads, heads), 0) == lax.broadcasted_iota(jnp.int32, (heads, heads), 1)
    a_column = jnp.sum(jnp.where(same, jnp.broadcast_to(a_log, (heads, heads)), 0.0), axis=1, keepdims=True)
    rate = -step * jnp.exp(a_column)
    row = lax.broadcasted_iota(jnp.int32, (length, length), 0)
    col = lax.broadcasted_iota(jnp.int32, (length, length), 1)
    upper = (row <= col).astype(F32)
    cum = jnp.dot(rate, upper, precision=lax.Precision.HIGHEST, preferred_element_type=F32)
    return step, cum


def pair_lanes(values, pair):
    rows = values.shape[0]
    lane = lax.broadcasted_iota(jnp.int32, (rows, LANES), 1)
    left = jnp.broadcast_to(values[:, 2 * pair : 2 * pair + 1], (rows, LANES))
    right = jnp.broadcast_to(values[:, 2 * pair + 1 : 2 * pair + 2], (rows, LANES))
    return jnp.where(lane < HEAD_DIM, left, right)


def unpacked(block):
    pairs = block.shape[0] // STATE
    tail = block[pairs * STATE :].astype(F32)
    totals = [tail[pair : pair + 1] + tail[pairs + pair : pairs + pair + 1] for pair in range(pairs)]
    return jnp.stack(totals), block[: pairs * STATE].astype(F32).reshape(pairs, STATE, LANES)


def pack(ref, total, state):
    pairs = state.shape[0]
    ref[0 : pairs * STATE, :] = state.reshape(pairs * STATE, LANES).astype(BF16)
    row = lax.broadcasted_iota(jnp.int32, (TILE, LANES), 0)
    tail = jnp.zeros((TILE, LANES), F32)
    for pair in range(pairs):
        wide = jnp.broadcast_to(total[pair], (TILE, LANES))
        high = wide.astype(BF16).astype(F32)
        tail = jnp.where(row == pair, high, jnp.where(row == pairs + pair, wide - high, tail))
    ref[pairs * STATE :, :] = tail.astype(BF16)


def state_kernel(x_hbm, b_hbm, dt_hbm, a_hbm, keep_ref, send_ref, *scratch):
    x_ref, b_ref, dt_ref, a_ref, packed_ref, sems = scratch
    loads = copies(sems, (dt_hbm, a_hbm, x_hbm, b_hbm), (dt_ref, a_ref, x_ref, b_ref))
    loads[0].wait()
    loads[1].wait()
    step, cum = decays(dt_ref[...], a_ref[...])
    length = cum.shape[1]
    total = cum[:, length - 1 :]
    tail = (jnp.exp(total - cum) * step).T
    total = jnp.broadcast_to(total, cum.shape).T[0:1]
    loads[2].wait()
    loads[3].wait()
    pairs = x_ref.shape[1] // LANES
    half = pairs // 2
    groups = b_ref.shape[1] // STATE
    totals, states = [], []
    for group in range(groups):
        turned = b_ref[:, group * STATE : (group + 1) * STATE].T
        for pair in range(group * pairs // groups, (group + 1) * pairs // groups):
            x_pair = x_ref[:, pair * LANES : (pair + 1) * LANES].astype(F32)
            weighted = (pair_lanes(tail, pair) * x_pair).astype(BF16)
            state = jnp.dot(turned, weighted, preferred_element_type=F32)
            totals.append(pair_lanes(total, pair))
            states.append(state)
    for at in range(2):
        span = slice(at * half, (at + 1) * half)
        pack(packed_ref.at[at], totals[span], jnp.stack(states[span]))
    keep_ref[...] = packed_ref[core_index()]
    send_ref[...] = packed_ref[1 - core_index()]


def chip_state_kernel(after_ref, keep_ref, got_ref, out_ref):
    first = core_index() == 0
    keep, got = unpacked(keep_ref[...]), unpacked(got_ref[...])
    early = [jnp.where(first, mine, other) for mine, other in zip(keep, got)]
    late = [jnp.where(first, other, mine) for mine, other in zip(keep, got)]
    pack(out_ref, early[0] + late[0], jnp.exp(late[0]) * early[1] + late[1])


def weights_kernel(after_ref, up_hbm, down_hbm, up_ref, down_ref, sems):
    for load in copies(sems, (up_hbm, down_hbm), (up_ref, down_ref)):
        load.wait()


def span_kernel(*rest):
    ins, out_ref, block_ref = rest[:-2], rest[-2], rest[-1]
    for mask, part in enumerate(ins):
        block_ref[chip_index() ^ mask] = part[...]
    total, state = unpacked(block_ref[0])
    for chip in range(1, len(ins)):
        here, own = unpacked(block_ref[chip])
        total, state = total + here, jnp.exp(here) * state + own
    pack(out_ref, total, state)


def before_kernel(chips, parts, flat, after_a, after_b, keep_ref, got_ref, *rest):
    ins, (mine_ref, send_ref, chip_ref, part_ref) = rest[:-4], rest[-4:]
    first = core_index() == 0
    totals, states = (jnp.where(first, k, g) for k, g in zip(unpacked(keep_ref[...]), unpacked(got_ref[...])))
    place = chip_index()
    if flat:
        place = lax.axis_index("seq") * (lax.axis_size("exp") // 2) + place
    for mask in range(chips):
        chip_ref[place ^ mask] = ins[mask][...]
    for mask in range(parts):
        part_ref[lax.axis_index("seq") ^ mask] = ins[chips + mask][...]
    carry = jnp.zeros(states.shape, F32)
    for ref, count, own in ((part_ref, parts, lax.axis_index("seq")), (chip_ref, chips, place)):
        for index in range(count - 1):
            total, state = unpacked(ref[index])
            carry = jnp.where(index < own, jnp.exp(total) * carry + state, carry)
    later = jnp.exp(totals) * carry + states
    mine_ref[...] = jnp.where(first, carry, later).astype(BF16)
    send_ref[...] = jnp.where(first, later, carry).astype(BF16)


def inside_kernel(x_hbm, z_hbm, b_hbm, c_hbm, dt_hbm, a_hbm, d_hbm, local_ref, grown_ref, c_ref, *scratch):
    x_ref, z_ref, b_ref, dt_ref, a_ref, d_ref, sems = scratch
    loads = copies(
        sems,
        (dt_hbm, a_hbm, d_hbm, b_hbm, c_hbm, x_hbm, z_hbm),
        (dt_ref, a_ref, d_ref, b_ref, c_ref, x_ref, z_ref),
    )
    for load in loads:
        load.wait()
    step_rows, cum_rows = decays(dt_ref[...], a_ref[...])
    cum = cum_rows.T
    grown = jnp.exp(cum)
    length = cum.shape[0]
    pairs = x_ref.shape[1] // LANES
    groups = b_ref.shape[1] // STATE
    row = lax.broadcasted_iota(jnp.int32, (length, length), 0)
    col = lax.broadcasted_iota(jnp.int32, (length, length), 1)
    lane = lax.broadcasted_iota(jnp.int32, (length, LANES), 1)
    for group in range(groups):
        span = slice(group * STATE, (group + 1) * STATE)
        scores = lax.dot_general(c_ref[:, span], b_ref[:, span], NT, preferred_element_type=F32)
        scores = jnp.where(row >= col, scores, 0.0)
        for pair in range(group * pairs // groups, (group + 1) * pairs // groups):
            at = slice(pair * LANES, (pair + 1) * LANES)
            x_pair = x_ref[:, at]
            halves = []
            for head in (2 * pair, 2 * pair + 1):
                distance = cum[:, head : head + 1] - cum_rows[head : head + 1, :]
                decay = jnp.exp(jnp.where(row >= col, distance, FAR))
                mixing = (scores * (decay * step_rows[head : head + 1, :])).astype(BF16)
                halves.append(jnp.dot(mixing, x_pair, preferred_element_type=F32))
            inside = jnp.where(lane < HEAD_DIM, halves[0], halves[1])
            skip = pair_lanes(d_ref[...], pair) * x_pair.astype(F32)
            z = z_ref[:, at].astype(F32)
            gate = z / (1.0 + jnp.exp(-z))
            local_ref[:, at] = (inside + skip) * gate
            grown_ref[:, at] = pair_lanes(grown, pair) * gate


def projection_kernel(norm_hbm, w_hbm, norm_ref, w_ref, sems):
    for load in copies(sems, (norm_hbm, w_hbm), (norm_ref, w_ref)):
        load.wait()


def prep_kernel(experts, width, after_ref, resid_hbm, routes_hbm, gates_hbm, gain_hbm, *rest):
    gate_ref, resid_ref, gain_ref, routes_ref, gates_ref, sems = rest
    loads = copies(
        sems,
        (routes_hbm, gates_hbm, resid_hbm, gain_hbm),
        (routes_ref, gates_ref, resid_ref, gain_ref.at[0]),
    )
    loads[0].wait()
    loads[1].wait()
    count, extent = gate_ref.shape
    start = width // LANES * LANES
    lane = lax.broadcasted_iota(jnp.int32, (extent, count), 0) + start - width
    expert = jnp.where(lane >= experts, lane - experts, lane)
    gate = jnp.zeros((extent, count), F32)
    for pick in range(routes_ref.shape[0]):
        gate = gate + jnp.where(routes_ref[pick] == expert, gates_ref[pick], 0.0)
    high = gate.astype(BF16).astype(F32)
    gate = jnp.where(lane < experts, high, jnp.where(lane < 2 * experts, gate - high, 0.0))
    gate_ref[...] = gate.T.astype(BF16)
    for load in loads[2:]:
        load.wait()


def half_product(half, local_ref, grown_ref, c_ref, norm_ref, w_ref, state_ref, normed_ref, count):
    pairs = state_ref.shape[0]
    width = pairs * LANES
    base = pl.multiple_of(half * width, width)
    groups = c_ref.shape[1] // STATE // 2
    per_group = pairs // groups
    for group in range(groups):
        c_group = c_ref[:, pl.ds(pl.multiple_of((half * groups + group) * STATE, STATE), STATE)]
        gated, squares = [], 0.0
        for pair in range(group * per_group, (group + 1) * per_group):
            span = pl.ds(pl.multiple_of(base + pair * LANES, LANES), LANES)
            carried = jnp.dot(c_group, state_ref[pair], preferred_element_type=F32)
            value = local_ref[:, span] + grown_ref[:, span] * carried
            gated.append(value)
            squares = squares + value * value
        mean = jnp.sum(squares, axis=1, keepdims=True) / (per_group * LANES)
        inverse = lax.rsqrt(mean + 1e-05)
        for offset, value in enumerate(gated):
            pair = group * per_group + offset
            gain = norm_ref[:, pl.ds(pl.multiple_of(base + pair * LANES, LANES), LANES)]
            normed_ref[:, pair * LANES : (pair + 1) * LANES] = (value * inverse * gain).astype(BF16)
    rows = normed_ref.shape[0] // count
    blocks = []
    for shift in range(count):
        owner = lax.axis_index("head") ^ (head_offset(shift - 1, count) if shift else 0)
        blocks.append(normed_ref[pl.ds(pl.multiple_of(owner * rows, rows), rows), :])
    weight = w_ref[:, pl.ds(base, width)]
    return lax.dot_general(jnp.concatenate(blocks, axis=0), weight, NT, preferred_element_type=F32)


def first_half_kernel(count, local_ref, grown_ref, c_ref, norm_ref, w_ref, mine_ref, out_ref, normed_ref):
    out_ref[...] = half_product(
        core_index(), local_ref, grown_ref, c_ref, norm_ref, w_ref, mine_ref, normed_ref, count
    )


def mixed_kernel(after_up, after_down, local_ref, grown_ref, c_ref, norm_ref, w_ref, got_ref, first_ref, *rest):
    outs, normed_ref = rest[:-1], rest[-1]
    product = first_ref[...] + half_product(
        1 - core_index(), local_ref, grown_ref, c_ref, norm_ref, w_ref, got_ref, normed_ref, len(outs)
    )
    rows = outs[0].shape[0]
    for shift, out in enumerate(outs):
        out[...] = product[shift * rows : (shift + 1) * rows].astype(BF16)


def relay_kernel(own_ref, got_ref, out_ref):
    got = jnp.where(core_index() == 0, got_ref[...].astype(F32), 0.0)
    out_ref[...] = (own_ref[...].astype(F32) + got).astype(BF16)


def rows_kernel(after_ref, resid_ref, gate_ref, gain_ref, *rest):
    parts, hidden_ref, rows_ref = rest[:-2], rest[-2], rest[-1]
    mixed = parts[0][...].astype(F32)
    for at, part in enumerate(parts[1:]):
        value = part[...].astype(F32)
        if at == 0 and len(parts) == 4:
            value = jnp.where(core_index() == 1, value, 0.0)
        mixed = mixed + value
    hidden = (resid_ref[0].astype(F32) + mixed).astype(BF16)
    hidden_ref[...] = hidden
    value = hidden.astype(F32)
    scale = lax.rsqrt(jnp.mean(value * value, axis=1, keepdims=True) + 1e-05)
    width = value.shape[1]
    rows_ref[:, width // LANES * LANES :] = gate_ref[...]
    rows_ref[:, :width] = (value * scale * gain_ref[...]).astype(BF16)


def expert_kernel(experts, count, carried, up_ref, down_ref, other_up_ref, other_down_ref, *rest):
    ins, done, outs = rest[:count], rest[count : count + len(carried)], rest[count + len(carried) :]
    width = up_ref.shape[2]
    start = width // LANES * LANES
    rows = jnp.concatenate([ref[:, :width] for ref in ins], axis=0)
    tail = jnp.concatenate([ref[:, start:] for ref in ins], axis=0).astype(F32)
    lane = lax.broadcasted_iota(jnp.int32, tail.shape, 1) + start - width
    own = lax.axis_index("head") * lax.axis_size("exp") + lax.axis_index("exp")
    other = own + 1 - 2 * core_index()
    total = 0.0
    for expert, up_of, down_of in ((own, up_ref, down_ref), (other, other_up_ref, other_down_ref)):
        up = lax.dot_general(rows, up_of[0], NT, preferred_element_type=F32)
        up = jnp.maximum(up, 0.0)
        activated = (up * up).astype(BF16)
        chosen = (lane == expert) | (lane == expert + experts)
        gate = jnp.sum(jnp.where(chosen, tail, 0.0), axis=1, keepdims=True)
        total = total + jnp.dot(activated, down_of[0], preferred_element_type=F32) * gate
    size = ins[0].shape[0]
    for at, out in enumerate(outs):
        out[0:size] = total[at * size : (at + 1) * size].astype(BF16)
    for at, ref in zip(carried, done):
        outs[at][size:] = ref[...]


def sum_kernel(*refs):
    rows = refs[-1].shape[0]
    total = refs[0][...].astype(F32)
    for ref in refs[1:-1]:
        total = total + ref[0:rows].astype(F32)
    refs[-1][...] = total.astype(BF16)


def last_kernel(hidden_ref, *rest):
    parts, out_ref = rest[:-1], rest[-1]
    rows = out_ref.shape[1]
    total = parts[0][...].astype(F32)
    for part in parts[1:]:
        total = total + part[part.shape[0] - rows :].astype(F32)
    out_ref[0] = (hidden_ref[...].astype(F32) + total).astype(BF16)


def swap(value, axis, mask):
    size = lax.axis_size(axis)
    return lax.ppermute(value, axis, [(i, i ^ mask) for i in range(size)])


def swap_slot(value, slot):
    heads, size = lax.axis_size("head"), lax.axis_size("exp")
    order = targets(heads)
    pairs = []
    for i in range(heads * size):
        head, exp = i // size, i % size
        pairs.append((i, (head ^ order[exp % 2][slot]) * size + exp))
    return lax.ppermute(value, ("head", "exp"), pairs)


def per_device(
    x_in, z_in, b_in, c_in, dt_in, a_log, d_skip, norm_w, w_out, resid, routes, gates, moe_gain, w_up, w_down
):
    length, heads = dt_in.shape
    channels = x_in.shape[1]
    model = w_out.shape[1]
    hidden_units = w_up.shape[2]
    seq_size, head_size, exp_size = lax.axis_size("seq"), lax.axis_size("head"), lax.axis_size("exp")
    chips = exp_size // 2
    rows = resid.shape[1]
    experts = head_size * exp_size
    pairs = channels // LANES
    half = pairs // 2
    dt_rows, a_row, d_row = dt_in.T, a_log[None], d_skip[None]
    dma = pltpu.SemaphoreType.DMA
    packed = struct((half * STATE + TILE, LANES), BF16)

    keep, send = call(
        state_kernel,
        "state",
        [packed, packed],
        [(HBM, x_in), (HBM, b_in), (HBM, dt_rows), (HBM, a_row)],
        [pltpu.VMEM(x_in.shape, BF16), pltpu.VMEM(b_in.shape, BF16), pltpu.VMEM(dt_rows.shape, F32),
         pltpu.VMEM(a_row.shape, F32), pltpu.VMEM((2, half * STATE + TILE, LANES), BF16), dma((4,))],
        megabytes=16,
    )
    local, grown, c_held = call(
        inside_kernel,
        "inside",
        [struct((length, channels), F32), struct((length, channels), F32), struct(c_in.shape, BF16)],
        [(HBM, value) for value in (x_in, z_in, b_in, c_in, dt_rows, a_row, d_row)],
        [pltpu.VMEM(x_in.shape, BF16), pltpu.VMEM(z_in.shape, BF16), pltpu.VMEM(b_in.shape, BF16),
         pltpu.VMEM(dt_rows.shape, F32), pltpu.VMEM(a_row.shape, F32), pltpu.VMEM(d_row.shape, F32), dma((7,))],
        megabytes=16,
    )
    wide = -(-(model + 2 * experts) // LANES) * LANES
    turned = [jnp.transpose(value, (2, 0, 1)) for value in (routes, gates)]
    norm_held, w_held = call(
        projection_kernel,
        "projection",
        [struct((1, channels), F32), struct((model, channels), BF16)],
        [(HBM, norm_w[None]), (HBM, w_out.T)],
        [dma((2,))],
    )
    gate_lanes, resid_held, gain_held = call(
        functools.partial(prep_kernel, experts, model),
        "prep",
        [struct((rows, wide - model // LANES * LANES), BF16), struct(resid.shape, BF16), struct((1, model), F32)],
        [(ANY, keep)] + [(HBM, value) for value in (resid, *turned, moe_gain)],
        [pltpu.VMEM(turned[0].shape, jnp.int32), pltpu.VMEM(turned[1].shape, F32), dma((4,))],
        megabytes=16,
    )
    up_turned = jnp.swapaxes(w_up, 1, 2)
    got = swap(send, "exp", 1)
    chip = call(chip_state_kernel, "chip_state", packed, [(ANY, gate_lanes), (VMEM, keep), (VMEM, got)])
    chip, up_after, down_after = lax.optimization_barrier((chip, up_turned, w_down))
    other_up, other_down = swap(up_after, "exp", 1), swap(down_after, "exp", 1)
    flat = seq_size * chips <= 8
    if flat:
        masks = [x * exp_size + 2 * y for x in range(seq_size) for y in range(chips)]
        exchanged = [chip] + [swap(chip, ("seq", "exp"), mask) for mask in masks[1:]]
        counts = (seq_size * chips, 0)
    else:
        along_y = [chip] + [swap(chip, "exp", 2 * d) for d in range(1, chips)]
        span = call(
            span_kernel,
            "span",
            packed,
            [(VMEM, value) for value in along_y],
            [pltpu.VMEM((chips, *packed.shape), BF16)],
        )
        exchanged = along_y + [span] + [swap(span, "seq", d) for d in range(1, seq_size)]
        counts = (chips, seq_size)
    before, before_send = call(
        functools.partial(before_kernel, *counts, flat),
        "before",
        [struct((half, STATE, LANES), BF16)] * 2,
        [(ANY, norm_held), (ANY, c_held)] + [(VMEM, value) for value in (keep, got, *exchanged)],
        [pltpu.VMEM((counts[0], *packed.shape), BF16), pltpu.VMEM((max(1, counts[1]), *packed.shape), BF16)],
        megabytes=24,
    )
    before_got = swap(before_send, "exp", 1)
    shared = [(VMEM, value) for value in (local, grown, c_held, norm_held, w_held)]
    normed_half = pltpu.VMEM((length, channels // 2), BF16)
    first = call(
        functools.partial(first_half_kernel, head_size),
        "first_half",
        struct((length, model), F32),
        shared + [(VMEM, before)],
        [normed_half],
    )
    mixed = call(
        mixed_kernel,
        "mixed",
        [struct((rows, model), BF16)] * head_size,
        [(ANY, other_up), (ANY, other_down)] + shared + [(VMEM, before_got), (VMEM, first)],
        [normed_half],
    )
    up_held, down_held = call(
        weights_kernel,
        "weights",
        [struct(up_turned.shape, BF16), struct(w_down.shape, BF16)],
        [(ANY, mixed[0]), (HBM, up_turned), (HBM, w_down)],
        [dma((2,))],
    )
    slots = list(range(head_size - 1))
    parts, last = [swap_slot(mixed[k + 1], k) for k in slots[:-1]], mixed[-1]
    if head_size == 4:
        last = call(relay_kernel, "relay", struct((rows, model), BF16), [(VMEM, last), (VMEM, parts[0])])
    parts = [mixed[0]] + parts + [swap_slot(last, slots[-1])]
    hidden, own_rows = call(
        rows_kernel,
        "rows",
        [struct((rows, model), BF16), struct((rows, wide), BF16)],
        [(ANY, up_held)] + [(VMEM, value) for value in (resid_held, gate_lanes, gain_held, *parts)],
    )

    def through_experts(members, carried=()):
        places = [at for at, _ in carried]
        return call(
            functools.partial(expert_kernel, experts, len(members), places),
            "experts",
            [struct((rows * (2 if at in places else 1), model), BF16) for at in range(len(members))],
            [(VMEM, value) for value in (up_held, down_held, other_up, other_down, *members)]
            + [(VMEM, value) for _, value in carried],
            megabytes=16,
        )

    both = ("head", "exp")
    group = [z * exp_size + 2 * d for z in (0, 1) for d in range(chips)][1:]

    def spread(block):
        return [block] + [swap(block, both, mask) for mask in group]

    sets = [spread(swap(own_rows, "head", high)) for high in range(2, head_size, 2)]
    near = through_experts(spread(own_rows))
    near, sets = lax.optimization_barrier((near, sets))
    joined = [at for at, mask in enumerate(group, 1) if mask == exp_size]
    arrived, later = [], [at for at, mask in enumerate(group, 1) if mask < exp_size]
    apart = [near[at] for at in later]
    for high, members in zip(range(2, head_size, 2), sets):
        pieces = through_experts(members, [(at, near[at]) for at in joined] if high == 2 else ())
        got = [swap(piece, both, mask) for piece, mask in zip(pieces[:0:-1], group[::-1])]
        total = call(sum_kernel, "sum", struct((rows, model), BF16), [(VMEM, v) for v in (pieces[0], *got)])
        if high == 2:
            total, apart = lax.optimization_barrier((total, apart))
            arrived += [part for part, mask in zip(got, group[::-1]) if mask == exp_size]
        arrived.append(swap(total, "head", high))
    arrived += [swap(near[at], both, mask) for at, mask in enumerate(group, 1) if mask > exp_size]
    arrived += [swap(piece, both, group[at - 1]) for piece, at in zip(apart, later)]
    return call(
        last_kernel,
        "last",
        struct(resid.shape, BF16),
        [(VMEM, value) for value in (hidden, near[0], *arrived)],
        pinned=False,
    )


def solution(mesh):
    placed = (
        P(("seq", "exp"), "head"),
        P(("seq", "exp"), "head"),
        P(("seq", "exp"), "head"),
        P(("seq", "exp"), "head"),
        P(("seq", "exp"), "head"),
        P("head"),
        P("head"),
        P("head"),
        P("head", None),
        P(("seq", "exp"), "head", None),
        P(("seq", "exp"), "head", None),
        P(("seq", "exp"), "head", None),
        P(),
        P(("head", "exp"), None, None),
        P(("head", "exp"), None, None),
    )
    return jax.shard_map(
        per_device,
        mesh=mesh,
        in_specs=placed,
        out_specs=P(("seq", "exp"), "head", None),
        check_vma=False,
    )
```

```python
import functools

import jax
import jax.numpy as jnp
from jax import lax
from jax.experimental import pallas as pl
from jax.experimental.pallas import tpu as pltpu
from jax.sharding import PartitionSpec as P

HEAD_DIM = 64
STATE = 128
LANES = 128
TILE = 16
FAR = -1e30
F32 = jnp.float32
BF16 = jnp.bfloat16
HBM = pl.BlockSpec(memory_space=pltpu.HBM)
VMEM = pl.BlockSpec(memory_space=pltpu.VMEM)
ANY = pl.BlockSpec(memory_space=pl.ANY)
NT = (((1,), (1,)), ((), ()))


def struct(shape, dtype):
    return jax.ShapeDtypeStruct(shape, dtype)


def call(kernel, name, outs, ins, scratch=(), megabytes=12, pinned=True):
    args = [pltpu.with_memory_space_constraint(arg, pltpu.HBM) if spec is HBM else arg for spec, arg in ins]
    return pl.pallas_call(
        kernel,
        out_shape=jax.tree.map(lambda out: pltpu.VMEM(out.shape, out.dtype), outs) if pinned else outs,
        in_specs=[spec for spec, _ in ins],
        out_specs=jax.tree.map(lambda _: VMEM, outs),
        scratch_shapes=list(scratch),
        name=name,
        compiler_params=pltpu.CompilerParams(vmem_limit_bytes=megabytes << 20),
    )(*args)


def offsets(count):
    down = list(range(count - 1, 0, -1))
    return [[3, 1, 2], [2, 3, 1]] if count == 4 else [down, down]


def targets(count):
    return [[1, 1, 2], [2, 3, 1]] if count == 4 else offsets(count)


def head_offset(slot, count):
    first, second = (order[slot] for order in offsets(count))
    return jnp.where(core_index() == 0, first, second)


def core_index():
    return lax.axis_index("exp") % 2


def chip_index():
    return lax.axis_index("exp") // 2


def copies(sems, sources, targets):
    made = [pltpu.make_async_copy(s, t, sems.at[i]) for i, (s, t) in enumerate(zip(sources, targets))]
    for copy in made:
        copy.start()
    return made


def decays(dt_rows, a_log):
    heads, length = dt_rows.shape
    step = jnp.maximum(dt_rows, 0.0) + jnp.log1p(jnp.exp(-jnp.abs(dt_rows)))
    same = lax.broadcasted_iota(jnp.int32, (heads, heads), 0) == lax.broadcasted_iota(jnp.int32, (heads, heads), 1)
    a_column = jnp.sum(jnp.where(same, jnp.broadcast_to(a_log, (heads, heads)), 0.0), axis=1, keepdims=True)
    rate = -step * jnp.exp(a_column)
    row = lax.broadcasted_iota(jnp.int32, (length, length), 0)
    col = lax.broadcasted_iota(jnp.int32, (length, length), 1)
    upper = (row <= col).astype(F32)
    cum = jnp.dot(rate, upper, precision=lax.Precision.HIGHEST, preferred_element_type=F32)
    return step, cum


def pair_lanes(values, pair):
    rows = values.shape[0]
    lane = lax.broadcasted_iota(jnp.int32, (rows, LANES), 1)
    left = jnp.broadcast_to(values[:, 2 * pair : 2 * pair + 1], (rows, LANES))
    right = jnp.broadcast_to(values[:, 2 * pair + 1 : 2 * pair + 2], (rows, LANES))
    return jnp.where(lane < HEAD_DIM, left, right)


def unpacked(block):
    pairs = block.shape[0] // STATE
    tail = block[pairs * STATE :].astype(F32)
    totals = [tail[pair : pair + 1] + tail[pairs + pair : pairs + pair + 1] for pair in range(pairs)]
    return jnp.stack(totals), block[: pairs * STATE].astype(F32).reshape(pairs, STATE, LANES)


def pack(ref, total, state):
    pairs = state.shape[0]
    ref[0 : pairs * STATE, :] = state.reshape(pairs * STATE, LANES).astype(BF16)
    row = lax.broadcasted_iota(jnp.int32, (TILE, LANES), 0)
    tail = jnp.zeros((TILE, LANES), F32)
    for pair in range(pairs):
        wide = jnp.broadcast_to(total[pair], (TILE, LANES))
        high = wide.astype(BF16).astype(F32)
        tail = jnp.where(row == pair, high, jnp.where(row == pairs + pair, wide - high, tail))
    ref[pairs * STATE :, :] = tail.astype(BF16)


def state_kernel(x_hbm, b_hbm, dt_hbm, a_hbm, keep_ref, send_ref, *scratch):
    x_ref, b_ref, dt_ref, a_ref, packed_ref, sems = scratch
    loads = copies(sems, (dt_hbm, a_hbm, x_hbm, b_hbm), (dt_ref, a_ref, x_ref, b_ref))
    loads[0].wait()
    loads[1].wait()
    step, cum = decays(dt_ref[...], a_ref[...])
    length = cum.shape[1]
    total = cum[:, length - 1 :]
    tail = (jnp.exp(total - cum) * step).T
    total = jnp.broadcast_to(total, cum.shape).T[0:1]
    loads[2].wait()
    loads[3].wait()
    pairs = x_ref.shape[1] // LANES
    half = pairs // 2
    groups = b_ref.shape[1] // STATE
    totals, states = [], []
    for group in range(groups):
        turned = b_ref[:, group * STATE : (group + 1) * STATE].T
        for pair in range(group * pairs // groups, (group + 1) * pairs // groups):
            x_pair = x_ref[:, pair * LANES : (pair + 1) * LANES].astype(F32)
            weighted = (pair_lanes(tail, pair) * x_pair).astype(BF16)
            state = jnp.dot(turned, weighted, preferred_element_type=F32)
            totals.append(pair_lanes(total, pair))
            states.append(state)
    for at in range(2):
        span = slice(at * half, (at + 1) * half)
        pack(packed_ref.at[at], totals[span], jnp.stack(states[span]))
    keep_ref[...] = packed_ref[core_index()]
    send_ref[...] = packed_ref[1 - core_index()]


def chip_state_kernel(after_ref, keep_ref, got_ref, out_ref):
    first = core_index() == 0
    keep, got = unpacked(keep_ref[...]), unpacked(got_ref[...])
    early = [jnp.where(first, mine, other) for mine, other in zip(keep, got)]
    late = [jnp.where(first, other, mine) for mine, other in zip(keep, got)]
    pack(out_ref, early[0] + late[0], jnp.exp(late[0]) * early[1] + late[1])


def weights_kernel(after_ref, up_hbm, down_hbm, up_ref, down_ref, sems):
    for load in copies(sems, (up_hbm, down_hbm), (up_ref, down_ref)):
        load.wait()


def span_kernel(*rest):
    ins, out_ref, block_ref = rest[:-2], rest[-2], rest[-1]
    for mask, part in enumerate(ins):
        block_ref[chip_index() ^ mask] = part[...]
    total, state = unpacked(block_ref[0])
    for chip in range(1, len(ins)):
        here, own = unpacked(block_ref[chip])
        total, state = total + here, jnp.exp(here) * state + own
    pack(out_ref, total, state)


def before_kernel(chips, parts, flat, after_a, after_b, keep_ref, got_ref, *rest):
    ins, (mine_ref, send_ref, chip_ref, part_ref) = rest[:-4], rest[-4:]
    first = core_index() == 0
    totals, states = (jnp.where(first, k, g) for k, g in zip(unpacked(keep_ref[...]), unpacked(got_ref[...])))
    place = chip_index()
    if flat:
        place = lax.axis_index("seq") * (lax.axis_size("exp") // 2) + place
    for mask in range(chips):
        chip_ref[place ^ mask] = ins[mask][...]
    for mask in range(parts):
        part_ref[lax.axis_index("seq") ^ mask] = ins[chips + mask][...]
    carry = jnp.zeros(states.shape, F32)
    for ref, count, own in ((part_ref, parts, lax.axis_index("seq")), (chip_ref, chips, place)):
        for index in range(count - 1):
            total, state = unpacked(ref[index])
            carry = jnp.where(index < own, jnp.exp(total) * carry + state, carry)
    later = jnp.exp(totals) * carry + states
    mine_ref[...] = jnp.where(first, carry, later).astype(BF16)
    send_ref[...] = jnp.where(first, later, carry).astype(BF16)


def inside_kernel(x_hbm, z_hbm, b_hbm, c_hbm, dt_hbm, a_hbm, d_hbm, local_ref, grown_ref, c_ref, *scratch):
    x_ref, z_ref, b_ref, dt_ref, a_ref, d_ref, sems = scratch
    loads = copies(
        sems,
        (dt_hbm, a_hbm, d_hbm, b_hbm, c_hbm, x_hbm, z_hbm),
        (dt_ref, a_ref, d_ref, b_ref, c_ref, x_ref, z_ref),
    )
    for load in loads:
        load.wait()
    step_rows, cum_rows = decays(dt_ref[...], a_ref[...])
    cum = cum_rows.T
    grown = jnp.exp(cum)
    length = cum.shape[0]
    pairs = x_ref.shape[1] // LANES
    groups = b_ref.shape[1] // STATE
    row = lax.broadcasted_iota(jnp.int32, (length, length), 0)
    col = lax.broadcasted_iota(jnp.int32, (length, length), 1)
    lane = lax.broadcasted_iota(jnp.int32, (length, LANES), 1)
    for group in range(groups):
        span = slice(group * STATE, (group + 1) * STATE)
        scores = lax.dot_general(c_ref[:, span], b_ref[:, span], NT, preferred_element_type=F32)
        scores = jnp.where(row >= col, scores, 0.0)
        for pair in range(group * pairs // groups, (group + 1) * pairs // groups):
            at = slice(pair * LANES, (pair + 1) * LANES)
            x_pair = x_ref[:, at]
            halves = []
            for head in (2 * pair, 2 * pair + 1):
                distance = cum[:, head : head + 1] - cum_rows[head : head + 1, :]
                decay = jnp.exp(jnp.where(row >= col, distance, FAR))
                mixing = (scores * (decay * step_rows[head : head + 1, :])).astype(BF16)
                halves.append(jnp.dot(mixing, x_pair, preferred_element_type=F32))
            inside = jnp.where(lane < HEAD_DIM, halves[0], halves[1])
            skip = pair_lanes(d_ref[...], pair) * x_pair.astype(F32)
            z = z_ref[:, at].astype(F32)
            gate = z / (1.0 + jnp.exp(-z))
            local_ref[:, at] = (inside + skip) * gate
            grown_ref[:, at] = pair_lanes(grown, pair) * gate


def projection_kernel(norm_hbm, w_hbm, norm_ref, w_ref, sems):
    for load in copies(sems, (norm_hbm, w_hbm), (norm_ref, w_ref)):
        load.wait()


def prep_kernel(experts, width, after_ref, resid_hbm, routes_hbm, gates_hbm, gain_hbm, *rest):
    gate_ref, resid_ref, gain_ref, routes_ref, gates_ref, sems = rest
    loads = copies(
        sems,
        (routes_hbm, gates_hbm, resid_hbm, gain_hbm),
        (routes_ref, gates_ref, resid_ref, gain_ref.at[0]),
    )
    loads[0].wait()
    loads[1].wait()
    count, extent = gate_ref.shape
    start = width // LANES * LANES
    lane = lax.broadcasted_iota(jnp.int32, (extent, count), 0) + start - width
    expert = jnp.where(lane >= experts, lane - experts, lane)
    gate = jnp.zeros((extent, count), F32)
    for pick in range(routes_ref.shape[0]):
        gate = gate + jnp.where(routes_ref[pick] == expert, gates_ref[pick], 0.0)
    high = gate.astype(BF16).astype(F32)
    gate = jnp.where(lane < experts, high, jnp.where(lane < 2 * experts, gate - high, 0.0))
    gate_ref[...] = gate.T.astype(BF16)
    for load in loads[2:]:
        load.wait()


def half_product(half, local_ref, grown_ref, c_ref, norm_ref, w_ref, state_ref, normed_ref, count):
    pairs = state_ref.shape[0]
    width = pairs * LANES
    base = pl.multiple_of(half * width, width)
    groups = c_ref.shape[1] // STATE // 2
    per_group = pairs // groups
    for group in range(groups):
        c_group = c_ref[:, pl.ds(pl.multiple_of((half * groups + group) * STATE, STATE), STATE)]
        gated, squares = [], 0.0
        for pair in range(group * per_group, (group + 1) * per_group):
            span = pl.ds(pl.multiple_of(base + pair * LANES, LANES), LANES)
            carried = jnp.dot(c_group, state_ref[pair], preferred_element_type=F32)
            value = local_ref[:, span] + grown_ref[:, span] * carried
            gated.append(value)
            squares = squares + value * value
        mean = jnp.sum(squares, axis=1, keepdims=True) / (per_group * LANES)
        inverse = lax.rsqrt(mean + 1e-05)
        for offset, value in enumerate(gated):
            pair = group * per_group + offset
            gain = norm_ref[:, pl.ds(pl.multiple_of(base + pair * LANES, LANES), LANES)]
            normed_ref[:, pair * LANES : (pair + 1) * LANES] = (value * inverse * gain).astype(BF16)
    rows = normed_ref.shape[0] // count
    blocks = []
    for shift in range(count):
        owner = lax.axis_index("head") ^ (head_offset(shift - 1, count) if shift else 0)
        blocks.append(normed_ref[pl.ds(pl.multiple_of(owner * rows, rows), rows), :])
    weight = w_ref[:, pl.ds(base, width)]
    return lax.dot_general(jnp.concatenate(blocks, axis=0), weight, NT, preferred_element_type=F32)


def first_half_kernel(count, local_ref, grown_ref, c_ref, norm_ref, w_ref, mine_ref, out_ref, normed_ref):
    out_ref[...] = half_product(
        core_index(), local_ref, grown_ref, c_ref, norm_ref, w_ref, mine_ref, normed_ref, count
    )


def mixed_kernel(after_up, after_down, local_ref, grown_ref, c_ref, norm_ref, w_ref, got_ref, first_ref, *rest):
    outs, normed_ref = rest[:-1], rest[-1]
    product = first_ref[...] + half_product(
        1 - core_index(), local_ref, grown_ref, c_ref, norm_ref, w_ref, got_ref, normed_ref, len(outs)
    )
    rows = outs[0].shape[0]
    for shift, out in enumerate(outs):
        out[...] = product[shift * rows : (shift + 1) * rows].astype(BF16)


def relay_kernel(own_ref, got_ref, out_ref):
    got = jnp.where(core_index() == 0, got_ref[...].astype(F32), 0.0)
    out_ref[...] = (own_ref[...].astype(F32) + got).astype(BF16)


def rows_kernel(after_ref, resid_ref, gate_ref, gain_ref, *rest):
    parts, hidden_ref, rows_ref = rest[:-2], rest[-2], rest[-1]
    mixed = parts[0][...].astype(F32)
    for at, part in enumerate(parts[1:]):
        value = part[...].astype(F32)
        if at == 0 and len(parts) == 4:
            value = jnp.where(core_index() == 1, value, 0.0)
        mixed = mixed + value
    hidden = (resid_ref[0].astype(F32) + mixed).astype(BF16)
    hidden_ref[...] = hidden
    value = hidden.astype(F32)
    scale = lax.rsqrt(jnp.mean(value * value, axis=1, keepdims=True) + 1e-05)
    width = value.shape[1]
    rows_ref[:, width // LANES * LANES :] = gate_ref[...]
    rows_ref[:, :width] = (value * scale * gain_ref[...]).astype(BF16)


def expert_kernel(experts, count, carried, up_ref, down_ref, other_up_ref, other_down_ref, *rest):
    ins, done, outs = rest[:count], rest[count : count + len(carried)], rest[count + len(carried) :]
    width = up_ref.shape[2]
    start = width // LANES * LANES
    rows = jnp.concatenate([ref[:, :width] for ref in ins], axis=0)
    tail = jnp.concatenate([ref[:, start:] for ref in ins], axis=0).astype(F32)
    lane = lax.broadcasted_iota(jnp.int32, tail.shape, 1) + start - width
    own = lax.axis_index("head") * lax.axis_size("exp") + lax.axis_index("exp")
    other = own + 1 - 2 * core_index()
    total = 0.0
    for expert, up_of, down_of in ((own, up_ref, down_ref), (other, other_up_ref, other_down_ref)):
        up = lax.dot_general(rows, up_of[0], NT, preferred_element_type=F32)
        up = jnp.maximum(up, 0.0)
        activated = (up * up).astype(BF16)
        chosen = (lane == expert) | (lane == expert + experts)
        gate = jnp.sum(jnp.where(chosen, tail, 0.0), axis=1, keepdims=True)
        total = total + jnp.dot(activated, down_of[0], preferred_element_type=F32) * gate
    size = ins[0].shape[0]
    for at, out in enumerate(outs):
        out[0:size] = total[at * size : (at + 1) * size].astype(BF16)
    for at, ref in zip(carried, done):
        outs[at][size:] = ref[...]


def sum_kernel(*refs):
    rows = refs[-1].shape[0]
    total = refs[0][...].astype(F32)
    for ref in refs[1:-1]:
        total = total + ref[0:rows].astype(F32)
    refs[-1][...] = total.astype(BF16)


def last_kernel(hidden_ref, *rest):
    parts, out_ref = rest[:-1], rest[-1]
    rows = out_ref.shape[1]
    total = parts[0][...].astype(F32)
    for part in parts[1:]:
        total = total + part[part.shape[0] - rows :].astype(F32)
    out_ref[0] = (hidden_ref[...].astype(F32) + total).astype(BF16)


def swap(value, axis, mask):
    size = lax.axis_size(axis)
    return lax.ppermute(value, axis, [(i, i ^ mask) for i in range(size)])


def swap_slot(value, slot):
    heads, size = lax.axis_size("head"), lax.axis_size("exp")
    order = targets(heads)
    pairs = []
    for i in range(heads * size):
        head, exp = i // size, i % size
        pairs.append((i, (head ^ order[exp % 2][slot]) * size + exp))
    return lax.ppermute(value, ("head", "exp"), pairs)


def per_device(
    x_in, z_in, b_in, c_in, dt_in, a_log, d_skip, norm_w, w_out, resid, routes, gates, moe_gain, w_up, w_down
):
    length, heads = dt_in.shape
    channels = x_in.shape[1]
    model = w_out.shape[1]
    hidden_units = w_up.shape[2]
    seq_size, head_size, exp_size = lax.axis_size("seq"), lax.axis_size("head"), lax.axis_size("exp")
    chips = exp_size // 2
    rows = resid.shape[1]
    experts = head_size * exp_size
    pairs = channels // LANES
    half = pairs // 2
    dt_rows, a_row, d_row = dt_in.T, a_log[None], d_skip[None]
    dma = pltpu.SemaphoreType.DMA
    packed = struct((half * STATE + TILE, LANES), BF16)

    keep, send = call(
        state_kernel,
        "state",
        [packed, packed],
        [(HBM, x_in), (HBM, b_in), (HBM, dt_rows), (HBM, a_row)],
        [pltpu.VMEM(x_in.shape, BF16), pltpu.VMEM(b_in.shape, BF16), pltpu.VMEM(dt_rows.shape, F32),
         pltpu.VMEM(a_row.shape, F32), pltpu.VMEM((2, half * STATE + TILE, LANES), BF16), dma((4,))],
        megabytes=16,
    )
    local, grown, c_held = call(
        inside_kernel,
        "inside",
        [struct((length, channels), F32), struct((length, channels), F32), struct(c_in.shape, BF16)],
        [(HBM, value) for value in (x_in, z_in, b_in, c_in, dt_rows, a_row, d_row)],
        [pltpu.VMEM(x_in.shape, BF16), pltpu.VMEM(z_in.shape, BF16), pltpu.VMEM(b_in.shape, BF16),
         pltpu.VMEM(dt_rows.shape, F32), pltpu.VMEM(a_row.shape, F32), pltpu.VMEM(d_row.shape, F32), dma((7,))],
        megabytes=16,
    )
    wide = -(-(model + 2 * experts) // LANES) * LANES
    turned = [jnp.transpose(value, (2, 0, 1)) for value in (routes, gates)]
    norm_held, w_held = call(
        projection_kernel,
        "projection",
        [struct((1, channels), F32), struct((model, channels), BF16)],
        [(HBM, norm_w[None]), (HBM, w_out.T)],
        [dma((2,))],
    )
    gate_lanes, resid_held, gain_held = call(
        functools.partial(prep_kernel, experts, model),
        "prep",
        [struct((rows, wide - model // LANES * LANES), BF16), struct(resid.shape, BF16), struct((1, model), F32)],
        [(ANY, keep)] + [(HBM, value) for value in (resid, *turned, moe_gain)],
        [pltpu.VMEM(turned[0].shape, jnp.int32), pltpu.VMEM(turned[1].shape, F32), dma((4,))],
        megabytes=16,
    )
    up_turned = jnp.swapaxes(w_up, 1, 2)
    got = swap(send, "exp", 1)
    chip = call(chip_state_kernel, "chip_state", packed, [(ANY, gate_lanes), (VMEM, keep), (VMEM, got)])
    chip, up_after, down_after = lax.optimization_barrier((chip, up_turned, w_down))
    other_up, other_down = swap(up_after, "exp", 1), swap(down_after, "exp", 1)
    flat = seq_size * chips <= 8
    if flat:
        masks = [x * exp_size + 2 * y for x in range(seq_size) for y in range(chips)]
        exchanged = [chip] + [swap(chip, ("seq", "exp"), mask) for mask in masks[1:]]
        counts = (seq_size * chips, 0)
    else:
        along_y = [chip] + [swap(chip, "exp", 2 * d) for d in range(1, chips)]
        span = call(
            span_kernel,
            "span",
            packed,
            [(VMEM, value) for value in along_y],
            [pltpu.VMEM((chips, *packed.shape), BF16)],
        )
        exchanged = along_y + [span] + [swap(span, "seq", d) for d in range(1, seq_size)]
        counts = (chips, seq_size)
    before, before_send = call(
        functools.partial(before_kernel, *counts, flat),
        "before",
        [struct((half, STATE, LANES), BF16)] * 2,
        [(ANY, norm_held), (ANY, c_held)] + [(VMEM, value) for value in (keep, got, *exchanged)],
        [pltpu.VMEM((counts[0], *packed.shape), BF16), pltpu.VMEM((max(1, counts[1]), *packed.shape), BF16)],
        megabytes=24,
    )
    before_got = swap(before_send, "exp", 1)
    shared = [(VMEM, value) for value in (local, grown, c_held, norm_held, w_held)]
    normed_half = pltpu.VMEM((length, channels // 2), BF16)
    first = call(
        functools.partial(first_half_kernel, head_size),
        "first_half",
        struct((length, model), F32),
        shared + [(VMEM, before)],
        [normed_half],
    )
    mixed = call(
        mixed_kernel,
        "mixed",
        [struct((rows, model), BF16)] * head_size,
        [(ANY, other_up), (ANY, other_down)] + shared + [(VMEM, before_got), (VMEM, first)],
        [normed_half],
    )
    up_held, down_held = call(
        weights_kernel,
        "weights",
        [struct(up_turned.shape, BF16), struct(w_down.shape, BF16)],
        [(ANY, mixed[0]), (HBM, up_turned), (HBM, w_down)],
        [dma((2,))],
    )
    slots = list(range(head_size - 1))
    parts, last = [swap_slot(mixed[k + 1], k) for k in slots[:-1]], mixed[-1]
    if head_size == 4:
        last = call(relay_kernel, "relay", struct((rows, model), BF16), [(VMEM, last), (VMEM, parts[0])])
    parts = [mixed[0]] + parts + [swap_slot(last, slots[-1])]
    hidden, own_rows = call(
        rows_kernel,
        "rows",
        [struct((rows, model), BF16), struct((rows, wide), BF16)],
        [(ANY, up_held)] + [(VMEM, value) for value in (resid_held, gate_lanes, gain_held, *parts)],
    )

    def through_experts(members, carried=()):
        places = [at for at, _ in carried]
        return call(
            functools.partial(expert_kernel, experts, len(members), places),
            "experts",
            [struct((rows * (2 if at in places else 1), model), BF16) for at in range(len(members))],
            [(VMEM, value) for value in (up_held, down_held, other_up, other_down, *members)]
            + [(VMEM, value) for _, value in carried],
            megabytes=16,
        )

    both = ("head", "exp")
    group = [z * exp_size + 2 * d for z in (0, 1) for d in range(chips)][1:]

    def spread(block):
        return [block] + [swap(block, both, mask) for mask in group]

    sets = [spread(swap(own_rows, "head", high)) for high in range(2, head_size, 2)]
    near = through_experts(spread(own_rows))
    near, sets = lax.optimization_barrier((near, sets))
    joined = [at for at, mask in enumerate(group, 1) if mask == exp_size]
    arrived, later = [], [at for at, mask in enumerate(group, 1) if mask < exp_size]
    apart = [near[at] for at in later]
    for high, members in zip(range(2, head_size, 2), sets):
        pieces = through_experts(members, [(at, near[at]) for at in joined] if high == 2 else ())
        got = [swap(piece, both, mask) for piece, mask in zip(pieces[:0:-1], group[::-1])]
        total = call(sum_kernel, "sum", struct((rows, model), BF16), [(VMEM, v) for v in (pieces[0], *got)])
        if high == 2:
            arrived += [part for part, mask in zip(got, group[::-1]) if mask == exp_size]
        arrived.append(swap(total, "head", high))
    arrived += [swap(near[at], both, mask) for at, mask in enumerate(group, 1) if mask > exp_size]
    arrived += [swap(piece, both, group[at - 1]) for piece, at in zip(apart, later)]
    return call(
        last_kernel,
        "last",
        struct(resid.shape, BF16),
        [(VMEM, value) for value in (hidden, near[0], *arrived)],
        pinned=False,
    )


def solution(mesh):
    placed = (
        P(("seq", "exp"), "head"),
        P(("seq", "exp"), "head"),
        P(("seq", "exp"), "head"),
        P(("seq", "exp"), "head"),
        P(("seq", "exp"), "head"),
        P("head"),
        P("head"),
        P("head"),
        P("head", None),
        P(("seq", "exp"), "head", None),
        P(("seq", "exp"), "head", None),
        P(("seq", "exp"), "head", None),
        P(),
        P(("head", "exp"), None, None),
        P(("head", "exp"), None, None),
    )
    return jax.shard_map(
        per_device,
        mesh=mesh,
        in_specs=placed,
        out_specs=P(("seq", "exp"), "head", None),
        check_vma=False,
    )
```

```python
import functools

import jax
import jax.numpy as jnp
from jax import lax
from jax.experimental import pallas as pl
from jax.experimental.pallas import tpu as pltpu
from jax.sharding import PartitionSpec as P

HEAD_DIM = 64
STATE = 128
LANES = 128
TILE = 16
FAR = -1e30
F32 = jnp.float32
BF16 = jnp.bfloat16
HBM = pl.BlockSpec(memory_space=pltpu.HBM)
VMEM = pl.BlockSpec(memory_space=pltpu.VMEM)
ANY = pl.BlockSpec(memory_space=pl.ANY)
NT = (((1,), (1,)), ((), ()))


def struct(shape, dtype):
    return jax.ShapeDtypeStruct(shape, dtype)


def call(kernel, name, outs, ins, scratch=(), megabytes=12, pinned=True):
    args = [pltpu.with_memory_space_constraint(arg, pltpu.HBM) if spec is HBM else arg for spec, arg in ins]
    return pl.pallas_call(
        kernel,
        out_shape=jax.tree.map(lambda out: pltpu.VMEM(out.shape, out.dtype), outs) if pinned else outs,
        in_specs=[spec for spec, _ in ins],
        out_specs=jax.tree.map(lambda _: VMEM, outs),
        scratch_shapes=list(scratch),
        name=name,
        compiler_params=pltpu.CompilerParams(vmem_limit_bytes=megabytes << 20),
    )(*args)


def offsets(count):
    down = list(range(count - 1, 0, -1))
    return [[3, 1, 2], [2, 3, 1]] if count == 4 else [down, down]


def targets(count):
    return [[1, 1, 2], [2, 3, 1]] if count == 4 else offsets(count)


def head_offset(slot, count):
    first, second = (order[slot] for order in offsets(count))
    return jnp.where(core_index() == 0, first, second)


def core_index():
    return lax.axis_index("exp") % 2


def chip_index():
    return lax.axis_index("exp") // 2


def copies(sems, sources, targets):
    made = [pltpu.make_async_copy(s, t, sems.at[i]) for i, (s, t) in enumerate(zip(sources, targets))]
    for copy in made:
        copy.start()
    return made


def decays(dt_rows, a_log):
    heads, length = dt_rows.shape
    step = jnp.maximum(dt_rows, 0.0) + jnp.log1p(jnp.exp(-jnp.abs(dt_rows)))
    same = lax.broadcasted_iota(jnp.int32, (heads, heads), 0) == lax.broadcasted_iota(jnp.int32, (heads, heads), 1)
    a_column = jnp.sum(jnp.where(same, jnp.broadcast_to(a_log, (heads, heads)), 0.0), axis=1, keepdims=True)
    rate = -step * jnp.exp(a_column)
    row = lax.broadcasted_iota(jnp.int32, (length, length), 0)
    col = lax.broadcasted_iota(jnp.int32, (length, length), 1)
    upper = (row <= col).astype(F32)
    cum = jnp.dot(rate, upper, precision=lax.Precision.HIGHEST, preferred_element_type=F32)
    return step, cum


def pair_lanes(values, pair):
    rows = values.shape[0]
    lane = lax.broadcasted_iota(jnp.int32, (rows, LANES), 1)
    left = jnp.broadcast_to(values[:, 2 * pair : 2 * pair + 1], (rows, LANES))
    right = jnp.broadcast_to(values[:, 2 * pair + 1 : 2 * pair + 2], (rows, LANES))
    return jnp.where(lane < HEAD_DIM, left, right)


def unpacked(block):
    pairs = block.shape[0] // STATE
    tail = block[pairs * STATE :].astype(F32)
    totals = [tail[pair : pair + 1] + tail[pairs + pair : pairs + pair + 1] for pair in range(pairs)]
    return jnp.stack(totals), block[: pairs * STATE].astype(F32).reshape(pairs, STATE, LANES)


def pack(ref, total, state):
    pairs = state.shape[0]
    ref[0 : pairs * STATE, :] = state.reshape(pairs * STATE, LANES).astype(BF16)
    row = lax.broadcasted_iota(jnp.int32, (TILE, LANES), 0)
    tail = jnp.zeros((TILE, LANES), F32)
    for pair in range(pairs):
        wide = jnp.broadcast_to(total[pair], (TILE, LANES))
        high = wide.astype(BF16).astype(F32)
        tail = jnp.where(row == pair, high, jnp.where(row == pairs + pair, wide - high, tail))
    ref[pairs * STATE :, :] = tail.astype(BF16)


def state_kernel(x_hbm, b_hbm, dt_hbm, a_hbm, keep_ref, send_ref, *scratch):
    x_ref, b_ref, dt_ref, a_ref, packed_ref, sems = scratch
    loads = copies(sems, (dt_hbm, a_hbm, x_hbm, b_hbm), (dt_ref, a_ref, x_ref, b_ref))
    loads[0].wait()
    loads[1].wait()
    step, cum = decays(dt_ref[...], a_ref[...])
    length = cum.shape[1]
    total = cum[:, length - 1 :]
    tail = (jnp.exp(total - cum) * step).T
    total = jnp.broadcast_to(total, cum.shape).T[0:1]
    loads[2].wait()
    loads[3].wait()
    pairs = x_ref.shape[1] // LANES
    half = pairs // 2
    groups = b_ref.shape[1] // STATE
    totals, states = [], []
    for group in range(groups):
        turned = b_ref[:, group * STATE : (group + 1) * STATE].T
        for pair in range(group * pairs // groups, (group + 1) * pairs // groups):
            x_pair = x_ref[:, pair * LANES : (pair + 1) * LANES].astype(F32)
            weighted = (pair_lanes(tail, pair) * x_pair).astype(BF16)
            state = jnp.dot(turned, weighted, preferred_element_type=F32)
            totals.append(pair_lanes(total, pair))
            states.append(state)
    for at in range(2):
        span = slice(at * half, (at + 1) * half)
        pack(packed_ref.at[at], totals[span], jnp.stack(states[span]))
    keep_ref[...] = packed_ref[core_index()]
    send_ref[...] = packed_ref[1 - core_index()]


def chip_state_kernel(after_ref, keep_ref, got_ref, out_ref):
    first = core_index() == 0
    keep, got = unpacked(keep_ref[...]), unpacked(got_ref[...])
    early = [jnp.where(first, mine, other) for mine, other in zip(keep, got)]
    late = [jnp.where(first, other, mine) for mine, other in zip(keep, got)]
    pack(out_ref, early[0] + late[0], jnp.exp(late[0]) * early[1] + late[1])


def weights_kernel(after_ref, up_hbm, down_hbm, up_ref, down_ref, sems):
    for load in copies(sems, (up_hbm, down_hbm), (up_ref, down_ref)):
        load.wait()


def span_kernel(*rest):
    ins, out_ref, block_ref = rest[:-2], rest[-2], rest[-1]
    for mask, part in enumerate(ins):
        block_ref[chip_index() ^ mask] = part[...]
    total, state = unpacked(block_ref[0])
    for chip in range(1, len(ins)):
        here, own = unpacked(block_ref[chip])
        total, state = total + here, jnp.exp(here) * state + own
    pack(out_ref, total, state)


def before_kernel(chips, parts, flat, after_a, after_b, keep_ref, got_ref, *rest):
    ins, (mine_ref, send_ref, chip_ref, part_ref) = rest[:-4], rest[-4:]
    first = core_index() == 0
    totals, states = (jnp.where(first, k, g) for k, g in zip(unpacked(keep_ref[...]), unpacked(got_ref[...])))
    place = chip_index()
    if flat:
        place = lax.axis_index("seq") * (lax.axis_size("exp") // 2) + place
    for mask in range(chips):
        chip_ref[place ^ mask] = ins[mask][...]
    for mask in range(parts):
        part_ref[lax.axis_index("seq") ^ mask] = ins[chips + mask][...]
    carry = jnp.zeros(states.shape, F32)
    for ref, count, own in ((part_ref, parts, lax.axis_index("seq")), (chip_ref, chips, place)):
        for index in range(count - 1):
            total, state = unpacked(ref[index])
            carry = jnp.where(index < own, jnp.exp(total) * carry + state, carry)
    later = jnp.exp(totals) * carry + states
    mine_ref[...] = jnp.where(first, carry, later).astype(BF16)
    send_ref[...] = jnp.where(first, later, carry).astype(BF16)


def inside_kernel(x_hbm, z_hbm, b_hbm, c_hbm, dt_hbm, a_hbm, d_hbm, local_ref, grown_ref, c_ref, *scratch):
    x_ref, z_ref, b_ref, dt_ref, a_ref, d_ref, sems = scratch
    loads = copies(
        sems,
        (dt_hbm, a_hbm, d_hbm, b_hbm, c_hbm, x_hbm, z_hbm),
        (dt_ref, a_ref, d_ref, b_ref, c_ref, x_ref, z_ref),
    )
    for load in loads:
        load.wait()
    step_rows, cum_rows = decays(dt_ref[...], a_ref[...])
    cum = cum_rows.T
    grown = jnp.exp(cum)
    length = cum.shape[0]
    pairs = x_ref.shape[1] // LANES
    groups = b_ref.shape[1] // STATE
    row = lax.broadcasted_iota(jnp.int32, (length, length), 0)
    col = lax.broadcasted_iota(jnp.int32, (length, length), 1)
    lane = lax.broadcasted_iota(jnp.int32, (length, LANES), 1)
    for group in range(groups):
        span = slice(group * STATE, (group + 1) * STATE)
        scores = lax.dot_general(c_ref[:, span], b_ref[:, span], NT, preferred_element_type=F32)
        scores = jnp.where(row >= col, scores, 0.0)
        for pair in range(group * pairs // groups, (group + 1) * pairs // groups):
            at = slice(pair * LANES, (pair + 1) * LANES)
            x_pair = x_ref[:, at]
            halves = []
            for head in (2 * pair, 2 * pair + 1):
                distance = cum[:, head : head + 1] - cum_rows[head : head + 1, :]
                decay = jnp.exp(jnp.where(row >= col, distance, FAR))
                mixing = (scores * (decay * step_rows[head : head + 1, :])).astype(BF16)
                halves.append(jnp.dot(mixing, x_pair, preferred_element_type=F32))
            inside = jnp.where(lane < HEAD_DIM, halves[0], halves[1])
            skip = pair_lanes(d_ref[...], pair) * x_pair.astype(F32)
            z = z_ref[:, at].astype(F32)
            gate = z / (1.0 + jnp.exp(-z))
            local_ref[:, at] = (inside + skip) * gate
            grown_ref[:, at] = pair_lanes(grown, pair) * gate


def projection_kernel(norm_hbm, w_hbm, norm_ref, w_ref, sems):
    for load in copies(sems, (norm_hbm, w_hbm), (norm_ref, w_ref)):
        load.wait()


def prep_kernel(experts, width, after_ref, resid_hbm, routes_hbm, gates_hbm, gain_hbm, *rest):
    gate_ref, resid_ref, gain_ref, routes_ref, gates_ref, sems = rest
    loads = copies(
        sems,
        (routes_hbm, gates_hbm, resid_hbm, gain_hbm),
        (routes_ref, gates_ref, resid_ref, gain_ref.at[0]),
    )
    loads[0].wait()
    loads[1].wait()
    count, extent = gate_ref.shape
    start = width // LANES * LANES
    lane = lax.broadcasted_iota(jnp.int32, (extent, count), 0) + start - width
    expert = jnp.where(lane >= experts, lane - experts, lane)
    gate = jnp.zeros((extent, count), F32)
    for pick in range(routes_ref.shape[0]):
        gate = gate + jnp.where(routes_ref[pick] == expert, gates_ref[pick], 0.0)
    high = gate.astype(BF16).astype(F32)
    gate = jnp.where(lane < experts, high, jnp.where(lane < 2 * experts, gate - high, 0.0))
    gate_ref[...] = gate.T.astype(BF16)
    for load in loads[2:]:
        load.wait()


def half_product(half, local_ref, grown_ref, c_ref, norm_ref, w_ref, state_ref, normed_ref, count):
    pairs = state_ref.shape[0]
    width = pairs * LANES
    base = pl.multiple_of(half * width, width)
    groups = c_ref.shape[1] // STATE // 2
    per_group = pairs // groups
    for group in range(groups):
        c_group = c_ref[:, pl.ds(pl.multiple_of((half * groups + group) * STATE, STATE), STATE)]
        gated, squares = [], 0.0
        for pair in range(group * per_group, (group + 1) * per_group):
            span = pl.ds(pl.multiple_of(base + pair * LANES, LANES), LANES)
            carried = jnp.dot(c_group, state_ref[pair], preferred_element_type=F32)
            value = local_ref[:, span] + grown_ref[:, span] * carried
            gated.append(value)
            squares = squares + value * value
        mean = jnp.sum(squares, axis=1, keepdims=True) / (per_group * LANES)
        inverse = lax.rsqrt(mean + 1e-05)
        for offset, value in enumerate(gated):
            pair = group * per_group + offset
            gain = norm_ref[:, pl.ds(pl.multiple_of(base + pair * LANES, LANES), LANES)]
            normed_ref[:, pair * LANES : (pair + 1) * LANES] = (value * inverse * gain).astype(BF16)
    rows = normed_ref.shape[0] // count
    blocks = []
    for shift in range(count):
        owner = lax.axis_index("head") ^ (head_offset(shift - 1, count) if shift else 0)
        blocks.append(normed_ref[pl.ds(pl.multiple_of(owner * rows, rows), rows), :])
    weight = w_ref[:, pl.ds(base, width)]
    return lax.dot_general(jnp.concatenate(blocks, axis=0), weight, NT, preferred_element_type=F32)


def first_half_kernel(count, local_ref, grown_ref, c_ref, norm_ref, w_ref, mine_ref, out_ref, normed_ref):
    out_ref[...] = half_product(
        core_index(), local_ref, grown_ref, c_ref, norm_ref, w_ref, mine_ref, normed_ref, count
    )


def mixed_kernel(after_up, after_down, local_ref, grown_ref, c_ref, norm_ref, w_ref, got_ref, first_ref, *rest):
    outs, normed_ref = rest[:-1], rest[-1]
    product = first_ref[...] + half_product(
        1 - core_index(), local_ref, grown_ref, c_ref, norm_ref, w_ref, got_ref, normed_ref, len(outs)
    )
    rows = outs[0].shape[0]
    for shift, out in enumerate(outs):
        out[...] = product[shift * rows : (shift + 1) * rows].astype(BF16)


def relay_kernel(own_ref, got_ref, out_ref):
    got = jnp.where(core_index() == 0, got_ref[...].astype(F32), 0.0)
    out_ref[...] = (own_ref[...].astype(F32) + got).astype(BF16)


def rows_kernel(after_ref, resid_ref, gate_ref, gain_ref, *rest):
    parts, hidden_ref, rows_ref = rest[:-2], rest[-2], rest[-1]
    mixed = parts[0][...].astype(F32)
    for at, part in enumerate(parts[1:]):
        value = part[...].astype(F32)
        if at == 0 and len(parts) == 4:
            value = jnp.where(core_index() == 1, value, 0.0)
        mixed = mixed + value
    hidden = (resid_ref[0].astype(F32) + mixed).astype(BF16)
    hidden_ref[...] = hidden
    value = hidden.astype(F32)
    scale = lax.rsqrt(jnp.mean(value * value, axis=1, keepdims=True) + 1e-05)
    width = value.shape[1]
    rows_ref[:, width // LANES * LANES :] = gate_ref[...]
    rows_ref[:, :width] = (value * scale * gain_ref[...]).astype(BF16)


def expert_kernel(experts, count, carried, up_ref, down_ref, other_up_ref, other_down_ref, *rest):
    ins, done, outs = rest[:count], rest[count : count + len(carried)], rest[count + len(carried) :]
    width = up_ref.shape[2]
    start = width // LANES * LANES
    rows = jnp.concatenate([ref[:, :width] for ref in ins], axis=0)
    tail = jnp.concatenate([ref[:, start:] for ref in ins], axis=0).astype(F32)
    lane = lax.broadcasted_iota(jnp.int32, tail.shape, 1) + start - width
    own = lax.axis_index("head") * lax.axis_size("exp") + lax.axis_index("exp")
    other = own + 1 - 2 * core_index()
    total = 0.0
    for expert, up_of, down_of in ((own, up_ref, down_ref), (other, other_up_ref, other_down_ref)):
        up = lax.dot_general(rows, up_of[0], NT, preferred_element_type=F32)
        up = jnp.maximum(up, 0.0)
        activated = (up * up).astype(BF16)
        chosen = (lane == expert) | (lane == expert + experts)
        gate = jnp.sum(jnp.where(chosen, tail, 0.0), axis=1, keepdims=True)
        total = total + jnp.dot(activated, down_of[0], preferred_element_type=F32) * gate
    size = ins[0].shape[0]
    for at, out in enumerate(outs):
        out[0:size] = total[at * size : (at + 1) * size].astype(BF16)
    for at, ref in zip(carried, done):
        outs[at][size:] = ref[...]


def sum_kernel(*refs):
    rows = refs[-1].shape[0]
    total = refs[0][...].astype(F32)
    for ref in refs[1:-1]:
        total = total + ref[0:rows].astype(F32)
    refs[-1][...] = total.astype(BF16)


def last_kernel(hidden_ref, *rest):
    parts, out_ref = rest[:-1], rest[-1]
    rows = out_ref.shape[1]
    total = parts[0][...].astype(F32)
    for part in parts[1:]:
        total = total + part[part.shape[0] - rows :].astype(F32)
    out_ref[0] = (hidden_ref[...].astype(F32) + total).astype(BF16)


def swap(value, axis, mask):
    size = lax.axis_size(axis)
    return lax.ppermute(value, axis, [(i, i ^ mask) for i in range(size)])


def swap_slot(value, slot):
    heads, size = lax.axis_size("head"), lax.axis_size("exp")
    order = targets(heads)
    pairs = []
    for i in range(heads * size):
        head, exp = i // size, i % size
        pairs.append((i, (head ^ order[exp % 2][slot]) * size + exp))
    return lax.ppermute(value, ("head", "exp"), pairs)


def per_device(
    x_in, z_in, b_in, c_in, dt_in, a_log, d_skip, norm_w, w_out, resid, routes, gates, moe_gain, w_up, w_down
):
    length, heads = dt_in.shape
    channels = x_in.shape[1]
    model = w_out.shape[1]
    hidden_units = w_up.shape[2]
    seq_size, head_size, exp_size = lax.axis_size("seq"), lax.axis_size("head"), lax.axis_size("exp")
    chips = exp_size // 2
    rows = resid.shape[1]
    experts = head_size * exp_size
    pairs = channels // LANES
    half = pairs // 2
    dt_rows, a_row, d_row = dt_in.T, a_log[None], d_skip[None]
    dma = pltpu.SemaphoreType.DMA
    packed = struct((half * STATE + TILE, LANES), BF16)

    keep, send = call(
        state_kernel,
        "state",
        [packed, packed],
        [(HBM, x_in), (HBM, b_in), (HBM, dt_rows), (HBM, a_row)],
        [pltpu.VMEM(x_in.shape, BF16), pltpu.VMEM(b_in.shape, BF16), pltpu.VMEM(dt_rows.shape, F32),
         pltpu.VMEM(a_row.shape, F32), pltpu.VMEM((2, half * STATE + TILE, LANES), BF16), dma((4,))],
        megabytes=16,
    )
    local, grown, c_held = call(
        inside_kernel,
        "inside",
        [struct((length, channels), F32), struct((length, channels), F32), struct(c_in.shape, BF16)],
        [(HBM, value) for value in (x_in, z_in, b_in, c_in, dt_rows, a_row, d_row)],
        [pltpu.VMEM(x_in.shape, BF16), pltpu.VMEM(z_in.shape, BF16), pltpu.VMEM(b_in.shape, BF16),
         pltpu.VMEM(dt_rows.shape, F32), pltpu.VMEM(a_row.shape, F32), pltpu.VMEM(d_row.shape, F32), dma((7,))],
        megabytes=16,
    )
    wide = -(-(model + 2 * experts) // LANES) * LANES
    turned = [jnp.transpose(value, (2, 0, 1)) for value in (routes, gates)]
    norm_held, w_held = call(
        projection_kernel,
        "projection",
        [struct((1, channels), F32), struct((model, channels), BF16)],
        [(HBM, norm_w[None]), (HBM, w_out.T)],
        [dma((2,))],
    )
    gate_lanes, resid_held, gain_held = call(
        functools.partial(prep_kernel, experts, model),
        "prep",
        [struct((rows, wide - model // LANES * LANES), BF16), struct(resid.shape, BF16), struct((1, model), F32)],
        [(ANY, keep)] + [(HBM, value) for value in (resid, *turned, moe_gain)],
        [pltpu.VMEM(turned[0].shape, jnp.int32), pltpu.VMEM(turned[1].shape, F32), dma((4,))],
        megabytes=16,
    )
    up_turned = jnp.swapaxes(w_up, 1, 2)
    got = swap(send, "exp", 1)
    chip = call(chip_state_kernel, "chip_state", packed, [(ANY, gate_lanes), (VMEM, keep), (VMEM, got)])
    chip, up_after, down_after = lax.optimization_barrier((chip, up_turned, w_down))
    other_up, other_down = swap(up_after, "exp", 1), swap(down_after, "exp", 1)
    flat = seq_size * chips <= 8
    if flat:
        masks = [x * exp_size + 2 * y for x in range(seq_size) for y in range(chips)]
        exchanged = [chip] + [swap(chip, ("seq", "exp"), mask) for mask in masks[1:]]
        counts = (seq_size * chips, 0)
    else:
        along_y = [chip] + [swap(chip, "exp", 2 * d) for d in range(1, chips)]
        span = call(
            span_kernel,
            "span",
            packed,
            [(VMEM, value) for value in along_y],
            [pltpu.VMEM((chips, *packed.shape), BF16)],
        )
        exchanged = along_y + [span] + [swap(span, "seq", d) for d in range(1, seq_size)]
        counts = (chips, seq_size)
    before, before_send = call(
        functools.partial(before_kernel, *counts, flat),
        "before",
        [struct((half, STATE, LANES), BF16)] * 2,
        [(ANY, norm_held), (ANY, c_held)] + [(VMEM, value) for value in (keep, got, *exchanged)],
        [pltpu.VMEM((counts[0], *packed.shape), BF16), pltpu.VMEM((max(1, counts[1]), *packed.shape), BF16)],
        megabytes=24,
    )
    before_got = swap(before_send, "exp", 1)
    shared = [(VMEM, value) for value in (local, grown, c_held, norm_held, w_held)]
    normed_half = pltpu.VMEM((length, channels // 2), BF16)
    first = call(
        functools.partial(first_half_kernel, head_size),
        "first_half",
        struct((length, model), F32),
        shared + [(VMEM, before)],
        [normed_half],
    )
    mixed = call(
        mixed_kernel,
        "mixed",
        [struct((rows, model), BF16)] * head_size,
        [(ANY, other_up), (ANY, other_down)] + shared + [(VMEM, before_got), (VMEM, first)],
        [normed_half],
    )
    up_held, down_held = call(
        weights_kernel,
        "weights",
        [struct(up_turned.shape, BF16), struct(w_down.shape, BF16)],
        [(ANY, mixed[0]), (HBM, up_turned), (HBM, w_down)],
        [dma((2,))],
    )
    slots = list(range(head_size - 1))
    parts, last = [swap_slot(mixed[k + 1], k) for k in slots[:-1]], mixed[-1]
    if head_size == 4:
        last = call(relay_kernel, "relay", struct((rows, model), BF16), [(VMEM, last), (VMEM, parts[0])])
    parts = [mixed[0]] + parts + [swap_slot(last, slots[-1])]
    hidden, own_rows = call(
        rows_kernel,
        "rows",
        [struct((rows, model), BF16), struct((rows, wide), BF16)],
        [(ANY, up_held)] + [(VMEM, value) for value in (resid_held, gate_lanes, gain_held, *parts)],
    )

    def through_experts(members, carried=()):
        places = [at for at, _ in carried]
        return call(
            functools.partial(expert_kernel, experts, len(members), places),
            "experts",
            [struct((rows * (2 if at in places else 1), model), BF16) for at in range(len(members))],
            [(VMEM, value) for value in (up_held, down_held, other_up, other_down, *members)]
            + [(VMEM, value) for _, value in carried],
            megabytes=16,
        )

    both = ("head", "exp")
    group = [z * exp_size + 2 * d for z in (0, 1) for d in range(chips)][1:]

    def spread(block):
        return [block] + [swap(block, both, mask) for mask in group]

    sets = [spread(swap(own_rows, "head", high)) for high in range(2, head_size, 2)]
    near = through_experts(spread(own_rows))
    near, sets = lax.optimization_barrier((near, sets))
    joined = [at for at, mask in enumerate(group, 1) if mask == exp_size]
    arrived, later = [], [at for at, mask in enumerate(group, 1) if mask < exp_size]
    apart = [near[at] for at in later]
    for high, members in zip(range(2, head_size, 2), sets):
        pieces = through_experts(members, [(at, near[at]) for at in joined] if high == 2 else ())
        got = [swap(piece, both, mask) for piece, mask in zip(pieces[1:], group)]
        total = call(sum_kernel, "sum", struct((rows, model), BF16), [(VMEM, v) for v in (pieces[0], *got)])
        if high == 2:
            arrived += [part for part, mask in zip(got, group) if mask == exp_size]
        arrived.append(swap(total, "head", high))
    arrived += [swap(near[at], both, mask) for at, mask in enumerate(group, 1) if mask > exp_size]
    arrived += [swap(piece, both, group[at - 1]) for piece, at in zip(apart, later)]
    return call(
        last_kernel,
        "last",
        struct(resid.shape, BF16),
        [(VMEM, value) for value in (hidden, near[0], *arrived)],
        pinned=False,
    )


def solution(mesh):
    placed = (
        P(("seq", "exp"), "head"),
        P(("seq", "exp"), "head"),
        P(("seq", "exp"), "head"),
        P(("seq", "exp"), "head"),
        P(("seq", "exp"), "head"),
        P("head"),
        P("head"),
        P("head"),
        P("head", None),
        P(("seq", "exp"), "head", None),
        P(("seq", "exp"), "head", None),
        P(("seq", "exp"), "head", None),
        P(),
        P(("head", "exp"), None, None),
        P(("head", "exp"), None, None),
    )
    return jax.shard_map(
        per_device,
        mesh=mesh,
        in_specs=placed,
        out_specs=P(("seq", "exp"), "head", None),
        check_vma=False,
    )
```

```python
import functools

import jax
import jax.numpy as jnp
from jax import lax
from jax.experimental import pallas as pl
from jax.experimental.pallas import tpu as pltpu
from jax.sharding import PartitionSpec as P

HEAD_DIM = 64
STATE = 128
LANES = 128
TILE = 16
FAR = -1e30
F32 = jnp.float32
BF16 = jnp.bfloat16
HBM = pl.BlockSpec(memory_space=pltpu.HBM)
VMEM = pl.BlockSpec(memory_space=pltpu.VMEM)
ANY = pl.BlockSpec(memory_space=pl.ANY)
NT = (((1,), (1,)), ((), ()))


def struct(shape, dtype):
    return jax.ShapeDtypeStruct(shape, dtype)


def call(kernel, name, outs, ins, scratch=(), megabytes=12, pinned=True):
    args = [pltpu.with_memory_space_constraint(arg, pltpu.HBM) if spec is HBM else arg for spec, arg in ins]
    return pl.pallas_call(
        kernel,
        out_shape=jax.tree.map(lambda out: pltpu.VMEM(out.shape, out.dtype), outs) if pinned else outs,
        in_specs=[spec for spec, _ in ins],
        out_specs=jax.tree.map(lambda _: VMEM, outs),
        scratch_shapes=list(scratch),
        name=name,
        compiler_params=pltpu.CompilerParams(vmem_limit_bytes=megabytes << 20),
    )(*args)


def offsets(count):
    down = list(range(count - 1, 0, -1))
    return [[3, 1, 2], [2, 3, 1]] if count == 4 else [down, down]


def targets(count):
    return [[1, 1, 2], [2, 3, 1]] if count == 4 else offsets(count)


def head_offset(slot, count):
    first, second = (order[slot] for order in offsets(count))
    return jnp.where(core_index() == 0, first, second)


def core_index():
    return lax.axis_index("exp") % 2


def chip_index():
    return lax.axis_index("exp") // 2


def copies(sems, sources, targets):
    made = [pltpu.make_async_copy(s, t, sems.at[i]) for i, (s, t) in enumerate(zip(sources, targets))]
    for copy in made:
        copy.start()
    return made


def decays(dt_rows, a_log):
    heads, length = dt_rows.shape
    step = jnp.maximum(dt_rows, 0.0) + jnp.log1p(jnp.exp(-jnp.abs(dt_rows)))
    same = lax.broadcasted_iota(jnp.int32, (heads, heads), 0) == lax.broadcasted_iota(jnp.int32, (heads, heads), 1)
    a_column = jnp.sum(jnp.where(same, jnp.broadcast_to(a_log, (heads, heads)), 0.0), axis=1, keepdims=True)
    rate = -step * jnp.exp(a_column)
    row = lax.broadcasted_iota(jnp.int32, (length, length), 0)
    col = lax.broadcasted_iota(jnp.int32, (length, length), 1)
    upper = (row <= col).astype(F32)
    cum = jnp.dot(rate, upper, precision=lax.Precision.HIGHEST, preferred_element_type=F32)
    return step, cum


def pair_lanes(values, pair):
    rows = values.shape[0]
    lane = lax.broadcasted_iota(jnp.int32, (rows, LANES), 1)
    left = jnp.broadcast_to(values[:, 2 * pair : 2 * pair + 1], (rows, LANES))
    right = jnp.broadcast_to(values[:, 2 * pair + 1 : 2 * pair + 2], (rows, LANES))
    return jnp.where(lane < HEAD_DIM, left, right)


def unpacked(block):
    pairs = block.shape[0] // STATE
    tail = block[pairs * STATE :].astype(F32)
    totals = [tail[pair : pair + 1] + tail[pairs + pair : pairs + pair + 1] for pair in range(pairs)]
    return jnp.stack(totals), block[: pairs * STATE].astype(F32).reshape(pairs, STATE, LANES)


def pack(ref, total, state):
    pairs = state.shape[0]
    ref[0 : pairs * STATE, :] = state.reshape(pairs * STATE, LANES).astype(BF16)
    row = lax.broadcasted_iota(jnp.int32, (TILE, LANES), 0)
    tail = jnp.zeros((TILE, LANES), F32)
    for pair in range(pairs):
        wide = jnp.broadcast_to(total[pair], (TILE, LANES))
        high = wide.astype(BF16).astype(F32)
        tail = jnp.where(row == pair, high, jnp.where(row == pairs + pair, wide - high, tail))
    ref[pairs * STATE :, :] = tail.astype(BF16)


def state_kernel(x_hbm, b_hbm, dt_hbm, a_hbm, keep_ref, send_ref, *scratch):
    x_ref, b_ref, dt_ref, a_ref, packed_ref, sems = scratch
    loads = copies(sems, (dt_hbm, a_hbm, x_hbm, b_hbm), (dt_ref, a_ref, x_ref, b_ref))
    loads[0].wait()
    loads[1].wait()
    step, cum = decays(dt_ref[...], a_ref[...])
    length = cum.shape[1]
    total = cum[:, length - 1 :]
    tail = (jnp.exp(total - cum) * step).T
    total = jnp.broadcast_to(total, cum.shape).T[0:1]
    loads[2].wait()
    loads[3].wait()
    pairs = x_ref.shape[1] // LANES
    half = pairs // 2
    groups = b_ref.shape[1] // STATE
    totals, states = [], []
    for group in range(groups):
        turned = b_ref[:, group * STATE : (group + 1) * STATE].T
        for pair in range(group * pairs // groups, (group + 1) * pairs // groups):
            x_pair = x_ref[:, pair * LANES : (pair + 1) * LANES].astype(F32)
            weighted = (pair_lanes(tail, pair) * x_pair).astype(BF16)
            state = jnp.dot(turned, weighted, preferred_element_type=F32)
            totals.append(pair_lanes(total, pair))
            states.append(state)
    for at in range(2):
        span = slice(at * half, (at + 1) * half)
        pack(packed_ref.at[at], totals[span], jnp.stack(states[span]))
    keep_ref[...] = packed_ref[core_index()]
    send_ref[...] = packed_ref[1 - core_index()]


def chip_state_kernel(after_ref, keep_ref, got_ref, out_ref):
    first = core_index() == 0
    keep, got = unpacked(keep_ref[...]), unpacked(got_ref[...])
    early = [jnp.where(first, mine, other) for mine, other in zip(keep, got)]
    late = [jnp.where(first, other, mine) for mine, other in zip(keep, got)]
    pack(out_ref, early[0] + late[0], jnp.exp(late[0]) * early[1] + late[1])


def weights_kernel(after_ref, up_hbm, down_hbm, up_ref, down_ref, sems):
    for load in copies(sems, (up_hbm, down_hbm), (up_ref, down_ref)):
        load.wait()


def span_kernel(*rest):
    ins, out_ref, block_ref = rest[:-2], rest[-2], rest[-1]
    for mask, part in enumerate(ins):
        block_ref[chip_index() ^ mask] = part[...]
    total, state = unpacked(block_ref[0])
    for chip in range(1, len(ins)):
        here, own = unpacked(block_ref[chip])
        total, state = total + here, jnp.exp(here) * state + own
    pack(out_ref, total, state)


def before_kernel(chips, parts, flat, after_a, after_b, keep_ref, got_ref, *rest):
    ins, (mine_ref, send_ref, chip_ref, part_ref) = rest[:-4], rest[-4:]
    first = core_index() == 0
    totals, states = (jnp.where(first, k, g) for k, g in zip(unpacked(keep_ref[...]), unpacked(got_ref[...])))
    place = chip_index()
    if flat:
        place = lax.axis_index("seq") * (lax.axis_size("exp") // 2) + place
    for mask in range(chips):
        chip_ref[place ^ mask] = ins[mask][...]
    for mask in range(parts):
        part_ref[lax.axis_index("seq") ^ mask] = ins[chips + mask][...]
    carry = jnp.zeros(states.shape, F32)
    for ref, count, own in ((part_ref, parts, lax.axis_index("seq")), (chip_ref, chips, place)):
        for index in range(count - 1):
            total, state = unpacked(ref[index])
            carry = jnp.where(index < own, jnp.exp(total) * carry + state, carry)
    later = jnp.exp(totals) * carry + states
    mine_ref[...] = jnp.where(first, carry, later).astype(BF16)
    send_ref[...] = jnp.where(first, later, carry).astype(BF16)


def inside_kernel(x_hbm, z_hbm, b_hbm, c_hbm, dt_hbm, a_hbm, d_hbm, local_ref, grown_ref, c_ref, *scratch):
    x_ref, z_ref, b_ref, dt_ref, a_ref, d_ref, sems = scratch
    loads = copies(
        sems,
        (dt_hbm, a_hbm, d_hbm, b_hbm, c_hbm, x_hbm, z_hbm),
        (dt_ref, a_ref, d_ref, b_ref, c_ref, x_ref, z_ref),
    )
    for load in loads:
        load.wait()
    step_rows, cum_rows = decays(dt_ref[...], a_ref[...])
    cum = cum_rows.T
    grown = jnp.exp(cum)
    length = cum.shape[0]
    pairs = x_ref.shape[1] // LANES
    groups = b_ref.shape[1] // STATE
    row = lax.broadcasted_iota(jnp.int32, (length, length), 0)
    col = lax.broadcasted_iota(jnp.int32, (length, length), 1)
    lane = lax.broadcasted_iota(jnp.int32, (length, LANES), 1)
    for group in range(groups):
        span = slice(group * STATE, (group + 1) * STATE)
        scores = lax.dot_general(c_ref[:, span], b_ref[:, span], NT, preferred_element_type=F32)
        scores = jnp.where(row >= col, scores, 0.0)
        for pair in range(group * pairs // groups, (group + 1) * pairs // groups):
            at = slice(pair * LANES, (pair + 1) * LANES)
            x_pair = x_ref[:, at]
            halves = []
            for head in (2 * pair, 2 * pair + 1):
                distance = cum[:, head : head + 1] - cum_rows[head : head + 1, :]
                decay = jnp.exp(jnp.where(row >= col, distance, FAR))
                mixing = (scores * (decay * step_rows[head : head + 1, :])).astype(BF16)
                halves.append(jnp.dot(mixing, x_pair, preferred_element_type=F32))
            inside = jnp.where(lane < HEAD_DIM, halves[0], halves[1])
            skip = pair_lanes(d_ref[...], pair) * x_pair.astype(F32)
            z = z_ref[:, at].astype(F32)
            gate = z / (1.0 + jnp.exp(-z))
            local_ref[:, at] = (inside + skip) * gate
            grown_ref[:, at] = pair_lanes(grown, pair) * gate


def projection_kernel(norm_hbm, w_hbm, norm_ref, w_ref, sems):
    for load in copies(sems, (norm_hbm, w_hbm), (norm_ref, w_ref)):
        load.wait()


def prep_kernel(experts, width, after_ref, resid_hbm, routes_hbm, gates_hbm, gain_hbm, *rest):
    gate_ref, resid_ref, gain_ref, routes_ref, gates_ref, sems = rest
    loads = copies(
        sems,
        (routes_hbm, gates_hbm, resid_hbm, gain_hbm),
        (routes_ref, gates_ref, resid_ref, gain_ref.at[0]),
    )
    loads[0].wait()
    loads[1].wait()
    count, extent = gate_ref.shape
    start = width // LANES * LANES
    lane = lax.broadcasted_iota(jnp.int32, (extent, count), 0) + start - width
    expert = jnp.where(lane >= experts, lane - experts, lane)
    gate = jnp.zeros((extent, count), F32)
    for pick in range(routes_ref.shape[0]):
        gate = gate + jnp.where(routes_ref[pick] == expert, gates_ref[pick], 0.0)
    high = gate.astype(BF16).astype(F32)
    gate = jnp.where(lane < experts, high, jnp.where(lane < 2 * experts, gate - high, 0.0))
    gate_ref[...] = gate.T.astype(BF16)
    for load in loads[2:]:
        load.wait()


def half_product(half, local_ref, grown_ref, c_ref, norm_ref, w_ref, state_ref, normed_ref, count):
    pairs = state_ref.shape[0]
    width = pairs * LANES
    base = pl.multiple_of(half * width, width)
    groups = c_ref.shape[1] // STATE // 2
    per_group = pairs // groups
    for group in range(groups):
        c_group = c_ref[:, pl.ds(pl.multiple_of((half * groups + group) * STATE, STATE), STATE)]
        gated, squares = [], 0.0
        for pair in range(group * per_group, (group + 1) * per_group):
            span = pl.ds(pl.multiple_of(base + pair * LANES, LANES), LANES)
            carried = jnp.dot(c_group, state_ref[pair], preferred_element_type=F32)
            value = local_ref[:, span] + grown_ref[:, span] * carried
            gated.append(value)
            squares = squares + value * value
        mean = jnp.sum(squares, axis=1, keepdims=True) / (per_group * LANES)
        inverse = lax.rsqrt(mean + 1e-05)
        for offset, value in enumerate(gated):
            pair = group * per_group + offset
            gain = norm_ref[:, pl.ds(pl.multiple_of(base + pair * LANES, LANES), LANES)]
            normed_ref[:, pair * LANES : (pair + 1) * LANES] = (value * inverse * gain).astype(BF16)
    rows = normed_ref.shape[0] // count
    blocks = []
    for shift in range(count):
        owner = lax.axis_index("head") ^ (head_offset(shift - 1, count) if shift else 0)
        blocks.append(normed_ref[pl.ds(pl.multiple_of(owner * rows, rows), rows), :])
    weight = w_ref[:, pl.ds(base, width)]
    return lax.dot_general(jnp.concatenate(blocks, axis=0), weight, NT, preferred_element_type=F32)


def first_half_kernel(count, local_ref, grown_ref, c_ref, norm_ref, w_ref, mine_ref, out_ref, normed_ref):
    out_ref[...] = half_product(
        core_index(), local_ref, grown_ref, c_ref, norm_ref, w_ref, mine_ref, normed_ref, count
    )


def mixed_kernel(after_up, after_down, local_ref, grown_ref, c_ref, norm_ref, w_ref, got_ref, first_ref, *rest):
    outs, normed_ref = rest[:-1], rest[-1]
    product = first_ref[...] + half_product(
        1 - core_index(), local_ref, grown_ref, c_ref, norm_ref, w_ref, got_ref, normed_ref, len(outs)
    )
    rows = outs[0].shape[0]
    for shift, out in enumerate(outs):
        out[...] = product[shift * rows : (shift + 1) * rows].astype(BF16)


def relay_kernel(own_ref, got_ref, out_ref):
    got = jnp.where(core_index() == 0, got_ref[...].astype(F32), 0.0)
    out_ref[...] = (own_ref[...].astype(F32) + got).astype(BF16)


def rows_kernel(after_ref, resid_ref, gate_ref, gain_ref, *rest):
    parts, hidden_ref, rows_ref = rest[:-2], rest[-2], rest[-1]
    mixed = parts[0][...].astype(F32)
    for at, part in enumerate(parts[1:]):
        value = part[...].astype(F32)
        if at == 0 and len(parts) == 4:
            value = jnp.where(core_index() == 1, value, 0.0)
        mixed = mixed + value
    hidden = (resid_ref[0].astype(F32) + mixed).astype(BF16)
    hidden_ref[...] = hidden
    value = hidden.astype(F32)
    scale = lax.rsqrt(jnp.mean(value * value, axis=1, keepdims=True) + 1e-05)
    width = value.shape[1]
    rows_ref[:, width // LANES * LANES :] = gate_ref[...]
    rows_ref[:, :width] = (value * scale * gain_ref[...]).astype(BF16)


def expert_kernel(experts, count, carried, up_ref, down_ref, other_up_ref, other_down_ref, *rest):
    ins, done, outs = rest[:count], rest[count : count + len(carried)], rest[count + len(carried) :]
    width = up_ref.shape[2]
    start = width // LANES * LANES
    rows = jnp.concatenate([ref[:, :width] for ref in ins], axis=0)
    tail = jnp.concatenate([ref[:, start:] for ref in ins], axis=0).astype(F32)
    lane = lax.broadcasted_iota(jnp.int32, tail.shape, 1) + start - width
    own = lax.axis_index("head") * lax.axis_size("exp") + lax.axis_index("exp")
    other = own + 1 - 2 * core_index()
    total = 0.0
    for expert, up_of, down_of in ((own, up_ref, down_ref), (other, other_up_ref, other_down_ref)):
        up = lax.dot_general(rows, up_of[0], NT, preferred_element_type=F32)
        up = jnp.maximum(up, 0.0)
        activated = (up * up).astype(BF16)
        chosen = (lane == expert) | (lane == expert + experts)
        gate = jnp.sum(jnp.where(chosen, tail, 0.0), axis=1, keepdims=True)
        total = total + jnp.dot(activated, down_of[0], preferred_element_type=F32) * gate
    size = ins[0].shape[0]
    for at, out in enumerate(outs):
        out[0:size] = total[at * size : (at + 1) * size].astype(BF16)
    for at, ref in zip(carried, done):
        outs[at][size:] = ref[...]


def sum_kernel(*refs):
    rows = refs[-1].shape[0]
    total = refs[0][...].astype(F32)
    for ref in refs[1:-1]:
        total = total + ref[0:rows].astype(F32)
    refs[-1][...] = total.astype(BF16)


def last_kernel(hidden_ref, *rest):
    parts, out_ref = rest[:-1], rest[-1]
    rows = out_ref.shape[1]
    total = parts[0][...].astype(F32)
    for part in parts[1:]:
        total = total + part[part.shape[0] - rows :].astype(F32)
    out_ref[0] = (hidden_ref[...].astype(F32) + total).astype(BF16)


def swap(value, axis, mask):
    size = lax.axis_size(axis)
    return lax.ppermute(value, axis, [(i, i ^ mask) for i in range(size)])


def swap_slot(value, slot):
    heads, size = lax.axis_size("head"), lax.axis_size("exp")
    order = targets(heads)
    pairs = []
    for i in range(heads * size):
        head, exp = i // size, i % size
        pairs.append((i, (head ^ order[exp % 2][slot]) * size + exp))
    return lax.ppermute(value, ("head", "exp"), pairs)


def per_device(
    x_in, z_in, b_in, c_in, dt_in, a_log, d_skip, norm_w, w_out, resid, routes, gates, moe_gain, w_up, w_down
):
    length, heads = dt_in.shape
    channels = x_in.shape[1]
    model = w_out.shape[1]
    hidden_units = w_up.shape[2]
    seq_size, head_size, exp_size = lax.axis_size("seq"), lax.axis_size("head"), lax.axis_size("exp")
    chips = exp_size // 2
    rows = resid.shape[1]
    experts = head_size * exp_size
    pairs = channels // LANES
    half = pairs // 2
    dt_rows, a_row, d_row = dt_in.T, a_log[None], d_skip[None]
    dma = pltpu.SemaphoreType.DMA
    packed = struct((half * STATE + TILE, LANES), BF16)

    keep, send = call(
        state_kernel,
        "state",
        [packed, packed],
        [(HBM, x_in), (HBM, b_in), (HBM, dt_rows), (HBM, a_row)],
        [pltpu.VMEM(x_in.shape, BF16), pltpu.VMEM(b_in.shape, BF16), pltpu.VMEM(dt_rows.shape, F32),
         pltpu.VMEM(a_row.shape, F32), pltpu.VMEM((2, half * STATE + TILE, LANES), BF16), dma((4,))],
        megabytes=16,
    )
    local, grown, c_held = call(
        inside_kernel,
        "inside",
        [struct((length, channels), F32), struct((length, channels), F32), struct(c_in.shape, BF16)],
        [(HBM, value) for value in (x_in, z_in, b_in, c_in, dt_rows, a_row, d_row)],
        [pltpu.VMEM(x_in.shape, BF16), pltpu.VMEM(z_in.shape, BF16), pltpu.VMEM(b_in.shape, BF16),
         pltpu.VMEM(dt_rows.shape, F32), pltpu.VMEM(a_row.shape, F32), pltpu.VMEM(d_row.shape, F32), dma((7,))],
        megabytes=16,
    )
    wide = -(-(model + 2 * experts) // LANES) * LANES
    turned = [jnp.transpose(value, (2, 0, 1)) for value in (routes, gates)]
    norm_held, w_held = call(
        projection_kernel,
        "projection",
        [struct((1, channels), F32), struct((model, channels), BF16)],
        [(HBM, norm_w[None]), (HBM, w_out.T)],
        [dma((2,))],
    )
    gate_lanes, resid_held, gain_held = call(
        functools.partial(prep_kernel, experts, model),
        "prep",
        [struct((rows, wide - model // LANES * LANES), BF16), struct(resid.shape, BF16), struct((1, model), F32)],
        [(ANY, keep)] + [(HBM, value) for value in (resid, *turned, moe_gain)],
        [pltpu.VMEM(turned[0].shape, jnp.int32), pltpu.VMEM(turned[1].shape, F32), dma((4,))],
        megabytes=16,
    )
    up_turned = jnp.swapaxes(w_up, 1, 2)
    got = swap(send, "exp", 1)
    chip = call(chip_state_kernel, "chip_state", packed, [(ANY, gate_lanes), (VMEM, keep), (VMEM, got)])
    chip, up_after, down_after = lax.optimization_barrier((chip, up_turned, w_down))
    other_up, other_down = swap(up_after, "exp", 1), swap(down_after, "exp", 1)
    flat = seq_size * chips <= 8
    if flat:
        masks = [x * exp_size + 2 * y for x in range(seq_size) for y in range(chips)]
        exchanged = [chip] + [swap(chip, ("seq", "exp"), mask) for mask in masks[1:]]
        counts = (seq_size * chips, 0)
    else:
        along_y = [chip] + [swap(chip, "exp", 2 * d) for d in range(1, chips)]
        span = call(
            span_kernel,
            "span",
            packed,
            [(VMEM, value) for value in along_y],
            [pltpu.VMEM((chips, *packed.shape), BF16)],
        )
        exchanged = along_y + [span] + [swap(span, "seq", d) for d in range(1, seq_size)]
        counts = (chips, seq_size)
    before, before_send = call(
        functools.partial(before_kernel, *counts, flat),
        "before",
        [struct((half, STATE, LANES), BF16)] * 2,
        [(ANY, norm_held), (ANY, c_held)] + [(VMEM, value) for value in (keep, got, *exchanged)],
        [pltpu.VMEM((counts[0], *packed.shape), BF16), pltpu.VMEM((max(1, counts[1]), *packed.shape), BF16)],
        megabytes=24,
    )
    before_got = swap(before_send, "exp", 1)
    shared = [(VMEM, value) for value in (local, grown, c_held, norm_held, w_held)]
    normed_half = pltpu.VMEM((length, channels // 2), BF16)
    first = call(
        functools.partial(first_half_kernel, head_size),
        "first_half",
        struct((length, model), F32),
        shared + [(VMEM, before)],
        [normed_half],
    )
    mixed = call(
        mixed_kernel,
        "mixed",
        [struct((rows, model), BF16)] * head_size,
        [(ANY, other_up), (ANY, other_down)] + shared + [(VMEM, before_got), (VMEM, first)],
        [normed_half],
    )
    up_held, down_held = call(
        weights_kernel,
        "weights",
        [struct(up_turned.shape, BF16), struct(w_down.shape, BF16)],
        [(ANY, mixed[0]), (HBM, up_turned), (HBM, w_down)],
        [dma((2,))],
    )
    slots = list(range(head_size - 1))
    parts, last = [swap_slot(mixed[k + 1], k) for k in slots[:-1]], mixed[-1]
    if head_size == 4:
        last = call(relay_kernel, "relay", struct((rows, model), BF16), [(VMEM, last), (VMEM, parts[0])])
    parts = [mixed[0]] + parts + [swap_slot(last, slots[-1])]
    hidden, own_rows = call(
        rows_kernel,
        "rows",
        [struct((rows, model), BF16), struct((rows, wide), BF16)],
        [(ANY, up_held)] + [(VMEM, value) for value in (resid_held, gate_lanes, gain_held, *parts)],
    )

    def through_experts(members, carried=()):
        places = [at for at, _ in carried]
        return call(
            functools.partial(expert_kernel, experts, len(members), places),
            "experts",
            [struct((rows * (2 if at in places else 1), model), BF16) for at in range(len(members))],
            [(VMEM, value) for value in (up_held, down_held, other_up, other_down, *members)]
            + [(VMEM, value) for _, value in carried],
            megabytes=16,
        )

    both = ("head", "exp")
    group = [z * exp_size + 2 * d for z in (0, 1) for d in range(chips)][1:]

    def spread(block):
        return [block] + [swap(block, both, mask) for mask in group]

    sets = [spread(swap(own_rows, "head", high)) for high in range(2, head_size, 2)]
    near = through_experts([own_rows] + [swap(own_rows, both, mask) for mask in group[::-1]])
    near, sets = lax.optimization_barrier(([near[0], *near[:0:-1]], sets))
    joined = [at for at, mask in enumerate(group, 1) if mask == exp_size]
    arrived, later = [], [at for at, mask in enumerate(group, 1) if mask < exp_size]
    apart = [near[at] for at in later]
    for high, members in zip(range(2, head_size, 2), sets):
        pieces = through_experts(members, [(at, near[at]) for at in joined] if high == 2 else ())
        got = [swap(piece, both, mask) for piece, mask in zip(pieces[1:], group)]
        total = call(sum_kernel, "sum", struct((rows, model), BF16), [(VMEM, v) for v in (pieces[0], *got)])
        if high == 2:
            arrived += [part for part, mask in zip(got, group) if mask == exp_size]
        arrived.append(swap(total, "head", high))
    arrived += [swap(near[at], both, mask) for at, mask in enumerate(group, 1) if mask > exp_size]
    arrived += [swap(piece, both, group[at - 1]) for piece, at in zip(apart, later)]
    return call(
        last_kernel,
        "last",
        struct(resid.shape, BF16),
        [(VMEM, value) for value in (hidden, near[0], *arrived)],
        pinned=False,
    )


def solution(mesh):
    placed = (
        P(("seq", "exp"), "head"),
        P(("seq", "exp"), "head"),
        P(("seq", "exp"), "head"),
        P(("seq", "exp"), "head"),
        P(("seq", "exp"), "head"),
        P("head"),
        P("head"),
        P("head"),
        P("head", None),
        P(("seq", "exp"), "head", None),
        P(("seq", "exp"), "head", None),
        P(("seq", "exp"), "head", None),
        P(),
        P(("head", "exp"), None, None),
        P(("head", "exp"), None, None),
    )
    return jax.shard_map(
        per_device,
        mesh=mesh,
        in_specs=placed,
        out_specs=P(("seq", "exp"), "head", None),
        check_vma=False,
    )
```

```python
import functools

import jax
import jax.numpy as jnp
from jax import lax
from jax.experimental import pallas as pl
from jax.experimental.pallas import tpu as pltpu
from jax.sharding import PartitionSpec as P

HEAD_DIM = 64
STATE = 128
LANES = 128
TILE = 16
FAR = -1e30
F32 = jnp.float32
BF16 = jnp.bfloat16
HBM = pl.BlockSpec(memory_space=pltpu.HBM)
VMEM = pl.BlockSpec(memory_space=pltpu.VMEM)
ANY = pl.BlockSpec(memory_space=pl.ANY)
NT = (((1,), (1,)), ((), ()))


def struct(shape, dtype):
    return jax.ShapeDtypeStruct(shape, dtype)


def call(kernel, name, outs, ins, scratch=(), megabytes=12, pinned=True):
    args = [pltpu.with_memory_space_constraint(arg, pltpu.HBM) if spec is HBM else arg for spec, arg in ins]
    return pl.pallas_call(
        kernel,
        out_shape=jax.tree.map(lambda out: pltpu.VMEM(out.shape, out.dtype), outs) if pinned else outs,
        in_specs=[spec for spec, _ in ins],
        out_specs=jax.tree.map(lambda _: VMEM, outs),
        scratch_shapes=list(scratch),
        name=name,
        compiler_params=pltpu.CompilerParams(vmem_limit_bytes=megabytes << 20),
    )(*args)


def offsets(count):
    down = list(range(count - 1, 0, -1))
    return [[3, 1, 2], [2, 3, 1]] if count == 4 else [down, down]


def targets(count):
    return [[1, 1, 2], [2, 3, 1]] if count == 4 else offsets(count)


def head_offset(slot, count):
    first, second = (order[slot] for order in offsets(count))
    return jnp.where(core_index() == 0, first, second)


def core_index():
    return lax.axis_index("exp") % 2


def chip_index():
    return lax.axis_index("exp") // 2


def copies(sems, sources, targets):
    made = [pltpu.make_async_copy(s, t, sems.at[i]) for i, (s, t) in enumerate(zip(sources, targets))]
    for copy in made:
        copy.start()
    return made


def decays(dt_rows, a_log):
    heads, length = dt_rows.shape
    step = jnp.maximum(dt_rows, 0.0) + jnp.log1p(jnp.exp(-jnp.abs(dt_rows)))
    same = lax.broadcasted_iota(jnp.int32, (heads, heads), 0) == lax.broadcasted_iota(jnp.int32, (heads, heads), 1)
    a_column = jnp.sum(jnp.where(same, jnp.broadcast_to(a_log, (heads, heads)), 0.0), axis=1, keepdims=True)
    rate = -step * jnp.exp(a_column)
    row = lax.broadcasted_iota(jnp.int32, (length, length), 0)
    col = lax.broadcasted_iota(jnp.int32, (length, length), 1)
    upper = (row <= col).astype(F32)
    cum = jnp.dot(rate, upper, precision=lax.Precision.HIGHEST, preferred_element_type=F32)
    return step, cum


def pair_lanes(values, pair):
    rows = values.shape[0]
    lane = lax.broadcasted_iota(jnp.int32, (rows, LANES), 1)
    left = jnp.broadcast_to(values[:, 2 * pair : 2 * pair + 1], (rows, LANES))
    right = jnp.broadcast_to(values[:, 2 * pair + 1 : 2 * pair + 2], (rows, LANES))
    return jnp.where(lane < HEAD_DIM, left, right)


def unpacked(block):
    pairs = block.shape[0] // STATE
    tail = block[pairs * STATE :].astype(F32)
    totals = [tail[pair : pair + 1] + tail[pairs + pair : pairs + pair + 1] for pair in range(pairs)]
    return jnp.stack(totals), block[: pairs * STATE].astype(F32).reshape(pairs, STATE, LANES)


def pack(ref, total, state):
    pairs = state.shape[0]
    ref[0 : pairs * STATE, :] = state.reshape(pairs * STATE, LANES).astype(BF16)
    row = lax.broadcasted_iota(jnp.int32, (TILE, LANES), 0)
    tail = jnp.zeros((TILE, LANES), F32)
    for pair in range(pairs):
        wide = jnp.broadcast_to(total[pair], (TILE, LANES))
        high = wide.astype(BF16).astype(F32)
        tail = jnp.where(row == pair, high, jnp.where(row == pairs + pair, wide - high, tail))
    ref[pairs * STATE :, :] = tail.astype(BF16)


def state_kernel(x_hbm, b_hbm, dt_hbm, a_hbm, keep_ref, send_ref, *scratch):
    x_ref, b_ref, dt_ref, a_ref, packed_ref, sems = scratch
    loads = copies(sems, (dt_hbm, a_hbm, x_hbm, b_hbm), (dt_ref, a_ref, x_ref, b_ref))
    loads[0].wait()
    loads[1].wait()
    step, cum = decays(dt_ref[...], a_ref[...])
    length = cum.shape[1]
    total = cum[:, length - 1 :]
    tail = (jnp.exp(total - cum) * step).T
    total = jnp.broadcast_to(total, cum.shape).T[0:1]
    loads[2].wait()
    loads[3].wait()
    pairs = x_ref.shape[1] // LANES
    half = pairs // 2
    groups = b_ref.shape[1] // STATE
    totals, states = [], []
    for group in range(groups):
        turned = b_ref[:, group * STATE : (group + 1) * STATE].T
        for pair in range(group * pairs // groups, (group + 1) * pairs // groups):
            x_pair = x_ref[:, pair * LANES : (pair + 1) * LANES].astype(F32)
            weighted = (pair_lanes(tail, pair) * x_pair).astype(BF16)
            state = jnp.dot(turned, weighted, preferred_element_type=F32)
            totals.append(pair_lanes(total, pair))
            states.append(state)
    for at in range(2):
        span = slice(at * half, (at + 1) * half)
        pack(packed_ref.at[at], totals[span], jnp.stack(states[span]))
    keep_ref[...] = packed_ref[core_index()]
    send_ref[...] = packed_ref[1 - core_index()]


def chip_state_kernel(after_ref, keep_ref, got_ref, out_ref):
    first = core_index() == 0
    keep, got = unpacked(keep_ref[...]), unpacked(got_ref[...])
    early = [jnp.where(first, mine, other) for mine, other in zip(keep, got)]
    late = [jnp.where(first, other, mine) for mine, other in zip(keep, got)]
    pack(out_ref, early[0] + late[0], jnp.exp(late[0]) * early[1] + late[1])


def weights_kernel(after_ref, up_hbm, down_hbm, up_ref, down_ref, sems):
    for load in copies(sems, (up_hbm, down_hbm), (up_ref, down_ref)):
        load.wait()


def span_kernel(*rest):
    ins, out_ref, block_ref = rest[:-2], rest[-2], rest[-1]
    for mask, part in enumerate(ins):
        block_ref[chip_index() ^ mask] = part[...]
    total, state = unpacked(block_ref[0])
    for chip in range(1, len(ins)):
        here, own = unpacked(block_ref[chip])
        total, state = total + here, jnp.exp(here) * state + own
    pack(out_ref, total, state)


def before_kernel(chips, parts, flat, after_a, after_b, keep_ref, got_ref, *rest):
    ins, (mine_ref, send_ref, chip_ref, part_ref) = rest[:-4], rest[-4:]
    first = core_index() == 0
    totals, states = (jnp.where(first, k, g) for k, g in zip(unpacked(keep_ref[...]), unpacked(got_ref[...])))
    place = chip_index()
    if flat:
        place = lax.axis_index("seq") * (lax.axis_size("exp") // 2) + place
    for mask in range(chips):
        chip_ref[place ^ mask] = ins[mask][...]
    for mask in range(parts):
        part_ref[lax.axis_index("seq") ^ mask] = ins[chips + mask][...]
    carry = jnp.zeros(states.shape, F32)
    for ref, count, own in ((part_ref, parts, lax.axis_index("seq")), (chip_ref, chips, place)):
        for index in range(count - 1):
            total, state = unpacked(ref[index])
            carry = jnp.where(index < own, jnp.exp(total) * carry + state, carry)
    later = jnp.exp(totals) * carry + states
    mine_ref[...] = jnp.where(first, carry, later).astype(BF16)
    send_ref[...] = jnp.where(first, later, carry).astype(BF16)


def inside_kernel(x_hbm, z_hbm, b_hbm, c_hbm, dt_hbm, a_hbm, d_hbm, local_ref, grown_ref, c_ref, *scratch):
    x_ref, z_ref, b_ref, dt_ref, a_ref, d_ref, sems = scratch
    loads = copies(
        sems,
        (dt_hbm, a_hbm, d_hbm, b_hbm, c_hbm, x_hbm, z_hbm),
        (dt_ref, a_ref, d_ref, b_ref, c_ref, x_ref, z_ref),
    )
    for load in loads:
        load.wait()
    step_rows, cum_rows = decays(dt_ref[...], a_ref[...])
    cum = cum_rows.T
    grown = jnp.exp(cum)
    length = cum.shape[0]
    pairs = x_ref.shape[1] // LANES
    groups = b_ref.shape[1] // STATE
    row = lax.broadcasted_iota(jnp.int32, (length, length), 0)
    col = lax.broadcasted_iota(jnp.int32, (length, length), 1)
    lane = lax.broadcasted_iota(jnp.int32, (length, LANES), 1)
    for group in range(groups):
        span = slice(group * STATE, (group + 1) * STATE)
        scores = lax.dot_general(c_ref[:, span], b_ref[:, span], NT, preferred_element_type=F32)
        scores = jnp.where(row >= col, scores, 0.0)
        for pair in range(group * pairs // groups, (group + 1) * pairs // groups):
            at = slice(pair * LANES, (pair + 1) * LANES)
            x_pair = x_ref[:, at]
            halves = []
            for head in (2 * pair, 2 * pair + 1):
                distance = cum[:, head : head + 1] - cum_rows[head : head + 1, :]
                decay = jnp.exp(jnp.where(row >= col, distance, FAR))
                mixing = (scores * (decay * step_rows[head : head + 1, :])).astype(BF16)
                halves.append(jnp.dot(mixing, x_pair, preferred_element_type=F32))
            inside = jnp.where(lane < HEAD_DIM, halves[0], halves[1])
            skip = pair_lanes(d_ref[...], pair) * x_pair.astype(F32)
            z = z_ref[:, at].astype(F32)
            gate = z / (1.0 + jnp.exp(-z))
            local_ref[:, at] = (inside + skip) * gate
            grown_ref[:, at] = pair_lanes(grown, pair) * gate


def projection_kernel(norm_hbm, w_hbm, norm_ref, w_ref, sems):
    for load in copies(sems, (norm_hbm, w_hbm), (norm_ref, w_ref)):
        load.wait()


def prep_kernel(experts, width, after_ref, resid_hbm, routes_hbm, gates_hbm, gain_hbm, *rest):
    gate_ref, resid_ref, gain_ref, routes_ref, gates_ref, sems = rest
    loads = copies(
        sems,
        (routes_hbm, gates_hbm, resid_hbm, gain_hbm),
        (routes_ref, gates_ref, resid_ref, gain_ref.at[0]),
    )
    loads[0].wait()
    loads[1].wait()
    count, extent = gate_ref.shape
    start = width // LANES * LANES
    lane = lax.broadcasted_iota(jnp.int32, (extent, count), 0) + start - width
    expert = jnp.where(lane >= experts, lane - experts, lane)
    gate = jnp.zeros((extent, count), F32)
    for pick in range(routes_ref.shape[0]):
        gate = gate + jnp.where(routes_ref[pick] == expert, gates_ref[pick], 0.0)
    high = gate.astype(BF16).astype(F32)
    gate = jnp.where(lane < experts, high, jnp.where(lane < 2 * experts, gate - high, 0.0))
    gate_ref[...] = gate.T.astype(BF16)
    for load in loads[2:]:
        load.wait()


def half_product(half, local_ref, grown_ref, c_ref, norm_ref, w_ref, state_ref, normed_ref, count):
    pairs = state_ref.shape[0]
    width = pairs * LANES
    base = pl.multiple_of(half * width, width)
    groups = c_ref.shape[1] // STATE // 2
    per_group = pairs // groups
    for group in range(groups):
        c_group = c_ref[:, pl.ds(pl.multiple_of((half * groups + group) * STATE, STATE), STATE)]
        gated, squares = [], 0.0
        for pair in range(group * per_group, (group + 1) * per_group):
            span = pl.ds(pl.multiple_of(base + pair * LANES, LANES), LANES)
            carried = jnp.dot(c_group, state_ref[pair], preferred_element_type=F32)
            value = local_ref[:, span] + grown_ref[:, span] * carried
            gated.append(value)
            squares = squares + value * value
        mean = jnp.sum(squares, axis=1, keepdims=True) / (per_group * LANES)
        inverse = lax.rsqrt(mean + 1e-05)
        for offset, value in enumerate(gated):
            pair = group * per_group + offset
            gain = norm_ref[:, pl.ds(pl.multiple_of(base + pair * LANES, LANES), LANES)]
            normed_ref[:, pair * LANES : (pair + 1) * LANES] = (value * inverse * gain).astype(BF16)
    rows = normed_ref.shape[0] // count
    blocks = []
    for shift in range(count):
        owner = lax.axis_index("head") ^ (head_offset(shift - 1, count) if shift else 0)
        blocks.append(normed_ref[pl.ds(pl.multiple_of(owner * rows, rows), rows), :])
    weight = w_ref[:, pl.ds(base, width)]
    return lax.dot_general(jnp.concatenate(blocks, axis=0), weight, NT, preferred_element_type=F32)


def first_half_kernel(count, local_ref, grown_ref, c_ref, norm_ref, w_ref, mine_ref, out_ref, normed_ref):
    out_ref[...] = half_product(
        core_index(), local_ref, grown_ref, c_ref, norm_ref, w_ref, mine_ref, normed_ref, count
    )


def mixed_kernel(after_up, after_down, local_ref, grown_ref, c_ref, norm_ref, w_ref, got_ref, first_ref, *rest):
    outs, normed_ref = rest[:-1], rest[-1]
    product = first_ref[...] + half_product(
        1 - core_index(), local_ref, grown_ref, c_ref, norm_ref, w_ref, got_ref, normed_ref, len(outs)
    )
    rows = outs[0].shape[0]
    for shift, out in enumerate(outs):
        out[...] = product[shift * rows : (shift + 1) * rows].astype(BF16)


def relay_kernel(own_ref, got_ref, out_ref):
    got = jnp.where(core_index() == 0, got_ref[...].astype(F32), 0.0)
    out_ref[...] = (own_ref[...].astype(F32) + got).astype(BF16)


def rows_kernel(after_ref, resid_ref, gate_ref, gain_ref, *rest):
    parts, hidden_ref, rows_ref = rest[:-2], rest[-2], rest[-1]
    mixed = parts[0][...].astype(F32)
    for at, part in enumerate(parts[1:]):
        value = part[...].astype(F32)
        if at == 0 and len(parts) == 4:
            value = jnp.where(core_index() == 1, value, 0.0)
        mixed = mixed + value
    hidden = (resid_ref[0].astype(F32) + mixed).astype(BF16)
    hidden_ref[...] = hidden
    value = hidden.astype(F32)
    scale = lax.rsqrt(jnp.mean(value * value, axis=1, keepdims=True) + 1e-05)
    width = value.shape[1]
    rows_ref[:, width // LANES * LANES :] = gate_ref[...]
    rows_ref[:, :width] = (value * scale * gain_ref[...]).astype(BF16)


def expert_kernel(experts, count, carried, up_ref, down_ref, other_up_ref, other_down_ref, *rest):
    ins, done, outs = rest[:count], rest[count : count + len(carried)], rest[count + len(carried) :]
    width = up_ref.shape[2]
    start = width // LANES * LANES
    rows = jnp.concatenate([ref[:, :width] for ref in ins], axis=0)
    tail = jnp.concatenate([ref[:, start:] for ref in ins], axis=0).astype(F32)
    lane = lax.broadcasted_iota(jnp.int32, tail.shape, 1) + start - width
    own = lax.axis_index("head") * lax.axis_size("exp") + lax.axis_index("exp")
    other = own + 1 - 2 * core_index()
    total = 0.0
    for expert, up_of, down_of in ((own, up_ref, down_ref), (other, other_up_ref, other_down_ref)):
        up = lax.dot_general(rows, up_of[0], NT, preferred_element_type=F32)
        up = jnp.maximum(up, 0.0)
        activated = (up * up).astype(BF16)
        chosen = (lane == expert) | (lane == expert + experts)
        gate = jnp.sum(jnp.where(chosen, tail, 0.0), axis=1, keepdims=True)
        total = total + jnp.dot(activated, down_of[0], preferred_element_type=F32) * gate
    size = ins[0].shape[0]
    for at, out in enumerate(outs):
        out[0:size] = total[at * size : (at + 1) * size].astype(BF16)
    for at, ref in zip(carried, done):
        outs[at][size:] = ref[...]


def sum_kernel(*refs):
    rows = refs[-1].shape[0]
    total = refs[0][...].astype(F32)
    for ref in refs[1:-1]:
        total = total + ref[0:rows].astype(F32)
    refs[-1][...] = total.astype(BF16)


def last_kernel(hidden_ref, *rest):
    parts, out_ref = rest[:-1], rest[-1]
    rows = out_ref.shape[1]
    total = parts[0][...].astype(F32)
    for part in parts[1:]:
        total = total + part[part.shape[0] - rows :].astype(F32)
    out_ref[0] = (hidden_ref[...].astype(F32) + total).astype(BF16)


def swap(value, axis, mask):
    size = lax.axis_size(axis)
    return lax.ppermute(value, axis, [(i, i ^ mask) for i in range(size)])


def swap_slot(value, slot):
    heads, size = lax.axis_size("head"), lax.axis_size("exp")
    order = targets(heads)
    pairs = []
    for i in range(heads * size):
        head, exp = i // size, i % size
        pairs.append((i, (head ^ order[exp % 2][slot]) * size + exp))
    return lax.ppermute(value, ("head", "exp"), pairs)


def per_device(
    x_in, z_in, b_in, c_in, dt_in, a_log, d_skip, norm_w, w_out, resid, routes, gates, moe_gain, w_up, w_down
):
    length, heads = dt_in.shape
    channels = x_in.shape[1]
    model = w_out.shape[1]
    hidden_units = w_up.shape[2]
    seq_size, head_size, exp_size = lax.axis_size("seq"), lax.axis_size("head"), lax.axis_size("exp")
    chips = exp_size // 2
    rows = resid.shape[1]
    experts = head_size * exp_size
    pairs = channels // LANES
    half = pairs // 2
    dt_rows, a_row, d_row = dt_in.T, a_log[None], d_skip[None]
    dma = pltpu.SemaphoreType.DMA
    packed = struct((half * STATE + TILE, LANES), BF16)

    keep, send = call(
        state_kernel,
        "state",
        [packed, packed],
        [(HBM, x_in), (HBM, b_in), (HBM, dt_rows), (HBM, a_row)],
        [pltpu.VMEM(x_in.shape, BF16), pltpu.VMEM(b_in.shape, BF16), pltpu.VMEM(dt_rows.shape, F32),
         pltpu.VMEM(a_row.shape, F32), pltpu.VMEM((2, half * STATE + TILE, LANES), BF16), dma((4,))],
        megabytes=16,
    )
    local, grown, c_held = call(
        inside_kernel,
        "inside",
        [struct((length, channels), F32), struct((length, channels), F32), struct(c_in.shape, BF16)],
        [(HBM, value) for value in (x_in, z_in, b_in, c_in, dt_rows, a_row, d_row)],
        [pltpu.VMEM(x_in.shape, BF16), pltpu.VMEM(z_in.shape, BF16), pltpu.VMEM(b_in.shape, BF16),
         pltpu.VMEM(dt_rows.shape, F32), pltpu.VMEM(a_row.shape, F32), pltpu.VMEM(d_row.shape, F32), dma((7,))],
        megabytes=16,
    )
    wide = -(-(model + 2 * experts) // LANES) * LANES
    turned = [jnp.transpose(value, (2, 0, 1)) for value in (routes, gates)]
    norm_held, w_held = call(
        projection_kernel,
        "projection",
        [struct((1, channels), F32), struct((model, channels), BF16)],
        [(HBM, norm_w[None]), (HBM, w_out.T)],
        [dma((2,))],
    )
    gate_lanes, resid_held, gain_held = call(
        functools.partial(prep_kernel, experts, model),
        "prep",
        [struct((rows, wide - model // LANES * LANES), BF16), struct(resid.shape, BF16), struct((1, model), F32)],
        [(ANY, keep)] + [(HBM, value) for value in (resid, *turned, moe_gain)],
        [pltpu.VMEM(turned[0].shape, jnp.int32), pltpu.VMEM(turned[1].shape, F32), dma((4,))],
        megabytes=16,
    )
    up_turned = jnp.swapaxes(w_up, 1, 2)
    got = swap(send, "exp", 1)
    chip = call(chip_state_kernel, "chip_state", packed, [(ANY, gate_lanes), (VMEM, keep), (VMEM, got)])
    chip, up_after, down_after = lax.optimization_barrier((chip, up_turned, w_down))
    other_up, other_down = swap(up_after, "exp", 1), swap(down_after, "exp", 1)
    flat = seq_size * chips <= 8
    if flat:
        masks = [x * exp_size + 2 * y for x in range(seq_size) for y in range(chips)]
        exchanged = [chip] + [swap(chip, ("seq", "exp"), mask) for mask in masks[1:]]
        counts = (seq_size * chips, 0)
    else:
        along_y = [chip] + [swap(chip, "exp", 2 * d) for d in range(1, chips)]
        span = call(
            span_kernel,
            "span",
            packed,
            [(VMEM, value) for value in along_y],
            [pltpu.VMEM((chips, *packed.shape), BF16)],
        )
        exchanged = along_y + [span] + [swap(span, "seq", d) for d in range(1, seq_size)]
        counts = (chips, seq_size)
    before, before_send = call(
        functools.partial(before_kernel, *counts, flat),
        "before",
        [struct((half, STATE, LANES), BF16)] * 2,
        [(ANY, norm_held), (ANY, c_held)] + [(VMEM, value) for value in (keep, got, *exchanged)],
        [pltpu.VMEM((counts[0], *packed.shape), BF16), pltpu.VMEM((max(1, counts[1]), *packed.shape), BF16)],
        megabytes=24,
    )
    before_got = swap(before_send, "exp", 1)
    shared = [(VMEM, value) for value in (local, grown, c_held, norm_held, w_held)]
    normed_half = pltpu.VMEM((length, channels // 2), BF16)
    first = call(
        functools.partial(first_half_kernel, head_size),
        "first_half",
        struct((length, model), F32),
        shared + [(VMEM, before)],
        [normed_half],
    )
    mixed = call(
        mixed_kernel,
        "mixed",
        [struct((rows, model), BF16)] * head_size,
        [(ANY, other_up), (ANY, other_down)] + shared + [(VMEM, before_got), (VMEM, first)],
        [normed_half],
    )
    up_held, down_held = call(
        weights_kernel,
        "weights",
        [struct(up_turned.shape, BF16), struct(w_down.shape, BF16)],
        [(ANY, mixed[0]), (HBM, up_turned), (HBM, w_down)],
        [dma((2,))],
    )
    slots = list(range(head_size - 1))
    parts, last = [swap_slot(mixed[k + 1], k) for k in slots[:-1]], mixed[-1]
    if head_size == 4:
        last = call(relay_kernel, "relay", struct((rows, model), BF16), [(VMEM, last), (VMEM, parts[0])])
    parts = [mixed[0]] + parts + [swap_slot(last, slots[-1])]
    hidden, own_rows = call(
        rows_kernel,
        "rows",
        [struct((rows, model), BF16), struct((rows, wide), BF16)],
        [(ANY, up_held)] + [(VMEM, value) for value in (resid_held, gate_lanes, gain_held, *parts)],
    )

    def through_experts(members, carried=()):
        places = [at for at, _ in carried]
        return call(
            functools.partial(expert_kernel, experts, len(members), places),
            "experts",
            [struct((rows * (2 if at in places else 1), model), BF16) for at in range(len(members))],
            [(VMEM, value) for value in (up_held, down_held, other_up, other_down, *members)]
            + [(VMEM, value) for _, value in carried],
            megabytes=16,
        )

    both = ("head", "exp")
    group = [z * exp_size + 2 * d for z in (0, 1) for d in range(chips)][1:]

    def spread(block):
        return [block] + [swap(block, both, mask) for mask in group]

    sets = [spread(swap(own_rows, "head", high)) for high in range(2, head_size, 2)]
    near = through_experts(spread(own_rows))
    near, sets = lax.optimization_barrier((near, sets))
    joined = []
    arrived, later = [], [at for at, mask in enumerate(group, 1) if mask < exp_size]
    apart = [near[at] for at in later]
    for high, members in zip(range(2, head_size, 2), sets):
        pieces = through_experts(members, [(at, near[at]) for at in joined] if high == 2 else ())
        got = [swap(piece, both, mask) for piece, mask in zip(pieces[1:], group)]
        total = call(sum_kernel, "sum", struct((rows, model), BF16), [(VMEM, v) for v in (pieces[0], *got)])
        arrived.append(swap(total, "head", high))
    arrived += [swap(near[at], both, mask) for at, mask in enumerate(group, 1) if mask >= exp_size]
    arrived += [swap(piece, both, group[at - 1]) for piece, at in zip(apart, later)]
    return call(
        last_kernel,
        "last",
        struct(resid.shape, BF16),
        [(VMEM, value) for value in (hidden, near[0], *arrived)],
        pinned=False,
    )


def solution(mesh):
    placed = (
        P(("seq", "exp"), "head"),
        P(("seq", "exp"), "head"),
        P(("seq", "exp"), "head"),
        P(("seq", "exp"), "head"),
        P(("seq", "exp"), "head"),
        P("head"),
        P("head"),
        P("head"),
        P("head", None),
        P(("seq", "exp"), "head", None),
        P(("seq", "exp"), "head", None),
        P(("seq", "exp"), "head", None),
        P(),
        P(("head", "exp"), None, None),
        P(("head", "exp"), None, None),
    )
    return jax.shard_map(
        per_device,
        mesh=mesh,
        in_specs=placed,
        out_specs=P(("seq", "exp"), "head", None),
        check_vma=False,
    )
```
